32 devices in a mesh: dp: 4 (over y, core), gx: 2 (over x), gy: 4 (over z).
Axes of the slice: x: 2, y: 2, z: 4, core: 2. Of those that a mesh axis runs over, the one named last changes fastest.
Arguments:
- inputs: bfloat16 [8, 1024, 2048], P('dp', 'gx', 'gy'), may hold values from -6 to 6
- lengths: int32 [8], P('dp'), may hold values from 384 to 1024, as said below
- attn_gain: bfloat16 [2048], P('gy'), may hold values from 0.5 to 1.5
- ffn_gain: bfloat16 [2048], P('gy'), may hold values from 0.5 to 1.5
- query_key: bfloat16 [2048, 32, 2, 64], P('gy', 'gx'), may hold values from -0.046875 to 0.046875
- value_proj: bfloat16 [2048, 32, 64], P('gy', 'gx'), may hold values from -0.125 to 0.125
- out_proj: bfloat16 [32, 64, 2048], P('gx', None, 'gy'), may hold values from -1.5 to 1.5
- gate_up: bfloat16 [2048, 32, 2, 160], P('gy', 'gx'), may hold values from -0.125 to 0.125
- down_proj: bfloat16 [32, 160, 2048], P('gx', None, 'gy'), may hold values from -0.078125 to 0.078125
- bias_table: bfloat16 [32, 32], P(None, ('gx', 'gy')), may hold values from -5 to 5
- cotangent: bfloat16 [8, 1024, 2048], P('dp', 'gx', 'gy'), may hold values from -6 to 6
Outputs:
- outputs: bfloat16 [8, 1024, 2048], P('dp', 'gx', 'gy')
- input_grad: float32 [8, 1024, 2048], P('dp', 'gx', 'gy')
- attn_gain_grad: float32 [2048], P('gy')
- ffn_gain_grad: float32 [2048], P('gy')
- query_key_grad: float32 [2048, 32, 2, 64], P('gy', 'gx')
- value_grad: float32 [2048, 32, 64], P('gy', 'gx')
- out_proj_grad: float32 [32, 64, 2048], P('gx', None, 'gy')
- gate_up_grad: float32 [2048, 32, 2, 160], P('gy', 'gx')
- down_grad: float32 [32, 160, 2048], P('gx', None, 'gy')
- table_grad: float32 [32, 32], P(None, ('gx', 'gy'))
The draws below stay inside these ranges and needn't reach their ends.
Inputs may be any that keep to these rules, and one draw needn't show every extreme that they name: lengths[s] counts the live leading slots of sequence s; one sequence has exactly 1024 and another exactly 384.
All inputs are finite; a program needn't handle non-finite values.
Results may differ from the reference program's by a relative error of at most 0.018.
Values may be sent and summed in bfloat16 or wider, within the bound.
No kernel may reach another device: no remote copies, remote signals or barrier semaphores. Data moves between devices by JAX's collectives and lax.ppermute only.
A program may use at most 256 MiB of HBM per device.

```python
import jax
import jax.numpy as jnp
from jax import lax

D = 2048
H = 32
HEAD = 64
FF = 5120
BUCKETS = 32
UNIT = 160
G = 32
L = 1024
MIN_LEN = 384
QBLK = 512
SEQS = 8


def draw_lengths(key, part):
    drawn_lengths = jax.random.randint(jax.random.fold_in(key, 11), (SEQS,), MIN_LEN, L + 1)
    longest = jax.random.randint(jax.random.fold_in(key, 12), (), 0, SEQS)
    shortest = (longest + 1) % SEQS
    positions = jnp.arange(SEQS)
    drawn_lengths = jnp.where(positions == longest, L, drawn_lengths)
    return jnp.where(positions == shortest, MIN_LEN, drawn_lengths).astype(jnp.int32)


def level_of(rng, extent, cuts, low, high):
    gain = 1.0
    for position, parts in cuts:
        steps = jax.random.uniform(jax.random.fold_in(jax.random.fold_in(rng, 6), position), (parts,), jnp.float32, low / len(cuts), high / len(cuts))
        gain = gain * jnp.repeat(jnp.exp(steps), extent[position] // parts).reshape((-1,) + (1,) * (len(extent) - 1 - position))
    return gain


def noise(rng, dims, width, limit, pieces=(), kind=jnp.bfloat16):
    drawn = jax.random.normal(rng, dims, jnp.float32) * width
    if len(pieces) > 0:
        drawn = level_of(rng, dims, pieces, -0.22, 0.18) * drawn
    return jnp.clip(drawn, min=-limit, max=limit).astype(kind)


def setup_inputs(seed: int = 0) -> dict:
    seeds = jax.random.split(jax.random.key(seed), 12)
    inputs = noise(seeds[0], (SEQS, L, D), 1.0, 6.0, ((0, 4), (1, 2), (2, 4)))
    lengths = draw_lengths(jax.random.fold_in(seeds[11], 71), 0)
    attn_gain = jnp.clip(1.0 + 0.1 * jax.random.normal(seeds[2], (D,), jnp.float32), 0.5, 1.5).astype(jnp.bfloat16)
    ffn_gain = jnp.clip(1.0 + 0.1 * jax.random.normal(seeds[3], (D,), jnp.float32), 0.5, 1.5).astype(jnp.bfloat16)
    query_key = noise(seeds[4], (D, H, 2, HEAD), (8 * D) ** -0.5, 0.046875, ((0, 4), (1, 2)))
    value_proj = noise(seeds[5], (D, H, HEAD), D ** -0.5, 0.125, ((0, 4), (1, 2)))
    out_proj = noise(seeds[6], (H, HEAD, D), (8 * H * HEAD // L) ** -0.5, 1.5, ((0, 2), (2, 4)))
    gate_up = noise(seeds[7], (D, G, 2, UNIT), D ** -0.5, 0.125, ((0, 4), (1, 2)))
    down_proj = noise(seeds[8], (G, UNIT, D), FF ** -0.5, 0.078125, ((0, 2), (2, 4)))
    bias_table = noise(seeds[9], (BUCKETS, H), 1.0, 5.0, ((1, 8),))
    cotangent = noise(seeds[10], (SEQS, L, D), 1.0, 6.0, ((0, 4), (1, 2), (2, 4)))
    return dict(inputs=inputs, lengths=lengths, attn_gain=attn_gain, ffn_gain=ffn_gain, query_key=query_key, value_proj=value_proj, out_proj=out_proj, gate_up=gate_up, down_proj=down_proj, bias_table=bias_table, cotangent=cotangent)


norm_eps = 1e-06
masked_score = -1e+30
bucket_edges = (12, 16, 23, 32, 46, 64, 91)
highest = lax.Precision.HIGHEST

@jax.custom_vjp
def low(v):
    return lax.optimization_barrier(v.astype(jnp.bfloat16)).astype(jnp.float32)

@jax.custom_vjp
def low_back(v):
    return v

def low_keep(v):
    return (low(v), None)

def low_pass(kept, grad):
    return (grad,)

def back_keep(v):
    return (v, None)

def back_low(kept, grad):
    return (low(grad),)
low.defvjp(low_keep, low_pass)
low_back.defvjp(back_keep, back_low)

def bucket_index(offset):
    magnitude = jnp.abs(offset)
    far_bucket = 8 + sum(((magnitude >= boundary).astype(jnp.int32) for boundary in bucket_edges))
    near_bucket = jnp.where(magnitude < 8, magnitude, far_bucket)
    return near_bucket + 16 * (offset > 0).astype(jnp.int32)

def encoder_layer(tokens, length, attn_gain, ffn_gain, query_key, value_proj, out_proj, gate_up, down_proj, bias_table):
    slot_ids = jnp.arange(L, dtype=jnp.int32)
    live_rows = (slot_ids < length).astype(jnp.float32)[:, None]
    key_live = (slot_ids < length)[None, None, :]
    scale_one = lax.rsqrt(lax.optimization_barrier(jnp.mean(tokens * tokens, axis=1, keepdims=True)) + norm_eps)
    normed = low(tokens * scale_one * attn_gain)
    stacked = jnp.concatenate([query_key, value_proj[:, :, None, :]], axis=2)
    projected = low_back(low(jnp.einsum('td,dhcs->thcs', normed, stacked, precision=highest)))
    queries = projected[:, :, 0]
    key_vecs = projected[:, :, 1]
    value_vecs = projected[:, :, 2]

    def attend(first_row):
        row_ids = first_row + jnp.arange(QBLK, dtype=jnp.int32)
        block_queries = lax.dynamic_slice_in_dim(queries, first_row, QBLK, 0)
        offsets = slot_ids[None, :] - row_ids[:, None]
        position_bias = jnp.transpose(bias_table[bucket_index(offsets)], (2, 0, 1))
        scores = low_back(jnp.einsum('qhs,khs->hqk', block_queries, key_vecs, precision=highest) + position_bias)
        scores = jnp.where(key_live, scores, masked_score)
        weights = jax.nn.softmax(scores, axis=-1)
        return jnp.einsum('hqk,khs->qhs', low(weights), value_vecs, precision=highest)
    starts = jnp.arange(0, L, QBLK, dtype=jnp.int32)
    attended = lax.map(jax.checkpoint(attend), starts).reshape(L, H, HEAD)
    heads_out = low_back(low(attended))
    attn_branch = jnp.einsum('ths,hsd->td', heads_out, out_proj, precision=highest)
    hidden = tokens + low_back(attn_branch)
    scale_two = lax.rsqrt(lax.optimization_barrier(jnp.mean(hidden * hidden, axis=1, keepdims=True)) + norm_eps)
    normed_two = low(hidden * scale_two * ffn_gain)
    gate_and_up = low_back(jnp.einsum('td,dgcu->tgcu', normed_two, gate_up, precision=highest))
    activated = low(jax.nn.gelu(gate_and_up[:, :, 0], approximate=True) * gate_and_up[:, :, 1])
    ffn_branch = jnp.einsum('tgu,gud->td', activated, down_proj, precision=highest)
    return live_rows * (hidden + ffn_branch)

def reference(inputs, lengths, attn_gain, ffn_gain, query_key, value_proj, out_proj, gate_up, down_proj, bias_table, cotangent):
    params = (attn_gain.astype(jnp.float32), ffn_gain.astype(jnp.float32), query_key.astype(jnp.float32), value_proj.astype(jnp.float32), out_proj.astype(jnp.float32), gate_up.astype(jnp.float32), down_proj.astype(jnp.float32), bias_table.astype(jnp.float32))

    def full_pass(tokens_all, *weight_set):

        def one_sequence(scan_carry, sequence_item):
            return (scan_carry, jax.checkpoint(encoder_layer)(sequence_item[0], sequence_item[1], *weight_set))
        _, result = lax.scan(one_sequence, jnp.zeros((), jnp.float32), (tokens_all, lengths))
        return result
    result, pullback = jax.vjp(full_pass, inputs.astype(jnp.float32), *params)
    gradients = pullback(cotangent.astype(jnp.float32))
    return (result.astype(jnp.bfloat16), gradients[0], gradients[1], gradients[2], gradients[3], gradients[4], gradients[5], gradients[6], gradients[7], gradients[8])
```

```python
import functools
import math

import jax
import jax.numpy as jnp
from jax import lax
from jax.experimental import pallas as pl
from jax.experimental.pallas import tpu as pltpu
from jax.sharding import Mesh
from jax.sharding import PartitionSpec as P

norm_eps = 1e-06
masked_score = -1e30
bucket_edges = (12, 16, 23, 32, 46, 64, 91)
BF = jnp.bfloat16
F32 = jnp.float32
LB = 128
VMEM = 60 * 1024 * 1024
swap = [(0, 1), (1, 0)]
gelu_a = math.sqrt(2.0 / math.pi)
gelu_b = 0.044715


def bucket_index(offset):
    magnitude = jnp.abs(offset)
    far_bucket = 8 + sum(((magnitude >= boundary).astype(jnp.int32) for boundary in bucket_edges))
    near_bucket = jnp.where(magnitude < 8, magnitude, far_bucket)
    return near_bucket + 16 * (offset > 0).astype(jnp.int32)


def cost(flops, moved):
    return pl.CostEstimate(flops=int(flops), bytes_accessed=int(moved), transcendentals=0)


def params(steps):
    return pltpu.CompilerParams(
        dimension_semantics=("arbitrary",) * steps, vmem_limit_bytes=VMEM
    )


def dot_nt(a, b):
    return lax.dot_general(a, b, (((1,), (1,)), ((), ())), preferred_element_type=F32)


def dot_nn(a, b):
    return lax.dot_general(a, b, (((1,), (0,)), ((), ())), preferred_element_type=F32)


def nt_kernel(act_ref, w_ref, out_ref):
    nz, total, _ = act_ref.shape
    for m in range(0, total, 256):
        acc = dot_nt(act_ref[0, m : m + 256], w_ref[0, 0])
        for z in range(1, nz):
            acc += dot_nt(act_ref[z, m : m + 256], w_ref[z, 0])
        out_ref[m : m + 256, :] = acc.astype(BF)


def mm_nt(act, w, first, rows):
    nz, total, width = act.shape
    nc = w.shape[1]
    if rows % 256:
        part = lax.slice_in_dim(w, first, first + rows, axis=2)
        out = jnp.einsum("ztf,zcrf->tcr", act, part, preferred_element_type=F32)
        return out.astype(BF).reshape(total, nc * rows)
    count, skip = rows // 256, first // 256
    return pl.pallas_call(
        nt_kernel,
        grid=(nc, count),
        in_specs=[
            pl.BlockSpec((nz, total, width), lambda c, i: (0, 0, 0)),
            pl.BlockSpec((nz, 1, 256, width), lambda c, i: (0, c, skip + i, 0)),
        ],
        out_specs=pl.BlockSpec((total, 256), lambda c, i: (0, c * count + i)),
        out_shape=jax.ShapeDtypeStruct((total, nc * rows), BF),
        compiler_params=params(2),
        cost_estimate=cost(
            2 * nz * total * width * nc * rows, 2 * nz * width * (total + nc * rows) + 2 * total * nc * rows
        ),
        name="product_nt",
    )(act, w)


def nn_kernel(grad_ref, w_ref, out_ref):
    total = grad_ref.shape[0]
    nc, rows = w_ref.shape[1], w_ref.shape[2]
    for m in range(0, total, 256):
        acc = dot_nn(grad_ref[m : m + 256, :rows], w_ref[0, 0])
        for c in range(1, nc):
            acc += dot_nn(grad_ref[m : m + 256, c * rows : (c + 1) * rows], w_ref[0, c])
        out_ref[0, m : m + 256] = acc.astype(BF)


def mm_nn(grad, w, first, rows):
    total = grad.shape[0]
    nz, nc, _, width = w.shape
    if rows % 128:
        part = lax.slice_in_dim(w, first, first + rows, axis=2)
        out = jnp.einsum(
            "tcr,zcrf->ztf", grad.reshape(total, nc, rows), part, preferred_element_type=F32
        )
        return out.astype(BF)
    skip = first // rows
    return pl.pallas_call(
        nn_kernel,
        grid=(nz,),
        in_specs=[
            pl.BlockSpec((total, nc * rows), lambda z: (0, 0)),
            pl.BlockSpec((1, nc, rows, width), lambda z: (z, 0, skip, 0)),
        ],
        out_specs=pl.BlockSpec((1, total, width), lambda z: (z, 0, 0)),
        out_shape=jax.ShapeDtypeStruct((nz, total, width), BF),
        compiler_params=params(1),
        cost_estimate=cost(
            2 * nz * total * width * nc * rows, 2 * nz * width * (total + nc * rows) + 2 * total * nc * rows
        ),
        name="product_nn",
    )(grad, w)


def tn_kernel(grad_ref, act_ref, out_ref):
    turned = grad_ref[...].T
    for z in range(act_ref.shape[0]):
        out_ref[z] = dot_nn(turned, act_ref[z]).astype(BF)


def mm_tn(grad, act):
    total, rows = grad.shape
    nz, _, width = act.shape
    if rows % 256:
        return jnp.einsum("tr,ztf->zrf", grad, act, preferred_element_type=F32).astype(BF)
    return pl.pallas_call(
        tn_kernel,
        grid=(rows // 256,),
        in_specs=[
            pl.BlockSpec((total, 256), lambda i: (0, i)),
            pl.BlockSpec((nz, total, width), lambda i: (0, 0, 0)),
        ],
        out_specs=pl.BlockSpec((nz, 256, width), lambda i: (0, i, 0)),
        out_shape=jax.ShapeDtypeStruct((nz, rows, width), BF),
        compiler_params=params(1),
        cost_estimate=cost(
            2 * nz * total * width * rows, 2 * nz * width * (total + rows) + 2 * total * rows
        ),
        name="product_tn",
    )(grad, act)


def gelu_parts(gate):
    curve = jnp.tanh(gelu_a * (gate + gelu_b * gate * gate * gate))
    value = 0.5 * gate * (1.0 + curve)
    slope = 0.5 * (1.0 + curve) + 0.5 * gate * (1.0 - curve * curve) * gelu_a * (
        1.0 + 3.0 * gelu_b * gate * gate
    )
    return value, slope


def ffn_in_kernel(act_ref, w_ref, gu_ref, active_ref):
    nz, total, _ = act_ref.shape
    half = active_ref.shape[1]
    for m in range(0, total, 256):
        acc = dot_nt(act_ref[0, m : m + 256], w_ref[0, 0])
        for z in range(1, nz):
            acc += dot_nt(act_ref[z, m : m + 256], w_ref[z, 0])
        gu_ref[m : m + 256, :] = acc.astype(BF)
        gate = acc[:, :half]
        value = 0.5 * gate * (1.0 + jnp.tanh(gelu_a * (gate + gelu_b * gate * gate * gate)))
        active_ref[m : m + 256, :] = (value * acc[:, half:]).astype(BF)


def ffn_in(act, w):
    nz, total, width = act.shape
    nc, rows = w.shape[1], w.shape[2]
    half = rows // 2
    if half % 128:
        gate_up = jnp.einsum("ztf,zcrf->tcr", act, w, preferred_element_type=F32)
        value, _ = gelu_parts(gate_up[:, :, :half])
        active = (value * gate_up[:, :, half:]).astype(BF)
        return gate_up.astype(BF).reshape(total, nc * rows), active.reshape(total, nc * half)
    block = total // 2
    return pl.pallas_call(
        ffn_in_kernel,
        grid=(nc, 2),
        in_specs=[
            pl.BlockSpec((nz, block, width), lambda c, m: (0, m, 0)),
            pl.BlockSpec((nz, 1, rows, width), lambda c, m: (0, c, 0, 0)),
        ],
        out_specs=[
            pl.BlockSpec((block, rows), lambda c, m: (m, c)),
            pl.BlockSpec((block, half), lambda c, m: (m, c)),
        ],
        out_shape=[
            jax.ShapeDtypeStruct((total, nc * rows), BF),
            jax.ShapeDtypeStruct((total, nc * half), BF),
        ],
        compiler_params=params(2),
        cost_estimate=cost(
            2 * nz * total * width * nc * rows, 2 * nz * width * (total + nc * rows) + 3 * total * nc * rows
        ),
        name="ffn_in",
    )(act, w)


def ffn_back_kernel(grad_ref, w_ref, gu_ref, out_ref):
    nz, total, _ = grad_ref.shape
    half = w_ref.shape[2]
    for m in range(0, total, 256):
        acc = dot_nt(grad_ref[0, m : m + 256], w_ref[0, 0])
        for z in range(1, nz):
            acc += dot_nt(grad_ref[z, m : m + 256], w_ref[z, 0])
        gate = gu_ref[m : m + 256, :half].astype(F32)
        up = gu_ref[m : m + 256, half:].astype(F32)
        value, slope = gelu_parts(gate)
        out_ref[m : m + 256, :half] = (acc * up * slope).astype(BF)
        out_ref[m : m + 256, half:] = (acc * value).astype(BF)


def ffn_back(grad, w, gate_up):
    nz, total, width = grad.shape
    nc, half = w.shape[1], w.shape[2]
    if half % 128:
        grad_act = jnp.einsum("ztf,zcrf->tcr", grad, w, preferred_element_type=F32)
        kept = gate_up.astype(F32).reshape(total, nc, 2 * half)
        value, slope = gelu_parts(kept[:, :, :half])
        both = jnp.concatenate([grad_act * kept[:, :, half:] * slope, grad_act * value], axis=2)
        return both.astype(BF).reshape(total, nc * 2 * half)
    block = total // 2
    return pl.pallas_call(
        ffn_back_kernel,
        grid=(nc, 2),
        in_specs=[
            pl.BlockSpec((nz, block, width), lambda c, m: (0, m, 0)),
            pl.BlockSpec((nz, 1, half, width), lambda c, m: (0, c, 0, 0)),
            pl.BlockSpec((block, 2 * half), lambda c, m: (m, c)),
        ],
        out_specs=pl.BlockSpec((block, 2 * half), lambda c, m: (m, c)),
        out_shape=jax.ShapeDtypeStruct((total, nc * 2 * half), BF),
        compiler_params=params(2),
        cost_estimate=cost(
            2 * nz * total * width * nc * half, 2 * nz * width * (total + nc * half) + 8 * total * nc * half
        ),
        name="ffn_back",
    )(grad, w, gate_up)


def near_buckets(tile, total):
    first = (total // LB - 2 + tile) * LB
    rows = lax.broadcasted_iota(jnp.int32, (LB, LB), 0)
    lanes = lax.broadcasted_iota(jnp.int32, (LB, LB), 1)
    return bucket_index(first + rows - (total - LB) - lanes)


def build_strips(table_ref, strip_ref, total, group):
    heads = strip_ref.shape[0]
    near = (total // LB - 2) * LB
    for h in range(heads):
        head = group * heads + h
        strip_ref[h, :near] = jnp.full((near, LB), table_ref[head, 15], F32)
        strip_ref[h, near + 3 * LB :] = jnp.full((near, LB), table_ref[head, 31], F32)

    def one_tile(tile, _):
        index = near_buckets(tile, total)
        vals = [jnp.full((LB, LB), table_ref[group * heads + h, 0], F32) for h in range(heads)]
        for b in range(1, 32):
            hit = index == b
            vals = [
                jnp.where(hit, table_ref[group * heads + h, b], vals[h]) for h in range(heads)
            ]
        for h in range(heads):
            strip_ref[h, pl.ds(pl.multiple_of(near + tile * LB, LB), LB)] = vals[h]
        return 0

    lax.fori_loop(0, 3, one_tile, 0)


def head_lanes(shape, h):
    lanes = lax.broadcasted_iota(jnp.int32, shape, 1)
    return lanes // 64 == h, lanes == ((h + 1) % 4) * 64


def mask_keys(keys, length, h):
    own, spare = head_lanes(keys.shape, h)
    dead = lax.broadcasted_iota(jnp.int32, keys.shape, 0) >= length
    mask = jnp.where(jnp.logical_and(spare, dead), masked_score, 0.0)
    return jnp.where(own, keys.astype(F32), mask).astype(BF)


def with_one(queries, h):
    _, spare = head_lanes(queries.shape, h)
    return jnp.where(spare, 1.0, queries.astype(F32)).astype(BF)


def own_lanes(values, h):
    own, _ = head_lanes(values.shape, h)
    return jnp.where(own, values.astype(F32), 0.0).astype(BF)


def block_bias(strip_ref, h, block, total):
    first = total - LB - 2 * block * LB
    left = strip_ref[h, pl.ds(pl.multiple_of(first, LB), total)]
    right = strip_ref[h, pl.ds(pl.multiple_of(first - LB, LB), total)]
    return jnp.concatenate([left, right], axis=1)


def attend_kernel(length_ref, table_ref, q_ref, k_ref, v_ref, out_ref, lse_ref, strip, heads_k, turned_v, turned_out):
    total = q_ref.shape[0]
    heads = strip.shape[0]
    build_strips(table_ref, strip, total, pl.program_id(0))
    turned_v[...] = v_ref[...].astype(F32).T.astype(BF)
    for h in range(heads):
        heads_k[h] = mask_keys(k_ref[...], length_ref[0], h)

    def one_block(block, _):
        spot = pl.ds(pl.multiple_of(block * 256, 256), 256)
        queries = q_ref[spot]
        for h in range(heads):
            scores = dot_nt(heads_k[h], with_one(queries, h)) + block_bias(strip, h, block, total)
            largest = jnp.max(scores, axis=0, keepdims=True)
            raised = jnp.exp(scores - largest)
            totals = jnp.sum(raised, axis=0, keepdims=True)
            out = dot_nn(turned_v[h * 64 : (h + 1) * 64], raised.astype(BF))
            turned_out[h * 64 : (h + 1) * 64, spot] = out * (1.0 / totals)
            lse_ref[0, h : h + 1, spot] = largest + jnp.log(totals)
        return 0

    lax.fori_loop(0, total // 256, one_block, 0)
    out_ref[...] = turned_out[...].T.astype(BF)


def attend_back_kernel(
    length_ref, table_ref, q_ref, k_ref, v_ref, grad_ref, lse_ref, out_ref, table_grad_ref,
    strip, strip_grad, heads_k, turned_k, turned_q, ds_ref, p_ref, dk_ref, dv_ref,
):
    total = q_ref.shape[0]
    heads = strip.shape[0]
    build_strips(table_ref, strip, total, pl.program_id(0))
    strip_grad[...] = jnp.zeros_like(strip_grad)
    dk_ref[...] = jnp.zeros_like(dk_ref)
    dv_ref[...] = jnp.zeros_like(dv_ref)
    turned_k[...] = k_ref[...].astype(F32).T.astype(BF)
    for h in range(heads):
        heads_k[h] = mask_keys(k_ref[...], length_ref[0], h)

    def one_block(block, _):
        spot = pl.ds(pl.multiple_of(block * 256, 256), 256)
        queries, grads = q_ref[spot], grad_ref[spot]
        own_q, own_g = [], []
        for h in range(heads):
            own_q.append(own_lanes(queries, h))
            own_g.append(own_lanes(grads, h))
            scores = dot_nt(heads_k[h], with_one(queries, h)) + block_bias(strip, h, block, total)
            probs = jnp.exp(scores - lse_ref[0, h : h + 1, spot])
            weighed = probs * dot_nt(v_ref[...], own_g[h])
            delta = jnp.sum(weighed, axis=0, keepdims=True)
            grad_scores = weighed - probs * delta
            first = total - LB - 2 * block * LB
            left = pl.ds(pl.multiple_of(first, LB), total)
            right = pl.ds(pl.multiple_of(first - LB, LB), total)
            strip_grad[h, left] += grad_scores[:, :LB]
            strip_grad[h, right] += grad_scores[:, LB:]
            rounded = grad_scores.astype(BF)
            ds_ref[:, h * 256 : (h + 1) * 256] = rounded
            p_ref[:, h * 256 : (h + 1) * 256] = probs.astype(BF)
            turned_q[h * 64 : (h + 1) * 64, spot] = dot_nn(turned_k[h * 64 : (h + 1) * 64], rounded)
        dk_ref[...] += dot_nn(ds_ref[...], jnp.concatenate(own_q, axis=0))
        dv_ref[...] += dot_nn(p_ref[...], jnp.concatenate(own_g, axis=0))
        return 0

    lax.fori_loop(0, total // 256, one_block, 0)
    out_ref[:, :256] = turned_q[...].T.astype(BF)
    out_ref[:, 256:512] = dk_ref[...].astype(BF)
    out_ref[:, 512:] = dv_ref[...].astype(BF)

    near = (total // LB - 2) * LB
    for h in range(heads):
        table_grad_ref[0, h] = jnp.zeros((32, LB), F32)
        table_grad_ref[0, h, 15:16] = jnp.sum(strip_grad[h, :near], axis=0, keepdims=True)
        table_grad_ref[0, h, 31:32] = jnp.sum(strip_grad[h, near + 3 * LB :], axis=0, keepdims=True)

    def one_tile(tile, _):
        index = near_buckets(tile, total)
        spot = pl.ds(pl.multiple_of(near + tile * LB, LB), LB)
        for h in range(heads):
            grads = strip_grad[h, spot]
            for b in range(32):
                picked = jnp.where(index == b, grads, 0.0)
                table_grad_ref[0, h, b : b + 1] += jnp.sum(picked, axis=0, keepdims=True)
        return 0

    lax.fori_loop(0, 3, one_tile, 0)


def block_specs(total):
    return [
        pl.BlockSpec(memory_space=pltpu.SMEM),
        pl.BlockSpec(memory_space=pltpu.SMEM),
        pl.BlockSpec((total, 256), lambda c: (0, 3 * c)),
        pl.BlockSpec((total, 256), lambda c: (0, 3 * c + 1)),
        pl.BlockSpec((total, 256), lambda c: (0, 3 * c + 2)),
    ]


def attend(projected, length, table, groups, heads):
    total = projected.shape[0]
    strip_rows = 2 * total - LB
    return pl.pallas_call(
        attend_kernel,
        grid=(groups,),
        in_specs=block_specs(total),
        out_specs=[
            pl.BlockSpec((total, 256), lambda c: (0, c)),
            pl.BlockSpec((1, 8, total), lambda c: (c, 0, 0)),
        ],
        out_shape=[
            jax.ShapeDtypeStruct((total, groups * 256), BF),
            jax.ShapeDtypeStruct((groups, 8, total), F32),
        ],
        scratch_shapes=[
            pltpu.VMEM((heads, strip_rows, LB), F32),
            pltpu.VMEM((heads, total, 256), BF),
            pltpu.VMEM((256, total), BF),
            pltpu.VMEM((256, total), F32),
        ],
        compiler_params=params(1),
        cost_estimate=cost(groups * heads * total * total * 2 * 256 * 2, 4 * total * groups * 256 * 2),
        name="attend",
    )(length, table, projected, projected, projected)


def attend_back(projected, length, table, grad_out, lse, groups, heads):
    total = projected.shape[0]
    strip_rows = 2 * total - LB
    return pl.pallas_call(
        attend_back_kernel,
        grid=(groups,),
        in_specs=block_specs(total)
        + [
            pl.BlockSpec((total, 256), lambda c: (0, c)),
            pl.BlockSpec((1, 8, total), lambda c: (c, 0, 0)),
        ],
        out_specs=[
            pl.BlockSpec((total, 768), lambda c: (0, c)),
            pl.BlockSpec((1, heads, 32, LB), lambda c: (c, 0, 0, 0)),
        ],
        out_shape=[
            jax.ShapeDtypeStruct((total, groups * 768), BF),
            jax.ShapeDtypeStruct((groups, heads, 32, LB), F32),
        ],
        scratch_shapes=[
            pltpu.VMEM((heads, strip_rows, LB), F32),
            pltpu.VMEM((heads, strip_rows, LB), F32),
            pltpu.VMEM((heads, total, 256), BF),
            pltpu.VMEM((256, total), BF),
            pltpu.VMEM((256, total), F32),
            pltpu.VMEM((total, heads * 256), BF),
            pltpu.VMEM((total, heads * 256), BF),
            pltpu.VMEM((total, 256), F32),
            pltpu.VMEM((total, 256), F32),
        ],
        compiler_params=params(1),
        cost_estimate=cost(groups * heads * total * total * 2 * 256 * 5, 8 * total * groups * 256 * 2),
        name="attend_back",
    )(length, table, projected, projected, projected, grad_out, lse)


def split_heads(projected, groups, heads):
    parts = projected.reshape(projected.shape[0], groups, 3, heads, 64)
    return [parts[:, :, i].reshape(projected.shape[0], groups * heads, 64) for i in range(3)]


def plain_scores(queries, keys, length, table):
    slots = jnp.arange(keys.shape[0], dtype=jnp.int32)
    picked = (bucket_index(slots[None, :] - slots[:, None])[:, :, None] == jnp.arange(32)).astype(F32)
    bias = jnp.einsum("qkb,hb->hqk", picked, table, precision=lax.Precision.HIGHEST)
    scores = jnp.einsum("qhs,khs->hqk", queries, keys, preferred_element_type=F32) + bias
    return jnp.where(slots < length[0], scores, masked_score), picked


def attend_plain(projected, length, table, groups, heads):
    queries, keys, values = split_heads(projected, groups, heads)
    scores, _ = plain_scores(queries, keys, length, table)
    lse = jax.nn.logsumexp(scores, axis=2)
    probs = jnp.exp(scores - lse[:, :, None]).astype(BF)
    out = jnp.einsum("hqk,khs->qhs", probs, values, preferred_element_type=F32)
    return out.astype(BF).reshape(projected.shape[0], -1), lse


def attend_back_plain(projected, length, table, grad_out, lse, groups, heads):
    total = projected.shape[0]
    queries, keys, values = split_heads(projected, groups, heads)
    grads = grad_out.reshape(queries.shape)
    scores, picked = plain_scores(queries, keys, length, table)
    probs = jnp.exp(scores - lse[:, :, None])
    weighed = probs * jnp.einsum("qhs,khs->hqk", grads, values, preferred_element_type=F32)
    wide = weighed - probs * jnp.sum(weighed, axis=2, keepdims=True)
    rounded = wide.astype(BF)
    parts = [
        jnp.einsum("hqk,khs->qhs", rounded, keys, preferred_element_type=F32),
        jnp.einsum("hqk,qhs->khs", rounded, queries, preferred_element_type=F32),
        jnp.einsum("hqk,qhs->khs", probs.astype(BF), grads, preferred_element_type=F32),
    ]
    parts = [part.astype(BF).reshape(total, groups, 1, heads * 64) for part in parts]
    table_grad = jnp.einsum("hqk,qkb->hb", wide, picked, precision=lax.Precision.HIGHEST)
    return (
        jnp.concatenate(parts, axis=2).reshape(total, -1),
        table_grad.reshape(groups, heads, 32, 1),
    )


def hop(value, axis):
    return lax.ppermute(value, axis, swap)


def pick(value, index, axis):
    return lax.dynamic_index_in_dim(value, index, axis, keepdims=False)


def paired(mine, other, axis):
    return jnp.where(
        lax.axis_index(axis) == 0, jnp.stack([mine, other]), jnp.stack([other, mine])
    )


def gather_tokens(part, nx):
    nz, t, width = part.shape
    if nx != 2:
        return lax.all_gather(part, ("x", "y"), axis=1, tiled=True)
    low, high = part[: nz // 2], part[nz // 2 :]
    low_x, high_y = hop(low, "x"), hop(high, "y")
    low_y, high_x = hop(low, "y"), hop(high, "x")
    low_xy, high_xy = hop(low_x, "y"), hop(high_y, "x")
    low_all = paired(paired(low, low_y, "y"), paired(low_x, low_xy, "y"), "x")
    high_all = paired(paired(high, high_y, "y"), paired(high_x, high_xy, "y"), "x")
    both = jnp.concatenate([low_all, high_all], axis=2)
    return both.transpose(2, 0, 1, 3, 4).reshape(nz, nx * 2 * t, width)


def scatter_tokens(whole, nx):
    nz, total, width = whole.shape
    if nx != 2:
        summed = lax.psum_scatter(
            whole.astype(F32), ("x", "y"), scatter_dimension=1, tiled=True
        )
        return summed
    x, y = lax.axis_index("x"), lax.axis_index("y")
    parts = whole.reshape(nz, nx, 2, total // (2 * nx), width)
    low, high = parts[: nz // 2], parts[nz // 2 :]
    low_in = hop(pick(low, 1 - x, 1), "x")
    high_in = hop(pick(high, 1 - y, 2), "y")
    low_own, high_own = pick(low, x, 1), pick(high, y, 2)

    def add(a, b, index):
        return pick(a, index, 1).astype(F32) + pick(b, index, 1).astype(F32)

    low_last = hop(add(low_own, low_in, 1 - y).astype(BF), "y")
    high_last = hop(add(high_own, high_in, 1 - x).astype(BF), "x")
    return jnp.concatenate(
        [
            add(low_own, low_in, y) + low_last.astype(F32),
            add(high_own, high_in, x) + high_last.astype(F32),
        ],
        axis=0,
    )


def to_groups(stored):
    count, slots, width = stored.shape
    y = lax.axis_index("y")
    halves = stored.reshape(count, 2, slots // 2, width)
    other = hop(pick(halves, 1 - y, 1), "y")
    both = paired(pick(halves, y, 1), other, "y").reshape(2 * count, slots // 2, width)
    return lax.all_to_all(both, "z", 0, 0, tiled=True)


def from_groups(mine):
    nz, t, width = mine.shape
    y = lax.axis_index("y")
    back = lax.all_to_all(mine, "z", 0, 0, tiled=True).reshape(2, nz // 2, t, width)
    other = hop(pick(back, 1 - y, 0), "y")
    both = paired(pick(back, y, 0), other, "y")
    return both.transpose(1, 0, 2, 3).reshape(nz // 2, 2 * t, width)


def body(
    nx, nz, nc, inputs, lengths, attn_gain, ffn_gain, query_key, value_proj, out_proj, gate_up, down_proj, bias_table, cotangent
):
    x, y = lax.axis_index("x"), lax.axis_index("y")
    c, z = lax.axis_index("c"), lax.axis_index("z")
    width = inputs.shape[2]
    features = nz * width
    quarter = y * nc + c
    parts = 2 * nc

    qkv_rows = jnp.concatenate(
        [jnp.transpose(query_key, (1, 2, 3, 0)), jnp.transpose(value_proj, (1, 2, 0))[:, None]], axis=1
    )
    gate_up_rows = jnp.transpose(gate_up, (1, 2, 3, 0))
    heads = qkv_rows.shape[0] // parts
    units = gate_up_rows.shape[0] // parts
    unit = gate_up_rows.shape[2]

    def own(rows, count):
        return lax.dynamic_slice_in_dim(rows, quarter * count, count, 0)

    def spread(rows):
        gathered = lax.all_gather(rows, ("z", "c"), axis=0, tiled=True)
        return gathered.reshape(nz, nc, rows.shape[0], width)

    own_qkv = own(qkv_rows, heads).transpose(1, 0, 2, 3).reshape(3 * heads * 64, width)
    own_out = own(out_proj, heads).reshape(heads * 64, width)
    own_gate_up = own(gate_up_rows, units).transpose(1, 0, 2, 3).reshape(2 * units * unit, width)
    own_down = own(down_proj, units).reshape(units * unit, width)
    qkv_count, out_count = 3 * heads * 64, heads * 64
    w_attn = spread(jnp.concatenate([own_qkv, own_out], axis=0))
    w_gate_up = spread(own_gate_up)
    w_down = spread(own_down)

    both_lengths = jnp.stack([lengths, lax.ppermute(lengths, "y", swap)])
    both_lengths = jnp.where(y == 0, both_lengths, both_lengths[::-1]).reshape(-1)
    length = lax.dynamic_slice_in_dim(both_lengths, z, 1, 0)
    small = jnp.concatenate([attn_gain, ffn_gain, bias_table.reshape(-1)])
    small = lax.all_gather(small, "z", axis=0)
    gain_one = small[:, None, :width].astype(F32)
    gain_two = small[:, None, width : 2 * width].astype(F32)
    table = small[:, 2 * width :].reshape(nz, bias_table.shape[0], -1).transpose(0, 2, 1)
    local_heads = nc * heads
    table = table.reshape(-1, bias_table.shape[0]).astype(F32)
    table = lax.dynamic_slice_in_dim(table, y * local_heads, local_heads, 0)

    tokens = to_groups(inputs).astype(F32)
    count = tokens.shape[1]
    slots = (x * 2 + y) * count + jnp.arange(count, dtype=jnp.int32)
    live = (slots < length).astype(F32)[None, :, None]
    upstream = live * to_groups(cotangent).astype(F32)

    def scale_of(values):
        squares = jnp.sum(values * values, axis=(0, 2), keepdims=True)
        return lax.rsqrt(squares / features + norm_eps)

    def norm_back(values, scale, gain, grad):
        inner = jnp.sum(values * gain * grad, axis=(0, 2), keepdims=True)
        out = scale * gain * grad - values * (scale * scale * scale) * inner / features
        return out, jnp.sum(values * scale * grad, axis=1)

    fits = heads == 4
    forward = attend if fits else attend_plain
    backward = attend_back if fits else attend_back_plain

    scale_one = scale_of(tokens)
    normed = gather_tokens((tokens * scale_one * gain_one).astype(BF), nx)
    grad_ffn = gather_tokens(upstream.astype(BF), nx)
    projected = mm_nt(normed, w_attn, 0, qkv_count)
    attended, lse = forward(projected, length, table, nc, heads)
    hidden = tokens + scatter_tokens(mm_nn(attended, w_attn, qkv_count, out_count), nx)
    scale_two = scale_of(hidden)
    normed_two = gather_tokens((hidden * scale_two * gain_two).astype(BF), nx)
    kept, activated = ffn_in(normed_two, w_gate_up)
    branch = scatter_tokens(mm_nn(activated, w_down, 0, units * unit), nx)
    outputs = from_groups((live * (hidden + branch)).astype(BF))

    def reduce(partial):
        flat = partial.reshape(nz * partial.shape[1], width)
        return lax.psum_scatter(flat, ("z", "c"), scatter_dimension=0, tiled=True)

    def share(part):
        return lax.all_gather(part, ("y", "c"), axis=0)

    down_part = reduce(mm_tn(activated, grad_ffn))
    grad_gate_up = ffn_back(grad_ffn, w_down, kept)
    grad_two = scatter_tokens(mm_nn(grad_gate_up, w_gate_up, 0, 2 * units * unit), nx)
    gate_up_part = reduce(mm_tn(grad_gate_up, normed_two))
    through, ffn_gain_part = norm_back(hidden, scale_two, gain_two, grad_two)
    grad_hidden = upstream + through
    grad_branch = gather_tokens(grad_hidden.astype(BF), nx)
    grad_attended = mm_nt(grad_branch, w_attn, qkv_count, out_count)
    grad_projected, table_part = backward(
        projected, length, table, grad_attended, lse, nc, heads
    )
    grad_one = scatter_tokens(mm_nn(grad_projected, w_attn, 0, qkv_count), nx)
    out_part = reduce(mm_tn(attended, grad_branch))
    qkv_part = reduce(mm_tn(grad_projected, normed))
    through, attn_gain_part = norm_back(tokens, scale_one, gain_one, grad_one)
    input_grad = from_groups((grad_hidden + through).astype(BF)).astype(F32)

    down_all = share(down_part).astype(F32).reshape(down_proj.shape)
    out_all = share(out_part).astype(F32).reshape(out_proj.shape)
    gate_up_all = share(gate_up_part).reshape(parts, 2, units, unit, width)
    gate_up_all = gate_up_all.transpose(4, 0, 2, 1, 3).astype(F32).reshape(gate_up.shape)
    qkv_all = share(qkv_part).reshape(parts, 3, heads, 64, width)
    qkv_all = qkv_all.transpose(4, 0, 2, 1, 3).astype(F32).reshape(width, parts * heads, 3, 64)

    table_part = jnp.sum(table_part, axis=3).reshape(local_heads, -1)
    every = jnp.zeros((nx * 2 * local_heads, table_part.shape[1]), F32)
    every = lax.dynamic_update_slice_in_dim(every, table_part, (x * 2 + y) * local_heads, 0)
    sums = lax.psum(
        (attn_gain_part, ffn_gain_part, every), ("y", "c", "x", "z")
    )
    mine = bias_table.shape[1]
    table_grad = lax.dynamic_slice_in_dim(sums[2], (x * nz + z) * mine, mine, 0).T
    return (
        outputs,
        input_grad,
        pick(sums[0], z, 0),
        pick(sums[1], z, 0),
        qkv_all[:, :, :2],
        qkv_all[:, :, 2],
        out_all,
        gate_up_all,
        down_all,
        table_grad,
    )


def solution(mesh):
    dp, nx, nz = (mesh.shape[name] for name in ("dp", "gx", "gy"))
    nc = dp // 2
    split = Mesh(mesh.devices.reshape(2, nc, nx, nz), ("y", "c", "x", "z"))
    seq = ("y", "c")
    return jax.shard_map(
        functools.partial(body, nx, nz, nc),
        mesh=split,
        in_specs=(
            P(seq, "x", "z"),
            P(seq),
            P("z"),
            P("z"),
            P("z", "x", None, None),
            P("z", "x", None),
            P("x", None, "z"),
            P("z", "x", None, None),
            P("x", None, "z"),
            P(None, ("x", "z")),
            P(seq, "x", "z"),
        ),
        out_specs=(
            P(seq, "x", "z"),
            P(seq, "x", "z"),
            P("z"),
            P("z"),
            P("z", "x", None, None),
            P("z", "x", None),
            P("x", None, "z"),
            P("z", "x", None, None),
            P("x", None, "z"),
            P(None, ("x", "z")),
        ),
        check_vma=False,
    )
```

```python
import functools
import math

import jax
import jax.numpy as jnp
from jax import lax
from jax.experimental import pallas as pl
from jax.experimental.pallas import tpu as pltpu
from jax.sharding import Mesh
from jax.sharding import PartitionSpec as P

norm_eps = 1e-06
masked_score = -1e30
bucket_edges = (12, 16, 23, 32, 46, 64, 91)
BF = jnp.bfloat16
F32 = jnp.float32
LB = 128
VMEM = 60 * 1024 * 1024
swap = [(0, 1), (1, 0)]
gelu_a = math.sqrt(2.0 / math.pi)
gelu_b = 0.044715


def bucket_index(offset):
    magnitude = jnp.abs(offset)
    far_bucket = 8 + sum(((magnitude >= boundary).astype(jnp.int32) for boundary in bucket_edges))
    near_bucket = jnp.where(magnitude < 8, magnitude, far_bucket)
    return near_bucket + 16 * (offset > 0).astype(jnp.int32)


def cost(flops, moved):
    return pl.CostEstimate(flops=int(flops), bytes_accessed=int(moved), transcendentals=0)


def params(steps):
    return pltpu.CompilerParams(
        dimension_semantics=("arbitrary",) * steps, vmem_limit_bytes=VMEM
    )


def dot_nt(a, b):
    return lax.dot_general(a, b, (((1,), (1,)), ((), ())), preferred_element_type=F32)


def dot_nn(a, b):
    return lax.dot_general(a, b, (((1,), (0,)), ((), ())), preferred_element_type=F32)


def spot_of(starts_ref, d, count):
    return pl.ds(pl.multiple_of(starts_ref[d], 256), count)


def piece_specs(pieces):
    shape = pieces[0].shape
    return [pl.BlockSpec(shape, lambda *_: (0, 0, 0)) for _ in pieces]


def nt_sum(piece_refs, d, w_of):
    half = piece_refs[0].shape[0]
    acc = None
    for z in range(2 * half):
        part = dot_nt(piece_refs[4 * (z // half) + d][z % half], w_of(z))
        acc = part if acc is None else acc + part
    return acc


def nt_kernel(starts_ref, *refs):
    pieces, (w_ref, out_ref) = refs[:8], refs[8:]
    for d in range(4):
        acc = nt_sum(pieces, d, lambda z: w_ref[z, 0])
        out_ref[spot_of(starts_ref, d, acc.shape[0]), :] = acc.astype(BF)


def mm_nt(pieces, w, first, rows, starts):
    nz, nc, _, width = w.shape
    total = 4 * pieces[0].shape[1]
    count, skip = rows // 256, first // 256
    return pl.pallas_call(
        nt_kernel,
        grid=(nc, count),
        in_specs=[pl.BlockSpec(memory_space=pltpu.SMEM)]
        + piece_specs(pieces)
        + [pl.BlockSpec((nz, 1, 256, width), lambda c, i: (0, c, skip + i, 0))],
        out_specs=pl.BlockSpec((total, 256), lambda c, i: (0, c * count + i)),
        out_shape=jax.ShapeDtypeStruct((total, nc * rows), BF),
        compiler_params=params(2),
        cost_estimate=cost(
            2 * nz * total * width * nc * rows, 2 * nz * width * (total + nc * rows) + 2 * total * nc * rows
        ),
        name="product_nt",
    )(starts, *pieces, w)


def nn_kernel(count, starts_ref, *refs):
    grads, (w_ref, low_out, low_keep, high_out, high_keep) = refs[:count], refs[count:]
    nc, rows, width = w_ref.shape[1:]
    t = grads[0].shape[0] // 4
    in_low = pl.program_id(0) < pl.num_programs(0) // 2
    for d in range(4):
        spot = spot_of(starts_ref, d, t)
        if count == 1:
            value = dot_nn(grads[0][spot, :], w_ref[0].reshape(nc * rows, width))
        else:
            value = sum(dot_nn(grads[c][spot, :], w_ref[0, c]) for c in range(count))
        value = value.astype(BF)
        dx, dy = d // 2, d % 2

        @pl.when(in_low)
        def _():
            (low_out if dx else low_keep)[dy, 0] = value

        @pl.when(jnp.logical_not(in_low))
        def _():
            (high_out if dy else high_keep)[dx, 0] = value


def mm_nn(grads, w, first, rows, starts):
    total = grads[0].shape[0]
    nz, nc, _, width = w.shape
    skip, half, t = first // rows, nz // 2, total // 4
    low = pl.BlockSpec((2, 1, t, width), lambda z: (0, jnp.minimum(z, half - 1), 0, 0))
    high = pl.BlockSpec((2, 1, t, width), lambda z: (0, jnp.maximum(z - half, 0), 0, 0))
    return pl.pallas_call(
        functools.partial(nn_kernel, len(grads)),
        grid=(nz,),
        in_specs=[pl.BlockSpec(memory_space=pltpu.SMEM)]
        + [pl.BlockSpec(grad.shape, lambda z: (0, 0)) for grad in grads]
        + [pl.BlockSpec((1, nc, rows, width), lambda z: (z, 0, skip, 0))],
        out_specs=[low, low, high, high],
        out_shape=[jax.ShapeDtypeStruct((2, half, t, width), BF)] * 4,
        compiler_params=params(1),
        cost_estimate=cost(
            2 * nz * total * width * nc * rows, 2 * nz * width * (total + nc * rows) + 2 * total * nc * rows
        ),
        name="product_nn",
    )(starts, *grads, w)


def tn_kernel(count, starts_ref, *refs):
    grads, pieces, out_ref = refs[:count], refs[count:-1], refs[-1]
    half, t, _ = pieces[0].shape

    def one(grad_ref):
        turned = [grad_ref[spot_of(starts_ref, d, t), :].T for d in range(4)]
        for z in range(2 * half):
            acc = dot_nn(turned[0], pieces[4 * (z // half)][z % half])
            for d in range(1, 4):
                acc += dot_nn(turned[d], pieces[4 * (z // half) + d][z % half])
            out_ref[z] = acc.astype(BF)

    if count == 1:
        one(grads[0])
    else:
        for c in range(count):

            @pl.when(pl.program_id(0) // (pl.num_programs(0) // count) == c)
            def _():
                one(grads[c])


def mm_tn(grads, pieces, starts):
    total, rows = grads[0].shape
    half, _, width = pieces[0].shape
    nz, count = 2 * half, len(grads)
    block = next(b for b in (640, 384, 256) if rows % b == 0)
    steps = rows // block

    def spec(c):
        return pl.BlockSpec((total, block), lambda i: (0, jnp.clip(i - c * steps, 0, steps - 1)))

    return pl.pallas_call(
        functools.partial(tn_kernel, count),
        grid=(count * steps,),
        in_specs=[pl.BlockSpec(memory_space=pltpu.SMEM)]
        + [spec(c) for c in range(count)]
        + piece_specs(pieces),
        out_specs=pl.BlockSpec((nz, block, width), lambda i: (0, i, 0)),
        out_shape=jax.ShapeDtypeStruct((nz, count * rows, width), BF),
        compiler_params=params(1),
        cost_estimate=cost(
            2 * nz * total * width * count * rows, 2 * nz * width * (total + count * rows) + 2 * total * count * rows
        ),
        name="product_tn",
    )(starts, *grads, *pieces)


def gelu_parts(gate):
    curve = jnp.tanh(gelu_a * (gate + gelu_b * gate * gate * gate))
    value = 0.5 * gate * (1.0 + curve)
    slope = 0.5 * (1.0 + curve) + 0.5 * gate * (1.0 - curve * curve) * gelu_a * (
        1.0 + 3.0 * gelu_b * gate * gate
    )
    return value, slope


def ffn_in_kernel(starts_ref, *refs):
    pieces, (w_ref, gate_ref, up_ref, active_ref) = refs[:8], refs[8:]
    _, _, _, block, width = w_ref.shape
    for d in range(4):
        acc = nt_sum(pieces, d, lambda z: w_ref[z, 0].reshape(2 * block, width))
        spot = spot_of(starts_ref, d, acc.shape[0])
        gate, up = acc[:, :block], acc[:, block:]
        value = 0.5 * gate * (1.0 + jnp.tanh(gelu_a * (gate + gelu_b * gate * gate * gate)))
        gate_ref[spot, :] = gate.astype(BF)
        up_ref[spot, :] = up.astype(BF)
        active_ref[spot, :] = (value * up).astype(BF)


def ffn_in(pieces, w, starts):
    nz, nc, rows, width = w.shape
    half, total = rows // 2, 4 * pieces[0].shape[1]
    count = half // 128
    block = pl.BlockSpec((total, 128), lambda c, i: (0, c * count + i))
    return pl.pallas_call(
        ffn_in_kernel,
        grid=(nc, count),
        in_specs=[pl.BlockSpec(memory_space=pltpu.SMEM)]
        + piece_specs(pieces)
        + [pl.BlockSpec((nz, 1, 2, 128, width), lambda c, i: (0, c, 0, i, 0))],
        out_specs=[block, block, block],
        out_shape=[jax.ShapeDtypeStruct((total, nc * half), BF)] * 3,
        compiler_params=params(2),
        cost_estimate=cost(
            2 * nz * total * width * nc * rows, 2 * nz * width * (total + nc * rows) + 3 * total * nc * rows
        ),
        name="ffn_in",
    )(starts, *pieces, w.reshape(nz, nc, 2, half, width))


def ffn_back_kernel(starts_ref, *refs):
    pieces, (w_ref, gate_ref, up_ref, out_ref) = refs[:8], refs[8:]
    half = w_ref.shape[2]
    for d in range(4):
        acc = nt_sum(pieces, d, lambda z: w_ref[z, 0])
        spot = spot_of(starts_ref, d, acc.shape[0])
        value, slope = gelu_parts(gate_ref[spot, :].astype(F32))
        out_ref[spot, :half] = (acc * up_ref[spot, :].astype(F32) * slope).astype(BF)
        out_ref[spot, half:] = (acc * value).astype(BF)


def ffn_back(pieces, w, gate, up, starts):
    nz, nc, half, width = w.shape
    total = gate.shape[0]
    kept = pl.BlockSpec((total, half), lambda c: (0, c))
    return pl.pallas_call(
        ffn_back_kernel,
        grid=(nc,),
        in_specs=[pl.BlockSpec(memory_space=pltpu.SMEM)]
        + piece_specs(pieces)
        + [pl.BlockSpec((nz, 1, half, width), lambda c: (0, c, 0, 0)), kept, kept],
        out_specs=pl.BlockSpec((total, 2 * half), lambda c: (0, c)),
        out_shape=jax.ShapeDtypeStruct((total, nc * 2 * half), BF),
        compiler_params=params(1),
        cost_estimate=cost(
            2 * nz * total * width * nc * half, 2 * nz * width * (total + nc * half) + 8 * total * nc * half
        ),
        name="ffn_back",
    )(starts, *pieces, w, gate, up)


def mm_nt_plain(act, w, first, rows, starts):
    part = lax.slice_in_dim(w, first, first + rows, axis=2)
    out = jnp.einsum("ztf,zcrf->tcr", act, part, preferred_element_type=F32)
    return out.astype(BF).reshape(act.shape[1], -1)


def mm_nn_plain(grads, w, first, rows, starts):
    grad = grads[0]
    part = lax.slice_in_dim(w, first, first + rows, axis=2)
    split = grad.reshape(grad.shape[0], w.shape[1], rows)
    out = jnp.einsum("tcr,zcrf->ztf", split, part, preferred_element_type=F32)
    return [out.astype(BF)]


def mm_tn_plain(grads, act, starts):
    return jnp.einsum("tr,ztf->zrf", grads[0], act, preferred_element_type=F32).astype(BF)


def ffn_in_plain(act, w, starts):
    _, nc, rows, _ = w.shape
    total = act.shape[1]
    both = jnp.einsum("ztf,zcrf->tcr", act, w, preferred_element_type=F32)
    gate, up = both[:, :, : rows // 2], both[:, :, rows // 2 :]
    value, _ = gelu_parts(gate)
    return [part.astype(BF).reshape(total, -1) for part in (gate, up, value * up)]


def ffn_back_plain(act, w, gate, up, starts):
    total, nc = gate.shape[0], w.shape[1]
    grad = jnp.einsum("ztf,zcrf->tcr", act, w, preferred_element_type=F32)
    value, slope = gelu_parts(gate.astype(F32).reshape(grad.shape))
    both = [grad * up.astype(F32).reshape(grad.shape) * slope, grad * value]
    return jnp.concatenate(both, axis=2).astype(BF).reshape(total, -1)


def near_buckets(tile, total):
    first = (total // LB - 2 + tile) * LB
    rows = lax.broadcasted_iota(jnp.int32, (LB, LB), 0)
    lanes = lax.broadcasted_iota(jnp.int32, (LB, LB), 1)
    return bucket_index(first + rows - (total - LB) - lanes)


def build_strips(table_ref, strip_ref, total, group):
    heads = strip_ref.shape[0]
    near = (total // LB - 2) * LB
    for h in range(heads):
        head = group * heads + h
        strip_ref[h, :near] = jnp.full((near, LB), table_ref[head, 15], F32)
        strip_ref[h, near + 3 * LB :] = jnp.full((near, LB), table_ref[head, 31], F32)

    def one_tile(tile, _):
        index = near_buckets(tile, total)
        vals = [jnp.full((LB, LB), table_ref[group * heads + h, 0], F32) for h in range(heads)]
        for b in range(1, 32):
            hit = index == b
            vals = [
                jnp.where(hit, table_ref[group * heads + h, b], vals[h]) for h in range(heads)
            ]
        for h in range(heads):
            strip_ref[h, pl.ds(pl.multiple_of(near + tile * LB, LB), LB)] = vals[h]
        return 0

    lax.fori_loop(0, 3, one_tile, 0)


def head_lanes(shape, h):
    lanes = lax.broadcasted_iota(jnp.int32, shape, 1)
    return lanes // 64 == h, lanes == ((h + 1) % 4) * 64


def mask_keys(keys, length, h):
    own, spare = head_lanes(keys.shape, h)
    dead = lax.broadcasted_iota(jnp.int32, keys.shape, 0) >= length
    mask = jnp.where(jnp.logical_and(spare, dead), masked_score, 0.0)
    return jnp.where(own, keys.astype(F32), mask).astype(BF)


def with_one(queries, h):
    _, spare = head_lanes(queries.shape, h)
    return jnp.where(spare, 1.0, queries.astype(F32)).astype(BF)


def own_lanes(values, h):
    own, _ = head_lanes(values.shape, h)
    return jnp.where(own, values.astype(F32), 0.0).astype(BF)


def block_bias(strip_ref, h, block, total):
    first = total - LB - 2 * block * LB
    left = strip_ref[h, pl.ds(pl.multiple_of(first, LB), total)]
    right = strip_ref[h, pl.ds(pl.multiple_of(first - LB, LB), total)]
    return jnp.concatenate([left, right], axis=1)


def attend_kernel(group, length_ref, table_ref, q_ref, k_ref, v_ref, out_ref, lse_ref, strip, heads_k, turned_v, turned_out):
    total = q_ref.shape[0]
    heads = strip.shape[0]
    build_strips(table_ref, strip, total, group)
    turned_v[...] = v_ref[...].astype(F32).T.astype(BF)
    for h in range(heads):
        heads_k[h] = mask_keys(k_ref[...], length_ref[0], h)

    def one_block(block, _):
        spot = pl.ds(pl.multiple_of(block * 256, 256), 256)
        queries = q_ref[spot]
        for h in range(heads):
            scores = dot_nt(heads_k[h], with_one(queries, h)) + block_bias(strip, h, block, total)
            largest = jnp.max(scores, axis=0, keepdims=True)
            raised = jnp.exp(scores - largest)
            totals = jnp.sum(raised, axis=0, keepdims=True)
            out = dot_nn(turned_v[h * 64 : (h + 1) * 64], raised.astype(BF))
            turned_out[h * 64 : (h + 1) * 64, spot] = out * (1.0 / totals)
            lse_ref[h : h + 1, spot] = largest + jnp.log(totals)
        return 0

    lax.fori_loop(0, total // 256, one_block, 0)
    out_ref[...] = turned_out[...].T.astype(BF)


def attend_back_kernel(
    group, length_ref, table_ref, q_ref, k_ref, v_ref, grad_ref, lse_ref, out_ref, table_grad_ref,
    strip, strip_grad, heads_k, turned_k, turned_q, ds_ref, p_ref, dk_ref, dv_ref,
):
    total = q_ref.shape[0]
    heads = strip.shape[0]
    build_strips(table_ref, strip, total, group)
    strip_grad[...] = jnp.zeros_like(strip_grad)
    dk_ref[...] = jnp.zeros_like(dk_ref)
    dv_ref[...] = jnp.zeros_like(dv_ref)
    turned_k[...] = k_ref[...].astype(F32).T.astype(BF)
    for h in range(heads):
        heads_k[h] = mask_keys(k_ref[...], length_ref[0], h)

    def one_block(block, _):
        spot = pl.ds(pl.multiple_of(block * 256, 256), 256)
        queries, grads = q_ref[spot], grad_ref[spot]
        own_q, own_g = [], []
        for h in range(heads):
            own_q.append(own_lanes(queries, h))
            own_g.append(own_lanes(grads, h))
            scores = dot_nt(heads_k[h], with_one(queries, h)) + block_bias(strip, h, block, total)
            probs = jnp.exp(scores - lse_ref[h : h + 1, spot])
            weighed = probs * dot_nt(v_ref[...], own_g[h])
            delta = jnp.sum(weighed, axis=0, keepdims=True)
            grad_scores = weighed - probs * delta
            first = total - LB - 2 * block * LB
            left = pl.ds(pl.multiple_of(first, LB), total)
            right = pl.ds(pl.multiple_of(first - LB, LB), total)
            strip_grad[h, left] += grad_scores[:, :LB]
            strip_grad[h, right] += grad_scores[:, LB:]
            rounded = grad_scores.astype(BF)
            ds_ref[:, h * 256 : (h + 1) * 256] = rounded
            p_ref[:, h * 256 : (h + 1) * 256] = probs.astype(BF)
            turned_q[h * 64 : (h + 1) * 64, spot] = dot_nn(turned_k[h * 64 : (h + 1) * 64], rounded)
        dk_ref[...] += dot_nn(ds_ref[...], jnp.concatenate(own_q, axis=0))
        dv_ref[...] += dot_nn(p_ref[...], jnp.concatenate(own_g, axis=0))
        return 0

    lax.fori_loop(0, total // 256, one_block, 0)
    out_ref[:, :256] = turned_q[...].T.astype(BF)
    out_ref[:, 256:512] = dk_ref[...].astype(BF)
    out_ref[:, 512:] = dv_ref[...].astype(BF)

    near = (total // LB - 2) * LB
    for h in range(heads):
        table_grad_ref[h] = jnp.zeros((32, LB), F32)
        table_grad_ref[h, 15:16] = jnp.sum(strip_grad[h, :near], axis=0, keepdims=True)
        table_grad_ref[h, 31:32] = jnp.sum(strip_grad[h, near + 3 * LB :], axis=0, keepdims=True)

    def one_tile(tile, _):
        index = near_buckets(tile, total)
        spot = pl.ds(pl.multiple_of(near + tile * LB, LB), LB)
        for h in range(heads):
            grads = strip_grad[h, spot]
            for b in range(32):
                picked = jnp.where(index == b, grads, 0.0)
                table_grad_ref[h, b : b + 1] += jnp.sum(picked, axis=0, keepdims=True)
        return 0

    lax.fori_loop(0, 3, one_tile, 0)


def block_specs(total, group):
    def spec(i):
        return pl.BlockSpec((total, 256), lambda _: (0, 3 * group + i))

    smem = pl.BlockSpec(memory_space=pltpu.SMEM)
    return [smem, smem, spec(0), spec(1), spec(2)]


def attend(group, projected, length, table):
    total = projected.shape[0]
    heads = 4
    return pl.pallas_call(
        functools.partial(attend_kernel, group),
        grid=(1,),
        in_specs=block_specs(total, group),
        out_specs=[
            pl.BlockSpec((total, 256), lambda _: (0, 0)),
            pl.BlockSpec((8, total), lambda _: (0, 0)),
        ],
        out_shape=[
            jax.ShapeDtypeStruct((total, 256), BF),
            jax.ShapeDtypeStruct((8, total), F32),
        ],
        scratch_shapes=[
            pltpu.VMEM((heads, 2 * total - LB, LB), F32),
            pltpu.VMEM((heads, total, 256), BF),
            pltpu.VMEM((256, total), BF),
            pltpu.VMEM((256, total), F32),
        ],
        compiler_params=params(1),
        cost_estimate=cost(heads * total * total * 2 * 256 * 2, 4 * total * 256 * 2),
        name="attend",
    )(length, table, projected, projected, projected)


def attend_back(group, projected, length, table, grad_out, lse):
    total = projected.shape[0]
    heads = 4
    return pl.pallas_call(
        functools.partial(attend_back_kernel, group),
        grid=(1,),
        in_specs=block_specs(total, group)
        + [
            pl.BlockSpec((total, 256), lambda _: (0, group)),
            pl.BlockSpec((8, total), lambda _: (0, 0)),
        ],
        out_specs=[
            pl.BlockSpec((total, 768), lambda _: (0, 0)),
            pl.BlockSpec((heads, 32, LB), lambda _: (0, 0, 0)),
        ],
        out_shape=[
            jax.ShapeDtypeStruct((total, 768), BF),
            jax.ShapeDtypeStruct((heads, 32, LB), F32),
        ],
        scratch_shapes=[
            pltpu.VMEM((heads, 2 * total - LB, LB), F32),
            pltpu.VMEM((heads, 2 * total - LB, LB), F32),
            pltpu.VMEM((heads, total, 256), BF),
            pltpu.VMEM((256, total), BF),
            pltpu.VMEM((256, total), F32),
            pltpu.VMEM((total, heads * 256), BF),
            pltpu.VMEM((total, heads * 256), BF),
            pltpu.VMEM((total, 256), F32),
            pltpu.VMEM((total, 256), F32),
        ],
        compiler_params=params(1),
        cost_estimate=cost(heads * total * total * 2 * 256 * 5, 8 * total * 256 * 2),
        name="attend_back",
    )(length, table, projected, projected, projected, grad_out, lse)


def split_heads(projected, groups, heads):
    parts = projected.reshape(projected.shape[0], groups, 3, heads, 64)
    return [parts[:, :, i].reshape(projected.shape[0], groups * heads, 64) for i in range(3)]


def plain_scores(queries, keys, length, table):
    slots = jnp.arange(keys.shape[0], dtype=jnp.int32)
    picked = (bucket_index(slots[None, :] - slots[:, None])[:, :, None] == jnp.arange(32)).astype(F32)
    bias = jnp.einsum("qkb,hb->hqk", picked, table, precision=lax.Precision.HIGHEST)
    scores = jnp.einsum("qhs,khs->hqk", queries, keys, preferred_element_type=F32) + bias
    return jnp.where(slots < length[0], scores, masked_score), picked


def attend_plain(projected, length, table, groups, heads):
    queries, keys, values = split_heads(projected, groups, heads)
    scores, _ = plain_scores(queries, keys, length, table)
    lse = jax.nn.logsumexp(scores, axis=2)
    probs = jnp.exp(scores - lse[:, :, None]).astype(BF)
    out = jnp.einsum("hqk,khs->qhs", probs, values, preferred_element_type=F32)
    return out.astype(BF).reshape(projected.shape[0], -1), lse


def attend_back_plain(projected, length, table, grad_out, lse, groups, heads):
    total = projected.shape[0]
    queries, keys, values = split_heads(projected, groups, heads)
    grads = grad_out.reshape(queries.shape)
    scores, picked = plain_scores(queries, keys, length, table)
    probs = jnp.exp(scores - lse[:, :, None])
    weighed = probs * jnp.einsum("qhs,khs->hqk", grads, values, preferred_element_type=F32)
    wide = weighed - probs * jnp.sum(weighed, axis=2, keepdims=True)
    rounded = wide.astype(BF)
    parts = [
        jnp.einsum("hqk,khs->qhs", rounded, keys, preferred_element_type=F32),
        jnp.einsum("hqk,qhs->khs", rounded, queries, preferred_element_type=F32),
        jnp.einsum("hqk,qhs->khs", probs.astype(BF), grads, preferred_element_type=F32),
    ]
    parts = [part.astype(BF).reshape(total, groups, 1, heads * 64) for part in parts]
    table_grad = jnp.einsum("hqk,qkb->hb", wide, picked, precision=lax.Precision.HIGHEST)
    return (
        jnp.concatenate(parts, axis=2).reshape(total, -1),
        table_grad.reshape(groups * heads, 32, 1),
    )


def hop(value, axis):
    return lax.ppermute(value, axis, swap)


def pick(value, index, axis):
    return lax.dynamic_index_in_dim(value, index, axis, keepdims=False)


def paired(mine, other, axis, place=0):
    return jnp.where(
        lax.axis_index(axis) == 0,
        jnp.stack([mine, other], axis=place),
        jnp.stack([other, mine], axis=place),
    )


def after(value, *others):
    return lax.optimization_barrier((value, *others))[0]


def gather_plain(part):
    return lax.all_gather(part, ("x", "y"), axis=1, tiled=True), (), ()


def gather_tokens(part):
    half = part.shape[0] // 2
    low, high = part[:half], part[half:]
    low_x, high_y = hop(low, "x"), hop(high, "y")
    low_y, high_x = hop(low, "y"), hop(high, "x")
    low_xy, high_xy = hop(low_x, "y"), hop(high_y, "x")
    pieces = [low, low_y, low_x, low_xy, high, high_y, high_x, high_xy]
    return pieces, (low_x, high_y), (low_y, low_xy, high_x, high_xy)


def scatter_plain(parts):
    whole = parts[0].astype(F32)
    return lax.psum_scatter(whole, ("x", "y"), scatter_dimension=1, tiled=True), (), ()


def scatter_tokens(parts):
    low_out, low_keep, high_out, high_keep = parts
    low_in, high_in = hop(low_out, "x"), hop(high_out, "y")

    def add(keep, arrived, index):
        return keep[index].astype(F32) + arrived[index].astype(F32)

    low_last = hop(add(low_keep, low_in, 1).astype(BF), "y")
    high_last = hop(add(high_keep, high_in, 1).astype(BF), "x")
    low = add(low_keep, low_in, 0) + low_last.astype(F32)
    high = add(high_keep, high_in, 0) + high_last.astype(F32)
    return jnp.concatenate([low, high], axis=0), (low_in, high_in), (low_last, high_last)


def place_kernel(write, here_ref, *refs):
    pieces, outs = refs[:4], refs[4:]
    step = pl.program_id(0)
    for near in range(4):
        y = here_ref[0] if near < 2 else 1 - here_ref[0]
        c = here_ref[1] if near % 2 == 0 else 1 - here_ref[1]

        @pl.when(step == 2 * y + c)
        def _():
            write(pieces[near], outs)


def place(pieces, here, shapes, write):
    return pl.pallas_call(
        functools.partial(place_kernel, write),
        grid=(4,),
        in_specs=[pl.BlockSpec(memory_space=pltpu.SMEM)]
        + [pl.BlockSpec(piece.shape, lambda q: (0, 0)) for piece in pieces],
        out_specs=[
            pl.BlockSpec(shape, lambda q, rank=len(shape): (q,) + (0,) * (rank - 1)) for shape in shapes
        ],
        out_shape=[jax.ShapeDtypeStruct((4 * shape[0], *shape[1:]), F32) for shape in shapes],
        compiler_params=params(1),
        cost_estimate=cost(0, 20 * pieces[0].size),
        name="place",
    )(here, *pieces)


def share(part):
    over_y = hop(part, "y")
    return [part, hop(part, "c"), over_y, hop(over_y, "c")], over_y


def share_plain(part):
    return lax.all_gather(part, ("y", "c"), axis=0), part


def to_groups(halves, other, extra):
    count, _, t, width = halves.shape
    y = lax.axis_index("y")
    both = paired(pick(halves, y, 1), other, "y").reshape(2 * count, t, width)
    if extra is not None:
        wide = jnp.broadcast_to(extra[None], (2 * count, *extra.shape))
        both = jnp.concatenate([both, wide], axis=1)
    return lax.all_to_all(both, "z", 0, 0, tiled=True)


def from_groups(mine):
    nz, t, width = mine.shape
    y = lax.axis_index("y")
    back = lax.all_to_all(mine, "z", 0, 0, tiled=True).reshape(2, nz // 2, t, width)
    other = hop(pick(back, 1 - y, 0), "y")
    both = paired(pick(back, y, 0), other, "y")
    return both.transpose(1, 0, 2, 3).reshape(nz // 2, 2 * t, width)


def sum_all(value, nx, nz):
    value = value + hop(value, "c")
    value = value + hop(value, "y")
    value = value + hop(value, "x") if nx == 2 else lax.psum(value, "x")
    step = 1
    while step < nz:
        value = value + lax.ppermute(value, "z", [(i, i ^ step) for i in range(nz)])
        step *= 2
    return value


def body(
    nx, nz, nc, inputs, lengths, attn_gain, ffn_gain, query_key, value_proj, out_proj, gate_up, down_proj, bias_table, cotangent
):
    x, y = lax.axis_index("x"), lax.axis_index("y")
    c, z = lax.axis_index("c"), lax.axis_index("z")
    width = inputs.shape[2]
    features = nz * width
    quarter = y * nc + c
    parts = 2 * nc
    buckets, mine = bias_table.shape
    count = inputs.shape[1] // 2

    stored_in = inputs.reshape(inputs.shape[0], 2, count, width)
    stored_cot = cotangent.reshape(stored_in.shape)
    leaving = pick(stored_in, 1 - y, 1)
    small = jnp.concatenate(
        [attn_gain[None], ffn_gain[None], jnp.pad(bias_table.reshape(1, -1), ((0, 0), (0, width - buckets * mine)))]
    )
    small = jnp.pad(small, ((0, 5), (0, 0)))

    query_key_rows = jnp.transpose(query_key, (1, 2, 3, 0))
    value_rows = jnp.transpose(value_proj, (1, 2, 0))
    gate_up_rows = jnp.transpose(gate_up, (1, 2, 3, 0))
    heads = value_rows.shape[0] // parts
    units = gate_up_rows.shape[0] // parts
    unit = gate_up_rows.shape[2]
    local_heads = nc * heads

    def own(rows, size):
        return lax.dynamic_slice_in_dim(rows, quarter * size, size, 0)

    def flat(rows):
        return rows.reshape(-1, width)

    def spread(rows):
        gathered = lax.all_gather(rows, ("z", "c"), axis=0, tiled=True)
        return gathered.reshape(nz, nc, rows.shape[0], width)

    own_pair = own(query_key_rows, heads)
    own_attn = [own_pair[:, 0], own_pair[:, 1], own(value_rows, heads), own(out_proj, heads)]
    own_attn = jnp.concatenate([flat(rows) for rows in own_attn])
    w_attn = spread(own_attn)
    other = after(hop(leaving, "y"), own_attn)
    own_pair = own(after(gate_up_rows, other), units)
    own_gate_up = jnp.concatenate([flat(own_pair[:, 0]), flat(own_pair[:, 1])])
    w_gate_up = spread(own_gate_up)
    own_down = flat(own(after(down_proj, other), units))
    w_down = spread(own_down)
    qkv_count, out_count = 3 * heads * 64, heads * 64

    arrived = after(to_groups(stored_in, other, small), own_gate_up, own_down)
    tokens = arrived[:, :count].astype(F32)
    small = arrived[:, count:]
    gain_one = small[:, :1].astype(F32)
    gain_two = small[:, 1:2].astype(F32)
    table = small[:, 2, : buckets * mine].reshape(nz, buckets, mine).transpose(0, 2, 1)
    table = table.reshape(-1, buckets).astype(F32)
    table = lax.dynamic_slice_in_dim(table, y * local_heads, local_heads, 0)

    both_lengths = jnp.stack([lengths, lax.ppermute(lengths, "y", swap)])
    both_lengths = jnp.where(y == 0, both_lengths, both_lengths[::-1]).reshape(-1)
    length = lax.dynamic_slice_in_dim(both_lengths, z, 1, 0)
    slots = (x * 2 + y) * count + jnp.arange(count, dtype=jnp.int32)
    live = (slots < length).astype(F32)[None, :, None]

    def scale_of(values):
        squares = jnp.sum(values * values, axis=(0, 2), keepdims=True)
        return lax.rsqrt(squares / features + norm_eps)

    def norm_back(values, scale, gain, grad):
        inner = jnp.sum(values * gain * grad, axis=(0, 2), keepdims=True)
        out = scale * gain * grad - values * (scale * scale * scale) * inner / features
        return out, jnp.sum(values * scale * grad, axis=1)

    def reduce(partial):
        rows = partial.reshape(nz * partial.shape[1], width)
        return lax.psum_scatter(rows, ("z", "c"), scatter_dimension=0, tiled=True)

    fits = nx == 2 and heads == 4 and count == 256 and units * unit % 640 == 0 and nz % 2 == 0
    if fits:
        forward, backward, gather, scatter = attend, attend_back, gather_tokens, scatter_tokens
        nt, nn, tn, ffn_one, ffn_two = mm_nt, mm_nn, mm_tn, ffn_in, ffn_back
        shared = share
    else:
        forward, backward, gather, scatter = attend_plain, attend_back_plain, gather_plain, scatter_plain
        nt, nn, tn, ffn_one, ffn_two = mm_nt_plain, mm_nn_plain, mm_tn_plain, ffn_in_plain, ffn_back_plain
        shared = share_plain
    near_x, near_y = jnp.array([0, 0, 1, 1]) ^ x, jnp.array([0, 1, 0, 1]) ^ y
    starts = ((near_x * 2 + near_y) * count).astype(jnp.int32)

    def attend_all(*last):
        if not fits:
            out, stats = forward(projected, length, table, nc, heads)
            return (out,), stats
        first = forward(0, projected, length, table)
        second = forward(1, after(projected, *last), length, table)
        return (first[0], second[0]), (first[1], second[1])

    def attend_back_all(grad, *last):
        if not fits:
            grads, table_grad = backward(projected, length, table, grad, lse, nc, heads)
            return (grads,), table_grad
        first = backward(0, projected, length, table, grad, lse[0])
        second = backward(1, after(projected, *last), length, table, grad, lse[1])
        return (first[0], second[0]), jnp.concatenate([first[1], second[1]])

    scale_one = scale_of(tokens)
    normed, _, _ = gather((tokens * scale_one * gain_one).astype(BF))
    cot_other = hop(pick(stored_cot, 1 - y, 1), "y")
    upstream = live * to_groups(stored_cot, after(cot_other, arrived), None).astype(F32)
    grad_ffn, cot_first, cot_last = gather(after(upstream.astype(BF), w_attn))
    projected = nt(normed, w_attn, 0, qkv_count, starts)
    attended, lse = attend_all(*cot_first)
    heads_out = [after(attended[0], *cot_last), *attended[1:]]
    hidden = tokens + scatter(nn(heads_out, w_attn, qkv_count, out_count, starts))[0]
    scale_two = scale_of(hidden)
    normed_two, _, _ = gather((hidden * scale_two * gain_two).astype(BF))
    gate, up, activated = ffn_one(normed_two, w_gate_up, starts)

    down_partial = tn([activated], grad_ffn, starts)
    down_part = reduce(down_partial)
    grad_gate_up = ffn_two(grad_ffn, w_down, after(gate, down_partial), up, starts)
    two_parts = nn([grad_gate_up], w_gate_up, 0, 2 * units * unit, starts)
    grad_two, two_first, _ = scatter(two_parts)
    gate_up_partial = tn([after(grad_gate_up, two_parts[0])], normed_two, starts)
    gate_up_part = reduce(after(gate_up_partial, down_part, *two_first))
    branch_parts = nn([after(activated, gate_up_partial)], w_down, 0, units * unit, starts)
    through, ffn_gain_part = norm_back(hidden, scale_two, gain_two, grad_two)
    grad_hidden = upstream + through
    grad_branch, _, branch_last = gather(after(grad_hidden.astype(BF), branch_parts[0]))
    grad_attended = nt(grad_branch, w_attn, qkv_count, out_count, starts)
    out_partial = tn(attended, grad_branch, starts)
    branch_parts = [after(part, *branch_last) for part in branch_parts]
    branch, branch_first, branch_last = scatter(branch_parts)
    down_pieces, down_last = shared(after(down_part, grad_attended))
    grad_projected, table_part = attend_back_all(after(grad_attended, out_partial), *branch_first)
    out_part = reduce(after(out_partial, gate_up_part, grad_projected[-1]))
    last = after(grad_projected[-1], *branch_last, down_last)
    grad_projected = [*grad_projected[:-1], last]
    qkv_partial = tn(grad_projected, normed, starts)
    qkv_part = reduce(after(qkv_partial, out_part))
    one_parts = nn(grad_projected, w_attn, 0, qkv_count, starts)
    grad_one, _, _ = scatter(one_parts)
    outputs = from_groups((live * (hidden + branch)).astype(BF))
    through, attn_gain_part = norm_back(tokens, scale_one, gain_one, grad_one)
    input_grad = from_groups((grad_hidden + through).astype(BF)).astype(F32)

    gate_up_pieces, _ = shared(after(gate_up_part, attn_gain_part))
    out_pieces, _ = shared(after(out_part, attn_gain_part))
    qkv_pieces, _ = shared(qkv_part)
    if fits:
        here = jnp.stack([y, c]).astype(jnp.int32)

        def write_rows(source, outs):
            outs[0][...] = source[...].astype(F32)

        def write_qkv(source, outs):
            for h in range(heads):
                for i in range(3):
                    value = source[(i * heads + h) * 64 : (i * heads + h + 1) * 64, :].astype(F32)
                    if i == 2:
                        outs[1][h] = value
                    else:
                        outs[0][h, i] = value

        def write_gate_up(source, outs):
            for u in range(units):
                for i in range(2):
                    first = (i * units + u) * unit
                    outs[0][u, i] = source[first : first + unit, :].astype(F32)

        (down_all,) = place(down_pieces, here, [(units * unit, width)], write_rows)
        (out_all,) = place(out_pieces, here, [(heads * 64, width)], write_rows)
        (gate_up_all,) = place(gate_up_pieces, here, [(units, 2, unit, width)], write_gate_up)
        query_key_all, value_all = place(
            qkv_pieces, here, [(heads, 2, 64, width), (heads, 64, width)], write_qkv
        )
    else:
        down_all, out_all = down_pieces.astype(F32), out_pieces.astype(F32)
        gate_up_all = gate_up_pieces.astype(F32).reshape(parts, 2, units, unit, width)
        gate_up_all = gate_up_all.transpose(0, 2, 1, 3, 4).reshape(-1, 2, unit, width)
        qkv_all = qkv_pieces.astype(F32).reshape(parts, 3, heads, 64, width)
        qkv_all = qkv_all.transpose(0, 2, 1, 3, 4).reshape(-1, 3, 64, width)
        query_key_all, value_all = qkv_all[:, :2], qkv_all[:, 2]
    down_all, out_all = down_all.reshape(down_proj.shape), out_all.reshape(out_proj.shape)

    table_part = jnp.sum(table_part, axis=2)
    every = jnp.zeros((nx * 2 * local_heads, table_part.shape[1]), F32)
    every = lax.dynamic_update_slice_in_dim(every, table_part, (x * 2 + y) * local_heads, 0)
    every = every.reshape(-1, width) if every.size % width == 0 else every
    if every.shape[1] == width:
        both = sum_all(jnp.concatenate([ffn_gain_part, every]), nx, nz)
        ffn_gain_grad, every = both[:nz], both[nz:].reshape(-1, buckets)
    else:
        ffn_gain_grad, every = sum_all(ffn_gain_part, nx, nz), sum_all(every, nx, nz)
    attn_gain_grad = sum_all(attn_gain_part, nx, nz)
    table_grad = lax.dynamic_slice_in_dim(every, (x * nz + z) * mine, mine, 0).T
    return (
        outputs,
        input_grad,
        pick(attn_gain_grad, z, 0),
        pick(ffn_gain_grad, z, 0),
        query_key_all.transpose(3, 0, 1, 2),
        value_all.transpose(2, 0, 1),
        out_all,
        gate_up_all.transpose(3, 0, 1, 2),
        down_all,
        table_grad,
    )


def solution(mesh):
    dp, nx, nz = (mesh.shape[name] for name in ("dp", "gx", "gy"))
    nc = dp // 2
    split = Mesh(mesh.devices.reshape(2, nc, nx, nz), ("y", "c", "x", "z"))
    seq = ("y", "c")
    return jax.shard_map(
        functools.partial(body, nx, nz, nc),
        mesh=split,
        in_specs=(
            P(seq, "x", "z"),
            P(seq),
            P("z"),
            P("z"),
            P("z", "x", None, None),
            P("z", "x", None),
            P("x", None, "z"),
            P("z", "x", None, None),
            P("x", None, "z"),
            P(None, ("x", "z")),
            P(seq, "x", "z"),
        ),
        out_specs=(
            P(seq, "x", "z"),
            P(seq, "x", "z"),
            P("z"),
            P("z"),
            P("z", "x", None, None),
            P("z", "x", None),
            P("x", None, "z"),
            P("z", "x", None, None),
            P("x", None, "z"),
            P(None, ("x", "z")),
        ),
        check_vma=False,
    )
```

```python
import functools
import math

import jax
import jax.numpy as jnp
from jax import lax
from jax.experimental import pallas as pl
from jax.experimental.pallas import tpu as pltpu
from jax.sharding import Mesh
from jax.sharding import PartitionSpec as P

norm_eps = 1e-06
masked_score = -1e30
bucket_edges = (12, 16, 23, 32, 46, 64, 91)
BF = jnp.bfloat16
F32 = jnp.float32
LB = 128
VMEM = 60 * 1024 * 1024
swap = [(0, 1), (1, 0)]
gelu_a = math.sqrt(2.0 / math.pi)
gelu_b = 0.044715


def bucket_index(offset):
    magnitude = jnp.abs(offset)
    far_bucket = 8 + sum(((magnitude >= boundary).astype(jnp.int32) for boundary in bucket_edges))
    near_bucket = jnp.where(magnitude < 8, magnitude, far_bucket)
    return near_bucket + 16 * (offset > 0).astype(jnp.int32)


def cost(flops, moved):
    return pl.CostEstimate(flops=int(flops), bytes_accessed=int(moved), transcendentals=0)


def params(steps):
    return pltpu.CompilerParams(
        dimension_semantics=("arbitrary",) * steps, vmem_limit_bytes=VMEM
    )


def dot_nt(a, b):
    return lax.dot_general(a, b, (((1,), (1,)), ((), ())), preferred_element_type=F32)


def dot_nn(a, b):
    return lax.dot_general(a, b, (((1,), (0,)), ((), ())), preferred_element_type=F32)


def spot_of(starts_ref, d, count):
    return pl.ds(pl.multiple_of(starts_ref[d], 256), count)


def piece_specs(pieces):
    shape = pieces[0].shape
    return [pl.BlockSpec(shape, lambda *_: (0, 0, 0)) for _ in pieces]


def nt_sum(piece_refs, d, w_of):
    half = piece_refs[0].shape[0]
    acc = None
    for z in range(2 * half):
        part = dot_nt(piece_refs[4 * (z // half) + d][z % half], w_of(z))
        acc = part if acc is None else acc + part
    return acc


def nt_kernel(starts_ref, *refs):
    pieces, (w_ref, out_ref) = refs[:8], refs[8:]
    for d in range(4):
        acc = nt_sum(pieces, d, lambda z: w_ref[z, 0])
        out_ref[spot_of(starts_ref, d, acc.shape[0]), :] = acc.astype(BF)


def mm_nt(pieces, w, first, rows, starts):
    nz, nc, _, width = w.shape
    total = 4 * pieces[0].shape[1]
    count, skip = rows // 256, first // 256
    return pl.pallas_call(
        nt_kernel,
        grid=(nc, count),
        in_specs=[pl.BlockSpec(memory_space=pltpu.SMEM)]
        + piece_specs(pieces)
        + [pl.BlockSpec((nz, 1, 256, width), lambda c, i: (0, c, skip + i, 0))],
        out_specs=pl.BlockSpec((total, 256), lambda c, i: (0, c * count + i)),
        out_shape=jax.ShapeDtypeStruct((total, nc * rows), BF),
        compiler_params=params(2),
        cost_estimate=cost(
            2 * nz * total * width * nc * rows, 2 * nz * width * (total + nc * rows) + 2 * total * nc * rows
        ),
        name="product_nt",
    )(starts, *pieces, w)


def nn_kernel(count, starts_ref, *refs):
    grads, (w_ref, low_out, low_keep, high_out, high_keep) = refs[:count], refs[count:]
    nc, rows, width = w_ref.shape[1:]
    t = grads[0].shape[0] // 4
    in_low = pl.program_id(0) < pl.num_programs(0) // 2

    def product(d):
        spot = spot_of(starts_ref, d, t)
        if count == 1:
            return dot_nn(grads[0][spot, :], w_ref[0].reshape(nc * rows, width)).astype(BF)
        return sum(dot_nn(grads[c][spot, :], w_ref[0, c]) for c in range(count)).astype(BF)

    @pl.when(in_low)
    def _():
        for d in range(4):
            (low_out if d // 2 else low_keep)[d % 2, 0] = product(d)

    @pl.when(jnp.logical_not(in_low))
    def _():
        for d in range(4):
            (high_out if d % 2 else high_keep)[d // 2, 0] = product(d)


def mm_nn(grads, w, first, rows, starts):
    total = grads[0].shape[0]
    nz, nc, _, width = w.shape
    skip, half, t = first // rows, nz // 2, total // 4
    low = pl.BlockSpec((2, 1, t, width), lambda z: (0, jnp.minimum(z, half - 1), 0, 0))
    high = pl.BlockSpec((2, 1, t, width), lambda z: (0, jnp.maximum(z - half, 0), 0, 0))
    return pl.pallas_call(
        functools.partial(nn_kernel, len(grads)),
        grid=(nz,),
        in_specs=[pl.BlockSpec(memory_space=pltpu.SMEM)]
        + [pl.BlockSpec(grad.shape, lambda z: (0, 0)) for grad in grads]
        + [pl.BlockSpec((1, nc, rows, width), lambda z: (z, 0, skip, 0))],
        out_specs=[low, low, high, high],
        out_shape=[jax.ShapeDtypeStruct((2, half, t, width), BF)] * 4,
        compiler_params=params(1),
        cost_estimate=cost(
            2 * nz * total * width * nc * rows, 2 * nz * width * (total + nc * rows) + 2 * total * nc * rows
        ),
        name="product_nn",
    )(starts, *grads, w)


def tn_kernel(count, starts_ref, *refs):
    grads, pieces, out_ref = refs[:count], refs[count:-1], refs[-1]
    half, t, _ = pieces[0].shape

    def one(grad_ref):
        turned = [grad_ref[spot_of(starts_ref, d, t), :].T for d in range(4)]
        for z in range(2 * half):
            acc = dot_nn(turned[0], pieces[4 * (z // half)][z % half])
            for d in range(1, 4):
                acc += dot_nn(turned[d], pieces[4 * (z // half) + d][z % half])
            out_ref[z] = acc.astype(BF)

    if count == 1:
        one(grads[0])
    else:
        for c in range(count):

            @pl.when(pl.program_id(0) // (pl.num_programs(0) // count) == c)
            def _():
                one(grads[c])


def mm_tn(grads, pieces, starts):
    total, rows = grads[0].shape
    half, _, width = pieces[0].shape
    nz, count = 2 * half, len(grads)
    block = next(b for b in (640, 384, 256) if rows % b == 0)
    steps = rows // block

    def spec(c):
        return pl.BlockSpec((total, block), lambda i: (0, jnp.clip(i - c * steps, 0, steps - 1)))

    return pl.pallas_call(
        functools.partial(tn_kernel, count),
        grid=(count * steps,),
        in_specs=[pl.BlockSpec(memory_space=pltpu.SMEM)]
        + [spec(c) for c in range(count)]
        + piece_specs(pieces),
        out_specs=pl.BlockSpec((nz, block, width), lambda i: (0, i, 0)),
        out_shape=jax.ShapeDtypeStruct((nz, count * rows, width), BF),
        compiler_params=params(1),
        cost_estimate=cost(
            2 * nz * total * width * count * rows, 2 * nz * width * (total + count * rows) + 2 * total * count * rows
        ),
        name="product_tn",
    )(starts, *grads, *pieces)


def gelu_parts(gate):
    curve = jnp.tanh(gelu_a * (gate + gelu_b * gate * gate * gate))
    value = 0.5 * gate * (1.0 + curve)
    slope = 0.5 * (1.0 + curve) + 0.5 * gate * (1.0 - curve * curve) * gelu_a * (
        1.0 + 3.0 * gelu_b * gate * gate
    )
    return value, slope


def ffn_in_kernel(starts_ref, *refs):
    pieces, (w_ref, gate_ref, up_ref, active_ref) = refs[:8], refs[8:]
    _, _, _, block, width = w_ref.shape
    for d in range(4):
        acc = nt_sum(pieces, d, lambda z: w_ref[z, 0].reshape(2 * block, width))
        spot = spot_of(starts_ref, d, acc.shape[0])
        gate, up = acc[:, :block], acc[:, block:]
        value = 0.5 * gate * (1.0 + jnp.tanh(gelu_a * (gate + gelu_b * gate * gate * gate)))
        gate_ref[spot, :] = gate.astype(BF)
        up_ref[spot, :] = up.astype(BF)
        active_ref[spot, :] = (value * up).astype(BF)


def ffn_in(pieces, w, starts):
    nz, nc, rows, width = w.shape
    half, total = rows // 2, 4 * pieces[0].shape[1]
    count = half // 128
    block = pl.BlockSpec((total, 128), lambda c, i: (0, c * count + i))
    return pl.pallas_call(
        ffn_in_kernel,
        grid=(nc, count),
        in_specs=[pl.BlockSpec(memory_space=pltpu.SMEM)]
        + piece_specs(pieces)
        + [pl.BlockSpec((nz, 1, 2, 128, width), lambda c, i: (0, c, 0, i, 0))],
        out_specs=[block, block, block],
        out_shape=[jax.ShapeDtypeStruct((total, nc * half), BF)] * 3,
        compiler_params=params(2),
        cost_estimate=cost(
            2 * nz * total * width * nc * rows, 2 * nz * width * (total + nc * rows) + 3 * total * nc * rows
        ),
        name="ffn_in",
    )(starts, *pieces, w.reshape(nz, nc, 2, half, width))


def ffn_back_kernel(starts_ref, *refs):
    pieces, (w_ref, gate_ref, up_ref, out_ref) = refs[:8], refs[8:]
    half = w_ref.shape[2]
    for d in range(4):
        acc = nt_sum(pieces, d, lambda z: w_ref[z, 0])
        spot = spot_of(starts_ref, d, acc.shape[0])
        value, slope = gelu_parts(gate_ref[spot, :].astype(F32))
        out_ref[spot, :half] = (acc * up_ref[spot, :].astype(F32) * slope).astype(BF)
        out_ref[spot, half:] = (acc * value).astype(BF)


def ffn_back(pieces, w, gate, up, starts):
    nz, nc, half, width = w.shape
    total = gate.shape[0]
    kept = pl.BlockSpec((total, half), lambda c: (0, c))
    return pl.pallas_call(
        ffn_back_kernel,
        grid=(nc,),
        in_specs=[pl.BlockSpec(memory_space=pltpu.SMEM)]
        + piece_specs(pieces)
        + [pl.BlockSpec((nz, 1, half, width), lambda c: (0, c, 0, 0)), kept, kept],
        out_specs=pl.BlockSpec((total, 2 * half), lambda c: (0, c)),
        out_shape=jax.ShapeDtypeStruct((total, nc * 2 * half), BF),
        compiler_params=params(1),
        cost_estimate=cost(
            2 * nz * total * width * nc * half, 2 * nz * width * (total + nc * half) + 8 * total * nc * half
        ),
        name="ffn_back",
    )(starts, *pieces, w, gate, up)


def mm_nt_plain(act, w, first, rows, starts):
    part = lax.slice_in_dim(w, first, first + rows, axis=2)
    out = jnp.einsum("ztf,zcrf->tcr", act, part, preferred_element_type=F32)
    return out.astype(BF).reshape(act.shape[1], -1)


def mm_nn_plain(grads, w, first, rows, starts):
    grad = grads[0]
    part = lax.slice_in_dim(w, first, first + rows, axis=2)
    split = grad.reshape(grad.shape[0], w.shape[1], rows)
    out = jnp.einsum("tcr,zcrf->ztf", split, part, preferred_element_type=F32)
    return [out.astype(BF)]


def mm_tn_plain(grads, act, starts):
    return jnp.einsum("tr,ztf->zrf", grads[0], act, preferred_element_type=F32).astype(BF)


def ffn_in_plain(act, w, starts):
    _, nc, rows, _ = w.shape
    total = act.shape[1]
    both = jnp.einsum("ztf,zcrf->tcr", act, w, preferred_element_type=F32)
    gate, up = both[:, :, : rows // 2], both[:, :, rows // 2 :]
    value, _ = gelu_parts(gate)
    return [part.astype(BF).reshape(total, -1) for part in (gate, up, value * up)]


def ffn_back_plain(act, w, gate, up, starts):
    total, nc = gate.shape[0], w.shape[1]
    grad = jnp.einsum("ztf,zcrf->tcr", act, w, preferred_element_type=F32)
    value, slope = gelu_parts(gate.astype(F32).reshape(grad.shape))
    both = [grad * up.astype(F32).reshape(grad.shape) * slope, grad * value]
    return jnp.concatenate(both, axis=2).astype(BF).reshape(total, -1)


def near_buckets(tile, total):
    first = (total // LB - 2 + tile) * LB
    rows = lax.broadcasted_iota(jnp.int32, (LB, LB), 0)
    lanes = lax.broadcasted_iota(jnp.int32, (LB, LB), 1)
    return bucket_index(first + rows - (total - LB) - lanes)


def build_strips(table_ref, strip_ref, total, group):
    heads = strip_ref.shape[0]
    near = (total // LB - 2) * LB
    for h in range(heads):
        head = group * heads + h
        strip_ref[h, :near] = jnp.full((near, LB), table_ref[head, 15], F32)
        strip_ref[h, near + 3 * LB :] = jnp.full((near, LB), table_ref[head, 31], F32)

    def one_tile(tile, _):
        index = near_buckets(tile, total)
        vals = [jnp.full((LB, LB), table_ref[group * heads + h, 0], F32) for h in range(heads)]
        for b in range(1, 32):
            hit = index == b
            vals = [
                jnp.where(hit, table_ref[group * heads + h, b], vals[h]) for h in range(heads)
            ]
        for h in range(heads):
            strip_ref[h, pl.ds(pl.multiple_of(near + tile * LB, LB), LB)] = vals[h]
        return 0

    lax.fori_loop(0, 3, one_tile, 0)


def head_lanes(shape, h):
    lanes = lax.broadcasted_iota(jnp.int32, shape, 1)
    return lanes // 64 == h, lanes == ((h + 1) % 4) * 64


def mask_keys(keys, length, h):
    own, spare = head_lanes(keys.shape, h)
    dead = lax.broadcasted_iota(jnp.int32, keys.shape, 0) >= length
    mask = jnp.where(jnp.logical_and(spare, dead), masked_score, 0.0)
    return jnp.where(own, keys.astype(F32), mask).astype(BF)


def with_one(queries, h):
    _, spare = head_lanes(queries.shape, h)
    return jnp.where(spare, 1.0, queries.astype(F32)).astype(BF)


def own_lanes(values, h):
    own, _ = head_lanes(values.shape, h)
    return jnp.where(own, values.astype(F32), 0.0).astype(BF)


def block_bias(strip_ref, h, block, total):
    first = total - LB - 2 * block * LB
    left = strip_ref[h, pl.ds(pl.multiple_of(first, LB), total)]
    right = strip_ref[h, pl.ds(pl.multiple_of(first - LB, LB), total)]
    return jnp.concatenate([left, right], axis=1)


def attend_kernel(group, length_ref, table_ref, q_ref, k_ref, v_ref, out_ref, lse_ref, strip, heads_k, turned_v, turned_out):
    total = q_ref.shape[0]
    heads = strip.shape[0]
    build_strips(table_ref, strip, total, group)
    turned_v[...] = v_ref[...].astype(F32).T.astype(BF)
    for h in range(heads):
        heads_k[h] = mask_keys(k_ref[...], length_ref[0], h)

    def one_block(block, _):
        spot = pl.ds(pl.multiple_of(block * 256, 256), 256)
        queries = q_ref[spot]
        for h in range(heads):
            scores = dot_nt(heads_k[h], with_one(queries, h)) + block_bias(strip, h, block, total)
            largest = jnp.max(scores, axis=0, keepdims=True)
            raised = jnp.exp(scores - largest)
            totals = jnp.sum(raised, axis=0, keepdims=True)
            out = dot_nn(turned_v[h * 64 : (h + 1) * 64], raised.astype(BF))
            turned_out[h * 64 : (h + 1) * 64, spot] = out * (1.0 / totals)
            lse_ref[h : h + 1, spot] = largest + jnp.log(totals)
        return 0

    lax.fori_loop(0, total // 256, one_block, 0)
    out_ref[...] = turned_out[...].T.astype(BF)


def attend_back_kernel(
    group, length_ref, table_ref, q_ref, k_ref, v_ref, grad_ref, lse_ref, out_ref, table_grad_ref,
    strip, strip_grad, heads_k, turned_k, turned_q, ds_ref, p_ref, dk_ref, dv_ref,
):
    total = q_ref.shape[0]
    heads = strip.shape[0]
    build_strips(table_ref, strip, total, group)
    strip_grad[...] = jnp.zeros_like(strip_grad)
    dk_ref[...] = jnp.zeros_like(dk_ref)
    dv_ref[...] = jnp.zeros_like(dv_ref)
    turned_k[...] = k_ref[...].astype(F32).T.astype(BF)
    for h in range(heads):
        heads_k[h] = mask_keys(k_ref[...], length_ref[0], h)

    def one_block(block, _):
        spot = pl.ds(pl.multiple_of(block * 256, 256), 256)
        queries, grads = q_ref[spot], grad_ref[spot]
        own_q, own_g = [], []
        for h in range(heads):
            own_q.append(own_lanes(queries, h))
            own_g.append(own_lanes(grads, h))
            scores = dot_nt(heads_k[h], with_one(queries, h)) + block_bias(strip, h, block, total)
            probs = jnp.exp(scores - lse_ref[h : h + 1, spot])
            weighed = probs * dot_nt(v_ref[...], own_g[h])
            delta = jnp.sum(weighed, axis=0, keepdims=True)
            grad_scores = weighed - probs * delta
            first = total - LB - 2 * block * LB
            left = pl.ds(pl.multiple_of(first, LB), total)
            right = pl.ds(pl.multiple_of(first - LB, LB), total)
            strip_grad[h, left] += grad_scores[:, :LB]
            strip_grad[h, right] += grad_scores[:, LB:]
            rounded = grad_scores.astype(BF)
            ds_ref[:, h * 256 : (h + 1) * 256] = rounded
            p_ref[:, h * 256 : (h + 1) * 256] = probs.astype(BF)
            turned_q[h * 64 : (h + 1) * 64, spot] = dot_nn(turned_k[h * 64 : (h + 1) * 64], rounded)
        dk_ref[...] += dot_nn(ds_ref[...], jnp.concatenate(own_q, axis=0))
        dv_ref[...] += dot_nn(p_ref[...], jnp.concatenate(own_g, axis=0))
        return 0

    lax.fori_loop(0, total // 256, one_block, 0)
    out_ref[:, :256] = turned_q[...].T.astype(BF)
    out_ref[:, 256:512] = dk_ref[...].astype(BF)
    out_ref[:, 512:] = dv_ref[...].astype(BF)

    near = (total // LB - 2) * LB
    for h in range(heads):
        table_grad_ref[h] = jnp.zeros((32, LB), F32)
        table_grad_ref[h, 15:16] = jnp.sum(strip_grad[h, :near], axis=0, keepdims=True)
        table_grad_ref[h, 31:32] = jnp.sum(strip_grad[h, near + 3 * LB :], axis=0, keepdims=True)

    def one_tile(tile, _):
        index = near_buckets(tile, total)
        spot = pl.ds(pl.multiple_of(near + tile * LB, LB), LB)
        for h in range(heads):
            grads = strip_grad[h, spot]
            for b in range(32):
                picked = jnp.where(index == b, grads, 0.0)
                table_grad_ref[h, b : b + 1] += jnp.sum(picked, axis=0, keepdims=True)
        return 0

    lax.fori_loop(0, 3, one_tile, 0)


def block_specs(total, group):
    def spec(i):
        return pl.BlockSpec((total, 256), lambda _: (0, 3 * group + i))

    smem = pl.BlockSpec(memory_space=pltpu.SMEM)
    return [smem, smem, spec(0), spec(1), spec(2)]


def attend(group, projected, length, table):
    total = projected.shape[0]
    heads = 4
    return pl.pallas_call(
        functools.partial(attend_kernel, group),
        grid=(1,),
        in_specs=block_specs(total, group),
        out_specs=[
            pl.BlockSpec((total, 256), lambda _: (0, 0)),
            pl.BlockSpec((8, total), lambda _: (0, 0)),
        ],
        out_shape=[
            jax.ShapeDtypeStruct((total, 256), BF),
            jax.ShapeDtypeStruct((8, total), F32),
        ],
        scratch_shapes=[
            pltpu.VMEM((heads, 2 * total - LB, LB), F32),
            pltpu.VMEM((heads, total, 256), BF),
            pltpu.VMEM((256, total), BF),
            pltpu.VMEM((256, total), F32),
        ],
        compiler_params=params(1),
        cost_estimate=cost(heads * total * total * 2 * 256 * 2, 4 * total * 256 * 2),
        name="attend",
    )(length, table, projected, projected, projected)


def attend_back(group, projected, length, table, grad_out, lse):
    total = projected.shape[0]
    heads = 4
    return pl.pallas_call(
        functools.partial(attend_back_kernel, group),
        grid=(1,),
        in_specs=block_specs(total, group)
        + [
            pl.BlockSpec((total, 256), lambda _: (0, group)),
            pl.BlockSpec((8, total), lambda _: (0, 0)),
        ],
        out_specs=[
            pl.BlockSpec((total, 768), lambda _: (0, 0)),
            pl.BlockSpec((heads, 32, LB), lambda _: (0, 0, 0)),
        ],
        out_shape=[
            jax.ShapeDtypeStruct((total, 768), BF),
            jax.ShapeDtypeStruct((heads, 32, LB), F32),
        ],
        scratch_shapes=[
            pltpu.VMEM((heads, 2 * total - LB, LB), F32),
            pltpu.VMEM((heads, 2 * total - LB, LB), F32),
            pltpu.VMEM((heads, total, 256), BF),
            pltpu.VMEM((256, total), BF),
            pltpu.VMEM((256, total), F32),
            pltpu.VMEM((total, heads * 256), BF),
            pltpu.VMEM((total, heads * 256), BF),
            pltpu.VMEM((total, 256), F32),
            pltpu.VMEM((total, 256), F32),
        ],
        compiler_params=params(1),
        cost_estimate=cost(heads * total * total * 2 * 256 * 5, 8 * total * 256 * 2),
        name="attend_back",
    )(length, table, projected, projected, projected, grad_out, lse)


def split_heads(projected, groups, heads):
    parts = projected.reshape(projected.shape[0], groups, 3, heads, 64)
    return [parts[:, :, i].reshape(projected.shape[0], groups * heads, 64) for i in range(3)]


def plain_scores(queries, keys, length, table):
    slots = jnp.arange(keys.shape[0], dtype=jnp.int32)
    picked = (bucket_index(slots[None, :] - slots[:, None])[:, :, None] == jnp.arange(32)).astype(F32)
    bias = jnp.einsum("qkb,hb->hqk", picked, table, precision=lax.Precision.HIGHEST)
    scores = jnp.einsum("qhs,khs->hqk", queries, keys, preferred_element_type=F32) + bias
    return jnp.where(slots < length[0], scores, masked_score), picked


def attend_plain(projected, length, table, groups, heads):
    queries, keys, values = split_heads(projected, groups, heads)
    scores, _ = plain_scores(queries, keys, length, table)
    lse = jax.nn.logsumexp(scores, axis=2)
    probs = jnp.exp(scores - lse[:, :, None]).astype(BF)
    out = jnp.einsum("hqk,khs->qhs", probs, values, preferred_element_type=F32)
    return out.astype(BF).reshape(projected.shape[0], -1), lse


def attend_back_plain(projected, length, table, grad_out, lse, groups, heads):
    total = projected.shape[0]
    queries, keys, values = split_heads(projected, groups, heads)
    grads = grad_out.reshape(queries.shape)
    scores, picked = plain_scores(queries, keys, length, table)
    probs = jnp.exp(scores - lse[:, :, None])
    weighed = probs * jnp.einsum("qhs,khs->hqk", grads, values, preferred_element_type=F32)
    wide = weighed - probs * jnp.sum(weighed, axis=2, keepdims=True)
    rounded = wide.astype(BF)
    parts = [
        jnp.einsum("hqk,khs->qhs", rounded, keys, preferred_element_type=F32),
        jnp.einsum("hqk,qhs->khs", rounded, queries, preferred_element_type=F32),
        jnp.einsum("hqk,qhs->khs", probs.astype(BF), grads, preferred_element_type=F32),
    ]
    parts = [part.astype(BF).reshape(total, groups, 1, heads * 64) for part in parts]
    table_grad = jnp.einsum("hqk,qkb->hb", wide, picked, precision=lax.Precision.HIGHEST)
    return (
        jnp.concatenate(parts, axis=2).reshape(total, -1),
        table_grad.reshape(groups * heads, 32, 1),
    )


def hop(value, axis):
    return lax.ppermute(value, axis, swap)


def pick(value, index, axis):
    return lax.dynamic_index_in_dim(value, index, axis, keepdims=False)


def paired(mine, other, axis, place=0):
    return jnp.where(
        lax.axis_index(axis) == 0,
        jnp.stack([mine, other], axis=place),
        jnp.stack([other, mine], axis=place),
    )


def after(value, *others):
    return lax.optimization_barrier((value, *others))[0]


def gather_plain(part, *beside):
    return lax.all_gather(part, ("x", "y"), axis=1, tiled=True), (), ()


def gather_tokens(part, *beside):
    half = part.shape[0] // 2
    low, high = part[:half], part[half:]
    low_x, high_y = hop(low, "x"), hop(high, "y")
    if beside:
        low_x, high_y = after(low_x, *beside), after(high_y, *beside)
    low_y, high_x = hop(low, "y"), hop(high, "x")
    low_xy, high_xy = hop(low_x, "y"), hop(high_y, "x")
    pieces = [low, low_y, low_x, low_xy, high, high_y, high_x, high_xy]
    return pieces, (low_x, high_y), (low_y, low_xy, high_x, high_xy)


def scatter_plain(parts, *beside):
    whole = parts[0].astype(F32)
    return lax.psum_scatter(whole, ("x", "y"), scatter_dimension=1, tiled=True), (), ()


def scatter_tokens(parts, *beside):
    low_out, low_keep, high_out, high_keep = parts
    low_in, high_in = hop(low_out, "x"), hop(high_out, "y")
    if beside:
        low_in, high_in = after(low_in, *beside), after(high_in, *beside)

    def add(keep, arrived, index):
        return keep[index].astype(F32) + arrived[index].astype(F32)

    low_last = hop(add(low_keep, low_in, 1).astype(BF), "y")
    high_last = hop(add(high_keep, high_in, 1).astype(BF), "x")
    low = add(low_keep, low_in, 0) + low_last.astype(F32)
    high = add(high_keep, high_in, 0) + high_last.astype(F32)
    return jnp.concatenate([low, high], axis=0), (low_in, high_in), (low_last, high_last)


def place_kernel(write, here_ref, *refs):
    pieces, outs = refs[:4], refs[4:]
    step = pl.program_id(0)
    for near in range(4):
        y = here_ref[0] if near < 2 else 1 - here_ref[0]
        c = here_ref[1] if near % 2 == 0 else 1 - here_ref[1]

        @pl.when(step == 2 * y + c)
        def _():
            write(pieces[near], outs)


def place(pieces, here, shapes, write):
    return pl.pallas_call(
        functools.partial(place_kernel, write),
        grid=(4,),
        in_specs=[pl.BlockSpec(memory_space=pltpu.SMEM)]
        + [pl.BlockSpec(piece.shape, lambda q: (0, 0)) for piece in pieces],
        out_specs=[
            pl.BlockSpec(shape, lambda q, rank=len(shape): (q,) + (0,) * (rank - 1)) for shape in shapes
        ],
        out_shape=[jax.ShapeDtypeStruct((4 * shape[0], *shape[1:]), F32) for shape in shapes],
        compiler_params=params(1),
        cost_estimate=cost(0, 20 * pieces[0].size),
        name="place",
    )(here, *pieces)


def share(part):
    over_y = hop(part, "y")
    return [part, hop(part, "c"), over_y, hop(over_y, "c")], over_y


def share_plain(part):
    return lax.all_gather(part, ("y", "c"), axis=0), part


def routes(nz, k):
    many = nz // 2
    pairs = []
    for y in range(2):
        for z in range(nz):
            piece = (z + k) % nz
            pairs.append((y * nz + z, (piece // many) * nz + y * many + piece % many))
    return pairs


def turned(pieces, shift):
    n = len(pieces)
    options = [jnp.stack([pieces[(i + s) % n] for i in range(n)]) for s in range(n)]
    return lax.select_n(lax.rem(shift + n, n), *options)


def to_groups(stored, extra, *earlier):
    count, _, t, width = stored.shape
    nz = 2 * count
    y, z = lax.axis_index("y"), lax.axis_index("z")
    arrived = []
    for k in range(nz):
        place = lax.rem(z + k, nz)
        corner = (lax.rem(place, count), lax.div(place, count), 0, 0)
        piece = lax.dynamic_slice(stored, corner, (1, 1, t, width)).reshape(t, width)
        if extra is not None:
            piece = jnp.concatenate([piece, extra])
        if earlier:
            piece = after(piece, *earlier)
        arrived.append(lax.ppermute(piece, ("y", "z"), routes(nz, k)))
    mine = y * count + lax.rem(z, count)
    return [arrived[(nz - i) % nz] for i in range(nz)], nz - mine


def from_groups(mine):
    nz, t, width = mine.shape
    y, z = lax.axis_index("y"), lax.axis_index("z")
    count = nz // 2
    own = y * count + lax.rem(z, count)
    arrived = []
    for k in range(nz):
        piece = pick(mine, lax.rem(own - k + nz, nz), 0)
        arrived.append(lax.ppermute(piece, ("y", "z"), [(b, a) for a, b in routes(nz, k)]))
    return arrived


def settle_kernel(shift_ref, *refs):
    pieces, out_ref = refs[:-1], refs[-1]
    count = len(pieces)
    for k in range(count):

        @pl.when(lax.rem(pl.program_id(0) + shift_ref[0], count) == k)
        def _():
            out_ref[0, 0] = pieces[k][...].astype(out_ref.dtype)


def settle(arrived, dtype):
    nz = len(arrived)
    t, width = arrived[0].shape
    count = nz // 2
    shift = (nz - lax.axis_index("z")).astype(jnp.int32).reshape(1)
    out = pl.pallas_call(
        settle_kernel,
        grid=(nz,),
        in_specs=[pl.BlockSpec(memory_space=pltpu.SMEM)]
        + [pl.BlockSpec((t, width), lambda i: (0, 0))] * nz,
        out_specs=pl.BlockSpec((1, 1, t, width), lambda i: (lax.rem(i, count), lax.div(i, count), 0, 0)),
        out_shape=jax.ShapeDtypeStruct((count, 2, t, width), dtype),
        compiler_params=params(1),
        cost_estimate=cost(0, 6 * nz * t * width),
        name="settle",
    )(shift, *arrived)
    return out.reshape(count, 2 * t, width)


def settle_plain(arrived, dtype):
    nz = len(arrived)
    t, width = arrived[0].shape
    back = turned(arrived, nz - lax.axis_index("z")).reshape(2, nz // 2, t, width)
    return back.transpose(1, 0, 2, 3).reshape(nz // 2, 2 * t, width).astype(dtype)


def sum_all(value, nx, nz, *earlier):
    value = value + hop(value, "c")
    value = value + hop(value, "x") if nx == 2 else lax.psum(value, "x")
    value = value + hop(value, "y")
    value = after(value, *earlier)
    step = 1
    while step < nz:
        value = value + lax.ppermute(value, "z", [(i, i ^ step) for i in range(nz)])
        step *= 2
    return value


def body(
    nx, nz, nc, inputs, lengths, attn_gain, ffn_gain, query_key, value_proj, out_proj, gate_up, down_proj, bias_table, cotangent
):
    x, y = lax.axis_index("x"), lax.axis_index("y")
    c, z = lax.axis_index("c"), lax.axis_index("z")
    width = inputs.shape[2]
    features = nz * width
    quarter = y * nc + c
    parts = 2 * nc
    buckets, mine = bias_table.shape
    count = inputs.shape[1] // 2

    stored_in = inputs.reshape(inputs.shape[0], 2, count, width)
    stored_cot = cotangent.reshape(stored_in.shape)
    small = jnp.concatenate(
        [attn_gain[None], ffn_gain[None], jnp.pad(bias_table.reshape(1, -1), ((0, 0), (0, width - buckets * mine)))]
    )
    small = jnp.pad(small, ((0, 5), (0, 0)))

    query_key_rows = jnp.transpose(query_key, (1, 2, 3, 0))
    value_rows = jnp.transpose(value_proj, (1, 2, 0))
    gate_up_rows = jnp.transpose(gate_up, (1, 2, 3, 0))
    heads = value_rows.shape[0] // parts
    units = gate_up_rows.shape[0] // parts
    unit = gate_up_rows.shape[2]
    local_heads = nc * heads

    def own(rows, size):
        return lax.dynamic_slice_in_dim(rows, quarter * size, size, 0)

    def flat(rows):
        return rows.reshape(-1, width)

    def spread(blocks):
        rows = jnp.concatenate([flat(block) for block in blocks])
        gathered = lax.all_gather(rows, ("z", "c"), axis=0, tiled=True)
        return gathered.reshape(nz, nc, rows.shape[0], width)

    own_pair = own(query_key_rows, heads)
    own_attn = [own_pair[:, 0], own_pair[:, 1], own(value_rows, heads), own(out_proj, heads)]
    w_attn = spread(own_attn[:-1])
    w_out = spread(own_attn[-1:])
    qkv_count, out_count = 3 * heads * 64, heads * 64

    arrived, shift = to_groups(stored_in, small)
    first_in = arrived[0]
    arrived = turned(arrived, shift)
    tokens = arrived[:, :count].astype(F32)
    small = arrived[:, count:]
    gain_one = small[:, :1].astype(F32)
    gain_two = small[:, 1:2].astype(F32)
    table = small[:, 2, : buckets * mine].reshape(nz, buckets, mine).transpose(0, 2, 1)
    table = table.reshape(-1, buckets).astype(F32)
    table = lax.dynamic_slice_in_dim(table, y * local_heads, local_heads, 0)

    both_lengths = jnp.stack([lengths, lax.ppermute(lengths, "y", swap)])
    both_lengths = jnp.where(y == 0, both_lengths, both_lengths[::-1]).reshape(-1)
    length = lax.dynamic_slice_in_dim(both_lengths, z, 1, 0)
    slots = (x * 2 + y) * count + jnp.arange(count, dtype=jnp.int32)
    live = (slots < length).astype(F32)[None, :, None]

    def scale_of(values):
        squares = jnp.sum(values * values, axis=(0, 2), keepdims=True)
        return lax.rsqrt(squares / features + norm_eps)

    def norm_back(values, scale, gain, grad):
        inner = jnp.sum(values * gain * grad, axis=(0, 2), keepdims=True)
        out = scale * gain * grad - values * (scale * scale * scale) * inner / features
        return out, jnp.sum(values * scale * grad, axis=1)

    def reduce(partial):
        rows = partial.reshape(nz * partial.shape[1], width)
        return lax.psum_scatter(rows, ("z", "c"), scatter_dimension=0, tiled=True)

    fits = nx == 2 and heads == 4 and count == 256 and units * unit % 640 == 0 and nz % 2 == 0
    if fits:
        forward, backward, gather, scatter = attend, attend_back, gather_tokens, scatter_tokens
        nt, nn, tn, ffn_one, ffn_two = mm_nt, mm_nn, mm_tn, ffn_in, ffn_back
        shared, stored_from = share, settle
    else:
        forward, backward, gather, scatter = attend_plain, attend_back_plain, gather_plain, scatter_plain
        nt, nn, tn, ffn_one, ffn_two = mm_nt_plain, mm_nn_plain, mm_tn_plain, ffn_in_plain, ffn_back_plain
        shared, stored_from = share_plain, settle_plain
    near_x, near_y = jnp.array([0, 0, 1, 1]) ^ x, jnp.array([0, 1, 0, 1]) ^ y
    starts = ((near_x * 2 + near_y) * count).astype(jnp.int32)

    def attend_back_all(grad, *last):
        if not fits:
            grads, table_grad = backward(projected, length, table, grad, lse, nc, heads)
            return (grads,), table_grad
        first = backward(0, projected, length, table, grad, lse[0])
        second = backward(1, after(projected, first[0], *last), length, table, grad, lse[1])
        return (first[0], second[0]), jnp.concatenate([first[1], second[1]])

    scale_one = scale_of(tokens)
    normed, normed_first, _ = gather((tokens * scale_one * gain_one).astype(BF))
    own_pair = own(after(gate_up_rows, *normed_first), units)
    w_gate_up = spread([own_pair[:, 0], own_pair[:, 1]])
    w_down = spread([own(after(down_proj, *normed_first), units)])
    upstream = live * turned(*to_groups(stored_cot, None, first_in)).astype(F32)
    upstream_rounded = after(upstream.astype(BF), w_attn)
    projected = nt(normed, w_attn, 0, qkv_count, starts)
    if fits:
        first = forward(0, projected, length, table)
        grad_ffn, cot_first, cot_last = gather(upstream_rounded, first[0])
        second = forward(1, after(projected, first[0], *cot_first), length, table)
        attended, lse = (first[0], second[0]), (first[1], second[1])
    else:
        grad_ffn, _, cot_last = gather(upstream_rounded)
        attended, lse = forward(projected, length, table, nc, heads)
        attended = (attended,)
    heads_out = [after(attended[0], *cot_last), *attended[1:]]
    hidden = tokens + scatter(nn(heads_out, w_out, 0, out_count, starts))[0]
    scale_two = scale_of(hidden)
    normed_two, _, _ = gather((hidden * scale_two * gain_two).astype(BF))
    gate, up, activated = ffn_one(normed_two, w_gate_up, starts)

    down_partial = tn([activated], grad_ffn, starts)
    down_part = reduce(down_partial)
    grad_gate_up = ffn_two(grad_ffn, w_down, after(gate, down_partial), up, starts)
    two_parts = nn([grad_gate_up], w_gate_up, 0, 2 * units * unit, starts)
    grad_two, two_first, _ = scatter(two_parts)
    gate_up_partial = tn([after(grad_gate_up, two_parts[0])], normed_two, starts)
    gate_up_part = reduce(after(gate_up_partial, down_part, *two_first))
    branch_parts = nn([after(activated, gate_up_partial)], w_down, 0, units * unit, starts)
    through, ffn_gain_part = norm_back(hidden, scale_two, gain_two, grad_two)
    grad_hidden = upstream + through
    grad_branch, _, branch_last = gather(after(grad_hidden.astype(BF), branch_parts[0]))
    grad_attended = nt(grad_branch, w_out, 0, out_count, starts)
    out_partial = tn(attended, grad_branch, starts)
    branch_parts = [after(part, *branch_last) for part in branch_parts]
    branch, branch_first, branch_last = scatter(branch_parts)
    down_pieces, down_last = shared(after(down_part, grad_attended))
    grad_projected, table_part = attend_back_all(after(grad_attended, out_partial), *branch_first)
    out_part = reduce(out_partial)
    last = after(grad_projected[-1], *branch_last, down_last)
    grad_projected = [*grad_projected[:-1], last]
    qkv_partial = tn(grad_projected, normed, starts)
    qkv_part = reduce(after(qkv_partial, out_part))
    one_parts = nn(grad_projected, w_attn, 0, qkv_count, starts)
    gate_up_pieces, gate_up_last = shared(after(gate_up_part, grad_projected[0]))
    outputs = from_groups((live * (hidden + branch)).astype(BF))
    grad_one, _, one_last = scatter(one_parts, gate_up_last, *outputs)
    through, attn_gain_part = norm_back(tokens, scale_one, gain_one, grad_one)
    input_grad = input_last = from_groups((grad_hidden + through).astype(BF))
    outputs = stored_from(outputs, BF)

    out_pieces, _ = shared(after(out_part, *one_last))
    qkv_pieces, _ = shared(after(qkv_part, *one_last))
    if fits:
        here = jnp.stack([y, c]).astype(jnp.int32)

        def write_rows(source, outs):
            outs[0][...] = source[...].astype(F32)

        def write_qkv(source, outs):
            for h in range(heads):
                for i in range(3):
                    value = source[(i * heads + h) * 64 : (i * heads + h + 1) * 64, :].astype(F32)
                    if i == 2:
                        outs[1][h] = value
                    else:
                        outs[0][h, i] = value

        def write_gate_up(source, outs):
            for u in range(units):
                for i in range(2):
                    first = (i * units + u) * unit
                    outs[0][u, i] = source[first : first + unit, :].astype(F32)

        (down_all,) = place(down_pieces, here, [(units * unit, width)], write_rows)
        (out_all,) = place(out_pieces, here, [(heads * 64, width)], write_rows)
        (gate_up_all,) = place(gate_up_pieces, here, [(units, 2, unit, width)], write_gate_up)
        query_key_all, value_all = place(
            qkv_pieces, here, [(heads, 2, 64, width), (heads, 64, width)], write_qkv
        )
    else:
        down_all, out_all = down_pieces.astype(F32), out_pieces.astype(F32)
        gate_up_all = gate_up_pieces.astype(F32).reshape(parts, 2, units, unit, width)
        gate_up_all = gate_up_all.transpose(0, 2, 1, 3, 4).reshape(-1, 2, unit, width)
        qkv_all = qkv_pieces.astype(F32).reshape(parts, 3, heads, 64, width)
        qkv_all = qkv_all.transpose(0, 2, 1, 3, 4).reshape(-1, 3, 64, width)
        query_key_all, value_all = qkv_all[:, :2], qkv_all[:, 2]
    input_grad = [after(part, down_all, out_all, gate_up_all) for part in input_grad]
    input_grad = stored_from(input_grad, F32)
    down_all, out_all = down_all.reshape(down_proj.shape), out_all.reshape(out_proj.shape)

    table_part = jnp.sum(table_part, axis=2)
    every = jnp.zeros((nx * 2 * local_heads, table_part.shape[1]), F32)
    every = lax.dynamic_update_slice_in_dim(every, table_part, (x * 2 + y) * local_heads, 0)
    both = jnp.concatenate([attn_gain_part, ffn_gain_part])
    if every.size % width == 0:
        both = sum_all(jnp.concatenate([both, every.reshape(-1, width)]), nx, nz, *input_last)
        every = both[2 * nz :].reshape(-1, buckets)
    else:
        both, every = sum_all(both, nx, nz), sum_all(every, nx, nz)
    attn_gain_grad, ffn_gain_grad = both[:nz], both[nz : 2 * nz]
    table_grad = lax.dynamic_slice_in_dim(every, (x * nz + z) * mine, mine, 0).T
    return (
        outputs,
        input_grad,
        pick(attn_gain_grad, z, 0),
        pick(ffn_gain_grad, z, 0),
        query_key_all.transpose(3, 0, 1, 2),
        value_all.transpose(2, 0, 1),
        out_all,
        gate_up_all.transpose(3, 0, 1, 2),
        down_all,
        table_grad,
    )


def solution(mesh):
    dp, nx, nz = (mesh.shape[name] for name in ("dp", "gx", "gy"))
    nc = dp // 2
    split = Mesh(mesh.devices.reshape(2, nc, nx, nz), ("y", "c", "x", "z"))
    seq = ("y", "c")
    return jax.shard_map(
        functools.partial(body, nx, nz, nc),
        mesh=split,
        in_specs=(
            P(seq, "x", "z"),
            P(seq),
            P("z"),
            P("z"),
            P("z", "x", None, None),
            P("z", "x", None),
            P("x", None, "z"),
            P("z", "x", None, None),
            P("x", None, "z"),
            P(None, ("x", "z")),
            P(seq, "x", "z"),
        ),
        out_specs=(
            P(seq, "x", "z"),
            P(seq, "x", "z"),
            P("z"),
            P("z"),
            P("z", "x", None, None),
            P("z", "x", None),
            P("x", None, "z"),
            P("z", "x", None, None),
            P("x", None, "z"),
            P(None, ("x", "z")),
        ),
        check_vma=False,
    )
```

```python
import functools
import math

import jax
import jax.numpy as jnp
from jax import lax
from jax.experimental import pallas as pl
from jax.experimental.pallas import tpu as pltpu
from jax.sharding import Mesh
from jax.sharding import PartitionSpec as P

norm_eps = 1e-06
masked_score = -1e30
bucket_edges = (12, 16, 23, 32, 46, 64, 91)
BF = jnp.bfloat16
F32 = jnp.float32
LB = 128
VMEM = 60 * 1024 * 1024
swap = [(0, 1), (1, 0)]
gelu_a = math.sqrt(2.0 / math.pi)
gelu_b = 0.044715


def bucket_index(offset):
    magnitude = jnp.abs(offset)
    far_bucket = 8 + sum(((magnitude >= boundary).astype(jnp.int32) for boundary in bucket_edges))
    near_bucket = jnp.where(magnitude < 8, magnitude, far_bucket)
    return near_bucket + 16 * (offset > 0).astype(jnp.int32)


def cost(flops, moved):
    return pl.CostEstimate(flops=int(flops), bytes_accessed=int(moved), transcendentals=0)


def params(steps):
    return pltpu.CompilerParams(
        dimension_semantics=("arbitrary",) * steps, vmem_limit_bytes=VMEM
    )


def dot_nt(a, b):
    return lax.dot_general(a, b, (((1,), (1,)), ((), ())), preferred_element_type=F32)


def dot_nn(a, b):
    return lax.dot_general(a, b, (((1,), (0,)), ((), ())), preferred_element_type=F32)


def spot_of(starts_ref, d, count):
    return pl.ds(pl.multiple_of(starts_ref[d], 256), count)


def piece_specs(pieces):
    shape = pieces[0].shape
    return [pl.BlockSpec(shape, lambda *_: (0, 0, 0)) for _ in pieces]


def nt_sum(piece_refs, d, w_of):
    half = piece_refs[0].shape[0]
    acc = None
    for z in range(2 * half):
        part = dot_nt(piece_refs[4 * (z // half) + d][z % half], w_of(z))
        acc = part if acc is None else acc + part
    return acc


def nt_kernel(starts_ref, *refs):
    pieces, (w_ref, out_ref) = refs[:8], refs[8:]
    for d in range(4):
        acc = nt_sum(pieces, d, lambda z: w_ref[z, 0])
        out_ref[spot_of(starts_ref, d, acc.shape[0]), :] = acc.astype(BF)


def mm_nt(pieces, w, first, rows, starts):
    nz, nc, _, width = w.shape
    total = 4 * pieces[0].shape[1]
    count, skip = rows // 256, first // 256
    return pl.pallas_call(
        nt_kernel,
        grid=(nc, count),
        in_specs=[pl.BlockSpec(memory_space=pltpu.SMEM)]
        + piece_specs(pieces)
        + [pl.BlockSpec((nz, 1, 256, width), lambda c, i: (0, c, skip + i, 0))],
        out_specs=pl.BlockSpec((total, 256), lambda c, i: (0, c * count + i)),
        out_shape=jax.ShapeDtypeStruct((total, nc * rows), BF),
        compiler_params=params(2),
        cost_estimate=cost(
            2 * nz * total * width * nc * rows, 2 * nz * width * (total + nc * rows) + 2 * total * nc * rows
        ),
        name="product_nt",
    )(starts, *pieces, w)


def nn_kernel(count, starts_ref, *refs):
    grads, (w_ref, low_out, low_keep, high_out, high_keep) = refs[:count], refs[count:]
    nc, rows, width = w_ref.shape[1:]
    t = grads[0].shape[0] // 4
    in_low = pl.program_id(0) < pl.num_programs(0) // 2

    def product(d):
        spot = spot_of(starts_ref, d, t)
        if count == 1:
            return dot_nn(grads[0][spot, :], w_ref[0].reshape(nc * rows, width)).astype(BF)
        return sum(dot_nn(grads[c][spot, :], w_ref[0, c]) for c in range(count)).astype(BF)

    @pl.when(in_low)
    def _():
        for d in range(4):
            (low_out if d // 2 else low_keep)[d % 2, 0] = product(d)

    @pl.when(jnp.logical_not(in_low))
    def _():
        for d in range(4):
            (high_out if d % 2 else high_keep)[d // 2, 0] = product(d)


def mm_nn(grads, w, first, rows, starts):
    total = grads[0].shape[0]
    nz, nc, _, width = w.shape
    skip, half, t = first // rows, nz // 2, total // 4
    low = pl.BlockSpec((2, 1, t, width), lambda z: (0, jnp.minimum(z, half - 1), 0, 0))
    high = pl.BlockSpec((2, 1, t, width), lambda z: (0, jnp.maximum(z - half, 0), 0, 0))
    return pl.pallas_call(
        functools.partial(nn_kernel, len(grads)),
        grid=(nz,),
        in_specs=[pl.BlockSpec(memory_space=pltpu.SMEM)]
        + [pl.BlockSpec(grad.shape, lambda z: (0, 0)) for grad in grads]
        + [pl.BlockSpec((1, nc, rows, width), lambda z: (z, 0, skip, 0))],
        out_specs=[low, low, high, high],
        out_shape=[jax.ShapeDtypeStruct((2, half, t, width), BF)] * 4,
        compiler_params=params(1),
        cost_estimate=cost(
            2 * nz * total * width * nc * rows, 2 * nz * width * (total + nc * rows) + 2 * total * nc * rows
        ),
        name="product_nn",
    )(starts, *grads, w)


def tn_kernel(count, starts_ref, *refs):
    grads, pieces, out_ref = refs[:count], refs[count:-1], refs[-1]
    half, t, _ = pieces[0].shape

    def one(grad_ref):
        turned = [grad_ref[spot_of(starts_ref, d, t), :].T for d in range(4)]
        for z in range(2 * half):
            acc = dot_nn(turned[0], pieces[4 * (z // half)][z % half])
            for d in range(1, 4):
                acc += dot_nn(turned[d], pieces[4 * (z // half) + d][z % half])
            out_ref[z] = acc.astype(BF)

    if count == 1:
        one(grads[0])
    else:
        for c in range(count):

            @pl.when(pl.program_id(0) // (pl.num_programs(0) // count) == c)
            def _():
                one(grads[c])


def mm_tn(grads, pieces, starts):
    total, rows = grads[0].shape
    half, _, width = pieces[0].shape
    nz, count = 2 * half, len(grads)
    block = next(b for b in (640, 384, 256) if rows % b == 0)
    steps = rows // block

    def spec(c):
        return pl.BlockSpec((total, block), lambda i: (0, jnp.clip(i - c * steps, 0, steps - 1)))

    return pl.pallas_call(
        functools.partial(tn_kernel, count),
        grid=(count * steps,),
        in_specs=[pl.BlockSpec(memory_space=pltpu.SMEM)]
        + [spec(c) for c in range(count)]
        + piece_specs(pieces),
        out_specs=pl.BlockSpec((nz, block, width), lambda i: (0, i, 0)),
        out_shape=jax.ShapeDtypeStruct((nz, count * rows, width), BF),
        compiler_params=params(1),
        cost_estimate=cost(
            2 * nz * total * width * count * rows, 2 * nz * width * (total + count * rows) + 2 * total * count * rows
        ),
        name="product_tn",
    )(starts, *grads, *pieces)


def gelu_parts(gate):
    curve = jnp.tanh(gelu_a * (gate + gelu_b * gate * gate * gate))
    value = 0.5 * gate * (1.0 + curve)
    slope = 0.5 * (1.0 + curve) + 0.5 * gate * (1.0 - curve * curve) * gelu_a * (
        1.0 + 3.0 * gelu_b * gate * gate
    )
    return value, slope


def ffn_in_kernel(starts_ref, *refs):
    pieces, (w_ref, gate_ref, up_ref, active_ref) = refs[:8], refs[8:]
    _, _, _, block, width = w_ref.shape
    for d in range(4):
        acc = nt_sum(pieces, d, lambda z: w_ref[z, 0].reshape(2 * block, width))
        spot = spot_of(starts_ref, d, acc.shape[0])
        gate, up = acc[:, :block], acc[:, block:]
        value = 0.5 * gate * (1.0 + jnp.tanh(gelu_a * (gate + gelu_b * gate * gate * gate)))
        gate_ref[spot, :] = gate.astype(BF)
        up_ref[spot, :] = up.astype(BF)
        active_ref[spot, :] = (value * up).astype(BF)


def ffn_in(pieces, w, starts):
    nz, nc, rows, width = w.shape
    half, total = rows // 2, 4 * pieces[0].shape[1]
    count = half // 128
    block = pl.BlockSpec((total, 128), lambda c, i: (0, c * count + i))
    return pl.pallas_call(
        ffn_in_kernel,
        grid=(nc, count),
        in_specs=[pl.BlockSpec(memory_space=pltpu.SMEM)]
        + piece_specs(pieces)
        + [pl.BlockSpec((nz, 1, 2, 128, width), lambda c, i: (0, c, 0, i, 0))],
        out_specs=[block, block, block],
        out_shape=[jax.ShapeDtypeStruct((total, nc * half), BF)] * 3,
        compiler_params=params(2),
        cost_estimate=cost(
            2 * nz * total * width * nc * rows, 2 * nz * width * (total + nc * rows) + 3 * total * nc * rows
        ),
        name="ffn_in",
    )(starts, *pieces, w.reshape(nz, nc, 2, half, width))


def ffn_back_kernel(starts_ref, *refs):
    pieces, (w_ref, gate_ref, up_ref, out_ref) = refs[:8], refs[8:]
    half = w_ref.shape[2]
    for d in range(4):
        acc = nt_sum(pieces, d, lambda z: w_ref[z, 0])
        spot = spot_of(starts_ref, d, acc.shape[0])
        value, slope = gelu_parts(gate_ref[spot, :].astype(F32))
        out_ref[spot, :half] = (acc * up_ref[spot, :].astype(F32) * slope).astype(BF)
        out_ref[spot, half:] = (acc * value).astype(BF)


def ffn_back(pieces, w, gate, up, starts):
    nz, nc, half, width = w.shape
    total = gate.shape[0]
    kept = pl.BlockSpec((total, half), lambda c: (0, c))
    return pl.pallas_call(
        ffn_back_kernel,
        grid=(nc,),
        in_specs=[pl.BlockSpec(memory_space=pltpu.SMEM)]
        + piece_specs(pieces)
        + [pl.BlockSpec((nz, 1, half, width), lambda c: (0, c, 0, 0)), kept, kept],
        out_specs=pl.BlockSpec((total, 2 * half), lambda c: (0, c)),
        out_shape=jax.ShapeDtypeStruct((total, nc * 2 * half), BF),
        compiler_params=params(1),
        cost_estimate=cost(
            2 * nz * total * width * nc * half, 2 * nz * width * (total + nc * half) + 8 * total * nc * half
        ),
        name="ffn_back",
    )(starts, *pieces, w, gate, up)


def mm_nt_plain(act, w, first, rows, starts):
    part = lax.slice_in_dim(w, first, first + rows, axis=2)
    out = jnp.einsum("ztf,zcrf->tcr", act, part, preferred_element_type=F32)
    return out.astype(BF).reshape(act.shape[1], -1)


def mm_nn_plain(grads, w, first, rows, starts):
    grad = grads[0]
    part = lax.slice_in_dim(w, first, first + rows, axis=2)
    split = grad.reshape(grad.shape[0], w.shape[1], rows)
    out = jnp.einsum("tcr,zcrf->ztf", split, part, preferred_element_type=F32)
    return [out.astype(BF)]


def mm_tn_plain(grads, act, starts):
    return jnp.einsum("tr,ztf->zrf", grads[0], act, preferred_element_type=F32).astype(BF)


def ffn_in_plain(act, w, starts):
    _, nc, rows, _ = w.shape
    total = act.shape[1]
    both = jnp.einsum("ztf,zcrf->tcr", act, w, preferred_element_type=F32)
    gate, up = both[:, :, : rows // 2], both[:, :, rows // 2 :]
    value, _ = gelu_parts(gate)
    return [part.astype(BF).reshape(total, -1) for part in (gate, up, value * up)]


def ffn_back_plain(act, w, gate, up, starts):
    total, nc = gate.shape[0], w.shape[1]
    grad = jnp.einsum("ztf,zcrf->tcr", act, w, preferred_element_type=F32)
    value, slope = gelu_parts(gate.astype(F32).reshape(grad.shape))
    both = [grad * up.astype(F32).reshape(grad.shape) * slope, grad * value]
    return jnp.concatenate(both, axis=2).astype(BF).reshape(total, -1)


def near_buckets(tile, total):
    first = (total // LB - 2 + tile) * LB
    rows = lax.broadcasted_iota(jnp.int32, (LB, LB), 0)
    lanes = lax.broadcasted_iota(jnp.int32, (LB, LB), 1)
    return bucket_index(first + rows - (total - LB) - lanes)


def build_strips(table_ref, strip_ref, total, group):
    heads = strip_ref.shape[0]
    near = (total // LB - 2) * LB
    for h in range(heads):
        head = group * heads + h
        strip_ref[h, :near] = jnp.full((near, LB), table_ref[head, 15], F32)
        strip_ref[h, near + 3 * LB :] = jnp.full((near, LB), table_ref[head, 31], F32)

    def one_tile(tile, _):
        index = near_buckets(tile, total)
        vals = [jnp.full((LB, LB), table_ref[group * heads + h, 0], F32) for h in range(heads)]
        for b in range(1, 32):
            hit = index == b
            vals = [
                jnp.where(hit, table_ref[group * heads + h, b], vals[h]) for h in range(heads)
            ]
        for h in range(heads):
            strip_ref[h, pl.ds(pl.multiple_of(near + tile * LB, LB), LB)] = vals[h]
        return 0

    lax.fori_loop(0, 3, one_tile, 0)


def head_lanes(shape, h):
    lanes = lax.broadcasted_iota(jnp.int32, shape, 1)
    return lanes // 64 == h, lanes == ((h + 1) % 4) * 64


def mask_keys(keys, length, h):
    own, spare = head_lanes(keys.shape, h)
    dead = lax.broadcasted_iota(jnp.int32, keys.shape, 0) >= length
    mask = jnp.where(jnp.logical_and(spare, dead), masked_score, 0.0)
    return jnp.where(own, keys.astype(F32), mask).astype(BF)


def with_one(queries, h):
    _, spare = head_lanes(queries.shape, h)
    return jnp.where(spare, 1.0, queries.astype(F32)).astype(BF)


def own_lanes(values, h):
    own, _ = head_lanes(values.shape, h)
    return jnp.where(own, values.astype(F32), 0.0).astype(BF)


def block_bias(strip_ref, h, block, total):
    first = total - LB - 2 * block * LB
    left = strip_ref[h, pl.ds(pl.multiple_of(first, LB), total)]
    right = strip_ref[h, pl.ds(pl.multiple_of(first - LB, LB), total)]
    return jnp.concatenate([left, right], axis=1)


def attend_kernel(group, length_ref, table_ref, q_ref, k_ref, v_ref, out_ref, lse_ref, strip, heads_k, turned_v, turned_out):
    total = q_ref.shape[0]
    heads = strip.shape[0]
    build_strips(table_ref, strip, total, group)
    turned_v[...] = v_ref[...].astype(F32).T.astype(BF)
    for h in range(heads):
        heads_k[h] = mask_keys(k_ref[...], length_ref[0], h)

    def one_block(block, _):
        spot = pl.ds(pl.multiple_of(block * 256, 256), 256)
        queries = q_ref[spot]
        for h in range(heads):
            scores = dot_nt(heads_k[h], with_one(queries, h)) + block_bias(strip, h, block, total)
            largest = jnp.max(scores, axis=0, keepdims=True)
            raised = jnp.exp(scores - largest)
            totals = jnp.sum(raised, axis=0, keepdims=True)
            out = dot_nn(turned_v[h * 64 : (h + 1) * 64], raised.astype(BF))
            turned_out[h * 64 : (h + 1) * 64, spot] = out * (1.0 / totals)
            lse_ref[h : h + 1, spot] = largest + jnp.log(totals)
        return 0

    lax.fori_loop(0, total // 256, one_block, 0)
    out_ref[...] = turned_out[...].T.astype(BF)


def attend_back_kernel(
    group, length_ref, table_ref, q_ref, k_ref, v_ref, grad_ref, lse_ref, out_ref, table_grad_ref,
    strip, strip_grad, heads_k, turned_k, turned_q, ds_ref, p_ref, dk_ref, dv_ref,
):
    total = q_ref.shape[0]
    heads = strip.shape[0]
    build_strips(table_ref, strip, total, group)
    strip_grad[...] = jnp.zeros_like(strip_grad)
    dk_ref[...] = jnp.zeros_like(dk_ref)
    dv_ref[...] = jnp.zeros_like(dv_ref)
    turned_k[...] = k_ref[...].astype(F32).T.astype(BF)
    for h in range(heads):
        heads_k[h] = mask_keys(k_ref[...], length_ref[0], h)

    def one_block(block, _):
        spot = pl.ds(pl.multiple_of(block * 256, 256), 256)
        queries, grads = q_ref[spot], grad_ref[spot]
        own_q, own_g = [], []
        for h in range(heads):
            own_q.append(own_lanes(queries, h))
            own_g.append(own_lanes(grads, h))
            scores = dot_nt(heads_k[h], with_one(queries, h)) + block_bias(strip, h, block, total)
            probs = jnp.exp(scores - lse_ref[h : h + 1, spot])
            weighed = probs * dot_nt(v_ref[...], own_g[h])
            delta = jnp.sum(weighed, axis=0, keepdims=True)
            grad_scores = weighed - probs * delta
            first = total - LB - 2 * block * LB
            left = pl.ds(pl.multiple_of(first, LB), total)
            right = pl.ds(pl.multiple_of(first - LB, LB), total)
            strip_grad[h, left] += grad_scores[:, :LB]
            strip_grad[h, right] += grad_scores[:, LB:]
            rounded = grad_scores.astype(BF)
            ds_ref[:, h * 256 : (h + 1) * 256] = rounded
            p_ref[:, h * 256 : (h + 1) * 256] = probs.astype(BF)
            turned_q[h * 64 : (h + 1) * 64, spot] = dot_nn(turned_k[h * 64 : (h + 1) * 64], rounded)
        dk_ref[...] += dot_nn(ds_ref[...], jnp.concatenate(own_q, axis=0))
        dv_ref[...] += dot_nn(p_ref[...], jnp.concatenate(own_g, axis=0))
        return 0

    lax.fori_loop(0, total // 256, one_block, 0)
    out_ref[:, :256] = turned_q[...].T.astype(BF)
    out_ref[:, 256:512] = dk_ref[...].astype(BF)
    out_ref[:, 512:] = dv_ref[...].astype(BF)

    near = (total // LB - 2) * LB
    for h in range(heads):
        table_grad_ref[h] = jnp.zeros((32, LB), F32)
        table_grad_ref[h, 15:16] = jnp.sum(strip_grad[h, :near], axis=0, keepdims=True)
        table_grad_ref[h, 31:32] = jnp.sum(strip_grad[h, near + 3 * LB :], axis=0, keepdims=True)

    def one_tile(tile, _):
        index = near_buckets(tile, total)
        spot = pl.ds(pl.multiple_of(near + tile * LB, LB), LB)
        for h in range(heads):
            grads = strip_grad[h, spot]
            for b in range(32):
                picked = jnp.where(index == b, grads, 0.0)
                table_grad_ref[h, b : b + 1] += jnp.sum(picked, axis=0, keepdims=True)
        return 0

    lax.fori_loop(0, 3, one_tile, 0)


def block_specs(total, group):
    def spec(i):
        return pl.BlockSpec((total, 256), lambda _: (0, 3 * group + i))

    smem = pl.BlockSpec(memory_space=pltpu.SMEM)
    return [smem, smem, spec(0), spec(1), spec(2)]


def attend(group, projected, length, table):
    total = projected.shape[0]
    heads = 4
    return pl.pallas_call(
        functools.partial(attend_kernel, group),
        grid=(1,),
        in_specs=block_specs(total, group),
        out_specs=[
            pl.BlockSpec((total, 256), lambda _: (0, 0)),
            pl.BlockSpec((8, total), lambda _: (0, 0)),
        ],
        out_shape=[
            jax.ShapeDtypeStruct((total, 256), BF),
            jax.ShapeDtypeStruct((8, total), F32),
        ],
        scratch_shapes=[
            pltpu.VMEM((heads, 2 * total - LB, LB), F32),
            pltpu.VMEM((heads, total, 256), BF),
            pltpu.VMEM((256, total), BF),
            pltpu.VMEM((256, total), F32),
        ],
        compiler_params=params(1),
        cost_estimate=cost(heads * total * total * 2 * 256 * 2, 4 * total * 256 * 2),
        name="attend",
    )(length, table, projected, projected, projected)


def attend_back(group, projected, length, table, grad_out, lse):
    total = projected.shape[0]
    heads = 4
    return pl.pallas_call(
        functools.partial(attend_back_kernel, group),
        grid=(1,),
        in_specs=block_specs(total, group)
        + [
            pl.BlockSpec((total, 256), lambda _: (0, group)),
            pl.BlockSpec((8, total), lambda _: (0, 0)),
        ],
        out_specs=[
            pl.BlockSpec((total, 768), lambda _: (0, 0)),
            pl.BlockSpec((heads, 32, LB), lambda _: (0, 0, 0)),
        ],
        out_shape=[
            jax.ShapeDtypeStruct((total, 768), BF),
            jax.ShapeDtypeStruct((heads, 32, LB), F32),
        ],
        scratch_shapes=[
            pltpu.VMEM((heads, 2 * total - LB, LB), F32),
            pltpu.VMEM((heads, 2 * total - LB, LB), F32),
            pltpu.VMEM((heads, total, 256), BF),
            pltpu.VMEM((256, total), BF),
            pltpu.VMEM((256, total), F32),
            pltpu.VMEM((total, heads * 256), BF),
            pltpu.VMEM((total, heads * 256), BF),
            pltpu.VMEM((total, 256), F32),
            pltpu.VMEM((total, 256), F32),
        ],
        compiler_params=params(1),
        cost_estimate=cost(heads * total * total * 2 * 256 * 5, 8 * total * 256 * 2),
        name="attend_back",
    )(length, table, projected, projected, projected, grad_out, lse)


def split_heads(projected, groups, heads):
    parts = projected.reshape(projected.shape[0], groups, 3, heads, 64)
    return [parts[:, :, i].reshape(projected.shape[0], groups * heads, 64) for i in range(3)]


def plain_scores(queries, keys, length, table):
    slots = jnp.arange(keys.shape[0], dtype=jnp.int32)
    picked = (bucket_index(slots[None, :] - slots[:, None])[:, :, None] == jnp.arange(32)).astype(F32)
    bias = jnp.einsum("qkb,hb->hqk", picked, table, precision=lax.Precision.HIGHEST)
    scores = jnp.einsum("qhs,khs->hqk", queries, keys, preferred_element_type=F32) + bias
    return jnp.where(slots < length[0], scores, masked_score), picked


def attend_plain(projected, length, table, groups, heads):
    queries, keys, values = split_heads(projected, groups, heads)
    scores, _ = plain_scores(queries, keys, length, table)
    lse = jax.nn.logsumexp(scores, axis=2)
    probs = jnp.exp(scores - lse[:, :, None]).astype(BF)
    out = jnp.einsum("hqk,khs->qhs", probs, values, preferred_element_type=F32)
    return out.astype(BF).reshape(projected.shape[0], -1), lse


def attend_back_plain(projected, length, table, grad_out, lse, groups, heads):
    total = projected.shape[0]
    queries, keys, values = split_heads(projected, groups, heads)
    grads = grad_out.reshape(queries.shape)
    scores, picked = plain_scores(queries, keys, length, table)
    probs = jnp.exp(scores - lse[:, :, None])
    weighed = probs * jnp.einsum("qhs,khs->hqk", grads, values, preferred_element_type=F32)
    wide = weighed - probs * jnp.sum(weighed, axis=2, keepdims=True)
    rounded = wide.astype(BF)
    parts = [
        jnp.einsum("hqk,khs->qhs", rounded, keys, preferred_element_type=F32),
        jnp.einsum("hqk,qhs->khs", rounded, queries, preferred_element_type=F32),
        jnp.einsum("hqk,qhs->khs", probs.astype(BF), grads, preferred_element_type=F32),
    ]
    parts = [part.astype(BF).reshape(total, groups, 1, heads * 64) for part in parts]
    table_grad = jnp.einsum("hqk,qkb->hb", wide, picked, precision=lax.Precision.HIGHEST)
    return (
        jnp.concatenate(parts, axis=2).reshape(total, -1),
        table_grad.reshape(groups * heads, 32, 1),
    )


def hop(value, axis):
    return lax.ppermute(value, axis, swap)


def pick(value, index, axis):
    return lax.dynamic_index_in_dim(value, index, axis, keepdims=False)


def paired(mine, other, axis, place=0):
    return jnp.where(
        lax.axis_index(axis) == 0,
        jnp.stack([mine, other], axis=place),
        jnp.stack([other, mine], axis=place),
    )


def after(value, *others):
    return lax.optimization_barrier((value, *others))[0]


def gather_plain(part, *beside):
    return lax.all_gather(part, ("x", "y"), axis=1, tiled=True), (), ()


def gather_tokens(part, *beside):
    half = part.shape[0] // 2
    low, high = part[:half], part[half:]
    low_x, high_y = hop(low, "x"), hop(high, "y")
    if beside:
        low_x, high_y = after(low_x, *beside), after(high_y, *beside)
    low_y, high_x = hop(low, "y"), hop(high, "x")
    low_xy, high_xy = hop(low_x, "y"), hop(high_y, "x")
    pieces = [low, low_y, low_x, low_xy, high, high_y, high_x, high_xy]
    return pieces, (low_x, high_y), (low_y, low_xy, high_x, high_xy)


def scatter_plain(parts, *beside):
    whole = parts[0].astype(F32)
    return lax.psum_scatter(whole, ("x", "y"), scatter_dimension=1, tiled=True), (), ()


def scatter_tokens(parts, *beside):
    low_out, low_keep, high_out, high_keep = parts
    low_in, high_in = hop(low_out, "x"), hop(high_out, "y")
    if beside:
        low_in, high_in = after(low_in, *beside), after(high_in, *beside)

    def add(keep, arrived, index):
        return keep[index].astype(F32) + arrived[index].astype(F32)

    low_last = hop(add(low_keep, low_in, 1).astype(BF), "y")
    high_last = hop(add(high_keep, high_in, 1).astype(BF), "x")
    low = add(low_keep, low_in, 0) + low_last.astype(F32)
    high = add(high_keep, high_in, 0) + high_last.astype(F32)
    return jnp.concatenate([low, high], axis=0), (low_in, high_in), (low_last, high_last)


def place_kernel(write, here_ref, *refs):
    pieces, outs = refs[:4], refs[4:]
    step = pl.program_id(0)
    for near in range(4):
        y = here_ref[0] if near < 2 else 1 - here_ref[0]
        c = here_ref[1] if near % 2 == 0 else 1 - here_ref[1]

        @pl.when(step == 2 * y + c)
        def _():
            write(pieces[near], outs)


def place(pieces, here, shapes, write):
    return pl.pallas_call(
        functools.partial(place_kernel, write),
        grid=(4,),
        in_specs=[pl.BlockSpec(memory_space=pltpu.SMEM)]
        + [pl.BlockSpec(piece.shape, lambda q: (0, 0)) for piece in pieces],
        out_specs=[
            pl.BlockSpec(shape, lambda q, rank=len(shape): (q,) + (0,) * (rank - 1)) for shape in shapes
        ],
        out_shape=[jax.ShapeDtypeStruct((4 * shape[0], *shape[1:]), F32) for shape in shapes],
        compiler_params=params(1),
        cost_estimate=cost(0, 20 * pieces[0].size),
        name="place",
    )(here, *pieces)


def share(part):
    over_y = hop(part, "y")
    return [part, hop(part, "c"), over_y, hop(over_y, "c")], over_y


def share_plain(part):
    return lax.all_gather(part, ("y", "c"), axis=0), part


def to_groups(halves, other, extra):
    count, _, t, width = halves.shape
    both = paired(pick(halves, lax.axis_index("y"), 1), other, "y").reshape(2 * count, t, width)
    if extra is not None:
        wide = jnp.broadcast_to(extra[None], (2 * count, *extra.shape))
        both = jnp.concatenate([both, wide], axis=1)
    return lax.all_to_all(both, "z", 0, 0, tiled=True)


def from_groups(mine):
    nz, t, width = mine.shape
    back = lax.all_to_all(mine, "z", 0, 0, tiled=True).reshape(2, nz // 2, t, width)
    leaving = pick(back, 1 - lax.axis_index("y"), 0)
    return (back, hop(leaving, "y")), leaving


def settle_kernel(y_ref, back_ref, other_ref, out_ref):
    j, y = pl.program_id(0), pl.program_id(1)

    @pl.when(y == y_ref[0])
    def _():
        out_ref[0, 0] = back_ref[y, j].astype(out_ref.dtype)

    @pl.when(y != y_ref[0])
    def _():
        out_ref[0, 0] = other_ref[j].astype(out_ref.dtype)


def settle(arrived, dtype):
    back, other = arrived
    _, count, t, width = back.shape
    y = lax.axis_index("y").astype(jnp.int32).reshape(1)
    out = pl.pallas_call(
        settle_kernel,
        grid=(count, 2),
        in_specs=[
            pl.BlockSpec(memory_space=pltpu.SMEM),
            pl.BlockSpec(back.shape, lambda j, y: (0, 0, 0, 0)),
            pl.BlockSpec(other.shape, lambda j, y: (0, 0, 0)),
        ],
        out_specs=pl.BlockSpec((1, 1, t, width), lambda j, y: (j, y, 0, 0)),
        out_shape=jax.ShapeDtypeStruct((count, 2, t, width), dtype),
        compiler_params=params(2),
        cost_estimate=cost(0, 12 * count * t * width),
        name="settle",
    )(y, back, other)
    return out.reshape(count, 2 * t, width)


def settle_plain(arrived, dtype):
    back, other = arrived
    _, count, t, width = back.shape
    both = paired(pick(back, lax.axis_index("y"), 0), other, "y")
    return both.transpose(1, 0, 2, 3).reshape(count, 2 * t, width).astype(dtype)


def sum_all(value, nx, nz, *earlier):
    value = value + hop(value, "c")
    value = value + hop(value, "x") if nx == 2 else lax.psum(value, "x")
    value = value + hop(value, "y")
    value = after(value, *earlier)
    step = 1
    while step < nz:
        value = value + lax.ppermute(value, "z", [(i, i ^ step) for i in range(nz)])
        step *= 2
    return value


def body(
    nx, nz, nc, inputs, lengths, attn_gain, ffn_gain, query_key, value_proj, out_proj, gate_up, down_proj, bias_table, cotangent
):
    x, y = lax.axis_index("x"), lax.axis_index("y")
    c, z = lax.axis_index("c"), lax.axis_index("z")
    width = inputs.shape[2]
    features = nz * width
    quarter = y * nc + c
    parts = 2 * nc
    buckets, mine = bias_table.shape
    count = inputs.shape[1] // 2

    stored_in = inputs.reshape(inputs.shape[0], 2, count, width)
    stored_cot = cotangent.reshape(stored_in.shape)
    small = jnp.concatenate(
        [attn_gain[None], ffn_gain[None], jnp.pad(bias_table.reshape(1, -1), ((0, 0), (0, width - buckets * mine)))]
    )
    small = jnp.pad(small, ((0, 5), (0, 0)))
    leaving = pick(stored_in, 1 - y, 1)

    query_key_rows = jnp.transpose(query_key, (1, 2, 3, 0))
    value_rows = jnp.transpose(value_proj, (1, 2, 0))
    gate_up_rows = jnp.transpose(gate_up, (1, 2, 3, 0))
    heads = value_rows.shape[0] // parts
    units = gate_up_rows.shape[0] // parts
    unit = gate_up_rows.shape[2]
    local_heads = nc * heads

    def own(rows, size):
        return lax.dynamic_slice_in_dim(rows, quarter * size, size, 0)

    def flat(rows):
        return rows.reshape(-1, width)

    def spread(rows):
        gathered = lax.all_gather(rows, ("z", "c"), axis=0, tiled=True)
        return gathered.reshape(nz, nc, rows.shape[0], width)

    own_pair = own(query_key_rows, heads)
    own_attn = [own_pair[:, 0], own_pair[:, 1], own(value_rows, heads), own(out_proj, heads)]
    own_attn = jnp.concatenate([flat(rows) for rows in own_attn])
    w_attn = spread(own_attn)
    other = after(hop(leaving, "y"), own_attn)
    own_pair = own(after(gate_up_rows, other), units)
    own_gate_up = jnp.concatenate([flat(own_pair[:, 0]), flat(own_pair[:, 1])])
    w_gate_up = spread(own_gate_up)
    own_down = flat(own(after(down_proj, other), units))
    w_down = spread(own_down)
    qkv_count, out_count = 3 * heads * 64, heads * 64

    arrived = after(to_groups(stored_in, other, small), own_gate_up, own_down)
    tokens = arrived[:, :count].astype(F32)
    small = arrived[:, count:]
    gain_one = small[:, :1].astype(F32)
    gain_two = small[:, 1:2].astype(F32)
    table = small[:, 2, : buckets * mine].reshape(nz, buckets, mine).transpose(0, 2, 1)
    table = table.reshape(-1, buckets).astype(F32)
    table = lax.dynamic_slice_in_dim(table, y * local_heads, local_heads, 0)

    both_lengths = jnp.stack([lengths, lax.ppermute(lengths, "y", swap)])
    both_lengths = jnp.where(y == 0, both_lengths, both_lengths[::-1]).reshape(-1)
    length = lax.dynamic_slice_in_dim(both_lengths, z, 1, 0)
    slots = (x * 2 + y) * count + jnp.arange(count, dtype=jnp.int32)
    live = (slots < length).astype(F32)[None, :, None]

    def scale_of(values):
        squares = jnp.sum(values * values, axis=(0, 2), keepdims=True)
        return lax.rsqrt(squares / features + norm_eps)

    def norm_back(values, scale, gain, grad):
        inner = jnp.sum(values * gain * grad, axis=(0, 2), keepdims=True)
        out = scale * gain * grad - values * (scale * scale * scale) * inner / features
        return out, jnp.sum(values * scale * grad, axis=1)

    def reduce(partial):
        rows = partial.reshape(nz * partial.shape[1], width)
        return lax.psum_scatter(rows, ("z", "c"), scatter_dimension=0, tiled=True)

    fits = nx == 2 and heads == 4 and count == 256 and units * unit % 640 == 0 and nz % 2 == 0
    if fits:
        forward, backward, gather, scatter = attend, attend_back, gather_tokens, scatter_tokens
        nt, nn, tn, ffn_one, ffn_two = mm_nt, mm_nn, mm_tn, ffn_in, ffn_back
        shared, stored_from = share, settle
    else:
        forward, backward, gather, scatter = attend_plain, attend_back_plain, gather_plain, scatter_plain
        nt, nn, tn, ffn_one, ffn_two = mm_nt_plain, mm_nn_plain, mm_tn_plain, ffn_in_plain, ffn_back_plain
        shared, stored_from = share_plain, settle_plain
    near_x, near_y = jnp.array([0, 0, 1, 1]) ^ x, jnp.array([0, 1, 0, 1]) ^ y
    starts = ((near_x * 2 + near_y) * count).astype(jnp.int32)

    def attend_back_all(grad, *last):
        if not fits:
            grads, table_grad = backward(projected, length, table, grad, lse, nc, heads)
            return (grads,), table_grad
        first = backward(0, projected, length, table, grad, lse[0])
        second = backward(1, after(projected, first[0], *last), length, table, grad, lse[1])
        return (first[0], second[0]), jnp.concatenate([first[1], second[1]])

    scale_one = scale_of(tokens)
    normed, _, _ = gather((tokens * scale_one * gain_one).astype(BF))
    cot_other = hop(pick(stored_cot, 1 - y, 1), "y")
    upstream = live * to_groups(stored_cot, after(cot_other, arrived), None).astype(F32)
    upstream_rounded = after(upstream.astype(BF), w_attn)
    projected = nt(normed, w_attn, 0, qkv_count, starts)
    if fits:
        first = forward(0, projected, length, table)
        grad_ffn, cot_first, cot_last = gather(upstream_rounded, first[0])
        second = forward(1, after(projected, first[0], *cot_first), length, table)
        attended, lse = (first[0], second[0]), (first[1], second[1])
    else:
        grad_ffn, _, cot_last = gather(upstream_rounded)
        attended, lse = forward(projected, length, table, nc, heads)
        attended = (attended,)
    heads_out = [after(attended[0], *cot_last), *attended[1:]]
    hidden = tokens + scatter(nn(heads_out, w_attn, qkv_count, out_count, starts))[0]
    scale_two = scale_of(hidden)
    normed_two, _, _ = gather((hidden * scale_two * gain_two).astype(BF))
    gate, up, activated = ffn_one(normed_two, w_gate_up, starts)

    down_partial = tn([activated], grad_ffn, starts)
    down_part = reduce(down_partial)
    grad_gate_up = ffn_two(grad_ffn, w_down, after(gate, down_partial), up, starts)
    two_parts = nn([grad_gate_up], w_gate_up, 0, 2 * units * unit, starts)
    grad_two, two_first, _ = scatter(two_parts)
    gate_up_partial = tn([after(grad_gate_up, two_parts[0])], normed_two, starts)
    gate_up_part = reduce(after(gate_up_partial, down_part, *two_first))
    branch_parts = nn([after(activated, gate_up_partial)], w_down, 0, units * unit, starts)
    through, ffn_gain_part = norm_back(hidden, scale_two, gain_two, grad_two)
    grad_hidden = upstream + through
    grad_branch, _, branch_last = gather(after(grad_hidden.astype(BF), branch_parts[0]))
    grad_attended = nt(grad_branch, w_attn, qkv_count, out_count, starts)
    out_partial = tn(attended, grad_branch, starts)
    branch_parts = [after(part, *branch_last) for part in branch_parts]
    branch, branch_first, branch_last = scatter(branch_parts)
    down_pieces, down_last = shared(after(down_part, grad_attended))
    grad_projected, table_part = attend_back_all(after(grad_attended, out_partial), *branch_first)
    last = after(grad_projected[-1], *branch_last, down_last)
    grad_projected = [*grad_projected[:-1], last]
    qkv_partial = tn(grad_projected, normed, starts)
    qkv_part = reduce(after(qkv_partial, gate_up_part))
    one_parts = nn(grad_projected, w_attn, 0, qkv_count, starts)
    gate_up_pieces, gate_up_last = shared(after(gate_up_part, grad_projected[0]))
    outputs, _ = from_groups((live * (hidden + branch)).astype(BF))
    grad_one, one_first, one_last = scatter(one_parts, outputs[0], gate_up_last)
    out_part = reduce(after(out_partial, *one_first))
    through, attn_gain_part = norm_back(tokens, scale_one, gain_one, grad_one)
    input_grad, input_leaves = from_groups((grad_hidden + through).astype(BF))
    outputs = stored_from(outputs, BF)

    out_pieces, _ = shared(after(out_part, input_leaves))
    qkv_pieces, _ = shared(after(qkv_part, *one_last))
    if fits:
        here = jnp.stack([y, c]).astype(jnp.int32)

        def write_rows(source, outs):
            outs[0][...] = source[...].astype(F32)

        def write_qkv(source, outs):
            for h in range(heads):
                for i in range(3):
                    value = source[(i * heads + h) * 64 : (i * heads + h + 1) * 64, :].astype(F32)
                    if i == 2:
                        outs[1][h] = value
                    else:
                        outs[0][h, i] = value

        def write_gate_up(source, outs):
            for u in range(units):
                for i in range(2):
                    first = (i * units + u) * unit
                    outs[0][u, i] = source[first : first + unit, :].astype(F32)

        (down_all,) = place(down_pieces, here, [(units * unit, width)], write_rows)
        (out_all,) = place(out_pieces, here, [(heads * 64, width)], write_rows)
        (gate_up_all,) = place(gate_up_pieces, here, [(units, 2, unit, width)], write_gate_up)
        query_key_all, value_all = place(
            qkv_pieces, here, [(heads, 2, 64, width), (heads, 64, width)], write_qkv
        )
    else:
        down_all, out_all = down_pieces.astype(F32), out_pieces.astype(F32)
        gate_up_all = gate_up_pieces.astype(F32).reshape(parts, 2, units, unit, width)
        gate_up_all = gate_up_all.transpose(0, 2, 1, 3, 4).reshape(-1, 2, unit, width)
        qkv_all = qkv_pieces.astype(F32).reshape(parts, 3, heads, 64, width)
        qkv_all = qkv_all.transpose(0, 2, 1, 3, 4).reshape(-1, 3, 64, width)
        query_key_all, value_all = qkv_all[:, :2], qkv_all[:, 2]
    back, other = input_grad
    input_grad = back, after(other, down_all, gate_up_all)
    input_grad = stored_from(input_grad, F32)
    down_all, out_all = down_all.reshape(down_proj.shape), out_all.reshape(out_proj.shape)

    table_part = jnp.sum(table_part, axis=2)
    every = jnp.zeros((nx * 2 * local_heads, table_part.shape[1]), F32)
    every = lax.dynamic_update_slice_in_dim(every, table_part, (x * 2 + y) * local_heads, 0)
    both = jnp.concatenate([attn_gain_part, ffn_gain_part])
    if every.size % width == 0:
        both = sum_all(jnp.concatenate([both, every.reshape(-1, width)]), nx, nz, input_leaves)
        every = both[2 * nz :].reshape(-1, buckets)
    else:
        both, every = sum_all(both, nx, nz), sum_all(every, nx, nz)
    attn_gain_grad, ffn_gain_grad = both[:nz], both[nz : 2 * nz]
    table_grad = lax.dynamic_slice_in_dim(every, (x * nz + z) * mine, mine, 0).T
    return (
        outputs,
        input_grad,
        pick(attn_gain_grad, z, 0),
        pick(ffn_gain_grad, z, 0),
        query_key_all.transpose(3, 0, 1, 2),
        value_all.transpose(2, 0, 1),
        out_all,
        gate_up_all.transpose(3, 0, 1, 2),
        down_all,
        table_grad,
    )


def solution(mesh):
    dp, nx, nz = (mesh.shape[name] for name in ("dp", "gx", "gy"))
    nc = dp // 2
    split = Mesh(mesh.devices.reshape(2, nc, nx, nz), ("y", "c", "x", "z"))
    seq = ("y", "c")
    return jax.shard_map(
        functools.partial(body, nx, nz, nc),
        mesh=split,
        in_specs=(
            P(seq, "x", "z"),
            P(seq),
            P("z"),
            P("z"),
            P("z", "x", None, None),
            P("z", "x", None),
            P("x", None, "z"),
            P("z", "x", None, None),
            P("x", None, "z"),
            P(None, ("x", "z")),
            P(seq, "x", "z"),
        ),
        out_specs=(
            P(seq, "x", "z"),
            P(seq, "x", "z"),
            P("z"),
            P("z"),
            P("z", "x", None, None),
            P("z", "x", None),
            P("x", None, "z"),
            P("z", "x", None, None),
            P("x", None, "z"),
            P(None, ("x", "z")),
        ),
        check_vma=False,
    )
```

```python
import functools
import math

import jax
import jax.numpy as jnp
from jax import lax
from jax.experimental import pallas as pl
from jax.experimental.pallas import tpu as pltpu
from jax.sharding import Mesh
from jax.sharding import PartitionSpec as P

norm_eps = 1e-06
masked_score = -1e30
bucket_edges = (12, 16, 23, 32, 46, 64, 91)
BF = jnp.bfloat16
F32 = jnp.float32
LB = 128
VMEM = 60 * 1024 * 1024
swap = [(0, 1), (1, 0)]
gelu_a = math.sqrt(2.0 / math.pi)
gelu_b = 0.044715


def bucket_index(offset):
    magnitude = jnp.abs(offset)
    far_bucket = 8 + sum(((magnitude >= boundary).astype(jnp.int32) for boundary in bucket_edges))
    near_bucket = jnp.where(magnitude < 8, magnitude, far_bucket)
    return near_bucket + 16 * (offset > 0).astype(jnp.int32)


def cost(flops, moved):
    return pl.CostEstimate(flops=int(flops), bytes_accessed=int(moved), transcendentals=0)


def params(steps):
    return pltpu.CompilerParams(
        dimension_semantics=("arbitrary",) * steps, vmem_limit_bytes=VMEM
    )


def dot_nt(a, b):
    return lax.dot_general(a, b, (((1,), (1,)), ((), ())), preferred_element_type=F32)


def dot_nn(a, b):
    return lax.dot_general(a, b, (((1,), (0,)), ((), ())), preferred_element_type=F32)


def spot_of(starts_ref, d, count):
    return pl.ds(pl.multiple_of(starts_ref[d], 256), count)


def piece_specs(pieces):
    shape = pieces[0].shape
    return [pl.BlockSpec(shape, lambda *_: (0, 0, 0)) for _ in pieces]


def nt_sum(piece_refs, d, w_of):
    half = piece_refs[0].shape[0]
    acc = None
    for z in range(2 * half):
        part = dot_nt(piece_refs[4 * (z // half) + d][z % half], w_of(z))
        acc = part if acc is None else acc + part
    return acc


def nt_kernel(starts_ref, *refs):
    pieces, (w_ref, out_ref) = refs[:8], refs[8:]
    for d in range(4):
        acc = nt_sum(pieces, d, lambda z: w_ref[z, 0])
        out_ref[spot_of(starts_ref, d, acc.shape[0]), :] = acc.astype(BF)


def mm_nt(pieces, w, first, rows, starts):
    nz, nc, _, width = w.shape
    total = 4 * pieces[0].shape[1]
    count, skip = rows // 256, first // 256
    return pl.pallas_call(
        nt_kernel,
        grid=(nc, count),
        in_specs=[pl.BlockSpec(memory_space=pltpu.SMEM)]
        + piece_specs(pieces)
        + [pl.BlockSpec((nz, 1, 256, width), lambda c, i: (0, c, skip + i, 0))],
        out_specs=pl.BlockSpec((total, 256), lambda c, i: (0, c * count + i)),
        out_shape=jax.ShapeDtypeStruct((total, nc * rows), BF),
        compiler_params=params(2),
        cost_estimate=cost(
            2 * nz * total * width * nc * rows, 2 * nz * width * (total + nc * rows) + 2 * total * nc * rows
        ),
        name="product_nt",
    )(starts, *pieces, w)


def nn_kernel(count, starts_ref, *refs):
    grads, (w_ref, low_out, low_keep, high_out, high_keep) = refs[:count], refs[count:]
    nc, rows, width = w_ref.shape[1:]
    t = grads[0].shape[0] // 4
    in_low = pl.program_id(0) < pl.num_programs(0) // 2

    def product(d):
        spot = spot_of(starts_ref, d, t)
        if count == 1:
            return dot_nn(grads[0][spot, :], w_ref[0].reshape(nc * rows, width)).astype(BF)
        return sum(dot_nn(grads[c][spot, :], w_ref[0, c]) for c in range(count)).astype(BF)

    @pl.when(in_low)
    def _():
        for d in range(4):
            (low_out if d // 2 else low_keep)[d % 2, 0] = product(d)

    @pl.when(jnp.logical_not(in_low))
    def _():
        for d in range(4):
            (high_out if d % 2 else high_keep)[d // 2, 0] = product(d)


def mm_nn(grads, w, first, rows, starts):
    total = grads[0].shape[0]
    nz, nc, _, width = w.shape
    skip, half, t = first // rows, nz // 2, total // 4
    low = pl.BlockSpec((2, 1, t, width), lambda z: (0, jnp.minimum(z, half - 1), 0, 0))
    high = pl.BlockSpec((2, 1, t, width), lambda z: (0, jnp.maximum(z - half, 0), 0, 0))
    return pl.pallas_call(
        functools.partial(nn_kernel, len(grads)),
        grid=(nz,),
        in_specs=[pl.BlockSpec(memory_space=pltpu.SMEM)]
        + [pl.BlockSpec(grad.shape, lambda z: (0, 0)) for grad in grads]
        + [pl.BlockSpec((1, nc, rows, width), lambda z: (z, 0, skip, 0))],
        out_specs=[low, low, high, high],
        out_shape=[jax.ShapeDtypeStruct((2, half, t, width), BF)] * 4,
        compiler_params=params(1),
        cost_estimate=cost(
            2 * nz * total * width * nc * rows, 2 * nz * width * (total + nc * rows) + 2 * total * nc * rows
        ),
        name="product_nn",
    )(starts, *grads, w)


def tn_kernel(count, starts_ref, *refs):
    grads, pieces, out_ref = refs[:count], refs[count:-1], refs[-1]
    half, t, _ = pieces[0].shape

    def one(grad_ref):
        turned = [grad_ref[spot_of(starts_ref, d, t), :].T for d in range(4)]
        for z in range(2 * half):
            acc = dot_nn(turned[0], pieces[4 * (z // half)][z % half])
            for d in range(1, 4):
                acc += dot_nn(turned[d], pieces[4 * (z // half) + d][z % half])
            out_ref[z] = acc.astype(BF)

    if count == 1:
        one(grads[0])
    else:
        for c in range(count):

            @pl.when(pl.program_id(0) // (pl.num_programs(0) // count) == c)
            def _():
                one(grads[c])


def mm_tn(grads, pieces, starts):
    total, rows = grads[0].shape
    half, _, width = pieces[0].shape
    nz, count = 2 * half, len(grads)
    block = next(b for b in (640, 384, 256) if rows % b == 0)
    steps = rows // block

    def spec(c):
        return pl.BlockSpec((total, block), lambda i: (0, jnp.clip(i - c * steps, 0, steps - 1)))

    return pl.pallas_call(
        functools.partial(tn_kernel, count),
        grid=(count * steps,),
        in_specs=[pl.BlockSpec(memory_space=pltpu.SMEM)]
        + [spec(c) for c in range(count)]
        + piece_specs(pieces),
        out_specs=pl.BlockSpec((nz, block, width), lambda i: (0, i, 0)),
        out_shape=jax.ShapeDtypeStruct((nz, count * rows, width), BF),
        compiler_params=params(1),
        cost_estimate=cost(
            2 * nz * total * width * count * rows, 2 * nz * width * (total + count * rows) + 2 * total * count * rows
        ),
        name="product_tn",
    )(starts, *grads, *pieces)


def gelu_parts(gate):
    curve = jnp.tanh(gelu_a * (gate + gelu_b * gate * gate * gate))
    value = 0.5 * gate * (1.0 + curve)
    slope = 0.5 * (1.0 + curve) + 0.5 * gate * (1.0 - curve * curve) * gelu_a * (
        1.0 + 3.0 * gelu_b * gate * gate
    )
    return value, slope


def ffn_in_kernel(starts_ref, *refs):
    pieces, (w_ref, gate_ref, up_ref, active_ref) = refs[:8], refs[8:]
    _, _, _, block, width = w_ref.shape
    for d in range(4):
        acc = nt_sum(pieces, d, lambda z: w_ref[z, 0].reshape(2 * block, width))
        spot = spot_of(starts_ref, d, acc.shape[0])
        gate, up = acc[:, :block], acc[:, block:]
        value = 0.5 * gate * (1.0 + jnp.tanh(gelu_a * (gate + gelu_b * gate * gate * gate)))
        gate_ref[spot, :] = gate.astype(BF)
        up_ref[spot, :] = up.astype(BF)
        active_ref[spot, :] = (value * up).astype(BF)


def ffn_in(pieces, w, starts):
    nz, nc, rows, width = w.shape
    half, total = rows // 2, 4 * pieces[0].shape[1]
    count = half // 128
    block = pl.BlockSpec((total, 128), lambda c, i: (0, c * count + i))
    return pl.pallas_call(
        ffn_in_kernel,
        grid=(nc, count),
        in_specs=[pl.BlockSpec(memory_space=pltpu.SMEM)]
        + piece_specs(pieces)
        + [pl.BlockSpec((nz, 1, 2, 128, width), lambda c, i: (0, c, 0, i, 0))],
        out_specs=[block, block, block],
        out_shape=[jax.ShapeDtypeStruct((total, nc * half), BF)] * 3,
        compiler_params=params(2),
        cost_estimate=cost(
            2 * nz * total * width * nc * rows, 2 * nz * width * (total + nc * rows) + 3 * total * nc * rows
        ),
        name="ffn_in",
    )(starts, *pieces, w.reshape(nz, nc, 2, half, width))


def ffn_back_kernel(starts_ref, *refs):
    pieces, (w_ref, gate_ref, up_ref, out_ref) = refs[:8], refs[8:]
    half = w_ref.shape[2]
    for d in range(4):
        acc = nt_sum(pieces, d, lambda z: w_ref[z, 0])
        spot = spot_of(starts_ref, d, acc.shape[0])
        value, slope = gelu_parts(gate_ref[spot, :].astype(F32))
        out_ref[spot, :half] = (acc * up_ref[spot, :].astype(F32) * slope).astype(BF)
        out_ref[spot, half:] = (acc * value).astype(BF)


def ffn_back(pieces, w, gate, up, starts):
    nz, nc, half, width = w.shape
    total = gate.shape[0]
    kept = pl.BlockSpec((total, half), lambda c: (0, c))
    return pl.pallas_call(
        ffn_back_kernel,
        grid=(nc,),
        in_specs=[pl.BlockSpec(memory_space=pltpu.SMEM)]
        + piece_specs(pieces)
        + [pl.BlockSpec((nz, 1, half, width), lambda c: (0, c, 0, 0)), kept, kept],
        out_specs=pl.BlockSpec((total, 2 * half), lambda c: (0, c)),
        out_shape=jax.ShapeDtypeStruct((total, nc * 2 * half), BF),
        compiler_params=params(1),
        cost_estimate=cost(
            2 * nz * total * width * nc * half, 2 * nz * width * (total + nc * half) + 8 * total * nc * half
        ),
        name="ffn_back",
    )(starts, *pieces, w, gate, up)


def mm_nt_plain(act, w, first, rows, starts):
    part = lax.slice_in_dim(w, first, first + rows, axis=2)
    out = jnp.einsum("ztf,zcrf->tcr", act, part, preferred_element_type=F32)
    return out.astype(BF).reshape(act.shape[1], -1)


def mm_nn_plain(grads, w, first, rows, starts):
    grad = grads[0]
    part = lax.slice_in_dim(w, first, first + rows, axis=2)
    split = grad.reshape(grad.shape[0], w.shape[1], rows)
    out = jnp.einsum("tcr,zcrf->ztf", split, part, preferred_element_type=F32)
    return [out.astype(BF)]


def mm_tn_plain(grads, act, starts):
    return jnp.einsum("tr,ztf->zrf", grads[0], act, preferred_element_type=F32).astype(BF)


def ffn_in_plain(act, w, starts):
    _, nc, rows, _ = w.shape
    total = act.shape[1]
    both = jnp.einsum("ztf,zcrf->tcr", act, w, preferred_element_type=F32)
    gate, up = both[:, :, : rows // 2], both[:, :, rows // 2 :]
    value, _ = gelu_parts(gate)
    return [part.astype(BF).reshape(total, -1) for part in (gate, up, value * up)]


def ffn_back_plain(act, w, gate, up, starts):
    total, nc = gate.shape[0], w.shape[1]
    grad = jnp.einsum("ztf,zcrf->tcr", act, w, preferred_element_type=F32)
    value, slope = gelu_parts(gate.astype(F32).reshape(grad.shape))
    both = [grad * up.astype(F32).reshape(grad.shape) * slope, grad * value]
    return jnp.concatenate(both, axis=2).astype(BF).reshape(total, -1)


def near_buckets(tile, total):
    first = (total // LB - 2 + tile) * LB
    rows = lax.broadcasted_iota(jnp.int32, (LB, LB), 0)
    lanes = lax.broadcasted_iota(jnp.int32, (LB, LB), 1)
    return bucket_index(first + rows - (total - LB) - lanes)


def build_strips(table_ref, strip_ref, total, group):
    heads = strip_ref.shape[0]
    near = (total // LB - 2) * LB
    for h in range(heads):
        head = group * heads + h
        strip_ref[h, :near] = jnp.full((near, LB), table_ref[head, 15], F32)
        strip_ref[h, near + 3 * LB :] = jnp.full((near, LB), table_ref[head, 31], F32)

    def one_tile(tile, _):
        index = near_buckets(tile, total)
        vals = [jnp.full((LB, LB), table_ref[group * heads + h, 0], F32) for h in range(heads)]
        for b in range(1, 32):
            hit = index == b
            vals = [
                jnp.where(hit, table_ref[group * heads + h, b], vals[h]) for h in range(heads)
            ]
        for h in range(heads):
            strip_ref[h, pl.ds(pl.multiple_of(near + tile * LB, LB), LB)] = vals[h]
        return 0

    lax.fori_loop(0, 3, one_tile, 0)


def head_lanes(shape, h):
    lanes = lax.broadcasted_iota(jnp.int32, shape, 1)
    return lanes // 64 == h, lanes == ((h + 1) % 4) * 64


def mask_keys(keys, length, h):
    own, spare = head_lanes(keys.shape, h)
    dead = lax.broadcasted_iota(jnp.int32, keys.shape, 0) >= length
    mask = jnp.where(jnp.logical_and(spare, dead), masked_score, 0.0)
    return jnp.where(own, keys.astype(F32), mask).astype(BF)


def with_one(queries, h):
    _, spare = head_lanes(queries.shape, h)
    return jnp.where(spare, 1.0, queries.astype(F32)).astype(BF)


def own_lanes(values, h):
    own, _ = head_lanes(values.shape, h)
    return jnp.where(own, values.astype(F32), 0.0).astype(BF)


def block_bias(strip_ref, h, block, total):
    first = total - LB - 2 * block * LB
    left = strip_ref[h, pl.ds(pl.multiple_of(first, LB), total)]
    right = strip_ref[h, pl.ds(pl.multiple_of(first - LB, LB), total)]
    return jnp.concatenate([left, right], axis=1)


def attend_kernel(group, length_ref, table_ref, q_ref, k_ref, v_ref, out_ref, lse_ref, strip, heads_k, turned_v, turned_out):
    total = q_ref.shape[0]
    heads = strip.shape[0]
    build_strips(table_ref, strip, total, group)
    turned_v[...] = v_ref[...].astype(F32).T.astype(BF)
    for h in range(heads):
        heads_k[h] = mask_keys(k_ref[...], length_ref[0], h)

    def one_block(block, _):
        spot = pl.ds(pl.multiple_of(block * 256, 256), 256)
        queries = q_ref[spot]
        for h in range(heads):
            scores = dot_nt(heads_k[h], with_one(queries, h)) + block_bias(strip, h, block, total)
            largest = jnp.max(scores, axis=0, keepdims=True)
            raised = jnp.exp(scores - largest)
            totals = jnp.sum(raised, axis=0, keepdims=True)
            out = dot_nn(turned_v[h * 64 : (h + 1) * 64], raised.astype(BF))
            turned_out[h * 64 : (h + 1) * 64, spot] = out * (1.0 / totals)
            lse_ref[h : h + 1, spot] = largest + jnp.log(totals)
        return 0

    lax.fori_loop(0, total // 256, one_block, 0)
    out_ref[...] = turned_out[...].T.astype(BF)


def attend_back_kernel(
    group, length_ref, table_ref, q_ref, k_ref, v_ref, grad_ref, lse_ref, out_ref, table_grad_ref,
    strip, strip_grad, heads_k, turned_k, turned_q, ds_ref, p_ref, dk_ref, dv_ref,
):
    total = q_ref.shape[0]
    heads = strip.shape[0]
    build_strips(table_ref, strip, total, group)
    strip_grad[...] = jnp.zeros_like(strip_grad)
    dk_ref[...] = jnp.zeros_like(dk_ref)
    dv_ref[...] = jnp.zeros_like(dv_ref)
    turned_k[...] = k_ref[...].astype(F32).T.astype(BF)
    for h in range(heads):
        heads_k[h] = mask_keys(k_ref[...], length_ref[0], h)

    def one_block(block, _):
        spot = pl.ds(pl.multiple_of(block * 256, 256), 256)
        queries, grads = q_ref[spot], grad_ref[spot]
        own_q, own_g = [], []
        for h in range(heads):
            own_q.append(own_lanes(queries, h))
            own_g.append(own_lanes(grads, h))
            scores = dot_nt(heads_k[h], with_one(queries, h)) + block_bias(strip, h, block, total)
            probs = jnp.exp(scores - lse_ref[h : h + 1, spot])
            weighed = probs * dot_nt(v_ref[...], own_g[h])
            delta = jnp.sum(weighed, axis=0, keepdims=True)
            grad_scores = weighed - probs * delta
            first = total - LB - 2 * block * LB
            left = pl.ds(pl.multiple_of(first, LB), total)
            right = pl.ds(pl.multiple_of(first - LB, LB), total)
            strip_grad[h, left] += grad_scores[:, :LB]
            strip_grad[h, right] += grad_scores[:, LB:]
            rounded = grad_scores.astype(BF)
            ds_ref[:, h * 256 : (h + 1) * 256] = rounded
            p_ref[:, h * 256 : (h + 1) * 256] = probs.astype(BF)
            turned_q[h * 64 : (h + 1) * 64, spot] = dot_nn(turned_k[h * 64 : (h + 1) * 64], rounded)
        dk_ref[...] += dot_nn(ds_ref[...], jnp.concatenate(own_q, axis=0))
        dv_ref[...] += dot_nn(p_ref[...], jnp.concatenate(own_g, axis=0))
        return 0

    lax.fori_loop(0, total // 256, one_block, 0)
    out_ref[:, :256] = turned_q[...].T.astype(BF)
    out_ref[:, 256:512] = dk_ref[...].astype(BF)
    out_ref[:, 512:] = dv_ref[...].astype(BF)

    near = (total // LB - 2) * LB
    for h in range(heads):
        table_grad_ref[h] = jnp.zeros((32, LB), F32)
        table_grad_ref[h, 15:16] = jnp.sum(strip_grad[h, :near], axis=0, keepdims=True)
        table_grad_ref[h, 31:32] = jnp.sum(strip_grad[h, near + 3 * LB :], axis=0, keepdims=True)

    def one_tile(tile, _):
        index = near_buckets(tile, total)
        spot = pl.ds(pl.multiple_of(near + tile * LB, LB), LB)
        for h in range(heads):
            grads = strip_grad[h, spot]
            for b in range(32):
                picked = jnp.where(index == b, grads, 0.0)
                table_grad_ref[h, b : b + 1] += jnp.sum(picked, axis=0, keepdims=True)
        return 0

    lax.fori_loop(0, 3, one_tile, 0)


def block_specs(total, group):
    def spec(i):
        return pl.BlockSpec((total, 256), lambda _: (0, 3 * group + i))

    smem = pl.BlockSpec(memory_space=pltpu.SMEM)
    return [smem, smem, spec(0), spec(1), spec(2)]


def attend(group, projected, length, table):
    total = projected.shape[0]
    heads = 4
    return pl.pallas_call(
        functools.partial(attend_kernel, group),
        grid=(1,),
        in_specs=block_specs(total, group),
        out_specs=[
            pl.BlockSpec((total, 256), lambda _: (0, 0)),
            pl.BlockSpec((8, total), lambda _: (0, 0)),
        ],
        out_shape=[
            jax.ShapeDtypeStruct((total, 256), BF),
            jax.ShapeDtypeStruct((8, total), F32),
        ],
        scratch_shapes=[
            pltpu.VMEM((heads, 2 * total - LB, LB), F32),
            pltpu.VMEM((heads, total, 256), BF),
            pltpu.VMEM((256, total), BF),
            pltpu.VMEM((256, total), F32),
        ],
        compiler_params=params(1),
        cost_estimate=cost(heads * total * total * 2 * 256 * 2, 4 * total * 256 * 2),
        name="attend",
    )(length, table, projected, projected, projected)


def attend_back(group, projected, length, table, grad_out, lse):
    total = projected.shape[0]
    heads = 4
    return pl.pallas_call(
        functools.partial(attend_back_kernel, group),
        grid=(1,),
        in_specs=block_specs(total, group)
        + [
            pl.BlockSpec((total, 256), lambda _: (0, group)),
            pl.BlockSpec((8, total), lambda _: (0, 0)),
        ],
        out_specs=[
            pl.BlockSpec((total, 768), lambda _: (0, 0)),
            pl.BlockSpec((heads, 32, LB), lambda _: (0, 0, 0)),
        ],
        out_shape=[
            jax.ShapeDtypeStruct((total, 768), BF),
            jax.ShapeDtypeStruct((heads, 32, LB), F32),
        ],
        scratch_shapes=[
            pltpu.VMEM((heads, 2 * total - LB, LB), F32),
            pltpu.VMEM((heads, 2 * total - LB, LB), F32),
            pltpu.VMEM((heads, total, 256), BF),
            pltpu.VMEM((256, total), BF),
            pltpu.VMEM((256, total), F32),
            pltpu.VMEM((total, heads * 256), BF),
            pltpu.VMEM((total, heads * 256), BF),
            pltpu.VMEM((total, 256), F32),
            pltpu.VMEM((total, 256), F32),
        ],
        compiler_params=params(1),
        cost_estimate=cost(heads * total * total * 2 * 256 * 5, 8 * total * 256 * 2),
        name="attend_back",
    )(length, table, projected, projected, projected, grad_out, lse)


def split_heads(projected, groups, heads):
    parts = projected.reshape(projected.shape[0], groups, 3, heads, 64)
    return [parts[:, :, i].reshape(projected.shape[0], groups * heads, 64) for i in range(3)]


def plain_scores(queries, keys, length, table):
    slots = jnp.arange(keys.shape[0], dtype=jnp.int32)
    picked = (bucket_index(slots[None, :] - slots[:, None])[:, :, None] == jnp.arange(32)).astype(F32)
    bias = jnp.einsum("qkb,hb->hqk", picked, table, precision=lax.Precision.HIGHEST)
    scores = jnp.einsum("qhs,khs->hqk", queries, keys, preferred_element_type=F32) + bias
    return jnp.where(slots < length[0], scores, masked_score), picked


def attend_plain(projected, length, table, groups, heads):
    queries, keys, values = split_heads(projected, groups, heads)
    scores, _ = plain_scores(queries, keys, length, table)
    lse = jax.nn.logsumexp(scores, axis=2)
    probs = jnp.exp(scores - lse[:, :, None]).astype(BF)
    out = jnp.einsum("hqk,khs->qhs", probs, values, preferred_element_type=F32)
    return out.astype(BF).reshape(projected.shape[0], -1), lse


def attend_back_plain(projected, length, table, grad_out, lse, groups, heads):
    total = projected.shape[0]
    queries, keys, values = split_heads(projected, groups, heads)
    grads = grad_out.reshape(queries.shape)
    scores, picked = plain_scores(queries, keys, length, table)
    probs = jnp.exp(scores - lse[:, :, None])
    weighed = probs * jnp.einsum("qhs,khs->hqk", grads, values, preferred_element_type=F32)
    wide = weighed - probs * jnp.sum(weighed, axis=2, keepdims=True)
    rounded = wide.astype(BF)
    parts = [
        jnp.einsum("hqk,khs->qhs", rounded, keys, preferred_element_type=F32),
        jnp.einsum("hqk,qhs->khs", rounded, queries, preferred_element_type=F32),
        jnp.einsum("hqk,qhs->khs", probs.astype(BF), grads, preferred_element_type=F32),
    ]
    parts = [part.astype(BF).reshape(total, groups, 1, heads * 64) for part in parts]
    table_grad = jnp.einsum("hqk,qkb->hb", wide, picked, precision=lax.Precision.HIGHEST)
    return (
        jnp.concatenate(parts, axis=2).reshape(total, -1),
        table_grad.reshape(groups * heads, 32, 1),
    )


def hop(value, axis):
    return lax.ppermute(value, axis, swap)


def pick(value, index, axis):
    return lax.dynamic_index_in_dim(value, index, axis, keepdims=False)


def paired(mine, other, axis, place=0):
    return jnp.where(
        lax.axis_index(axis) == 0,
        jnp.stack([mine, other], axis=place),
        jnp.stack([other, mine], axis=place),
    )


def after(value, *others):
    return lax.optimization_barrier((value, *others))[0]


def gather_plain(part, *beside):
    return lax.all_gather(part, ("x", "y"), axis=1, tiled=True), (), ()


def gather_tokens(part, *beside):
    half = part.shape[0] // 2
    low, high = part[:half], part[half:]
    low_x, high_y = hop(low, "x"), hop(high, "y")
    if beside:
        low_x, high_y = after(low_x, *beside), after(high_y, *beside)
    low_y, high_x = hop(low, "y"), hop(high, "x")
    low_xy, high_xy = hop(low_x, "y"), hop(high_y, "x")
    pieces = [low, low_y, low_x, low_xy, high, high_y, high_x, high_xy]
    return pieces, (low_x, high_y), (low_y, low_xy, high_x, high_xy)


def scatter_plain(parts, *beside):
    whole = parts[0].astype(F32)
    return lax.psum_scatter(whole, ("x", "y"), scatter_dimension=1, tiled=True), (), ()


def scatter_tokens(parts, *beside):
    low_out, low_keep, high_out, high_keep = parts
    low_in, high_in = hop(low_out, "x"), hop(high_out, "y")
    if beside:
        low_in, high_in = after(low_in, *beside), after(high_in, *beside)

    def add(keep, arrived, index):
        return keep[index].astype(F32) + arrived[index].astype(F32)

    low_last = hop(add(low_keep, low_in, 1).astype(BF), "y")
    high_last = hop(add(high_keep, high_in, 1).astype(BF), "x")
    low = add(low_keep, low_in, 0) + low_last.astype(F32)
    high = add(high_keep, high_in, 0) + high_last.astype(F32)
    return jnp.concatenate([low, high], axis=0), (low_in, high_in), (low_last, high_last)


def place_kernel(write, here_ref, *refs):
    pieces, outs = refs[:4], refs[4:]
    step = pl.program_id(0)
    for near in range(4):
        y = here_ref[0] if near < 2 else 1 - here_ref[0]
        c = here_ref[1] if near % 2 == 0 else 1 - here_ref[1]

        @pl.when(step == 2 * y + c)
        def _():
            write(pieces[near], outs)


def place(pieces, here, shapes, write):
    return pl.pallas_call(
        functools.partial(place_kernel, write),
        grid=(4,),
        in_specs=[pl.BlockSpec(memory_space=pltpu.SMEM)]
        + [pl.BlockSpec(piece.shape, lambda q: (0, 0)) for piece in pieces],
        out_specs=[
            pl.BlockSpec(shape, lambda q, rank=len(shape): (q,) + (0,) * (rank - 1)) for shape in shapes
        ],
        out_shape=[jax.ShapeDtypeStruct((4 * shape[0], *shape[1:]), F32) for shape in shapes],
        compiler_params=params(1),
        cost_estimate=cost(0, 20 * pieces[0].size),
        name="place",
    )(here, *pieces)


def share(part):
    over_y = hop(part, "y")
    return [part, hop(part, "c"), over_y, hop(over_y, "c")], over_y


def share_plain(part):
    return lax.all_gather(part, ("y", "c"), axis=0), part


def to_groups(halves, other, extra):
    count, _, t, width = halves.shape
    both = paired(pick(halves, lax.axis_index("y"), 1), other, "y").reshape(2 * count, t, width)
    if extra is not None:
        wide = jnp.broadcast_to(extra[None], (2 * count, *extra.shape))
        both = jnp.concatenate([both, wide], axis=1)
    return lax.all_to_all(both, "z", 0, 0, tiled=True)


def from_groups(mine):
    nz, t, width = mine.shape
    back = lax.all_to_all(mine, "z", 0, 0, tiled=True).reshape(2, nz // 2, t, width)
    leaving = pick(back, 1 - lax.axis_index("y"), 0)
    return (back, hop(leaving, "y")), leaving


def settle_kernel(y_ref, back_ref, other_ref, out_ref):
    j, y = pl.program_id(0), pl.program_id(1)

    @pl.when(y == y_ref[0])
    def _():
        out_ref[0, 0] = back_ref[y, j].astype(out_ref.dtype)

    @pl.when(y != y_ref[0])
    def _():
        out_ref[0, 0] = other_ref[j].astype(out_ref.dtype)


def settle(arrived, dtype):
    back, other = arrived
    _, count, t, width = back.shape
    y = lax.axis_index("y").astype(jnp.int32).reshape(1)
    out = pl.pallas_call(
        settle_kernel,
        grid=(count, 2),
        in_specs=[
            pl.BlockSpec(memory_space=pltpu.SMEM),
            pl.BlockSpec(back.shape, lambda j, y: (0, 0, 0, 0)),
            pl.BlockSpec(other.shape, lambda j, y: (0, 0, 0)),
        ],
        out_specs=pl.BlockSpec((1, 1, t, width), lambda j, y: (j, y, 0, 0)),
        out_shape=jax.ShapeDtypeStruct((count, 2, t, width), dtype),
        compiler_params=params(2),
        cost_estimate=cost(0, 12 * count * t * width),
        name="settle",
    )(y, back, other)
    return out.reshape(count, 2 * t, width)


def settle_plain(arrived, dtype):
    back, other = arrived
    _, count, t, width = back.shape
    both = paired(pick(back, lax.axis_index("y"), 0), other, "y")
    return both.transpose(1, 0, 2, 3).reshape(count, 2 * t, width).astype(dtype)


def sum_plane(value, nx):
    value = value + hop(value, "c")
    value = value + hop(value, "x") if nx == 2 else lax.psum(value, "x")
    return value + hop(value, "y")


def sum_line(value, nz):
    step = 1
    while step < nz:
        value = value + lax.ppermute(value, "z", [(i, i ^ step) for i in range(nz)])
        step *= 2
    return value


def body(
    nx, nz, nc, inputs, lengths, attn_gain, ffn_gain, query_key, value_proj, out_proj, gate_up, down_proj, bias_table, cotangent
):
    x, y = lax.axis_index("x"), lax.axis_index("y")
    c, z = lax.axis_index("c"), lax.axis_index("z")
    width = inputs.shape[2]
    features = nz * width
    quarter = y * nc + c
    parts = 2 * nc
    buckets, mine = bias_table.shape
    count = inputs.shape[1] // 2

    stored_in = inputs.reshape(inputs.shape[0], 2, count, width)
    stored_cot = cotangent.reshape(stored_in.shape)
    small = jnp.concatenate(
        [attn_gain[None], ffn_gain[None], jnp.pad(bias_table.reshape(1, -1), ((0, 0), (0, width - buckets * mine)))]
    )
    small = jnp.pad(small, ((0, 5), (0, 0)))
    leaving = pick(stored_in, 1 - y, 1)

    query_key_rows = jnp.transpose(query_key, (1, 2, 3, 0))
    value_rows = jnp.transpose(value_proj, (1, 2, 0))
    gate_up_rows = jnp.transpose(gate_up, (1, 2, 3, 0))
    heads = value_rows.shape[0] // parts
    units = gate_up_rows.shape[0] // parts
    unit = gate_up_rows.shape[2]
    local_heads = nc * heads

    def own(rows, size):
        return lax.dynamic_slice_in_dim(rows, quarter * size, size, 0)

    def flat(rows):
        return rows.reshape(-1, width)

    def spread(rows):
        gathered = lax.all_gather(rows, ("z", "c"), axis=0, tiled=True)
        return gathered.reshape(nz, nc, rows.shape[0], width)

    own_pair = own(query_key_rows, heads)
    own_attn = [own_pair[:, 0], own_pair[:, 1], own(value_rows, heads), own(out_proj, heads)]
    own_attn = jnp.concatenate([flat(rows) for rows in own_attn])
    w_attn = spread(own_attn)
    other = after(hop(leaving, "y"), own_attn)
    own_pair = own(after(gate_up_rows, other), units)
    own_gate_up = jnp.concatenate([flat(own_pair[:, 0]), flat(own_pair[:, 1])])
    w_gate_up = spread(own_gate_up)
    own_down = flat(own(after(down_proj, other), units))
    w_down = spread(own_down)
    qkv_count, out_count = 3 * heads * 64, heads * 64

    arrived = after(to_groups(stored_in, other, small), own_gate_up, own_down)
    tokens = arrived[:, :count].astype(F32)
    small = arrived[:, count:]
    gain_one = small[:, :1].astype(F32)
    gain_two = small[:, 1:2].astype(F32)
    table = small[:, 2, : buckets * mine].reshape(nz, buckets, mine).transpose(0, 2, 1)
    table = table.reshape(-1, buckets).astype(F32)
    table = lax.dynamic_slice_in_dim(table, y * local_heads, local_heads, 0)

    both_lengths = jnp.stack([lengths, lax.ppermute(lengths, "y", swap)])
    both_lengths = jnp.where(y == 0, both_lengths, both_lengths[::-1]).reshape(-1)
    length = lax.dynamic_slice_in_dim(both_lengths, z, 1, 0)
    slots = (x * 2 + y) * count + jnp.arange(count, dtype=jnp.int32)
    live = (slots < length).astype(F32)[None, :, None]

    def scale_of(values):
        squares = jnp.sum(values * values, axis=(0, 2), keepdims=True)
        return lax.rsqrt(squares / features + norm_eps)

    def norm_back(values, scale, gain, grad):
        inner = jnp.sum(values * gain * grad, axis=(0, 2), keepdims=True)
        out = scale * gain * grad - values * (scale * scale * scale) * inner / features
        return out, jnp.sum(values * scale * grad, axis=1)

    def reduce(partial):
        rows = partial.reshape(nz * partial.shape[1], width)
        return lax.psum_scatter(rows, ("z", "c"), scatter_dimension=0, tiled=True)

    fits = nx == 2 and heads == 4 and count == 256 and units * unit % 640 == 0 and nz % 2 == 0
    if fits:
        forward, backward, gather, scatter = attend, attend_back, gather_tokens, scatter_tokens
        nt, nn, tn, ffn_one, ffn_two = mm_nt, mm_nn, mm_tn, ffn_in, ffn_back
        shared, stored_from = share, settle
    else:
        forward, backward, gather, scatter = attend_plain, attend_back_plain, gather_plain, scatter_plain
        nt, nn, tn, ffn_one, ffn_two = mm_nt_plain, mm_nn_plain, mm_tn_plain, ffn_in_plain, ffn_back_plain
        shared, stored_from = share_plain, settle_plain
    near_x, near_y = jnp.array([0, 0, 1, 1]) ^ x, jnp.array([0, 1, 0, 1]) ^ y
    starts = ((near_x * 2 + near_y) * count).astype(jnp.int32)

    def attend_back_all(grad, *last):
        if not fits:
            grads, table_grad = backward(projected, length, table, grad, lse, nc, heads)
            return (grads,), table_grad
        first = backward(0, projected, length, table, grad, lse[0])
        second = backward(1, after(projected, first[0], *last), length, table, grad, lse[1])
        return (first[0], second[0]), jnp.concatenate([first[1], second[1]])

    scale_one = scale_of(tokens)
    normed, _, _ = gather((tokens * scale_one * gain_one).astype(BF))
    cot_other = hop(pick(stored_cot, 1 - y, 1), "y")
    upstream = live * to_groups(stored_cot, after(cot_other, arrived), None).astype(F32)
    upstream_rounded = after(upstream.astype(BF), w_attn)
    projected = nt(normed, w_attn, 0, qkv_count, starts)
    if fits:
        first = forward(0, projected, length, table)
        grad_ffn, cot_first, cot_last = gather(upstream_rounded, first[0])
        second = forward(1, after(projected, first[0], *cot_first), length, table)
        attended, lse = (first[0], second[0]), (first[1], second[1])
    else:
        grad_ffn, _, cot_last = gather(upstream_rounded)
        attended, lse = forward(projected, length, table, nc, heads)
        attended = (attended,)
    heads_out = [after(attended[0], *cot_last), *attended[1:]]
    hidden = tokens + scatter(nn(heads_out, w_attn, qkv_count, out_count, starts))[0]
    scale_two = scale_of(hidden)
    normed_two, _, _ = gather((hidden * scale_two * gain_two).astype(BF))
    gate, up, activated = ffn_one(normed_two, w_gate_up, starts)

    down_partial = tn([activated], grad_ffn, starts)
    down_part = reduce(down_partial)
    grad_gate_up = ffn_two(grad_ffn, w_down, after(gate, down_partial), up, starts)
    two_parts = nn([grad_gate_up], w_gate_up, 0, 2 * units * unit, starts)
    grad_two, two_first, _ = scatter(two_parts)
    gate_up_partial = tn([after(grad_gate_up, two_parts[0])], normed_two, starts)
    gate_up_part = reduce(after(gate_up_partial, down_part, *two_first))
    branch_parts = nn([after(activated, gate_up_partial)], w_down, 0, units * unit, starts)
    through, ffn_gain_part = norm_back(hidden, scale_two, gain_two, grad_two)
    grad_hidden = upstream + through
    grad_branch, _, branch_last = gather(after(grad_hidden.astype(BF), branch_parts[0]))
    grad_attended = nt(grad_branch, w_attn, qkv_count, out_count, starts)
    out_partial = tn(attended, grad_branch, starts)
    branch_parts = [after(part, *branch_last) for part in branch_parts]
    branch, branch_first, branch_last = scatter(branch_parts)
    down_pieces, down_last = shared(after(down_part, grad_attended))
    grad_projected, table_part = attend_back_all(after(grad_attended, out_partial), *branch_first)
    out_part = reduce(after(out_partial, gate_up_part, grad_projected[0], *branch_first))
    outputs = (live * (hidden + branch)).astype(BF)
    last = after(grad_projected[-1], *branch_last, down_last)
    grad_projected = [*grad_projected[:-1], last]
    outputs, _ = from_groups(outputs)
    qkv_partial = tn(grad_projected, normed, starts)
    qkv_part = reduce(after(qkv_partial, out_part))
    one_parts = nn(grad_projected, w_attn, 0, qkv_count, starts)
    gate_up_pieces, gate_up_last = shared(after(gate_up_part, grad_projected[0]))
    grad_one, _, one_last = scatter(one_parts, outputs[0], gate_up_last)
    through, attn_gain_part = norm_back(tokens, scale_one, gain_one, grad_one)
    input_grad, input_leaves = from_groups((grad_hidden + through).astype(BF))
    outputs = stored_from(outputs, BF)

    table_part = jnp.sum(table_part, axis=2)
    every = jnp.zeros((nx * 2 * local_heads, table_part.shape[1]), F32)
    every = lax.dynamic_update_slice_in_dim(every, table_part, (x * 2 + y) * local_heads, 0)
    spare = -every.size % width
    every = jnp.pad(every.reshape(-1), (0, spare)).reshape(-1, width)
    sums = sum_plane(jnp.concatenate([attn_gain_part, ffn_gain_part, every]), nx)
    all_sums = sum_line(after(sums, input_leaves), nz)
    attn_gain_grad, ffn_gain_grad = all_sums[:nz], all_sums[nz : 2 * nz]
    every = all_sums[2 * nz :].reshape(-1)[: nx * 2 * local_heads * buckets].reshape(-1, buckets)

    out_pieces, _ = shared(after(out_part, *one_last))
    if fits:
        here = jnp.stack([y, c]).astype(jnp.int32)

        def write_rows(source, outs):
            outs[0][...] = source[...].astype(F32)

        def write_qkv(source, outs):
            for h in range(heads):
                for i in range(3):
                    value = source[(i * heads + h) * 64 : (i * heads + h + 1) * 64, :].astype(F32)
                    if i == 2:
                        outs[1][h] = value
                    else:
                        outs[0][h, i] = value

        def write_gate_up(source, outs):
            for u in range(units):
                for i in range(2):
                    first = (i * units + u) * unit
                    outs[0][u, i] = source[first : first + unit, :].astype(F32)

        (down_all,) = place(down_pieces, here, [(units * unit, width)], write_rows)
        (out_all,) = place(out_pieces, here, [(heads * 64, width)], write_rows)
        (gate_up_all,) = place(gate_up_pieces, here, [(units, 2, unit, width)], write_gate_up)
        qkv_part = after(qkv_part, sums, down_all, out_all, gate_up_all, outputs, *one_last)
        query_key_all, value_all = place(
            shared(qkv_part)[0], here, [(heads, 2, 64, width), (heads, 64, width)], write_qkv
        )
    else:
        down_all, out_all = down_pieces.astype(F32), out_pieces.astype(F32)
        gate_up_all = gate_up_pieces.astype(F32).reshape(parts, 2, units, unit, width)
        gate_up_all = gate_up_all.transpose(0, 2, 1, 3, 4).reshape(-1, 2, unit, width)
        qkv_all = shared(qkv_part)[0].astype(F32).reshape(parts, 3, heads, 64, width)
        qkv_all = qkv_all.transpose(0, 2, 1, 3, 4).reshape(-1, 3, 64, width)
        query_key_all, value_all = qkv_all[:, :2], qkv_all[:, 2]
    input_grad = stored_from(input_grad, F32)
    down_all, out_all = down_all.reshape(down_proj.shape), out_all.reshape(out_proj.shape)

    table_grad = lax.dynamic_slice_in_dim(every, (x * nz + z) * mine, mine, 0).T
    return (
        outputs,
        input_grad,
        pick(attn_gain_grad, z, 0),
        pick(ffn_gain_grad, z, 0),
        query_key_all.transpose(3, 0, 1, 2),
        value_all.transpose(2, 0, 1),
        out_all,
        gate_up_all.transpose(3, 0, 1, 2),
        down_all,
        table_grad,
    )


def solution(mesh):
    dp, nx, nz = (mesh.shape[name] for name in ("dp", "gx", "gy"))
    nc = dp // 2
    split = Mesh(mesh.devices.reshape(2, nc, nx, nz), ("y", "c", "x", "z"))
    seq = ("y", "c")
    return jax.shard_map(
        functools.partial(body, nx, nz, nc),
        mesh=split,
        in_specs=(
            P(seq, "x", "z"),
            P(seq),
            P("z"),
            P("z"),
            P("z", "x", None, None),
            P("z", "x", None),
            P("x", None, "z"),
            P("z", "x", None, None),
            P("x", None, "z"),
            P(None, ("x", "z")),
            P(seq, "x", "z"),
        ),
        out_specs=(
            P(seq, "x", "z"),
            P(seq, "x", "z"),
            P("z"),
            P("z"),
            P("z", "x", None, None),
            P("z", "x", None),
            P("x", None, "z"),
            P("z", "x", None, None),
            P("x", None, "z"),
            P(None, ("x", "z")),
        ),
        check_vma=False,
    )
```

```python
import functools
import math

import jax
import jax.numpy as jnp
from jax import lax
from jax.experimental import pallas as pl
from jax.experimental.pallas import tpu as pltpu
from jax.sharding import Mesh
from jax.sharding import PartitionSpec as P

norm_eps = 1e-06
masked_score = -1e30
bucket_edges = (12, 16, 23, 32, 46, 64, 91)
BF = jnp.bfloat16
F32 = jnp.float32
LB = 128
VMEM = 60 * 1024 * 1024
swap = [(0, 1), (1, 0)]
gelu_a = math.sqrt(2.0 / math.pi)
gelu_b = 0.044715


def bucket_index(offset):
    magnitude = jnp.abs(offset)
    far_bucket = 8 + sum(((magnitude >= boundary).astype(jnp.int32) for boundary in bucket_edges))
    near_bucket = jnp.where(magnitude < 8, magnitude, far_bucket)
    return near_bucket + 16 * (offset > 0).astype(jnp.int32)


def cost(flops, moved):
    return pl.CostEstimate(flops=int(flops) // 4, bytes_accessed=int(moved) // 4, transcendentals=0)


def params(steps):
    return pltpu.CompilerParams(
        dimension_semantics=("arbitrary",) * steps, vmem_limit_bytes=VMEM
    )


def dot_nt(a, b):
    return lax.dot_general(a, b, (((1,), (1,)), ((), ())), preferred_element_type=F32)


def dot_nn(a, b):
    return lax.dot_general(a, b, (((1,), (0,)), ((), ())), preferred_element_type=F32)


def spot_of(starts_ref, d, count):
    return pl.ds(pl.multiple_of(starts_ref[d], 256), count)


def piece_specs(pieces):
    shape = pieces[0].shape
    return [pl.BlockSpec(shape, lambda *_: (0, 0, 0)) for _ in pieces]


def nt_sum(piece_refs, d, w_of):
    half = piece_refs[0].shape[0]
    acc = None
    for z in range(2 * half):
        part = dot_nt(piece_refs[4 * (z // half) + d][z % half], w_of(z))
        acc = part if acc is None else acc + part
    return acc


def nt_kernel(starts_ref, *refs):
    pieces, (w_ref, out_ref) = refs[:8], refs[8:]
    for d in range(4):
        acc = nt_sum(pieces, d, lambda z: w_ref[z, 0])
        out_ref[spot_of(starts_ref, d, acc.shape[0]), :] = acc.astype(BF)


def mm_nt(pieces, w, first, rows, starts):
    nz, nc, _, width = w.shape
    total = 4 * pieces[0].shape[1]
    count, skip = rows // 256, first // 256
    return pl.pallas_call(
        nt_kernel,
        grid=(nc, count),
        in_specs=[pl.BlockSpec(memory_space=pltpu.SMEM)]
        + piece_specs(pieces)
        + [pl.BlockSpec((nz, 1, 256, width), lambda c, i: (0, c, skip + i, 0))],
        out_specs=pl.BlockSpec((total, 256), lambda c, i: (0, c * count + i)),
        out_shape=jax.ShapeDtypeStruct((total, nc * rows), BF),
        compiler_params=params(2),
        cost_estimate=cost(
            2 * nz * total * width * nc * rows, 2 * nz * width * (total + nc * rows) + 2 * total * nc * rows
        ),
        name="product_nt",
    )(starts, *pieces, w)


def nn_kernel(count, starts_ref, *refs):
    grads, (w_ref, low_out, low_keep, high_out, high_keep) = refs[:count], refs[count:]
    nc, rows, width = w_ref.shape[1:]
    t = grads[0].shape[0] // 4
    in_low = pl.program_id(0) < pl.num_programs(0) // 2

    def product(d):
        spot = spot_of(starts_ref, d, t)
        if count == 1:
            return dot_nn(grads[0][spot, :], w_ref[0].reshape(nc * rows, width)).astype(BF)
        return sum(dot_nn(grads[c][spot, :], w_ref[0, c]) for c in range(count)).astype(BF)

    @pl.when(in_low)
    def _():
        for d in range(4):
            (low_out if d // 2 else low_keep)[d % 2, 0] = product(d)

    @pl.when(jnp.logical_not(in_low))
    def _():
        for d in range(4):
            (high_out if d % 2 else high_keep)[d // 2, 0] = product(d)


def mm_nn(grads, w, first, rows, starts):
    total = grads[0].shape[0]
    nz, nc, _, width = w.shape
    skip, half, t = first // rows, nz // 2, total // 4
    low = pl.BlockSpec((2, 1, t, width), lambda z: (0, jnp.minimum(z, half - 1), 0, 0))
    high = pl.BlockSpec((2, 1, t, width), lambda z: (0, jnp.maximum(z - half, 0), 0, 0))
    return pl.pallas_call(
        functools.partial(nn_kernel, len(grads)),
        grid=(nz,),
        in_specs=[pl.BlockSpec(memory_space=pltpu.SMEM)]
        + [pl.BlockSpec(grad.shape, lambda z: (0, 0)) for grad in grads]
        + [pl.BlockSpec((1, nc, rows, width), lambda z: (z, 0, skip, 0))],
        out_specs=[low, low, high, high],
        out_shape=[jax.ShapeDtypeStruct((2, half, t, width), BF)] * 4,
        compiler_params=params(1),
        cost_estimate=cost(
            2 * nz * total * width * nc * rows, 2 * nz * width * (total + nc * rows) + 2 * total * nc * rows
        ),
        name="product_nn",
    )(starts, *grads, w)


def tn_kernel(count, starts_ref, *refs):
    grads, pieces, out_ref = refs[:count], refs[count:-1], refs[-1]
    half, t, _ = pieces[0].shape

    def one(grad_ref):
        turned = [grad_ref[spot_of(starts_ref, d, t), :].T for d in range(4)]
        for z in range(2 * half):
            acc = dot_nn(turned[0], pieces[4 * (z // half)][z % half])
            for d in range(1, 4):
                acc += dot_nn(turned[d], pieces[4 * (z // half) + d][z % half])
            out_ref[z] = acc.astype(BF)

    if count == 1:
        one(grads[0])
    else:
        for c in range(count):

            @pl.when(pl.program_id(0) // (pl.num_programs(0) // count) == c)
            def _():
                one(grads[c])


def mm_tn(grads, pieces, starts):
    total, rows = grads[0].shape
    half, _, width = pieces[0].shape
    nz, count = 2 * half, len(grads)
    block = next(b for b in (640, 384, 256) if rows % b == 0)
    steps = rows // block

    def spec(c):
        return pl.BlockSpec((total, block), lambda i: (0, jnp.clip(i - c * steps, 0, steps - 1)))

    return pl.pallas_call(
        functools.partial(tn_kernel, count),
        grid=(count * steps,),
        in_specs=[pl.BlockSpec(memory_space=pltpu.SMEM)]
        + [spec(c) for c in range(count)]
        + piece_specs(pieces),
        out_specs=pl.BlockSpec((nz, block, width), lambda i: (0, i, 0)),
        out_shape=jax.ShapeDtypeStruct((nz, count * rows, width), BF),
        compiler_params=params(1),
        cost_estimate=cost(
            2 * nz * total * width * count * rows, 2 * nz * width * (total + count * rows) + 2 * total * count * rows
        ),
        name="product_tn",
    )(starts, *grads, *pieces)


def gelu_parts(gate):
    curve = jnp.tanh(gelu_a * (gate + gelu_b * gate * gate * gate))
    value = 0.5 * gate * (1.0 + curve)
    slope = 0.5 * (1.0 + curve) + 0.5 * gate * (1.0 - curve * curve) * gelu_a * (
        1.0 + 3.0 * gelu_b * gate * gate
    )
    return value, slope


def ffn_in_kernel(starts_ref, *refs):
    pieces, (w_ref, gate_ref, up_ref, active_ref) = refs[:8], refs[8:]
    _, _, _, block, width = w_ref.shape
    for d in range(4):
        acc = nt_sum(pieces, d, lambda z: w_ref[z, 0].reshape(2 * block, width))
        spot = spot_of(starts_ref, d, acc.shape[0])
        gate, up = acc[:, :block], acc[:, block:]
        value = 0.5 * gate * (1.0 + jnp.tanh(gelu_a * (gate + gelu_b * gate * gate * gate)))
        gate_ref[spot, :] = gate.astype(BF)
        up_ref[spot, :] = up.astype(BF)
        active_ref[spot, :] = (value * up).astype(BF)


def ffn_in(pieces, w, starts):
    nz, nc, rows, width = w.shape
    half, total = rows // 2, 4 * pieces[0].shape[1]
    count = half // 128
    block = pl.BlockSpec((total, 128), lambda c, i: (0, c * count + i))
    return pl.pallas_call(
        ffn_in_kernel,
        grid=(nc, count),
        in_specs=[pl.BlockSpec(memory_space=pltpu.SMEM)]
        + piece_specs(pieces)
        + [pl.BlockSpec((nz, 1, 2, 128, width), lambda c, i: (0, c, 0, i, 0))],
        out_specs=[block, block, block],
        out_shape=[jax.ShapeDtypeStruct((total, nc * half), BF)] * 3,
        compiler_params=params(2),
        cost_estimate=cost(
            2 * nz * total * width * nc * rows, 2 * nz * width * (total + nc * rows) + 3 * total * nc * rows
        ),
        name="ffn_in",
    )(starts, *pieces, w.reshape(nz, nc, 2, half, width))


def ffn_back_kernel(starts_ref, *refs):
    pieces, (w_ref, gate_ref, up_ref, out_ref) = refs[:8], refs[8:]
    half = w_ref.shape[2]
    for d in range(4):
        acc = nt_sum(pieces, d, lambda z: w_ref[z, 0])
        spot = spot_of(starts_ref, d, acc.shape[0])
        value, slope = gelu_parts(gate_ref[spot, :].astype(F32))
        out_ref[spot, :half] = (acc * up_ref[spot, :].astype(F32) * slope).astype(BF)
        out_ref[spot, half:] = (acc * value).astype(BF)


def ffn_back(pieces, w, gate, up, starts):
    nz, nc, half, width = w.shape
    total = gate.shape[0]
    kept = pl.BlockSpec((total, half), lambda c: (0, c))
    return pl.pallas_call(
        ffn_back_kernel,
        grid=(nc,),
        in_specs=[pl.BlockSpec(memory_space=pltpu.SMEM)]
        + piece_specs(pieces)
        + [pl.BlockSpec((nz, 1, half, width), lambda c: (0, c, 0, 0)), kept, kept],
        out_specs=pl.BlockSpec((total, 2 * half), lambda c: (0, c)),
        out_shape=jax.ShapeDtypeStruct((total, nc * 2 * half), BF),
        compiler_params=params(1),
        cost_estimate=cost(
            2 * nz * total * width * nc * half, 2 * nz * width * (total + nc * half) + 8 * total * nc * half
        ),
        name="ffn_back",
    )(starts, *pieces, w, gate, up)


def mm_nt_plain(act, w, first, rows, starts):
    part = lax.slice_in_dim(w, first, first + rows, axis=2)
    out = jnp.einsum("ztf,zcrf->tcr", act, part, preferred_element_type=F32)
    return out.astype(BF).reshape(act.shape[1], -1)


def mm_nn_plain(grads, w, first, rows, starts):
    grad = grads[0]
    part = lax.slice_in_dim(w, first, first + rows, axis=2)
    split = grad.reshape(grad.shape[0], w.shape[1], rows)
    out = jnp.einsum("tcr,zcrf->ztf", split, part, preferred_element_type=F32)
    return [out.astype(BF)]


def mm_tn_plain(grads, act, starts):
    return jnp.einsum("tr,ztf->zrf", grads[0], act, preferred_element_type=F32).astype(BF)


def ffn_in_plain(act, w, starts):
    _, nc, rows, _ = w.shape
    total = act.shape[1]
    both = jnp.einsum("ztf,zcrf->tcr", act, w, preferred_element_type=F32)
    gate, up = both[:, :, : rows // 2], both[:, :, rows // 2 :]
    value, _ = gelu_parts(gate)
    return [part.astype(BF).reshape(total, -1) for part in (gate, up, value * up)]


def ffn_back_plain(act, w, gate, up, starts):
    total, nc = gate.shape[0], w.shape[1]
    grad = jnp.einsum("ztf,zcrf->tcr", act, w, preferred_element_type=F32)
    value, slope = gelu_parts(gate.astype(F32).reshape(grad.shape))
    both = [grad * up.astype(F32).reshape(grad.shape) * slope, grad * value]
    return jnp.concatenate(both, axis=2).astype(BF).reshape(total, -1)


def near_buckets(tile, total):
    first = (total // LB - 2 + tile) * LB
    rows = lax.broadcasted_iota(jnp.int32, (LB, LB), 0)
    lanes = lax.broadcasted_iota(jnp.int32, (LB, LB), 1)
    return bucket_index(first + rows - (total - LB) - lanes)


def build_strips(table_ref, strip_ref, total, group):
    heads = strip_ref.shape[0]
    near = (total // LB - 2) * LB
    for h in range(heads):
        head = group * heads + h
        strip_ref[h, :near] = jnp.full((near, LB), table_ref[head, 15], F32)
        strip_ref[h, near + 3 * LB :] = jnp.full((near, LB), table_ref[head, 31], F32)

    def one_tile(tile, _):
        index = near_buckets(tile, total)
        vals = [jnp.full((LB, LB), table_ref[group * heads + h, 0], F32) for h in range(heads)]
        for b in range(1, 32):
            hit = index == b
            vals = [
                jnp.where(hit, table_ref[group * heads + h, b], vals[h]) for h in range(heads)
            ]
        for h in range(heads):
            strip_ref[h, pl.ds(pl.multiple_of(near + tile * LB, LB), LB)] = vals[h]
        return 0

    lax.fori_loop(0, 3, one_tile, 0)


def head_lanes(shape, h):
    lanes = lax.broadcasted_iota(jnp.int32, shape, 1)
    return lanes // 64 == h, lanes == ((h + 1) % 4) * 64


def mask_keys(keys, length, h):
    own, spare = head_lanes(keys.shape, h)
    dead = lax.broadcasted_iota(jnp.int32, keys.shape, 0) >= length
    mask = jnp.where(jnp.logical_and(spare, dead), masked_score, 0.0)
    return jnp.where(own, keys.astype(F32), mask).astype(BF)


def with_one(queries, h):
    _, spare = head_lanes(queries.shape, h)
    return jnp.where(spare, 1.0, queries.astype(F32)).astype(BF)


def own_lanes(values, h):
    own, _ = head_lanes(values.shape, h)
    return jnp.where(own, values.astype(F32), 0.0).astype(BF)


def block_bias(strip_ref, h, block, total):
    first = total - LB - 2 * block * LB
    left = strip_ref[h, pl.ds(pl.multiple_of(first, LB), total)]
    right = strip_ref[h, pl.ds(pl.multiple_of(first - LB, LB), total)]
    return jnp.concatenate([left, right], axis=1)


def attend_kernel(group, length_ref, table_ref, q_ref, k_ref, v_ref, out_ref, lse_ref, strip, heads_k, turned_v, turned_out):
    total = q_ref.shape[0]
    heads = strip.shape[0]
    build_strips(table_ref, strip, total, group)
    turned_v[...] = v_ref[...].astype(F32).T.astype(BF)
    for h in range(heads):
        heads_k[h] = mask_keys(k_ref[...], length_ref[0], h)

    def one_block(block, _):
        spot = pl.ds(pl.multiple_of(block * 256, 256), 256)
        queries = q_ref[spot]
        for h in range(heads):
            scores = dot_nt(heads_k[h], with_one(queries, h)) + block_bias(strip, h, block, total)
            largest = jnp.max(scores, axis=0, keepdims=True)
            raised = jnp.exp(scores - largest)
            totals = jnp.sum(raised, axis=0, keepdims=True)
            out = dot_nn(turned_v[h * 64 : (h + 1) * 64], raised.astype(BF))
            turned_out[h * 64 : (h + 1) * 64, spot] = out * (1.0 / totals)
            lse_ref[h : h + 1, spot] = largest + jnp.log(totals)
        return 0

    lax.fori_loop(0, total // 256, one_block, 0)
    out_ref[...] = turned_out[...].T.astype(BF)


def attend_back_kernel(
    group, length_ref, table_ref, q_ref, k_ref, v_ref, grad_ref, lse_ref, out_ref, table_grad_ref,
    strip, strip_grad, heads_k, turned_k, turned_q, ds_ref, p_ref, dk_ref, dv_ref,
):
    total = q_ref.shape[0]
    heads = strip.shape[0]
    build_strips(table_ref, strip, total, group)
    strip_grad[...] = jnp.zeros_like(strip_grad)
    dk_ref[...] = jnp.zeros_like(dk_ref)
    dv_ref[...] = jnp.zeros_like(dv_ref)
    turned_k[...] = k_ref[...].astype(F32).T.astype(BF)
    for h in range(heads):
        heads_k[h] = mask_keys(k_ref[...], length_ref[0], h)

    def one_block(block, _):
        spot = pl.ds(pl.multiple_of(block * 256, 256), 256)
        queries, grads = q_ref[spot], grad_ref[spot]
        own_q, own_g = [], []
        for h in range(heads):
            own_q.append(own_lanes(queries, h))
            own_g.append(own_lanes(grads, h))
            scores = dot_nt(heads_k[h], with_one(queries, h)) + block_bias(strip, h, block, total)
            probs = jnp.exp(scores - lse_ref[h : h + 1, spot])
            weighed = probs * dot_nt(v_ref[...], own_g[h])
            delta = jnp.sum(weighed, axis=0, keepdims=True)
            grad_scores = weighed - probs * delta
            first = total - LB - 2 * block * LB
            left = pl.ds(pl.multiple_of(first, LB), total)
            right = pl.ds(pl.multiple_of(first - LB, LB), total)
            strip_grad[h, left] += grad_scores[:, :LB]
            strip_grad[h, right] += grad_scores[:, LB:]
            rounded = grad_scores.astype(BF)
            ds_ref[:, h * 256 : (h + 1) * 256] = rounded
            p_ref[:, h * 256 : (h + 1) * 256] = probs.astype(BF)
            turned_q[h * 64 : (h + 1) * 64, spot] = dot_nn(turned_k[h * 64 : (h + 1) * 64], rounded)
        dk_ref[...] += dot_nn(ds_ref[...], jnp.concatenate(own_q, axis=0))
        dv_ref[...] += dot_nn(p_ref[...], jnp.concatenate(own_g, axis=0))
        return 0

    lax.fori_loop(0, total // 256, one_block, 0)
    out_ref[:, :256] = turned_q[...].T.astype(BF)
    out_ref[:, 256:512] = dk_ref[...].astype(BF)
    out_ref[:, 512:] = dv_ref[...].astype(BF)

    near = (total // LB - 2) * LB
    for h in range(heads):
        table_grad_ref[h] = jnp.zeros((32, LB), F32)
        table_grad_ref[h, 15:16] = jnp.sum(strip_grad[h, :near], axis=0, keepdims=True)
        table_grad_ref[h, 31:32] = jnp.sum(strip_grad[h, near + 3 * LB :], axis=0, keepdims=True)

    def one_tile(tile, _):
        index = near_buckets(tile, total)
        spot = pl.ds(pl.multiple_of(near + tile * LB, LB), LB)
        for h in range(heads):
            grads = strip_grad[h, spot]
            for b in range(32):
                picked = jnp.where(index == b, grads, 0.0)
                table_grad_ref[h, b : b + 1] += jnp.sum(picked, axis=0, keepdims=True)
        return 0

    lax.fori_loop(0, 3, one_tile, 0)


def block_specs(total, group):
    def spec(i):
        return pl.BlockSpec((total, 256), lambda _: (0, 3 * group + i))

    smem = pl.BlockSpec(memory_space=pltpu.SMEM)
    return [smem, smem, spec(0), spec(1), spec(2)]


def attend(group, projected, length, table):
    total = projected.shape[0]
    heads = 4
    return pl.pallas_call(
        functools.partial(attend_kernel, group),
        grid=(1,),
        in_specs=block_specs(total, group),
        out_specs=[
            pl.BlockSpec((total, 256), lambda _: (0, 0)),
            pl.BlockSpec((8, total), lambda _: (0, 0)),
        ],
        out_shape=[
            jax.ShapeDtypeStruct((total, 256), BF),
            jax.ShapeDtypeStruct((8, total), F32),
        ],
        scratch_shapes=[
            pltpu.VMEM((heads, 2 * total - LB, LB), F32),
            pltpu.VMEM((heads, total, 256), BF),
            pltpu.VMEM((256, total), BF),
            pltpu.VMEM((256, total), F32),
        ],
        compiler_params=params(1),
        cost_estimate=cost(heads * total * total * 2 * 256 * 2, 4 * total * 256 * 2),
        name="attend",
    )(length, table, projected, projected, projected)


def attend_back(group, projected, length, table, grad_out, lse):
    total = projected.shape[0]
    heads = 4
    return pl.pallas_call(
        functools.partial(attend_back_kernel, group),
        grid=(1,),
        in_specs=block_specs(total, group)
        + [
            pl.BlockSpec((total, 256), lambda _: (0, group)),
            pl.BlockSpec((8, total), lambda _: (0, 0)),
        ],
        out_specs=[
            pl.BlockSpec((total, 768), lambda _: (0, 0)),
            pl.BlockSpec((heads, 32, LB), lambda _: (0, 0, 0)),
        ],
        out_shape=[
            jax.ShapeDtypeStruct((total, 768), BF),
            jax.ShapeDtypeStruct((heads, 32, LB), F32),
        ],
        scratch_shapes=[
            pltpu.VMEM((heads, 2 * total - LB, LB), F32),
            pltpu.VMEM((heads, 2 * total - LB, LB), F32),
            pltpu.VMEM((heads, total, 256), BF),
            pltpu.VMEM((256, total), BF),
            pltpu.VMEM((256, total), F32),
            pltpu.VMEM((total, heads * 256), BF),
            pltpu.VMEM((total, heads * 256), BF),
            pltpu.VMEM((total, 256), F32),
            pltpu.VMEM((total, 256), F32),
        ],
        compiler_params=params(1),
        cost_estimate=cost(heads * total * total * 2 * 256 * 5, 8 * total * 256 * 2),
        name="attend_back",
    )(length, table, projected, projected, projected, grad_out, lse)


def split_heads(projected, groups, heads):
    parts = projected.reshape(projected.shape[0], groups, 3, heads, 64)
    return [parts[:, :, i].reshape(projected.shape[0], groups * heads, 64) for i in range(3)]


def plain_scores(queries, keys, length, table):
    slots = jnp.arange(keys.shape[0], dtype=jnp.int32)
    picked = (bucket_index(slots[None, :] - slots[:, None])[:, :, None] == jnp.arange(32)).astype(F32)
    bias = jnp.einsum("qkb,hb->hqk", picked, table, precision=lax.Precision.HIGHEST)
    scores = jnp.einsum("qhs,khs->hqk", queries, keys, preferred_element_type=F32) + bias
    return jnp.where(slots < length[0], scores, masked_score), picked


def attend_plain(projected, length, table, groups, heads):
    queries, keys, values = split_heads(projected, groups, heads)
    scores, _ = plain_scores(queries, keys, length, table)
    lse = jax.nn.logsumexp(scores, axis=2)
    probs = jnp.exp(scores - lse[:, :, None]).astype(BF)
    out = jnp.einsum("hqk,khs->qhs", probs, values, preferred_element_type=F32)
    return out.astype(BF).reshape(projected.shape[0], -1), lse


def attend_back_plain(projected, length, table, grad_out, lse, groups, heads):
    total = projected.shape[0]
    queries, keys, values = split_heads(projected, groups, heads)
    grads = grad_out.reshape(queries.shape)
    scores, picked = plain_scores(queries, keys, length, table)
    probs = jnp.exp(scores - lse[:, :, None])
    weighed = probs * jnp.einsum("qhs,khs->hqk", grads, values, preferred_element_type=F32)
    wide = weighed - probs * jnp.sum(weighed, axis=2, keepdims=True)
    rounded = wide.astype(BF)
    parts = [
        jnp.einsum("hqk,khs->qhs", rounded, keys, preferred_element_type=F32),
        jnp.einsum("hqk,qhs->khs", rounded, queries, preferred_element_type=F32),
        jnp.einsum("hqk,qhs->khs", probs.astype(BF), grads, preferred_element_type=F32),
    ]
    parts = [part.astype(BF).reshape(total, groups, 1, heads * 64) for part in parts]
    table_grad = jnp.einsum("hqk,qkb->hb", wide, picked, precision=lax.Precision.HIGHEST)
    return (
        jnp.concatenate(parts, axis=2).reshape(total, -1),
        table_grad.reshape(groups * heads, 32, 1),
    )


def hop(value, axis):
    return lax.ppermute(value, axis, swap)


def pick(value, index, axis):
    return lax.dynamic_index_in_dim(value, index, axis, keepdims=False)


def paired(mine, other, axis, place=0):
    return jnp.where(
        lax.axis_index(axis) == 0,
        jnp.stack([mine, other], axis=place),
        jnp.stack([other, mine], axis=place),
    )


def after(value, *others):
    return lax.optimization_barrier((value, *others))[0]


def gather_plain(part, *beside):
    return lax.all_gather(part, ("x", "y"), axis=1, tiled=True), (), ()


def gather_tokens(part, *beside):
    half = part.shape[0] // 2
    low, high = part[:half], part[half:]
    low_x, high_y = hop(low, "x"), hop(high, "y")
    if beside:
        low_x, high_y = after(low_x, *beside), after(high_y, *beside)
    low_y, high_x = hop(low, "y"), hop(high, "x")
    low_xy, high_xy = hop(low_x, "y"), hop(high_y, "x")
    pieces = [low, low_y, low_x, low_xy, high, high_y, high_x, high_xy]
    return pieces, (low_x, high_y), (low_y, low_xy, high_x, high_xy)


def scatter_plain(parts, beside=(), beside_last=()):
    whole = parts[0].astype(F32)
    return lax.psum_scatter(whole, ("x", "y"), scatter_dimension=1, tiled=True), (), ()


def scatter_tokens(parts, beside=(), beside_last=()):
    low_out, low_keep, high_out, high_keep = parts
    low_in, high_in = hop(low_out, "x"), hop(high_out, "y")
    if beside:
        low_in, high_in = after(low_in, *beside), after(high_in, *beside)

    def add(keep, arrived, index):
        return keep[index].astype(F32) + arrived[index].astype(F32)

    low_last = hop(add(low_keep, low_in, 1).astype(BF), "y")
    high_last = hop(add(high_keep, high_in, 1).astype(BF), "x")
    if beside_last:
        low_last, high_last = after(low_last, *beside_last), after(high_last, *beside_last)
    low = add(low_keep, low_in, 0) + low_last.astype(F32)
    high = add(high_keep, high_in, 0) + high_last.astype(F32)
    return jnp.concatenate([low, high], axis=0), (low_in, high_in), (low_last, high_last)


def place_kernel(write, here_ref, *refs):
    pieces, outs = refs[:4], refs[4:]
    step = pl.program_id(0)
    for near in range(4):
        y = here_ref[0] if near < 2 else 1 - here_ref[0]
        c = here_ref[1] if near % 2 == 0 else 1 - here_ref[1]

        @pl.when(step == 2 * y + c)
        def _():
            write(pieces[near], outs)


def place(pieces, here, shapes, write):
    return pl.pallas_call(
        functools.partial(place_kernel, write),
        grid=(4,),
        in_specs=[pl.BlockSpec(memory_space=pltpu.SMEM)]
        + [pl.BlockSpec(piece.shape, lambda q: (0, 0)) for piece in pieces],
        out_specs=[
            pl.BlockSpec(shape, lambda q, rank=len(shape): (q,) + (0,) * (rank - 1)) for shape in shapes
        ],
        out_shape=[jax.ShapeDtypeStruct((4 * shape[0], *shape[1:]), F32) for shape in shapes],
        compiler_params=params(1),
        cost_estimate=cost(0, pieces[0].size),
        name="place",
    )(here, *pieces)


def share(part, *beside):
    over_y = hop(part, "y")
    if beside:
        over_y = after(over_y, *beside)
    return [part, hop(part, "c"), over_y, hop(over_y, "c")], over_y


def share_plain(part):
    return lax.all_gather(part, ("y", "c"), axis=0), part


def to_groups(halves, other, extra):
    count, _, t, width = halves.shape
    both = paired(pick(halves, lax.axis_index("y"), 1), other, "y").reshape(2 * count, t, width)
    if extra is not None:
        wide = jnp.broadcast_to(extra[None], (2 * count, *extra.shape))
        both = jnp.concatenate([both, wide], axis=1)
    return lax.all_to_all(both, "z", 0, 0, tiled=True)


def from_groups(mine):
    nz, t, width = mine.shape
    back = lax.all_to_all(mine, "z", 0, 0, tiled=True).reshape(2, nz // 2, t, width)
    leaving = pick(back, 1 - lax.axis_index("y"), 0)
    return (back, hop(leaving, "y")), leaving


def settle_kernel(y_ref, back_ref, other_ref, out_ref):
    j, y = pl.program_id(0), pl.program_id(1)

    @pl.when(y == y_ref[0])
    def _():
        out_ref[0, 0] = back_ref[y, j].astype(out_ref.dtype)

    @pl.when(y != y_ref[0])
    def _():
        out_ref[0, 0] = other_ref[j].astype(out_ref.dtype)


def settle(arrived, dtype):
    back, other = arrived
    _, count, t, width = back.shape
    y = lax.axis_index("y").astype(jnp.int32).reshape(1)
    out = pl.pallas_call(
        settle_kernel,
        grid=(count, 2),
        in_specs=[
            pl.BlockSpec(memory_space=pltpu.SMEM),
            pl.BlockSpec(back.shape, lambda j, y: (0, 0, 0, 0)),
            pl.BlockSpec(other.shape, lambda j, y: (0, 0, 0)),
        ],
        out_specs=pl.BlockSpec((1, 1, t, width), lambda j, y: (j, y, 0, 0)),
        out_shape=jax.ShapeDtypeStruct((count, 2, t, width), dtype),
        compiler_params=params(2),
        cost_estimate=cost(0, count * t * width),
        name="settle",
    )(y, back, other)
    return out.reshape(count, 2 * t, width)


def settle_plain(arrived, dtype):
    back, other = arrived
    _, count, t, width = back.shape
    both = paired(pick(back, lax.axis_index("y"), 0), other, "y")
    return both.transpose(1, 0, 2, 3).reshape(count, 2 * t, width).astype(dtype)


def sum_plane(value, nx):
    value = value + hop(value, "c")
    value = value + hop(value, "x") if nx == 2 else lax.psum(value, "x")
    return value + hop(value, "y")


def sum_line(value, nz):
    step = 1
    while step < nz:
        value = value + lax.ppermute(value, "z", [(i, i ^ step) for i in range(nz)])
        step *= 2
    return value


def body(
    nx, nz, nc, inputs, lengths, attn_gain, ffn_gain, query_key, value_proj, out_proj, gate_up, down_proj, bias_table, cotangent
):
    x, y = lax.axis_index("x"), lax.axis_index("y")
    c, z = lax.axis_index("c"), lax.axis_index("z")
    width = inputs.shape[2]
    features = nz * width
    quarter = y * nc + c
    parts = 2 * nc
    buckets, mine = bias_table.shape
    count = inputs.shape[1] // 2

    stored_in = inputs.reshape(inputs.shape[0], 2, count, width)
    stored_cot = cotangent.reshape(stored_in.shape)
    small = jnp.concatenate(
        [attn_gain[None], ffn_gain[None], jnp.pad(bias_table.reshape(1, -1), ((0, 0), (0, width - buckets * mine)))]
    )
    small = jnp.pad(small, ((0, 5), (0, 0)))
    leaving = pick(stored_in, 1 - y, 1)

    query_key_rows = jnp.transpose(query_key, (1, 2, 3, 0))
    value_rows = jnp.transpose(value_proj, (1, 2, 0))
    gate_up_rows = jnp.transpose(gate_up, (1, 2, 3, 0))
    heads = value_rows.shape[0] // parts
    units = gate_up_rows.shape[0] // parts
    unit = gate_up_rows.shape[2]
    local_heads = nc * heads

    def own(rows, size):
        return lax.dynamic_slice_in_dim(rows, quarter * size, size, 0)

    def flat(rows):
        return rows.reshape(-1, width)

    def spread(rows):
        gathered = lax.all_gather(rows, ("z", "c"), axis=0, tiled=True)
        return gathered.reshape(nz, nc, rows.shape[0], width)

    own_pair = own(query_key_rows, heads)
    own_attn = [own_pair[:, 0], own_pair[:, 1], own(value_rows, heads), own(out_proj, heads)]
    own_attn = jnp.concatenate([flat(rows) for rows in own_attn])
    w_attn = spread(own_attn)
    other = after(hop(leaving, "y"), own_attn)
    own_pair = own(after(gate_up_rows, other), units)
    own_gate_up = jnp.concatenate([flat(own_pair[:, 0]), flat(own_pair[:, 1])])
    w_gate_up = spread(own_gate_up)
    own_down = flat(own(after(down_proj, other), units))
    w_down = spread(own_down)
    qkv_count, out_count = 3 * heads * 64, heads * 64

    arrived = after(to_groups(stored_in, other, small), own_gate_up, own_down)
    tokens = arrived[:, :count].astype(F32)
    small = arrived[:, count:]
    gain_one = small[:, :1].astype(F32)
    gain_two = small[:, 1:2].astype(F32)
    table = small[:, 2, : buckets * mine].reshape(nz, buckets, mine).transpose(0, 2, 1)
    table = table.reshape(-1, buckets).astype(F32)
    table = lax.dynamic_slice_in_dim(table, y * local_heads, local_heads, 0)

    both_lengths = jnp.stack([lengths, lax.ppermute(lengths, "y", swap)])
    both_lengths = jnp.where(y == 0, both_lengths, both_lengths[::-1]).reshape(-1)
    length = lax.dynamic_slice_in_dim(both_lengths, z, 1, 0)
    slots = (x * 2 + y) * count + jnp.arange(count, dtype=jnp.int32)
    live = (slots < length).astype(F32)[None, :, None]

    def scale_of(values):
        squares = jnp.sum(values * values, axis=(0, 2), keepdims=True)
        return lax.rsqrt(squares / features + norm_eps)

    def norm_back(values, scale, gain, grad):
        inner = jnp.sum(values * gain * grad, axis=(0, 2), keepdims=True)
        out = scale * gain * grad - values * (scale * scale * scale) * inner / features
        return out, jnp.sum(values * scale * grad, axis=1)

    def reduce(partial):
        rows = partial.reshape(nz * partial.shape[1], width)
        return lax.psum_scatter(rows, ("z", "c"), scatter_dimension=0, tiled=True)

    fits = nx == 2 and heads == 4 and count == 256 and units * unit % 640 == 0 and nz % 2 == 0
    if fits:
        forward, backward, gather, scatter = attend, attend_back, gather_tokens, scatter_tokens
        nt, nn, tn, ffn_one, ffn_two = mm_nt, mm_nn, mm_tn, ffn_in, ffn_back
        shared, stored_from = share, settle
    else:
        forward, backward, gather, scatter = attend_plain, attend_back_plain, gather_plain, scatter_plain
        nt, nn, tn, ffn_one, ffn_two = mm_nt_plain, mm_nn_plain, mm_tn_plain, ffn_in_plain, ffn_back_plain
        shared, stored_from = share_plain, settle_plain
    near_x, near_y = jnp.array([0, 0, 1, 1]) ^ x, jnp.array([0, 1, 0, 1]) ^ y
    starts = ((near_x * 2 + near_y) * count).astype(jnp.int32)

    def attend_back_all(grad, *last):
        if not fits:
            grads, table_grad = backward(projected, length, table, grad, lse, nc, heads)
            return (grads,), table_grad
        first = backward(0, projected, length, table, grad, lse[0])
        second = backward(1, after(projected, first[0], *last), length, table, grad, lse[1])
        return (first[0], second[0]), jnp.concatenate([first[1], second[1]])

    scale_one = scale_of(tokens)
    normed, _, _ = gather((tokens * scale_one * gain_one).astype(BF))
    cot_other = hop(pick(stored_cot, 1 - y, 1), "y")
    upstream = live * to_groups(stored_cot, after(cot_other, arrived), None).astype(F32)
    upstream_rounded = after(upstream.astype(BF), w_attn)
    projected = nt(normed, w_attn, 0, qkv_count, starts)
    if fits:
        first = forward(0, projected, length, table)
        grad_ffn, cot_first, cot_last = gather(upstream_rounded, first[0])
        second = forward(1, after(projected, first[0], *cot_first), length, table)
        attended, lse = (first[0], second[0]), (first[1], second[1])
    else:
        grad_ffn, _, cot_last = gather(upstream_rounded)
        attended, lse = forward(projected, length, table, nc, heads)
        attended = (attended,)
    heads_out = [after(attended[0], *cot_last), *attended[1:]]
    hidden = tokens + scatter(nn(heads_out, w_attn, qkv_count, out_count, starts))[0]
    scale_two = scale_of(hidden)
    normed_two, _, _ = gather((hidden * scale_two * gain_two).astype(BF))
    gate, up, activated = ffn_one(normed_two, w_gate_up, starts)

    down_partial = tn([activated], grad_ffn, starts)
    down_part = reduce(down_partial)
    grad_gate_up = ffn_two(grad_ffn, w_down, after(gate, down_partial), up, starts)
    two_parts = nn([grad_gate_up], w_gate_up, 0, 2 * units * unit, starts)
    grad_two, two_first, _ = scatter(two_parts)
    gate_up_partial = tn([after(grad_gate_up, two_parts[0])], normed_two, starts)
    gate_up_part = reduce(after(gate_up_partial, down_part, *two_first))
    branch_parts = nn([after(activated, gate_up_partial)], w_down, 0, units * unit, starts)
    through, ffn_gain_part = norm_back(hidden, scale_two, gain_two, grad_two)
    grad_hidden = upstream + through
    grad_branch, _, branch_last = gather(after(grad_hidden.astype(BF), branch_parts[0]))
    grad_attended = nt(grad_branch, w_attn, qkv_count, out_count, starts)
    out_partial = tn(attended, grad_branch, starts)
    branch_parts = [after(part, *branch_last) for part in branch_parts]
    branch, branch_first, branch_last = scatter(branch_parts)
    down_pieces, down_last = shared(after(down_part, grad_attended))
    grad_projected, table_part = attend_back_all(after(grad_attended, out_partial), *branch_first)
    out_part = reduce(after(out_partial, gate_up_part, grad_projected[0], *branch_first))
    outputs = (live * (hidden + branch)).astype(BF)
    last = after(grad_projected[-1], *branch_last, down_last)
    grad_projected = [*grad_projected[:-1], last]
    outputs, _ = from_groups(outputs)
    qkv_partial = tn(grad_projected, normed, starts)
    qkv_part = reduce(after(qkv_partial, out_part))
    one_parts = nn(grad_projected, w_attn, 0, qkv_count, starts)
    gate_up_pieces, gate_up_last = shared(after(gate_up_part, grad_projected[0]))
    grad_one, _, one_last = scatter(one_parts, (gate_up_last,), (outputs[0],))
    through, attn_gain_part = norm_back(tokens, scale_one, gain_one, grad_one)
    input_grad, input_leaves = from_groups((grad_hidden + through).astype(BF))
    outputs = stored_from(outputs, BF)

    table_part = jnp.sum(table_part, axis=2)
    every = jnp.zeros((nx * 2 * local_heads, table_part.shape[1]), F32)
    every = lax.dynamic_update_slice_in_dim(every, table_part, (x * 2 + y) * local_heads, 0)
    spare = -every.size % width
    every = jnp.pad(every.reshape(-1), (0, spare)).reshape(-1, width)
    sums = sum_plane(jnp.concatenate([attn_gain_part, ffn_gain_part, every]), nx)
    all_sums = sum_line(after(sums, input_leaves), nz)
    attn_gain_grad, ffn_gain_grad = all_sums[:nz], all_sums[nz : 2 * nz]
    every = all_sums[2 * nz :].reshape(-1)[: nx * 2 * local_heads * buckets].reshape(-1, buckets)

    out_pieces, _ = shared(after(out_part, *one_last))
    if fits:
        here = jnp.stack([y, c]).astype(jnp.int32)

        def write_rows(source, outs):
            outs[0][...] = source[...].astype(F32)

        def write_qkv(source, outs):
            for h in range(heads):
                for i in range(3):
                    value = source[(i * heads + h) * 64 : (i * heads + h + 1) * 64, :].astype(F32)
                    if i == 2:
                        outs[1][h] = value
                    else:
                        outs[0][h, i] = value

        def write_gate_up(source, outs):
            for u in range(units):
                for i in range(2):
                    first = (i * units + u) * unit
                    outs[0][u, i] = source[first : first + unit, :].astype(F32)

        (down_all,) = place(down_pieces, here, [(units * unit, width)], write_rows)
        (out_all,) = place(out_pieces, here, [(heads * 64, width)], write_rows)
        (gate_up_all,) = place(gate_up_pieces, here, [(units, 2, unit, width)], write_gate_up)
        qkv_pieces, _ = shared(after(qkv_part, sums, *one_last), down_all, out_all, gate_up_all, outputs)
        query_key_all, value_all = place(
            qkv_pieces, here, [(heads, 2, 64, width), (heads, 64, width)], write_qkv
        )
    else:
        down_all, out_all = down_pieces.astype(F32), out_pieces.astype(F32)
        gate_up_all = gate_up_pieces.astype(F32).reshape(parts, 2, units, unit, width)
        gate_up_all = gate_up_all.transpose(0, 2, 1, 3, 4).reshape(-1, 2, unit, width)
        qkv_all = shared(qkv_part)[0].astype(F32).reshape(parts, 3, heads, 64, width)
        qkv_all = qkv_all.transpose(0, 2, 1, 3, 4).reshape(-1, 3, 64, width)
        query_key_all, value_all = qkv_all[:, :2], qkv_all[:, 2]
    input_grad = stored_from(input_grad, F32)
    down_all, out_all = down_all.reshape(down_proj.shape), out_all.reshape(out_proj.shape)

    table_grad = lax.dynamic_slice_in_dim(every, (x * nz + z) * mine, mine, 0).T
    return (
        outputs,
        input_grad,
        pick(attn_gain_grad, z, 0),
        pick(ffn_gain_grad, z, 0),
        query_key_all.transpose(3, 0, 1, 2),
        value_all.transpose(2, 0, 1),
        out_all,
        gate_up_all.transpose(3, 0, 1, 2),
        down_all,
        table_grad,
    )


def solution(mesh):
    dp, nx, nz = (mesh.shape[name] for name in ("dp", "gx", "gy"))
    nc = dp // 2
    split = Mesh(mesh.devices.reshape(2, nc, nx, nz), ("y", "c", "x", "z"))
    seq = ("y", "c")
    return jax.shard_map(
        functools.partial(body, nx, nz, nc),
        mesh=split,
        in_specs=(
            P(seq, "x", "z"),
            P(seq),
            P("z"),
            P("z"),
            P("z", "x", None, None),
            P("z", "x", None),
            P("x", None, "z"),
            P("z", "x", None, None),
            P("x", None, "z"),
            P(None, ("x", "z")),
            P(seq, "x", "z"),
        ),
        out_specs=(
            P(seq, "x", "z"),
            P(seq, "x", "z"),
            P("z"),
            P("z"),
            P("z", "x", None, None),
            P("z", "x", None),
            P("x", None, "z"),
            P("z", "x", None, None),
            P("x", None, "z"),
            P(None, ("x", "z")),
        ),
        check_vma=False,
    )
```

```python
import functools
import math

import jax
import jax.numpy as jnp
from jax import lax
from jax.experimental import pallas as pl
from jax.experimental.pallas import tpu as pltpu
from jax.sharding import Mesh
from jax.sharding import PartitionSpec as P

norm_eps = 1e-06
masked_score = -1e30
bucket_edges = (12, 16, 23, 32, 46, 64, 91)
BF = jnp.bfloat16
F32 = jnp.float32
LB = 128
VMEM = 60 * 1024 * 1024
swap = [(0, 1), (1, 0)]
gelu_a = math.sqrt(2.0 / math.pi)
gelu_b = 0.044715


def bucket_index(offset):
    magnitude = jnp.abs(offset)
    far_bucket = 8 + sum(((magnitude >= boundary).astype(jnp.int32) for boundary in bucket_edges))
    near_bucket = jnp.where(magnitude < 8, magnitude, far_bucket)
    return near_bucket + 16 * (offset > 0).astype(jnp.int32)


def cost(flops, moved):
    return pl.CostEstimate(flops=int(flops) // 16, bytes_accessed=int(moved) // 16, transcendentals=0)


def params(steps):
    return pltpu.CompilerParams(
        dimension_semantics=("arbitrary",) * steps, vmem_limit_bytes=VMEM
    )


def dot_nt(a, b):
    return lax.dot_general(a, b, (((1,), (1,)), ((), ())), preferred_element_type=F32)


def dot_nn(a, b):
    return lax.dot_general(a, b, (((1,), (0,)), ((), ())), preferred_element_type=F32)


def spot_of(starts_ref, d, count):
    return pl.ds(pl.multiple_of(starts_ref[d], 256), count)


def piece_specs(pieces):
    shape = pieces[0].shape
    return [pl.BlockSpec(shape, lambda *_: (0, 0, 0)) for _ in pieces]


def nt_sum(piece_refs, d, w_of):
    half = piece_refs[0].shape[0]
    acc = None
    for z in range(2 * half):
        part = dot_nt(piece_refs[4 * (z // half) + d][z % half], w_of(z))
        acc = part if acc is None else acc + part
    return acc


def nt_kernel(starts_ref, *refs):
    pieces, (w_ref, out_ref) = refs[:8], refs[8:]
    for d in range(4):
        acc = nt_sum(pieces, d, lambda z: w_ref[z, 0])
        out_ref[spot_of(starts_ref, d, acc.shape[0]), :] = acc.astype(BF)


def mm_nt(pieces, w, first, rows, starts):
    nz, nc, _, width = w.shape
    total = 4 * pieces[0].shape[1]
    count, skip = rows // 256, first // 256
    return pl.pallas_call(
        nt_kernel,
        grid=(nc, count),
        in_specs=[pl.BlockSpec(memory_space=pltpu.SMEM)]
        + piece_specs(pieces)
        + [pl.BlockSpec((nz, 1, 256, width), lambda c, i: (0, c, skip + i, 0))],
        out_specs=pl.BlockSpec((total, 256), lambda c, i: (0, c * count + i)),
        out_shape=jax.ShapeDtypeStruct((total, nc * rows), BF),
        compiler_params=params(2),
        cost_estimate=cost(
            2 * nz * total * width * nc * rows, 2 * nz * width * (total + nc * rows) + 2 * total * nc * rows
        ),
        name="product_nt",
    )(starts, *pieces, w)


def nn_kernel(count, starts_ref, *refs):
    grads, (w_ref, low_out, low_keep, high_out, high_keep) = refs[:count], refs[count:]
    nc, rows, width = w_ref.shape[1:]
    t = grads[0].shape[0] // 4
    in_low = pl.program_id(0) < pl.num_programs(0) // 2

    def product(d):
        spot = spot_of(starts_ref, d, t)
        if count == 1:
            return dot_nn(grads[0][spot, :], w_ref[0].reshape(nc * rows, width)).astype(BF)
        return sum(dot_nn(grads[c][spot, :], w_ref[0, c]) for c in range(count)).astype(BF)

    @pl.when(in_low)
    def _():
        for d in range(4):
            (low_out if d // 2 else low_keep)[d % 2, 0] = product(d)

    @pl.when(jnp.logical_not(in_low))
    def _():
        for d in range(4):
            (high_out if d % 2 else high_keep)[d // 2, 0] = product(d)


def mm_nn(grads, w, first, rows, starts):
    total = grads[0].shape[0]
    nz, nc, _, width = w.shape
    skip, half, t = first // rows, nz // 2, total // 4
    low = pl.BlockSpec((2, 1, t, width), lambda z: (0, jnp.minimum(z, half - 1), 0, 0))
    high = pl.BlockSpec((2, 1, t, width), lambda z: (0, jnp.maximum(z - half, 0), 0, 0))
    return pl.pallas_call(
        functools.partial(nn_kernel, len(grads)),
        grid=(nz,),
        in_specs=[pl.BlockSpec(memory_space=pltpu.SMEM)]
        + [pl.BlockSpec(grad.shape, lambda z: (0, 0)) for grad in grads]
        + [pl.BlockSpec((1, nc, rows, width), lambda z: (z, 0, skip, 0))],
        out_specs=[low, low, high, high],
        out_shape=[jax.ShapeDtypeStruct((2, half, t, width), BF)] * 4,
        compiler_params=params(1),
        cost_estimate=cost(
            2 * nz * total * width * nc * rows, 2 * nz * width * (total + nc * rows) + 2 * total * nc * rows
        ),
        name="product_nn",
    )(starts, *grads, w)


def tn_kernel(count, starts_ref, *refs):
    grads, pieces, out_ref = refs[:count], refs[count:-1], refs[-1]
    half, t, _ = pieces[0].shape

    def one(grad_ref):
        turned = [grad_ref[spot_of(starts_ref, d, t), :].T for d in range(4)]
        for z in range(2 * half):
            acc = dot_nn(turned[0], pieces[4 * (z // half)][z % half])
            for d in range(1, 4):
                acc += dot_nn(turned[d], pieces[4 * (z // half) + d][z % half])
            out_ref[z] = acc.astype(BF)

    if count == 1:
        one(grads[0])
    else:
        for c in range(count):

            @pl.when(pl.program_id(0) // (pl.num_programs(0) // count) == c)
            def _():
                one(grads[c])


def mm_tn(grads, pieces, starts):
    total, rows = grads[0].shape
    half, _, width = pieces[0].shape
    nz, count = 2 * half, len(grads)
    block = next(b for b in (640, 384, 256) if rows % b == 0)
    steps = rows // block

    def spec(c):
        return pl.BlockSpec((total, block), lambda i: (0, jnp.clip(i - c * steps, 0, steps - 1)))

    return pl.pallas_call(
        functools.partial(tn_kernel, count),
        grid=(count * steps,),
        in_specs=[pl.BlockSpec(memory_space=pltpu.SMEM)]
        + [spec(c) for c in range(count)]
        + piece_specs(pieces),
        out_specs=pl.BlockSpec((nz, block, width), lambda i: (0, i, 0)),
        out_shape=jax.ShapeDtypeStruct((nz, count * rows, width), BF),
        compiler_params=params(1),
        cost_estimate=cost(
            2 * nz * total * width * count * rows, 2 * nz * width * (total + count * rows) + 2 * total * count * rows
        ),
        name="product_tn",
    )(starts, *grads, *pieces)


def gelu_parts(gate):
    curve = jnp.tanh(gelu_a * (gate + gelu_b * gate * gate * gate))
    value = 0.5 * gate * (1.0 + curve)
    slope = 0.5 * (1.0 + curve) + 0.5 * gate * (1.0 - curve * curve) * gelu_a * (
        1.0 + 3.0 * gelu_b * gate * gate
    )
    return value, slope


def ffn_in_kernel(starts_ref, *refs):
    pieces, (w_ref, gate_ref, up_ref, active_ref) = refs[:8], refs[8:]
    _, _, _, block, width = w_ref.shape
    for d in range(4):
        acc = nt_sum(pieces, d, lambda z: w_ref[z, 0].reshape(2 * block, width))
        spot = spot_of(starts_ref, d, acc.shape[0])
        gate, up = acc[:, :block], acc[:, block:]
        value = 0.5 * gate * (1.0 + jnp.tanh(gelu_a * (gate + gelu_b * gate * gate * gate)))
        gate_ref[spot, :] = gate.astype(BF)
        up_ref[spot, :] = up.astype(BF)
        active_ref[spot, :] = (value * up).astype(BF)


def ffn_in(pieces, w, starts):
    nz, nc, rows, width = w.shape
    half, total = rows // 2, 4 * pieces[0].shape[1]
    count = half // 128
    block = pl.BlockSpec((total, 128), lambda c, i: (0, c * count + i))
    return pl.pallas_call(
        ffn_in_kernel,
        grid=(nc, count),
        in_specs=[pl.BlockSpec(memory_space=pltpu.SMEM)]
        + piece_specs(pieces)
        + [pl.BlockSpec((nz, 1, 2, 128, width), lambda c, i: (0, c, 0, i, 0))],
        out_specs=[block, block, block],
        out_shape=[jax.ShapeDtypeStruct((total, nc * half), BF)] * 3,
        compiler_params=params(2),
        cost_estimate=cost(
            2 * nz * total * width * nc * rows, 2 * nz * width * (total + nc * rows) + 3 * total * nc * rows
        ),
        name="ffn_in",
    )(starts, *pieces, w.reshape(nz, nc, 2, half, width))


def ffn_back_kernel(starts_ref, *refs):
    pieces, (w_ref, gate_ref, up_ref, out_ref) = refs[:8], refs[8:]
    half = w_ref.shape[2]
    for d in range(4):
        acc = nt_sum(pieces, d, lambda z: w_ref[z, 0])
        spot = spot_of(starts_ref, d, acc.shape[0])
        value, slope = gelu_parts(gate_ref[spot, :].astype(F32))
        out_ref[spot, :half] = (acc * up_ref[spot, :].astype(F32) * slope).astype(BF)
        out_ref[spot, half:] = (acc * value).astype(BF)


def ffn_back(pieces, w, gate, up, starts):
    nz, nc, half, width = w.shape
    total = gate.shape[0]
    kept = pl.BlockSpec((total, half), lambda c: (0, c))
    return pl.pallas_call(
        ffn_back_kernel,
        grid=(nc,),
        in_specs=[pl.BlockSpec(memory_space=pltpu.SMEM)]
        + piece_specs(pieces)
        + [pl.BlockSpec((nz, 1, half, width), lambda c: (0, c, 0, 0)), kept, kept],
        out_specs=pl.BlockSpec((total, 2 * half), lambda c: (0, c)),
        out_shape=jax.ShapeDtypeStruct((total, nc * 2 * half), BF),
        compiler_params=params(1),
        cost_estimate=cost(
            2 * nz * total * width * nc * half, 2 * nz * width * (total + nc * half) + 8 * total * nc * half
        ),
        name="ffn_back",
    )(starts, *pieces, w, gate, up)


def mm_nt_plain(act, w, first, rows, starts):
    part = lax.slice_in_dim(w, first, first + rows, axis=2)
    out = jnp.einsum("ztf,zcrf->tcr", act, part, preferred_element_type=F32)
    return out.astype(BF).reshape(act.shape[1], -1)


def mm_nn_plain(grads, w, first, rows, starts):
    grad = grads[0]
    part = lax.slice_in_dim(w, first, first + rows, axis=2)
    split = grad.reshape(grad.shape[0], w.shape[1], rows)
    out = jnp.einsum("tcr,zcrf->ztf", split, part, preferred_element_type=F32)
    return [out.astype(BF)]


def mm_tn_plain(grads, act, starts):
    return jnp.einsum("tr,ztf->zrf", grads[0], act, preferred_element_type=F32).astype(BF)


def ffn_in_plain(act, w, starts):
    _, nc, rows, _ = w.shape
    total = act.shape[1]
    both = jnp.einsum("ztf,zcrf->tcr", act, w, preferred_element_type=F32)
    gate, up = both[:, :, : rows // 2], both[:, :, rows // 2 :]
    value, _ = gelu_parts(gate)
    return [part.astype(BF).reshape(total, -1) for part in (gate, up, value * up)]


def ffn_back_plain(act, w, gate, up, starts):
    total, nc = gate.shape[0], w.shape[1]
    grad = jnp.einsum("ztf,zcrf->tcr", act, w, preferred_element_type=F32)
    value, slope = gelu_parts(gate.astype(F32).reshape(grad.shape))
    both = [grad * up.astype(F32).reshape(grad.shape) * slope, grad * value]
    return jnp.concatenate(both, axis=2).astype(BF).reshape(total, -1)


def near_buckets(tile, total):
    first = (total // LB - 2 + tile) * LB
    rows = lax.broadcasted_iota(jnp.int32, (LB, LB), 0)
    lanes = lax.broadcasted_iota(jnp.int32, (LB, LB), 1)
    return bucket_index(first + rows - (total - LB) - lanes)


def build_strips(table_ref, strip_ref, total, group):
    heads = strip_ref.shape[0]
    near = (total // LB - 2) * LB
    for h in range(heads):
        head = group * heads + h
        strip_ref[h, :near] = jnp.full((near, LB), table_ref[head, 15], F32)
        strip_ref[h, near + 3 * LB :] = jnp.full((near, LB), table_ref[head, 31], F32)

    def one_tile(tile, _):
        index = near_buckets(tile, total)
        vals = [jnp.full((LB, LB), table_ref[group * heads + h, 0], F32) for h in range(heads)]
        for b in range(1, 32):
            hit = index == b
            vals = [
                jnp.where(hit, table_ref[group * heads + h, b], vals[h]) for h in range(heads)
            ]
        for h in range(heads):
            strip_ref[h, pl.ds(pl.multiple_of(near + tile * LB, LB), LB)] = vals[h]
        return 0

    lax.fori_loop(0, 3, one_tile, 0)


def head_lanes(shape, h):
    lanes = lax.broadcasted_iota(jnp.int32, shape, 1)
    return lanes // 64 == h, lanes == ((h + 1) % 4) * 64


def mask_keys(keys, length, h):
    own, spare = head_lanes(keys.shape, h)
    dead = lax.broadcasted_iota(jnp.int32, keys.shape, 0) >= length
    mask = jnp.where(jnp.logical_and(spare, dead), masked_score, 0.0)
    return jnp.where(own, keys.astype(F32), mask).astype(BF)


def with_one(queries, h):
    _, spare = head_lanes(queries.shape, h)
    return jnp.where(spare, 1.0, queries.astype(F32)).astype(BF)


def own_lanes(values, h):
    own, _ = head_lanes(values.shape, h)
    return jnp.where(own, values.astype(F32), 0.0).astype(BF)


def block_bias(strip_ref, h, block, total):
    first = total - LB - 2 * block * LB
    left = strip_ref[h, pl.ds(pl.multiple_of(first, LB), total)]
    right = strip_ref[h, pl.ds(pl.multiple_of(first - LB, LB), total)]
    return jnp.concatenate([left, right], axis=1)


def attend_kernel(group, length_ref, table_ref, q_ref, k_ref, v_ref, out_ref, lse_ref, strip, heads_k, turned_v, turned_out):
    total = q_ref.shape[0]
    heads = strip.shape[0]
    build_strips(table_ref, strip, total, group)
    turned_v[...] = v_ref[...].astype(F32).T.astype(BF)
    for h in range(heads):
        heads_k[h] = mask_keys(k_ref[...], length_ref[0], h)

    def one_block(block, _):
        spot = pl.ds(pl.multiple_of(block * 256, 256), 256)
        queries = q_ref[spot]
        for h in range(heads):
            scores = dot_nt(heads_k[h], with_one(queries, h)) + block_bias(strip, h, block, total)
            largest = jnp.max(scores, axis=0, keepdims=True)
            raised = jnp.exp(scores - largest)
            totals = jnp.sum(raised, axis=0, keepdims=True)
            out = dot_nn(turned_v[h * 64 : (h + 1) * 64], raised.astype(BF))
            turned_out[h * 64 : (h + 1) * 64, spot] = out * (1.0 / totals)
            lse_ref[h : h + 1, spot] = largest + jnp.log(totals)
        return 0

    lax.fori_loop(0, total // 256, one_block, 0)
    out_ref[...] = turned_out[...].T.astype(BF)


def attend_back_kernel(
    group, length_ref, table_ref, q_ref, k_ref, v_ref, grad_ref, lse_ref, out_ref, table_grad_ref,
    strip, strip_grad, heads_k, turned_k, turned_q, ds_ref, p_ref, dk_ref, dv_ref,
):
    total = q_ref.shape[0]
    heads = strip.shape[0]
    build_strips(table_ref, strip, total, group)
    strip_grad[...] = jnp.zeros_like(strip_grad)
    dk_ref[...] = jnp.zeros_like(dk_ref)
    dv_ref[...] = jnp.zeros_like(dv_ref)
    turned_k[...] = k_ref[...].astype(F32).T.astype(BF)
    for h in range(heads):
        heads_k[h] = mask_keys(k_ref[...], length_ref[0], h)

    def one_block(block, _):
        spot = pl.ds(pl.multiple_of(block * 256, 256), 256)
        queries, grads = q_ref[spot], grad_ref[spot]
        own_q, own_g = [], []
        for h in range(heads):
            own_q.append(own_lanes(queries, h))
            own_g.append(own_lanes(grads, h))
            scores = dot_nt(heads_k[h], with_one(queries, h)) + block_bias(strip, h, block, total)
            probs = jnp.exp(scores - lse_ref[h : h + 1, spot])
            weighed = probs * dot_nt(v_ref[...], own_g[h])
            delta = jnp.sum(weighed, axis=0, keepdims=True)
            grad_scores = weighed - probs * delta
            first = total - LB - 2 * block * LB
            left = pl.ds(pl.multiple_of(first, LB), total)
            right = pl.ds(pl.multiple_of(first - LB, LB), total)
            strip_grad[h, left] += grad_scores[:, :LB]
            strip_grad[h, right] += grad_scores[:, LB:]
            rounded = grad_scores.astype(BF)
            ds_ref[:, h * 256 : (h + 1) * 256] = rounded
            p_ref[:, h * 256 : (h + 1) * 256] = probs.astype(BF)
            turned_q[h * 64 : (h + 1) * 64, spot] = dot_nn(turned_k[h * 64 : (h + 1) * 64], rounded)
        dk_ref[...] += dot_nn(ds_ref[...], jnp.concatenate(own_q, axis=0))
        dv_ref[...] += dot_nn(p_ref[...], jnp.concatenate(own_g, axis=0))
        return 0

    lax.fori_loop(0, total // 256, one_block, 0)
    out_ref[:, :256] = turned_q[...].T.astype(BF)
    out_ref[:, 256:512] = dk_ref[...].astype(BF)
    out_ref[:, 512:] = dv_ref[...].astype(BF)

    near = (total // LB - 2) * LB
    for h in range(heads):
        table_grad_ref[h] = jnp.zeros((32, LB), F32)
        table_grad_ref[h, 15:16] = jnp.sum(strip_grad[h, :near], axis=0, keepdims=True)
        table_grad_ref[h, 31:32] = jnp.sum(strip_grad[h, near + 3 * LB :], axis=0, keepdims=True)

    def one_tile(tile, _):
        index = near_buckets(tile, total)
        spot = pl.ds(pl.multiple_of(near + tile * LB, LB), LB)
        for h in range(heads):
            grads = strip_grad[h, spot]
            for b in range(32):
                picked = jnp.where(index == b, grads, 0.0)
                table_grad_ref[h, b : b + 1] += jnp.sum(picked, axis=0, keepdims=True)
        return 0

    lax.fori_loop(0, 3, one_tile, 0)


def block_specs(total, group):
    def spec(i):
        return pl.BlockSpec((total, 256), lambda _: (0, 3 * group + i))

    smem = pl.BlockSpec(memory_space=pltpu.SMEM)
    return [smem, smem, spec(0), spec(1), spec(2)]


def attend(group, projected, length, table):
    total = projected.shape[0]
    heads = 4
    return pl.pallas_call(
        functools.partial(attend_kernel, group),
        grid=(1,),
        in_specs=block_specs(total, group),
        out_specs=[
            pl.BlockSpec((total, 256), lambda _: (0, 0)),
            pl.BlockSpec((8, total), lambda _: (0, 0)),
        ],
        out_shape=[
            jax.ShapeDtypeStruct((total, 256), BF),
            jax.ShapeDtypeStruct((8, total), F32),
        ],
        scratch_shapes=[
            pltpu.VMEM((heads, 2 * total - LB, LB), F32),
            pltpu.VMEM((heads, total, 256), BF),
            pltpu.VMEM((256, total), BF),
            pltpu.VMEM((256, total), F32),
        ],
        compiler_params=params(1),
        cost_estimate=cost(heads * total * total * 2 * 256 * 2, 4 * total * 256 * 2),
        name="attend",
    )(length, table, projected, projected, projected)


def attend_back(group, projected, length, table, grad_out, lse):
    total = projected.shape[0]
    heads = 4
    return pl.pallas_call(
        functools.partial(attend_back_kernel, group),
        grid=(1,),
        in_specs=block_specs(total, group)
        + [
            pl.BlockSpec((total, 256), lambda _: (0, group)),
            pl.BlockSpec((8, total), lambda _: (0, 0)),
        ],
        out_specs=[
            pl.BlockSpec((total, 768), lambda _: (0, 0)),
            pl.BlockSpec((heads, 32, LB), lambda _: (0, 0, 0)),
        ],
        out_shape=[
            jax.ShapeDtypeStruct((total, 768), BF),
            jax.ShapeDtypeStruct((heads, 32, LB), F32),
        ],
        scratch_shapes=[
            pltpu.VMEM((heads, 2 * total - LB, LB), F32),
            pltpu.VMEM((heads, 2 * total - LB, LB), F32),
            pltpu.VMEM((heads, total, 256), BF),
            pltpu.VMEM((256, total), BF),
            pltpu.VMEM((256, total), F32),
            pltpu.VMEM((total, heads * 256), BF),
            pltpu.VMEM((total, heads * 256), BF),
            pltpu.VMEM((total, 256), F32),
            pltpu.VMEM((total, 256), F32),
        ],
        compiler_params=params(1),
        cost_estimate=cost(heads * total * total * 2 * 256 * 5, 8 * total * 256 * 2),
        name="attend_back",
    )(length, table, projected, projected, projected, grad_out, lse)


def split_heads(projected, groups, heads):
    parts = projected.reshape(projected.shape[0], groups, 3, heads, 64)
    return [parts[:, :, i].reshape(projected.shape[0], groups * heads, 64) for i in range(3)]


def plain_scores(queries, keys, length, table):
    slots = jnp.arange(keys.shape[0], dtype=jnp.int32)
    picked = (bucket_index(slots[None, :] - slots[:, None])[:, :, None] == jnp.arange(32)).astype(F32)
    bias = jnp.einsum("qkb,hb->hqk", picked, table, precision=lax.Precision.HIGHEST)
    scores = jnp.einsum("qhs,khs->hqk", queries, keys, preferred_element_type=F32) + bias
    return jnp.where(slots < length[0], scores, masked_score), picked


def attend_plain(projected, length, table, groups, heads):
    queries, keys, values = split_heads(projected, groups, heads)
    scores, _ = plain_scores(queries, keys, length, table)
    lse = jax.nn.logsumexp(scores, axis=2)
    probs = jnp.exp(scores - lse[:, :, None]).astype(BF)
    out = jnp.einsum("hqk,khs->qhs", probs, values, preferred_element_type=F32)
    return out.astype(BF).reshape(projected.shape[0], -1), lse


def attend_back_plain(projected, length, table, grad_out, lse, groups, heads):
    total = projected.shape[0]
    queries, keys, values = split_heads(projected, groups, heads)
    grads = grad_out.reshape(queries.shape)
    scores, picked = plain_scores(queries, keys, length, table)
    probs = jnp.exp(scores - lse[:, :, None])
    weighed = probs * jnp.einsum("qhs,khs->hqk", grads, values, preferred_element_type=F32)
    wide = weighed - probs * jnp.sum(weighed, axis=2, keepdims=True)
    rounded = wide.astype(BF)
    parts = [
        jnp.einsum("hqk,khs->qhs", rounded, keys, preferred_element_type=F32),
        jnp.einsum("hqk,qhs->khs", rounded, queries, preferred_element_type=F32),
        jnp.einsum("hqk,qhs->khs", probs.astype(BF), grads, preferred_element_type=F32),
    ]
    parts = [part.astype(BF).reshape(total, groups, 1, heads * 64) for part in parts]
    table_grad = jnp.einsum("hqk,qkb->hb", wide, picked, precision=lax.Precision.HIGHEST)
    return (
        jnp.concatenate(parts, axis=2).reshape(total, -1),
        table_grad.reshape(groups * heads, 32, 1),
    )


def hop(value, axis):
    return lax.ppermute(value, axis, swap)


def pick(value, index, axis):
    return lax.dynamic_index_in_dim(value, index, axis, keepdims=False)


def paired(mine, other, axis, place=0):
    return jnp.where(
        lax.axis_index(axis) == 0,
        jnp.stack([mine, other], axis=place),
        jnp.stack([other, mine], axis=place),
    )


def after(value, *others):
    return lax.optimization_barrier((value, *others))[0]


def gather_plain(part, *beside):
    return lax.all_gather(part, ("x", "y"), axis=1, tiled=True), (), ()


def gather_tokens(part, *beside):
    half = part.shape[0] // 2
    low, high = part[:half], part[half:]
    low_x, high_y = hop(low, "x"), hop(high, "y")
    if beside:
        low_x, high_y = after(low_x, *beside), after(high_y, *beside)
    low_y, high_x = hop(low, "y"), hop(high, "x")
    low_xy, high_xy = hop(low_x, "y"), hop(high_y, "x")
    pieces = [low, low_y, low_x, low_xy, high, high_y, high_x, high_xy]
    return pieces, (low_x, high_y), (low_y, low_xy, high_x, high_xy)


def scatter_plain(parts, beside=(), beside_last=()):
    whole = parts[0].astype(F32)
    return lax.psum_scatter(whole, ("x", "y"), scatter_dimension=1, tiled=True), (), ()


def scatter_tokens(parts, beside=(), beside_last=()):
    low_out, low_keep, high_out, high_keep = parts
    low_in, high_in = hop(low_out, "x"), hop(high_out, "y")
    if beside:
        low_in, high_in = after(low_in, *beside), after(high_in, *beside)

    def add(keep, arrived, index):
        return keep[index].astype(F32) + arrived[index].astype(F32)

    low_last = hop(add(low_keep, low_in, 1).astype(BF), "y")
    high_last = hop(add(high_keep, high_in, 1).astype(BF), "x")
    if beside_last:
        low_last, high_last = after(low_last, *beside_last), after(high_last, *beside_last)
    low = add(low_keep, low_in, 0) + low_last.astype(F32)
    high = add(high_keep, high_in, 0) + high_last.astype(F32)
    return jnp.concatenate([low, high], axis=0), (low_in, high_in), (low_last, high_last)


def place_kernel(write, here_ref, *refs):
    pieces, outs = refs[:4], refs[4:]
    step = pl.program_id(0)
    for near in range(4):
        y = here_ref[0] if near < 2 else 1 - here_ref[0]
        c = here_ref[1] if near % 2 == 0 else 1 - here_ref[1]

        @pl.when(step == 2 * y + c)
        def _():
            write(pieces[near], outs)


def place(pieces, here, shapes, write):
    return pl.pallas_call(
        functools.partial(place_kernel, write),
        grid=(4,),
        in_specs=[pl.BlockSpec(memory_space=pltpu.SMEM)]
        + [pl.BlockSpec(piece.shape, lambda q: (0, 0)) for piece in pieces],
        out_specs=[
            pl.BlockSpec(shape, lambda q, rank=len(shape): (q,) + (0,) * (rank - 1)) for shape in shapes
        ],
        out_shape=[jax.ShapeDtypeStruct((4 * shape[0], *shape[1:]), F32) for shape in shapes],
        compiler_params=params(1),
        cost_estimate=cost(0, pieces[0].size),
        name="place",
    )(here, *pieces)


def share(part, *beside):
    over_y = hop(part, "y")
    if beside:
        over_y = after(over_y, *beside)
    return [part, hop(part, "c"), over_y, hop(over_y, "c")], over_y


def share_plain(part):
    return lax.all_gather(part, ("y", "c"), axis=0), part


def to_groups(halves, other, extra):
    count, _, t, width = halves.shape
    both = paired(pick(halves, lax.axis_index("y"), 1), other, "y").reshape(2 * count, t, width)
    if extra is not None:
        wide = jnp.broadcast_to(extra[None], (2 * count, *extra.shape))
        both = jnp.concatenate([both, wide], axis=1)
    return lax.all_to_all(both, "z", 0, 0, tiled=True)


def from_groups(mine):
    nz, t, width = mine.shape
    back = lax.all_to_all(mine, "z", 0, 0, tiled=True).reshape(2, nz // 2, t, width)
    leaving = pick(back, 1 - lax.axis_index("y"), 0)
    return (back, hop(leaving, "y")), leaving


def settle_kernel(y_ref, back_ref, other_ref, out_ref):
    j, y = pl.program_id(0), pl.program_id(1)

    @pl.when(y == y_ref[0])
    def _():
        out_ref[0, 0] = back_ref[y, j].astype(out_ref.dtype)

    @pl.when(y != y_ref[0])
    def _():
        out_ref[0, 0] = other_ref[j].astype(out_ref.dtype)


def settle(arrived, dtype):
    back, other = arrived
    _, count, t, width = back.shape
    y = lax.axis_index("y").astype(jnp.int32).reshape(1)
    out = pl.pallas_call(
        settle_kernel,
        grid=(count, 2),
        in_specs=[
            pl.BlockSpec(memory_space=pltpu.SMEM),
            pl.BlockSpec(back.shape, lambda j, y: (0, 0, 0, 0)),
            pl.BlockSpec(other.shape, lambda j, y: (0, 0, 0)),
        ],
        out_specs=pl.BlockSpec((1, 1, t, width), lambda j, y: (j, y, 0, 0)),
        out_shape=jax.ShapeDtypeStruct((count, 2, t, width), dtype),
        compiler_params=params(2),
        cost_estimate=cost(0, count * t * width),
        name="settle",
    )(y, back, other)
    return out.reshape(count, 2 * t, width)


def settle_plain(arrived, dtype):
    back, other = arrived
    _, count, t, width = back.shape
    both = paired(pick(back, lax.axis_index("y"), 0), other, "y")
    return both.transpose(1, 0, 2, 3).reshape(count, 2 * t, width).astype(dtype)


def sum_plane(value, nx, *earlier):
    value = value + after(hop(value, "c"), *earlier)
    value = value + hop(value, "x") if nx == 2 else lax.psum(value, "x")
    return value + hop(value, "y")


def sum_line(value, nz):
    step = 1
    while step < nz:
        value = value + lax.ppermute(value, "z", [(i, i ^ step) for i in range(nz)])
        step *= 2
    return value


def body(
    nx, nz, nc, inputs, lengths, attn_gain, ffn_gain, query_key, value_proj, out_proj, gate_up, down_proj, bias_table, cotangent
):
    x, y = lax.axis_index("x"), lax.axis_index("y")
    c, z = lax.axis_index("c"), lax.axis_index("z")
    width = inputs.shape[2]
    features = nz * width
    quarter = y * nc + c
    parts = 2 * nc
    buckets, mine = bias_table.shape
    count = inputs.shape[1] // 2

    stored_in = inputs.reshape(inputs.shape[0], 2, count, width)
    stored_cot = cotangent.reshape(stored_in.shape)
    small = jnp.concatenate(
        [attn_gain[None], ffn_gain[None], jnp.pad(bias_table.reshape(1, -1), ((0, 0), (0, width - buckets * mine)))]
    )
    small = jnp.pad(small, ((0, 5), (0, 0)))
    leaving = pick(stored_in, 1 - y, 1)

    query_key_rows = jnp.transpose(query_key, (1, 2, 3, 0))
    value_rows = jnp.transpose(value_proj, (1, 2, 0))
    gate_up_rows = jnp.transpose(gate_up, (1, 2, 3, 0))
    heads = value_rows.shape[0] // parts
    units = gate_up_rows.shape[0] // parts
    unit = gate_up_rows.shape[2]
    local_heads = nc * heads

    def own(rows, size):
        return lax.dynamic_slice_in_dim(rows, quarter * size, size, 0)

    def flat(rows):
        return rows.reshape(-1, width)

    def spread(rows):
        gathered = lax.all_gather(rows, ("z", "c"), axis=0, tiled=True)
        return gathered.reshape(nz, nc, rows.shape[0], width)

    own_pair = own(query_key_rows, heads)
    own_attn = [own_pair[:, 0], own_pair[:, 1], own(value_rows, heads), own(out_proj, heads)]
    own_attn = jnp.concatenate([flat(rows) for rows in own_attn])
    w_attn = spread(own_attn)
    other = after(hop(leaving, "y"), own_attn)
    own_pair = own(after(gate_up_rows, other), units)
    own_gate_up = jnp.concatenate([flat(own_pair[:, 0]), flat(own_pair[:, 1])])
    w_gate_up = spread(own_gate_up)
    own_down = flat(own(after(down_proj, other), units))
    w_down = spread(own_down)
    qkv_count, out_count = 3 * heads * 64, heads * 64

    arrived = after(to_groups(stored_in, other, small), own_gate_up, own_down)
    tokens = arrived[:, :count].astype(F32)
    small = arrived[:, count:]
    gain_one = small[:, :1].astype(F32)
    gain_two = small[:, 1:2].astype(F32)
    table = small[:, 2, : buckets * mine].reshape(nz, buckets, mine).transpose(0, 2, 1)
    table = table.reshape(-1, buckets).astype(F32)
    table = lax.dynamic_slice_in_dim(table, y * local_heads, local_heads, 0)

    both_lengths = jnp.stack([lengths, lax.ppermute(lengths, "y", swap)])
    both_lengths = jnp.where(y == 0, both_lengths, both_lengths[::-1]).reshape(-1)
    length = lax.dynamic_slice_in_dim(both_lengths, z, 1, 0)
    slots = (x * 2 + y) * count + jnp.arange(count, dtype=jnp.int32)
    live = (slots < length).astype(F32)[None, :, None]

    def scale_of(values):
        squares = jnp.sum(values * values, axis=(0, 2), keepdims=True)
        return lax.rsqrt(squares / features + norm_eps)

    def norm_back(values, scale, gain, grad):
        inner = jnp.sum(values * gain * grad, axis=(0, 2), keepdims=True)
        out = scale * gain * grad - values * (scale * scale * scale) * inner / features
        return out, jnp.sum(values * scale * grad, axis=1)

    def reduce(partial):
        rows = partial.reshape(nz * partial.shape[1], width)
        return lax.psum_scatter(rows, ("z", "c"), scatter_dimension=0, tiled=True)

    fits = nx == 2 and heads == 4 and count == 256 and units * unit % 640 == 0 and nz % 2 == 0
    if fits:
        forward, backward, gather, scatter = attend, attend_back, gather_tokens, scatter_tokens
        nt, nn, tn, ffn_one, ffn_two = mm_nt, mm_nn, mm_tn, ffn_in, ffn_back
        shared, stored_from = share, settle
    else:
        forward, backward, gather, scatter = attend_plain, attend_back_plain, gather_plain, scatter_plain
        nt, nn, tn, ffn_one, ffn_two = mm_nt_plain, mm_nn_plain, mm_tn_plain, ffn_in_plain, ffn_back_plain
        shared, stored_from = share_plain, settle_plain
    near_x, near_y = jnp.array([0, 0, 1, 1]) ^ x, jnp.array([0, 1, 0, 1]) ^ y
    starts = ((near_x * 2 + near_y) * count).astype(jnp.int32)

    def attend_back_all(grad, *last):
        if not fits:
            grads, table_grad = backward(projected, length, table, grad, lse, nc, heads)
            return (grads,), table_grad
        first = backward(0, projected, length, table, grad, lse[0])
        second = backward(1, after(projected, first[0], *last), length, table, grad, lse[1])
        return (first[0], second[0]), jnp.concatenate([first[1], second[1]])

    scale_one = scale_of(tokens)
    normed, _, _ = gather((tokens * scale_one * gain_one).astype(BF))
    cot_other = hop(pick(stored_cot, 1 - y, 1), "y")
    upstream = live * to_groups(stored_cot, after(cot_other, arrived), None).astype(F32)
    upstream_rounded = after(upstream.astype(BF), w_attn)
    projected = nt(normed, w_attn, 0, qkv_count, starts)
    if fits:
        first = forward(0, projected, length, table)
        grad_ffn, cot_first, cot_last = gather(upstream_rounded, first[0])
        second = forward(1, after(projected, first[0], *cot_first), length, table)
        attended, lse = (first[0], second[0]), (first[1], second[1])
    else:
        grad_ffn, _, cot_last = gather(upstream_rounded)
        attended, lse = forward(projected, length, table, nc, heads)
        attended = (attended,)
    heads_out = [after(attended[0], *cot_last), *attended[1:]]
    hidden = tokens + scatter(nn(heads_out, w_attn, qkv_count, out_count, starts))[0]
    scale_two = scale_of(hidden)
    normed_two, _, _ = gather((hidden * scale_two * gain_two).astype(BF))
    gate, up, activated = ffn_one(normed_two, w_gate_up, starts)

    down_partial = tn([activated], grad_ffn, starts)
    down_part = reduce(down_partial)
    grad_gate_up = ffn_two(grad_ffn, w_down, after(gate, down_partial), up, starts)
    two_parts = nn([grad_gate_up], w_gate_up, 0, 2 * units * unit, starts)
    grad_two, two_first, _ = scatter(two_parts)
    gate_up_partial = tn([after(grad_gate_up, two_parts[0])], normed_two, starts)
    gate_up_part = reduce(after(gate_up_partial, down_part, *two_first))
    branch_parts = nn([after(activated, gate_up_partial)], w_down, 0, units * unit, starts)
    through, ffn_gain_part = norm_back(hidden, scale_two, gain_two, grad_two)
    grad_hidden = upstream + through
    grad_branch, _, branch_here = gather(after(grad_hidden.astype(BF), branch_parts[0]))
    grad_attended = nt(grad_branch, w_attn, qkv_count, out_count, starts)
    out_partial = tn(attended, grad_branch, starts)
    branch_parts = [after(part, *branch_here) for part in branch_parts]
    branch, branch_first, branch_last = scatter(branch_parts)
    down_pieces, down_last = shared(after(down_part, *branch_here))
    grad_projected, table_part = attend_back_all(after(grad_attended, out_partial), *branch_first)
    out_part = reduce(after(out_partial, gate_up_part, grad_projected[0], *branch_first, down_last))
    outputs = (live * (hidden + branch)).astype(BF)
    outputs, _ = from_groups(outputs)
    qkv_partial = tn(grad_projected, normed, starts)
    gate_up_pieces, gate_up_last = shared(after(gate_up_part, grad_projected[0]))
    qkv_part = reduce(after(qkv_partial, out_part, *branch_last, gate_up_last))
    one_parts = nn(grad_projected, w_attn, 0, qkv_count, starts)
    grad_one, _, one_last = scatter(one_parts, (), (outputs[0],))
    through, attn_gain_part = norm_back(tokens, scale_one, gain_one, grad_one)
    input_grad, input_leaves = from_groups((grad_hidden + through).astype(BF))

    out_pieces, out_last = shared(out_part)

    table_part = jnp.sum(table_part, axis=2)
    every = jnp.zeros((nx * 2 * local_heads, table_part.shape[1]), F32)
    every = lax.dynamic_update_slice_in_dim(every, table_part, (x * 2 + y) * local_heads, 0)
    spare = -every.size % width
    every = jnp.pad(every.reshape(-1), (0, spare)).reshape(-1, width)
    sums = sum_plane(jnp.concatenate([attn_gain_part, ffn_gain_part, every]), nx, out_last, outputs[1])
    all_sums = sum_line(after(sums, input_leaves), nz)
    attn_gain_grad, ffn_gain_grad = all_sums[:nz], all_sums[nz : 2 * nz]
    every = all_sums[2 * nz :].reshape(-1)[: nx * 2 * local_heads * buckets].reshape(-1, buckets)

    outputs = stored_from(outputs, BF)
    if fits:
        here = jnp.stack([y, c]).astype(jnp.int32)

        def write_rows(source, outs):
            outs[0][...] = source[...].astype(F32)

        def write_qkv(source, outs):
            for h in range(heads):
                for i in range(3):
                    value = source[(i * heads + h) * 64 : (i * heads + h + 1) * 64, :].astype(F32)
                    if i == 2:
                        outs[1][h] = value
                    else:
                        outs[0][h, i] = value

        def write_gate_up(source, outs):
            for u in range(units):
                for i in range(2):
                    first = (i * units + u) * unit
                    outs[0][u, i] = source[first : first + unit, :].astype(F32)

        (down_all,) = place(down_pieces, here, [(units * unit, width)], write_rows)
        (out_all,) = place(out_pieces, here, [(heads * 64, width)], write_rows)
        (gate_up_all,) = place(gate_up_pieces, here, [(units, 2, unit, width)], write_gate_up)
        qkv_pieces, _ = shared(after(qkv_part, sums, *one_last), down_all, out_all, gate_up_all, outputs)
        query_key_all, value_all = place(
            qkv_pieces, here, [(heads, 2, 64, width), (heads, 64, width)], write_qkv
        )
    else:
        down_all, out_all = down_pieces.astype(F32), out_pieces.astype(F32)
        gate_up_all = gate_up_pieces.astype(F32).reshape(parts, 2, units, unit, width)
        gate_up_all = gate_up_all.transpose(0, 2, 1, 3, 4).reshape(-1, 2, unit, width)
        qkv_all = shared(qkv_part)[0].astype(F32).reshape(parts, 3, heads, 64, width)
        qkv_all = qkv_all.transpose(0, 2, 1, 3, 4).reshape(-1, 3, 64, width)
        query_key_all, value_all = qkv_all[:, :2], qkv_all[:, 2]
    input_grad = stored_from(input_grad, F32)
    down_all, out_all = down_all.reshape(down_proj.shape), out_all.reshape(out_proj.shape)

    table_grad = lax.dynamic_slice_in_dim(every, (x * nz + z) * mine, mine, 0).T
    return (
        outputs,
        input_grad,
        pick(attn_gain_grad, z, 0),
        pick(ffn_gain_grad, z, 0),
        query_key_all.transpose(3, 0, 1, 2),
        value_all.transpose(2, 0, 1),
        out_all,
        gate_up_all.transpose(3, 0, 1, 2),
        down_all,
        table_grad,
    )


def solution(mesh):
    dp, nx, nz = (mesh.shape[name] for name in ("dp", "gx", "gy"))
    nc = dp // 2
    split = Mesh(mesh.devices.reshape(2, nc, nx, nz), ("y", "c", "x", "z"))
    seq = ("y", "c")
    return jax.shard_map(
        functools.partial(body, nx, nz, nc),
        mesh=split,
        in_specs=(
            P(seq, "x", "z"),
            P(seq),
            P("z"),
            P("z"),
            P("z", "x", None, None),
            P("z", "x", None),
            P("x", None, "z"),
            P("z", "x", None, None),
            P("x", None, "z"),
            P(None, ("x", "z")),
            P(seq, "x", "z"),
        ),
        out_specs=(
            P(seq, "x", "z"),
            P(seq, "x", "z"),
            P("z"),
            P("z"),
            P("z", "x", None, None),
            P("z", "x", None),
            P("x", None, "z"),
            P("z", "x", None, None),
            P("x", None, "z"),
            P(None, ("x", "z")),
        ),
        check_vma=False,
    )
```

```python
import functools
import math

import jax
import jax.numpy as jnp
from jax import lax
from jax.experimental import pallas as pl
from jax.experimental.pallas import tpu as pltpu
from jax.sharding import Mesh
from jax.sharding import PartitionSpec as P

norm_eps = 1e-06
masked_score = -1e30
bucket_edges = (12, 16, 23, 32, 46, 64, 91)
BF = jnp.bfloat16
F32 = jnp.float32
LB = 128
VMEM = 60 * 1024 * 1024
swap = [(0, 1), (1, 0)]
gelu_a = math.sqrt(2.0 / math.pi)
gelu_b = 0.044715


def bucket_index(offset):
    magnitude = jnp.abs(offset)
    far_bucket = 8 + sum(((magnitude >= boundary).astype(jnp.int32) for boundary in bucket_edges))
    near_bucket = jnp.where(magnitude < 8, magnitude, far_bucket)
    return near_bucket + 16 * (offset > 0).astype(jnp.int32)


def cost(flops, moved):
    return pl.CostEstimate(flops=int(flops) // 16, bytes_accessed=int(moved) // 16, transcendentals=0)


def params(steps):
    return pltpu.CompilerParams(
        dimension_semantics=("arbitrary",) * steps, vmem_limit_bytes=VMEM
    )


def dot_nt(a, b):
    return lax.dot_general(a, b, (((1,), (1,)), ((), ())), preferred_element_type=F32)


def dot_nn(a, b):
    return lax.dot_general(a, b, (((1,), (0,)), ((), ())), preferred_element_type=F32)


def spot_of(starts_ref, d, count):
    return pl.ds(pl.multiple_of(starts_ref[d], 256), count)


def piece_specs(pieces):
    shape = pieces[0].shape
    return [pl.BlockSpec(shape, lambda *_: (0, 0, 0)) for _ in pieces]


def nt_sum(piece_refs, d, w_of):
    half = piece_refs[0].shape[0]
    acc = None
    for z in range(2 * half):
        part = dot_nt(piece_refs[4 * (z // half) + d][z % half], w_of(z))
        acc = part if acc is None else acc + part
    return acc


def nt_kernel(starts_ref, *refs):
    pieces, (w_ref, out_ref) = refs[:8], refs[8:]
    for d in range(4):
        acc = nt_sum(pieces, d, lambda z: w_ref[z, 0])
        out_ref[spot_of(starts_ref, d, acc.shape[0]), :] = acc.astype(BF)


def mm_nt(pieces, w, first, rows, starts):
    nz, nc, _, width = w.shape
    total = 4 * pieces[0].shape[1]
    count, skip = rows // 256, first // 256
    return pl.pallas_call(
        nt_kernel,
        grid=(nc, count),
        in_specs=[pl.BlockSpec(memory_space=pltpu.SMEM)]
        + piece_specs(pieces)
        + [pl.BlockSpec((nz, 1, 256, width), lambda c, i: (0, c, skip + i, 0))],
        out_specs=pl.BlockSpec((total, 256), lambda c, i: (0, c * count + i)),
        out_shape=jax.ShapeDtypeStruct((total, nc * rows), BF),
        compiler_params=params(2),
        cost_estimate=cost(
            2 * nz * total * width * nc * rows, 2 * nz * width * (total + nc * rows) + 2 * total * nc * rows
        ),
        name="product_nt",
    )(starts, *pieces, w)


def nn_kernel(count, starts_ref, *refs):
    grads, (w_ref, low_out, low_keep, high_out, high_keep) = refs[:count], refs[count:]
    nc, rows, width = w_ref.shape[1:]
    t = grads[0].shape[0] // 4
    in_low = pl.program_id(0) < pl.num_programs(0) // 2

    def product(d):
        spot = spot_of(starts_ref, d, t)
        if count == 1:
            return dot_nn(grads[0][spot, :], w_ref[0].reshape(nc * rows, width)).astype(BF)
        return sum(dot_nn(grads[c][spot, :], w_ref[0, c]) for c in range(count)).astype(BF)

    @pl.when(in_low)
    def _():
        for d in range(4):
            (low_out if d // 2 else low_keep)[d % 2, 0] = product(d)

    @pl.when(jnp.logical_not(in_low))
    def _():
        for d in range(4):
            (high_out if d % 2 else high_keep)[d // 2, 0] = product(d)


def mm_nn(grads, w, first, rows, starts):
    total = grads[0].shape[0]
    nz, nc, _, width = w.shape
    skip, half, t = first // rows, nz // 2, total // 4
    low = pl.BlockSpec((2, 1, t, width), lambda z: (0, jnp.minimum(z, half - 1), 0, 0))
    high = pl.BlockSpec((2, 1, t, width), lambda z: (0, jnp.maximum(z - half, 0), 0, 0))
    return pl.pallas_call(
        functools.partial(nn_kernel, len(grads)),
        grid=(nz,),
        in_specs=[pl.BlockSpec(memory_space=pltpu.SMEM)]
        + [pl.BlockSpec(grad.shape, lambda z: (0, 0)) for grad in grads]
        + [pl.BlockSpec((1, nc, rows, width), lambda z: (z, 0, skip, 0))],
        out_specs=[low, low, high, high],
        out_shape=[jax.ShapeDtypeStruct((2, half, t, width), BF)] * 4,
        compiler_params=params(1),
        cost_estimate=cost(
            2 * nz * total * width * nc * rows, 2 * nz * width * (total + nc * rows) + 2 * total * nc * rows
        ),
        name="product_nn",
    )(starts, *grads, w)


def tn_kernel(count, starts_ref, *refs):
    grads, pieces, out_ref = refs[:count], refs[count:-1], refs[-1]
    half, t, _ = pieces[0].shape

    def one(grad_ref):
        turned = [grad_ref[spot_of(starts_ref, d, t), :].T for d in range(4)]
        for z in range(2 * half):
            acc = dot_nn(turned[0], pieces[4 * (z // half)][z % half])
            for d in range(1, 4):
                acc += dot_nn(turned[d], pieces[4 * (z // half) + d][z % half])
            out_ref[z] = acc.astype(BF)

    if count == 1:
        one(grads[0])
    else:
        for c in range(count):

            @pl.when(pl.program_id(0) // (pl.num_programs(0) // count) == c)
            def _():
                one(grads[c])


def mm_tn(grads, pieces, starts):
    total, rows = grads[0].shape
    half, _, width = pieces[0].shape
    nz, count = 2 * half, len(grads)
    block = next(b for b in (640, 384, 256) if rows % b == 0)
    steps = rows // block

    def spec(c):
        return pl.BlockSpec((total, block), lambda i: (0, jnp.clip(i - c * steps, 0, steps - 1)))

    return pl.pallas_call(
        functools.partial(tn_kernel, count),
        grid=(count * steps,),
        in_specs=[pl.BlockSpec(memory_space=pltpu.SMEM)]
        + [spec(c) for c in range(count)]
        + piece_specs(pieces),
        out_specs=pl.BlockSpec((nz, block, width), lambda i: (0, i, 0)),
        out_shape=jax.ShapeDtypeStruct((nz, count * rows, width), BF),
        compiler_params=params(1),
        cost_estimate=cost(
            2 * nz * total * width * count * rows, 2 * nz * width * (total + count * rows) + 2 * total * count * rows
        ),
        name="product_tn",
    )(starts, *grads, *pieces)


def gelu_parts(gate):
    curve = jnp.tanh(gelu_a * (gate + gelu_b * gate * gate * gate))
    value = 0.5 * gate * (1.0 + curve)
    slope = 0.5 * (1.0 + curve) + 0.5 * gate * (1.0 - curve * curve) * gelu_a * (
        1.0 + 3.0 * gelu_b * gate * gate
    )
    return value, slope


def ffn_in_kernel(starts_ref, *refs):
    pieces, (w_ref, gate_ref, up_ref, active_ref) = refs[:8], refs[8:]
    _, _, _, block, width = w_ref.shape
    for d in range(4):
        acc = nt_sum(pieces, d, lambda z: w_ref[z, 0].reshape(2 * block, width))
        spot = spot_of(starts_ref, d, acc.shape[0])
        gate, up = acc[:, :block], acc[:, block:]
        value = 0.5 * gate * (1.0 + jnp.tanh(gelu_a * (gate + gelu_b * gate * gate * gate)))
        gate_ref[spot, :] = gate.astype(BF)
        up_ref[spot, :] = up.astype(BF)
        active_ref[spot, :] = (value * up).astype(BF)


def ffn_in(pieces, w, starts):
    nz, nc, rows, width = w.shape
    half, total = rows // 2, 4 * pieces[0].shape[1]
    count = half // 128
    block = pl.BlockSpec((total, 128), lambda c, i: (0, c * count + i))
    return pl.pallas_call(
        ffn_in_kernel,
        grid=(nc, count),
        in_specs=[pl.BlockSpec(memory_space=pltpu.SMEM)]
        + piece_specs(pieces)
        + [pl.BlockSpec((nz, 1, 2, 128, width), lambda c, i: (0, c, 0, i, 0))],
        out_specs=[block, block, block],
        out_shape=[jax.ShapeDtypeStruct((total, nc * half), BF)] * 3,
        compiler_params=params(2),
        cost_estimate=cost(
            2 * nz * total * width * nc * rows, 2 * nz * width * (total + nc * rows) + 3 * total * nc * rows
        ),
        name="ffn_in",
    )(starts, *pieces, w.reshape(nz, nc, 2, half, width))


def ffn_back_kernel(starts_ref, *refs):
    pieces, (w_ref, gate_ref, up_ref, out_ref) = refs[:8], refs[8:]
    half = w_ref.shape[2]
    for d in range(4):
        acc = nt_sum(pieces, d, lambda z: w_ref[z, 0])
        spot = spot_of(starts_ref, d, acc.shape[0])
        value, slope = gelu_parts(gate_ref[spot, :].astype(F32))
        out_ref[spot, :half] = (acc * up_ref[spot, :].astype(F32) * slope).astype(BF)
        out_ref[spot, half:] = (acc * value).astype(BF)


def ffn_back(pieces, w, gate, up, starts):
    nz, nc, half, width = w.shape
    total = gate.shape[0]
    kept = pl.BlockSpec((total, half), lambda c: (0, c))
    return pl.pallas_call(
        ffn_back_kernel,
        grid=(nc,),
        in_specs=[pl.BlockSpec(memory_space=pltpu.SMEM)]
        + piece_specs(pieces)
        + [pl.BlockSpec((nz, 1, half, width), lambda c: (0, c, 0, 0)), kept, kept],
        out_specs=pl.BlockSpec((total, 2 * half), lambda c: (0, c)),
        out_shape=jax.ShapeDtypeStruct((total, nc * 2 * half), BF),
        compiler_params=params(1),
        cost_estimate=cost(
            2 * nz * total * width * nc * half, 2 * nz * width * (total + nc * half) + 8 * total * nc * half
        ),
        name="ffn_back",
    )(starts, *pieces, w, gate, up)


def mm_nt_plain(act, w, first, rows, starts):
    part = lax.slice_in_dim(w, first, first + rows, axis=2)
    out = jnp.einsum("ztf,zcrf->tcr", act, part, preferred_element_type=F32)
    return out.astype(BF).reshape(act.shape[1], -1)


def mm_nn_plain(grads, w, first, rows, starts):
    grad = grads[0]
    part = lax.slice_in_dim(w, first, first + rows, axis=2)
    split = grad.reshape(grad.shape[0], w.shape[1], rows)
    out = jnp.einsum("tcr,zcrf->ztf", split, part, preferred_element_type=F32)
    return [out.astype(BF)]


def mm_tn_plain(grads, act, starts):
    return jnp.einsum("tr,ztf->zrf", grads[0], act, preferred_element_type=F32).astype(BF)


def ffn_in_plain(act, w, starts):
    _, nc, rows, _ = w.shape
    total = act.shape[1]
    both = jnp.einsum("ztf,zcrf->tcr", act, w, preferred_element_type=F32)
    gate, up = both[:, :, : rows // 2], both[:, :, rows // 2 :]
    value, _ = gelu_parts(gate)
    return [part.astype(BF).reshape(total, -1) for part in (gate, up, value * up)]


def ffn_back_plain(act, w, gate, up, starts):
    total, nc = gate.shape[0], w.shape[1]
    grad = jnp.einsum("ztf,zcrf->tcr", act, w, preferred_element_type=F32)
    value, slope = gelu_parts(gate.astype(F32).reshape(grad.shape))
    both = [grad * up.astype(F32).reshape(grad.shape) * slope, grad * value]
    return jnp.concatenate(both, axis=2).astype(BF).reshape(total, -1)


def near_buckets(tile, total):
    first = (total // LB - 2 + tile) * LB
    rows = lax.broadcasted_iota(jnp.int32, (LB, LB), 0)
    lanes = lax.broadcasted_iota(jnp.int32, (LB, LB), 1)
    return bucket_index(first + rows - (total - LB) - lanes)


def build_strips(table_ref, strip_ref, total, group):
    heads = strip_ref.shape[0]
    near = (total // LB - 2) * LB
    for h in range(heads):
        head = group * heads + h
        strip_ref[h, :near] = jnp.full((near, LB), table_ref[head, 15], F32)
        strip_ref[h, near + 3 * LB :] = jnp.full((near, LB), table_ref[head, 31], F32)

    def one_tile(tile, _):
        index = near_buckets(tile, total)
        vals = [jnp.full((LB, LB), table_ref[group * heads + h, 0], F32) for h in range(heads)]
        for b in range(1, 32):
            hit = index == b
            vals = [
                jnp.where(hit, table_ref[group * heads + h, b], vals[h]) for h in range(heads)
            ]
        for h in range(heads):
            strip_ref[h, pl.ds(pl.multiple_of(near + tile * LB, LB), LB)] = vals[h]
        return 0

    lax.fori_loop(0, 3, one_tile, 0)


def head_lanes(shape, h):
    lanes = lax.broadcasted_iota(jnp.int32, shape, 1)
    return lanes // 64 == h, lanes == ((h + 1) % 4) * 64


def mask_keys(keys, length, h):
    own, spare = head_lanes(keys.shape, h)
    dead = lax.broadcasted_iota(jnp.int32, keys.shape, 0) >= length
    mask = jnp.where(jnp.logical_and(spare, dead), masked_score, 0.0)
    return jnp.where(own, keys.astype(F32), mask).astype(BF)


def with_one(queries, h):
    _, spare = head_lanes(queries.shape, h)
    return jnp.where(spare, 1.0, queries.astype(F32)).astype(BF)


def own_lanes(values, h):
    own, _ = head_lanes(values.shape, h)
    return jnp.where(own, values.astype(F32), 0.0).astype(BF)


def block_bias(strip_ref, h, block, total):
    first = total - LB - 2 * block * LB
    left = strip_ref[h, pl.ds(pl.multiple_of(first, LB), total)]
    right = strip_ref[h, pl.ds(pl.multiple_of(first - LB, LB), total)]
    return jnp.concatenate([left, right], axis=1)


def attend_kernel(group, length_ref, table_ref, q_ref, k_ref, v_ref, out_ref, lse_ref, strip, heads_k, turned_v, turned_out):
    total = q_ref.shape[0]
    heads = strip.shape[0]
    build_strips(table_ref, strip, total, group)
    turned_v[...] = v_ref[...].astype(F32).T.astype(BF)
    for h in range(heads):
        heads_k[h] = mask_keys(k_ref[...], length_ref[0], h)

    def one_block(block, _):
        spot = pl.ds(pl.multiple_of(block * 256, 256), 256)
        queries = q_ref[spot]
        for h in range(heads):
            scores = dot_nt(heads_k[h], with_one(queries, h)) + block_bias(strip, h, block, total)
            largest = jnp.max(scores, axis=0, keepdims=True)
            raised = jnp.exp(scores - largest)
            totals = jnp.sum(raised, axis=0, keepdims=True)
            out = dot_nn(turned_v[h * 64 : (h + 1) * 64], raised.astype(BF))
            turned_out[h * 64 : (h + 1) * 64, spot] = out * (1.0 / totals)
            lse_ref[h : h + 1, spot] = largest + jnp.log(totals)
        return 0

    lax.fori_loop(0, total // 256, one_block, 0)
    out_ref[...] = turned_out[...].T.astype(BF)


def attend_back_kernel(
    group, length_ref, table_ref, q_ref, k_ref, v_ref, grad_ref, lse_ref, out_ref, table_grad_ref,
    strip, strip_grad, heads_k, turned_k, turned_q, ds_ref, p_ref, dk_ref, dv_ref,
):
    total = q_ref.shape[0]
    heads = strip.shape[0]
    build_strips(table_ref, strip, total, group)
    strip_grad[...] = jnp.zeros_like(strip_grad)
    dk_ref[...] = jnp.zeros_like(dk_ref)
    dv_ref[...] = jnp.zeros_like(dv_ref)
    turned_k[...] = k_ref[...].astype(F32).T.astype(BF)
    for h in range(heads):
        heads_k[h] = mask_keys(k_ref[...], length_ref[0], h)

    def one_block(block, _):
        spot = pl.ds(pl.multiple_of(block * 256, 256), 256)
        queries, grads = q_ref[spot], grad_ref[spot]
        own_q, own_g = [], []
        for h in range(heads):
            own_q.append(own_lanes(queries, h))
            own_g.append(own_lanes(grads, h))
            scores = dot_nt(heads_k[h], with_one(queries, h)) + block_bias(strip, h, block, total)
            probs = jnp.exp(scores - lse_ref[h : h + 1, spot])
            weighed = probs * dot_nt(v_ref[...], own_g[h])
            delta = jnp.sum(weighed, axis=0, keepdims=True)
            grad_scores = weighed - probs * delta
            first = total - LB - 2 * block * LB
            left = pl.ds(pl.multiple_of(first, LB), total)
            right = pl.ds(pl.multiple_of(first - LB, LB), total)
            strip_grad[h, left] += grad_scores[:, :LB]
            strip_grad[h, right] += grad_scores[:, LB:]
            rounded = grad_scores.astype(BF)
            ds_ref[:, h * 256 : (h + 1) * 256] = rounded
            p_ref[:, h * 256 : (h + 1) * 256] = probs.astype(BF)
            turned_q[h * 64 : (h + 1) * 64, spot] = dot_nn(turned_k[h * 64 : (h + 1) * 64], rounded)
        dk_ref[...] += dot_nn(ds_ref[...], jnp.concatenate(own_q, axis=0))
        dv_ref[...] += dot_nn(p_ref[...], jnp.concatenate(own_g, axis=0))
        return 0

    lax.fori_loop(0, total // 256, one_block, 0)
    out_ref[:, :256] = turned_q[...].T.astype(BF)
    out_ref[:, 256:512] = dk_ref[...].astype(BF)
    out_ref[:, 512:] = dv_ref[...].astype(BF)

    near = (total // LB - 2) * LB
    for h in range(heads):
        table_grad_ref[h] = jnp.zeros((32, LB), F32)
        table_grad_ref[h, 15:16] = jnp.sum(strip_grad[h, :near], axis=0, keepdims=True)
        table_grad_ref[h, 31:32] = jnp.sum(strip_grad[h, near + 3 * LB :], axis=0, keepdims=True)

    def one_tile(tile, _):
        index = near_buckets(tile, total)
        spot = pl.ds(pl.multiple_of(near + tile * LB, LB), LB)
        for h in range(heads):
            grads = strip_grad[h, spot]
            for b in range(32):
                picked = jnp.where(index == b, grads, 0.0)
                table_grad_ref[h, b : b + 1] += jnp.sum(picked, axis=0, keepdims=True)
        return 0

    lax.fori_loop(0, 3, one_tile, 0)


def block_specs(total, group):
    def spec(i):
        return pl.BlockSpec((total, 256), lambda _: (0, 3 * group + i))

    smem = pl.BlockSpec(memory_space=pltpu.SMEM)
    return [smem, smem, spec(0), spec(1), spec(2)]


def attend(group, projected, length, table):
    total = projected.shape[0]
    heads = 4
    return pl.pallas_call(
        functools.partial(attend_kernel, group),
        grid=(1,),
        in_specs=block_specs(total, group),
        out_specs=[
            pl.BlockSpec((total, 256), lambda _: (0, 0)),
            pl.BlockSpec((8, total), lambda _: (0, 0)),
        ],
        out_shape=[
            jax.ShapeDtypeStruct((total, 256), BF),
            jax.ShapeDtypeStruct((8, total), F32),
        ],
        scratch_shapes=[
            pltpu.VMEM((heads, 2 * total - LB, LB), F32),
            pltpu.VMEM((heads, total, 256), BF),
            pltpu.VMEM((256, total), BF),
            pltpu.VMEM((256, total), F32),
        ],
        compiler_params=params(1),
        cost_estimate=cost(heads * total * total * 2 * 256 * 2, 4 * total * 256 * 2),
        name="attend",
    )(length, table, projected, projected, projected)


def attend_back(group, projected, length, table, grad_out, lse):
    total = projected.shape[0]
    heads = 4
    return pl.pallas_call(
        functools.partial(attend_back_kernel, group),
        grid=(1,),
        in_specs=block_specs(total, group)
        + [
            pl.BlockSpec((total, 256), lambda _: (0, group)),
            pl.BlockSpec((8, total), lambda _: (0, 0)),
        ],
        out_specs=[
            pl.BlockSpec((total, 768), lambda _: (0, 0)),
            pl.BlockSpec((heads, 32, LB), lambda _: (0, 0, 0)),
        ],
        out_shape=[
            jax.ShapeDtypeStruct((total, 768), BF),
            jax.ShapeDtypeStruct((heads, 32, LB), F32),
        ],
        scratch_shapes=[
            pltpu.VMEM((heads, 2 * total - LB, LB), F32),
            pltpu.VMEM((heads, 2 * total - LB, LB), F32),
            pltpu.VMEM((heads, total, 256), BF),
            pltpu.VMEM((256, total), BF),
            pltpu.VMEM((256, total), F32),
            pltpu.VMEM((total, heads * 256), BF),
            pltpu.VMEM((total, heads * 256), BF),
            pltpu.VMEM((total, 256), F32),
            pltpu.VMEM((total, 256), F32),
        ],
        compiler_params=params(1),
        cost_estimate=cost(heads * total * total * 2 * 256 * 5, 8 * total * 256 * 2),
        name="attend_back",
    )(length, table, projected, projected, projected, grad_out, lse)


def split_heads(projected, groups, heads):
    parts = projected.reshape(projected.shape[0], groups, 3, heads, 64)
    return [parts[:, :, i].reshape(projected.shape[0], groups * heads, 64) for i in range(3)]


def plain_scores(queries, keys, length, table):
    slots = jnp.arange(keys.shape[0], dtype=jnp.int32)
    picked = (bucket_index(slots[None, :] - slots[:, None])[:, :, None] == jnp.arange(32)).astype(F32)
    bias = jnp.einsum("qkb,hb->hqk", picked, table, precision=lax.Precision.HIGHEST)
    scores = jnp.einsum("qhs,khs->hqk", queries, keys, preferred_element_type=F32) + bias
    return jnp.where(slots < length[0], scores, masked_score), picked


def attend_plain(projected, length, table, groups, heads):
    queries, keys, values = split_heads(projected, groups, heads)
    scores, _ = plain_scores(queries, keys, length, table)
    lse = jax.nn.logsumexp(scores, axis=2)
    probs = jnp.exp(scores - lse[:, :, None]).astype(BF)
    out = jnp.einsum("hqk,khs->qhs", probs, values, preferred_element_type=F32)
    return out.astype(BF).reshape(projected.shape[0], -1), lse


def attend_back_plain(projected, length, table, grad_out, lse, groups, heads):
    total = projected.shape[0]
    queries, keys, values = split_heads(projected, groups, heads)
    grads = grad_out.reshape(queries.shape)
    scores, picked = plain_scores(queries, keys, length, table)
    probs = jnp.exp(scores - lse[:, :, None])
    weighed = probs * jnp.einsum("qhs,khs->hqk", grads, values, preferred_element_type=F32)
    wide = weighed - probs * jnp.sum(weighed, axis=2, keepdims=True)
    rounded = wide.astype(BF)
    parts = [
        jnp.einsum("hqk,khs->qhs", rounded, keys, preferred_element_type=F32),
        jnp.einsum("hqk,qhs->khs", rounded, queries, preferred_element_type=F32),
        jnp.einsum("hqk,qhs->khs", probs.astype(BF), grads, preferred_element_type=F32),
    ]
    parts = [part.astype(BF).reshape(total, groups, 1, heads * 64) for part in parts]
    table_grad = jnp.einsum("hqk,qkb->hb", wide, picked, precision=lax.Precision.HIGHEST)
    return (
        jnp.concatenate(parts, axis=2).reshape(total, -1),
        table_grad.reshape(groups * heads, 32, 1),
    )


def hop(value, axis):
    return lax.ppermute(value, axis, swap)


def pick(value, index, axis):
    return lax.dynamic_index_in_dim(value, index, axis, keepdims=False)


def paired(mine, other, axis, place=0):
    return jnp.where(
        lax.axis_index(axis) == 0,
        jnp.stack([mine, other], axis=place),
        jnp.stack([other, mine], axis=place),
    )


def after(value, *others):
    return lax.optimization_barrier((value, *others))[0]


def gather_plain(part, *beside):
    return lax.all_gather(part, ("x", "y"), axis=1, tiled=True), (), ()


def gather_tokens(part, *beside):
    half = part.shape[0] // 2
    low, high = part[:half], part[half:]
    low_x, high_y = hop(low, "x"), hop(high, "y")
    if beside:
        low_x, high_y = after(low_x, *beside), after(high_y, *beside)
    low_y, high_x = hop(low, "y"), hop(high, "x")
    low_xy, high_xy = hop(low_x, "y"), hop(high_y, "x")
    pieces = [low, low_y, low_x, low_xy, high, high_y, high_x, high_xy]
    return pieces, (low_x, high_y), (low_y, low_xy, high_x, high_xy)


def scatter_plain(parts, beside=(), beside_last=()):
    whole = parts[0].astype(F32)
    return lax.psum_scatter(whole, ("x", "y"), scatter_dimension=1, tiled=True), (), ()


def scatter_tokens(parts, beside=(), beside_last=()):
    low_out, low_keep, high_out, high_keep = parts
    low_in, high_in = hop(low_out, "x"), hop(high_out, "y")
    if beside:
        low_in, high_in = after(low_in, *beside), after(high_in, *beside)

    def add(keep, arrived, index):
        return keep[index].astype(F32) + arrived[index].astype(F32)

    low_last = hop(add(low_keep, low_in, 1).astype(BF), "y")
    high_last = hop(add(high_keep, high_in, 1).astype(BF), "x")
    if beside_last:
        low_last, high_last = after(low_last, *beside_last), after(high_last, *beside_last)
    low = add(low_keep, low_in, 0) + low_last.astype(F32)
    high = add(high_keep, high_in, 0) + high_last.astype(F32)
    return jnp.concatenate([low, high], axis=0), (low_in, high_in), (low_last, high_last)


def place_kernel(write, here_ref, *refs):
    pieces, outs = refs[:4], refs[4:]
    step = pl.program_id(0)
    for near in range(4):
        y = here_ref[0] if near < 2 else 1 - here_ref[0]
        c = here_ref[1] if near % 2 == 0 else 1 - here_ref[1]

        @pl.when(step == 2 * y + c)
        def _():
            write(pieces[near], outs)


def place(pieces, here, shapes, write):
    return pl.pallas_call(
        functools.partial(place_kernel, write),
        grid=(4,),
        in_specs=[pl.BlockSpec(memory_space=pltpu.SMEM)]
        + [pl.BlockSpec(piece.shape, lambda q: (0, 0)) for piece in pieces],
        out_specs=[
            pl.BlockSpec(shape, lambda q, rank=len(shape): (q,) + (0,) * (rank - 1)) for shape in shapes
        ],
        out_shape=[jax.ShapeDtypeStruct((4 * shape[0], *shape[1:]), F32) for shape in shapes],
        compiler_params=params(1),
        cost_estimate=cost(0, pieces[0].size),
        name="place",
    )(here, *pieces)


def share(part, *beside):
    over_y = hop(part, "y")
    if beside:
        over_y = after(over_y, *beside)
    return [part, hop(part, "c"), over_y, hop(over_y, "c")], over_y


def share_plain(part):
    return lax.all_gather(part, ("y", "c"), axis=0), part


def to_groups(halves, other, extra):
    count, _, t, width = halves.shape
    both = paired(pick(halves, lax.axis_index("y"), 1), other, "y").reshape(2 * count, t, width)
    if extra is not None:
        wide = jnp.broadcast_to(extra[None], (2 * count, *extra.shape))
        both = jnp.concatenate([both, wide], axis=1)
    return lax.all_to_all(both, "z", 0, 0, tiled=True)


def from_groups(mine):
    nz, t, width = mine.shape
    back = lax.all_to_all(mine, "z", 0, 0, tiled=True).reshape(2, nz // 2, t, width)
    leaving = pick(back, 1 - lax.axis_index("y"), 0)
    return (back, hop(leaving, "y")), leaving


def settle_kernel(y_ref, back_ref, other_ref, out_ref):
    j, y = pl.program_id(0), pl.program_id(1)

    @pl.when(y == y_ref[0])
    def _():
        out_ref[0, 0] = back_ref[y, j].astype(out_ref.dtype)

    @pl.when(y != y_ref[0])
    def _():
        out_ref[0, 0] = other_ref[j].astype(out_ref.dtype)


def settle(arrived, dtype):
    back, other = arrived
    _, count, t, width = back.shape
    y = lax.axis_index("y").astype(jnp.int32).reshape(1)
    out = pl.pallas_call(
        settle_kernel,
        grid=(count, 2),
        in_specs=[
            pl.BlockSpec(memory_space=pltpu.SMEM),
            pl.BlockSpec(back.shape, lambda j, y: (0, 0, 0, 0)),
            pl.BlockSpec(other.shape, lambda j, y: (0, 0, 0)),
        ],
        out_specs=pl.BlockSpec((1, 1, t, width), lambda j, y: (j, y, 0, 0)),
        out_shape=jax.ShapeDtypeStruct((count, 2, t, width), dtype),
        compiler_params=params(2),
        cost_estimate=cost(0, count * t * width),
        name="settle",
    )(y, back, other)
    return out.reshape(count, 2 * t, width)


def settle_plain(arrived, dtype):
    back, other = arrived
    _, count, t, width = back.shape
    both = paired(pick(back, lax.axis_index("y"), 0), other, "y")
    return both.transpose(1, 0, 2, 3).reshape(count, 2 * t, width).astype(dtype)


def sum_plane(value, nx, *earlier):
    value = value + after(hop(value, "c"), *earlier)
    value = value + hop(value, "x") if nx == 2 else lax.psum(value, "x")
    return value + hop(value, "y")


def sum_line(value, nz):
    step = 1
    while step < nz:
        value = value + lax.ppermute(value, "z", [(i, i ^ step) for i in range(nz)])
        step *= 2
    return value


def body(
    nx, nz, nc, inputs, lengths, attn_gain, ffn_gain, query_key, value_proj, out_proj, gate_up, down_proj, bias_table, cotangent
):
    x, y = lax.axis_index("x"), lax.axis_index("y")
    c, z = lax.axis_index("c"), lax.axis_index("z")
    width = inputs.shape[2]
    features = nz * width
    quarter = y * nc + c
    parts = 2 * nc
    buckets, mine = bias_table.shape
    count = inputs.shape[1] // 2

    stored_in = inputs.reshape(inputs.shape[0], 2, count, width)
    stored_cot = cotangent.reshape(stored_in.shape)
    small = jnp.concatenate(
        [attn_gain[None], ffn_gain[None], jnp.pad(bias_table.reshape(1, -1), ((0, 0), (0, width - buckets * mine)))]
    )
    small = jnp.pad(small, ((0, 5), (0, 0)))
    leaving = pick(stored_in, 1 - y, 1)

    query_key_rows = jnp.transpose(query_key, (1, 2, 3, 0))
    value_rows = jnp.transpose(value_proj, (1, 2, 0))
    gate_up_rows = jnp.transpose(gate_up, (1, 2, 3, 0))
    heads = value_rows.shape[0] // parts
    units = gate_up_rows.shape[0] // parts
    unit = gate_up_rows.shape[2]
    local_heads = nc * heads

    def own(rows, size):
        return lax.dynamic_slice_in_dim(rows, quarter * size, size, 0)

    def flat(rows):
        return rows.reshape(-1, width)

    def spread(rows):
        gathered = lax.all_gather(rows, ("z", "c"), axis=0, tiled=True)
        return gathered.reshape(nz, nc, rows.shape[0], width)

    own_pair = own(query_key_rows, heads)
    own_attn = [own_pair[:, 0], own_pair[:, 1], own(value_rows, heads), own(out_proj, heads)]
    own_attn = jnp.concatenate([flat(rows) for rows in own_attn])
    w_attn = spread(own_attn)
    other = after(hop(leaving, "y"), own_attn)
    own_pair = own(after(gate_up_rows, other), units)
    own_gate_up = jnp.concatenate([flat(own_pair[:, 0]), flat(own_pair[:, 1])])
    w_gate_up = spread(own_gate_up)
    own_down = flat(own(after(down_proj, other), units))
    w_down = spread(own_down)
    qkv_count, out_count = 3 * heads * 64, heads * 64

    both_lengths = jnp.stack([lengths, lax.ppermute(lengths, "y", swap)])
    both_lengths = jnp.where(y == 0, both_lengths, both_lengths[::-1]).reshape(-1)
    length = lax.dynamic_slice_in_dim(both_lengths, z, 1, 0)
    slots = (x * 2 + y) * count + jnp.arange(count, dtype=jnp.int32)
    near_x, near_y = jnp.array([0, 0, 1, 1]) ^ x, jnp.array([0, 1, 0, 1]) ^ y
    starts = ((near_x * 2 + near_y) * count).astype(jnp.int32)
    arrived = after(to_groups(stored_in, other, small), own_gate_up, own_down, length, starts)
    tokens = arrived[:, :count].astype(F32)
    small = arrived[:, count:]
    gain_one = small[:, :1].astype(F32)
    gain_two = small[:, 1:2].astype(F32)
    table = small[:, 2, : buckets * mine].reshape(nz, buckets, mine).transpose(0, 2, 1)
    table = table.reshape(-1, buckets).astype(F32)
    table = lax.dynamic_slice_in_dim(table, y * local_heads, local_heads, 0)

    live = (slots < length).astype(F32)[None, :, None]

    def scale_of(values):
        squares = jnp.sum(values * values, axis=(0, 2), keepdims=True)
        return lax.rsqrt(squares / features + norm_eps)

    def norm_back(values, scale, gain, grad):
        inner = jnp.sum(values * gain * grad, axis=(0, 2), keepdims=True)
        out = scale * gain * grad - values * (scale * scale * scale) * inner / features
        return out, jnp.sum(values * scale * grad, axis=1)

    def reduce(partial):
        rows = partial.reshape(nz * partial.shape[1], width)
        return lax.psum_scatter(rows, ("z", "c"), scatter_dimension=0, tiled=True)

    fits = nx == 2 and heads == 4 and count == 256 and units * unit % 640 == 0 and nz % 2 == 0
    if fits:
        forward, backward, gather, scatter = attend, attend_back, gather_tokens, scatter_tokens
        nt, nn, tn, ffn_one, ffn_two = mm_nt, mm_nn, mm_tn, ffn_in, ffn_back
        shared, stored_from = share, settle
    else:
        forward, backward, gather, scatter = attend_plain, attend_back_plain, gather_plain, scatter_plain
        nt, nn, tn, ffn_one, ffn_two = mm_nt_plain, mm_nn_plain, mm_tn_plain, ffn_in_plain, ffn_back_plain
        shared, stored_from = share_plain, settle_plain
    def attend_back_all(grad, *last):
        if not fits:
            grads, table_grad = backward(projected, length, table, grad, lse, nc, heads)
            return (grads,), table_grad
        first = backward(0, projected, length, table, grad, lse[0])
        second = backward(1, after(projected, first[0], *last), length, table, grad, lse[1])
        return (first[0], second[0]), jnp.concatenate([first[1], second[1]])

    scale_one = scale_of(tokens)
    normed, _, _ = gather((tokens * scale_one * gain_one).astype(BF), table, live)
    cot_other = hop(pick(stored_cot, 1 - y, 1), "y")
    upstream = live * to_groups(stored_cot, after(cot_other, arrived), None).astype(F32)
    upstream_rounded = after(upstream.astype(BF), w_attn)
    projected = nt(normed, w_attn, 0, qkv_count, starts)
    if fits:
        first = forward(0, projected, length, table)
        grad_ffn, cot_first, cot_last = gather(upstream_rounded, first[0])
        second = forward(1, after(projected, first[0], *cot_first), length, table)
        attended, lse = (first[0], second[0]), (first[1], second[1])
    else:
        grad_ffn, _, cot_last = gather(upstream_rounded)
        attended, lse = forward(projected, length, table, nc, heads)
        attended = (attended,)
    heads_out = [after(attended[0], *cot_last), *attended[1:]]
    hidden = tokens + scatter(nn(heads_out, w_attn, qkv_count, out_count, starts))[0]
    scale_two = scale_of(hidden)
    normed_two, _, _ = gather((hidden * scale_two * gain_two).astype(BF))
    gate, up, activated = ffn_one(normed_two, w_gate_up, starts)

    down_partial = tn([activated], grad_ffn, starts)
    down_part = reduce(down_partial)
    grad_gate_up = ffn_two(grad_ffn, w_down, after(gate, down_partial), up, starts)
    two_parts = nn([grad_gate_up], w_gate_up, 0, 2 * units * unit, starts)
    grad_two, two_first, _ = scatter(two_parts)
    gate_up_partial = tn([after(grad_gate_up, two_parts[0])], normed_two, starts)
    gate_up_part = reduce(after(gate_up_partial, down_part, *two_first))
    branch_parts = nn([after(activated, gate_up_partial)], w_down, 0, units * unit, starts)
    through, ffn_gain_part = norm_back(hidden, scale_two, gain_two, grad_two)
    grad_hidden = upstream + through
    grad_branch, _, branch_here = gather(after(grad_hidden.astype(BF), branch_parts[0]))
    grad_attended = nt(grad_branch, w_attn, qkv_count, out_count, starts)
    out_partial = tn(attended, grad_branch, starts)
    branch_parts = [after(part, *branch_here) for part in branch_parts]
    branch, branch_first, branch_last = scatter(branch_parts)
    down_pieces, down_last = shared(after(down_part, *branch_here))
    grad_projected, table_part = attend_back_all(after(grad_attended, out_partial), *branch_first)
    out_part = reduce(after(out_partial, gate_up_part, grad_projected[0], *branch_first, down_last))
    outputs = (live * (hidden + branch)).astype(BF)
    outputs, _ = from_groups(outputs)
    qkv_partial = tn(grad_projected, normed, starts)
    gate_up_pieces, gate_up_last = shared(after(gate_up_part, grad_projected[0]))
    qkv_part = reduce(after(qkv_partial, out_part, *branch_last, gate_up_last))
    one_parts = nn(grad_projected, w_attn, 0, qkv_count, starts)
    if fits:
        here = jnp.stack([y, c]).astype(jnp.int32)

        def write_rows(source, outs):
            outs[0][...] = source[...].astype(F32)

        def write_qkv(source, outs):
            for h in range(heads):
                for i in range(3):
                    value = source[(i * heads + h) * 64 : (i * heads + h + 1) * 64, :].astype(F32)
                    if i == 2:
                        outs[1][h] = value
                    else:
                        outs[0][h, i] = value

        def write_gate_up(source, outs):
            for u in range(units):
                for i in range(2):
                    first = (i * units + u) * unit
                    outs[0][u, i] = source[first : first + unit, :].astype(F32)

        (down_all,) = place(down_pieces, here, [(units * unit, width)], write_rows)
        (gate_up_all,) = place(gate_up_pieces, here, [(units, 2, unit, width)], write_gate_up)
    beside = (outputs[0], down_all, gate_up_all) if fits else ()
    grad_one, _, one_last = scatter(one_parts, (), beside)
    through, attn_gain_part = norm_back(tokens, scale_one, gain_one, grad_one)
    input_grad, input_leaves = from_groups((grad_hidden + through).astype(BF))

    out_pieces, out_last = shared(out_part)

    table_part = jnp.sum(table_part, axis=2)
    every = jnp.zeros((nx * 2 * local_heads, table_part.shape[1]), F32)
    every = lax.dynamic_update_slice_in_dim(every, table_part, (x * 2 + y) * local_heads, 0)
    spare = -every.size % width
    every = jnp.pad(every.reshape(-1), (0, spare)).reshape(-1, width)
    sums = sum_plane(jnp.concatenate([attn_gain_part, ffn_gain_part, every]), nx, out_last, outputs[1])
    all_sums = sum_line(after(sums, input_leaves), nz)
    attn_gain_grad, ffn_gain_grad = all_sums[:nz], all_sums[nz : 2 * nz]
    every = all_sums[2 * nz :].reshape(-1)[: nx * 2 * local_heads * buckets].reshape(-1, buckets)

    other_half = outputs[1]
    outputs = stored_from(outputs, BF)
    if fits:
        (out_all,) = place(out_pieces, here, [(heads * 64, width)], write_rows)
        qkv_pieces, _ = shared(after(qkv_part, out_last, other_half, *one_last), out_all, outputs, sums)
        query_key_all, value_all = place(
            qkv_pieces, here, [(heads, 2, 64, width), (heads, 64, width)], write_qkv
        )
    else:
        down_all, out_all = down_pieces.astype(F32), out_pieces.astype(F32)
        gate_up_all = gate_up_pieces.astype(F32).reshape(parts, 2, units, unit, width)
        gate_up_all = gate_up_all.transpose(0, 2, 1, 3, 4).reshape(-1, 2, unit, width)
        qkv_all = shared(qkv_part)[0].astype(F32).reshape(parts, 3, heads, 64, width)
        qkv_all = qkv_all.transpose(0, 2, 1, 3, 4).reshape(-1, 3, 64, width)
        query_key_all, value_all = qkv_all[:, :2], qkv_all[:, 2]
    input_grad = stored_from(input_grad, F32)
    down_all, out_all = down_all.reshape(down_proj.shape), out_all.reshape(out_proj.shape)

    table_grad = lax.dynamic_slice_in_dim(every, (x * nz + z) * mine, mine, 0).T
    return (
        outputs,
        input_grad,
        pick(attn_gain_grad, z, 0),
        pick(ffn_gain_grad, z, 0),
        query_key_all.transpose(3, 0, 1, 2),
        value_all.transpose(2, 0, 1),
        out_all,
        gate_up_all.transpose(3, 0, 1, 2),
        down_all,
        table_grad,
    )


def solution(mesh):
    dp, nx, nz = (mesh.shape[name] for name in ("dp", "gx", "gy"))
    nc = dp // 2
    split = Mesh(mesh.devices.reshape(2, nc, nx, nz), ("y", "c", "x", "z"))
    seq = ("y", "c")
    return jax.shard_map(
        functools.partial(body, nx, nz, nc),
        mesh=split,
        in_specs=(
            P(seq, "x", "z"),
            P(seq),
            P("z"),
            P("z"),
            P("z", "x", None, None),
            P("z", "x", None),
            P("x", None, "z"),
            P("z", "x", None, None),
            P("x", None, "z"),
            P(None, ("x", "z")),
            P(seq, "x", "z"),
        ),
        out_specs=(
            P(seq, "x", "z"),
            P(seq, "x", "z"),
            P("z"),
            P("z"),
            P("z", "x", None, None),
            P("z", "x", None),
            P("x", None, "z"),
            P("z", "x", None, None),
            P("x", None, "z"),
            P(None, ("x", "z")),
        ),
        check_vma=False,
    )
```

```python
import functools
import math

import jax
import jax.numpy as jnp
from jax import lax
from jax.experimental import pallas as pl
from jax.experimental.pallas import tpu as pltpu
from jax.sharding import Mesh
from jax.sharding import PartitionSpec as P

norm_eps = 1e-06
masked_score = -1e30
bucket_edges = (12, 16, 23, 32, 46, 64, 91)
BF = jnp.bfloat16
F32 = jnp.float32
LB = 128
VMEM = 60 * 1024 * 1024
swap = [(0, 1), (1, 0)]
gelu_a = math.sqrt(2.0 / math.pi)
gelu_b = 0.044715


def bucket_index(offset):
    magnitude = jnp.abs(offset)
    far_bucket = 8 + sum(((magnitude >= boundary).astype(jnp.int32) for boundary in bucket_edges))
    near_bucket = jnp.where(magnitude < 8, magnitude, far_bucket)
    return near_bucket + 16 * (offset > 0).astype(jnp.int32)


def cost(flops, moved):
    return pl.CostEstimate(flops=int(flops) // 16, bytes_accessed=int(moved) // 16, transcendentals=0)


def params(steps):
    return pltpu.CompilerParams(
        dimension_semantics=("arbitrary",) * steps, vmem_limit_bytes=VMEM
    )


def dot_nt(a, b):
    return lax.dot_general(a, b, (((1,), (1,)), ((), ())), preferred_element_type=F32)


def dot_nn(a, b):
    return lax.dot_general(a, b, (((1,), (0,)), ((), ())), preferred_element_type=F32)


def spot_of(starts_ref, d, count):
    return pl.ds(pl.multiple_of(starts_ref[d], 256), count)


def piece_specs(pieces):
    shape = pieces[0].shape
    return [pl.BlockSpec(shape, lambda *_: (0, 0, 0)) for _ in pieces]


def nt_sum(piece_refs, d, w_of):
    half = piece_refs[0].shape[0]
    acc = None
    for z in range(2 * half):
        part = dot_nt(piece_refs[4 * (z // half) + d][z % half], w_of(z))
        acc = part if acc is None else acc + part
    return acc


def nt_kernel(starts_ref, *refs):
    pieces, (w_ref, out_ref) = refs[:8], refs[8:]
    for d in range(4):
        acc = nt_sum(pieces, d, lambda z: w_ref[z, 0])
        out_ref[spot_of(starts_ref, d, acc.shape[0]), :] = acc.astype(BF)


def mm_nt(pieces, w, first, rows, starts):
    nz, nc, _, width = w.shape
    total = 4 * pieces[0].shape[1]
    count, skip = rows // 256, first // 256
    return pl.pallas_call(
        nt_kernel,
        grid=(nc, count),
        in_specs=[pl.BlockSpec(memory_space=pltpu.SMEM)]
        + piece_specs(pieces)
        + [pl.BlockSpec((nz, 1, 256, width), lambda c, i: (0, c, skip + i, 0))],
        out_specs=pl.BlockSpec((total, 256), lambda c, i: (0, c * count + i)),
        out_shape=jax.ShapeDtypeStruct((total, nc * rows), BF),
        compiler_params=params(2),
        cost_estimate=cost(
            2 * nz * total * width * nc * rows, 2 * nz * width * (total + nc * rows) + 2 * total * nc * rows
        ),
        name="product_nt",
    )(starts, *pieces, w)


def nn_kernel(count, starts_ref, *refs):
    grads, (w_ref, low_out, low_keep, high_out, high_keep) = refs[:count], refs[count:]
    nc, rows, width = w_ref.shape[1:]
    t = grads[0].shape[0] // 4
    in_low = pl.program_id(0) < pl.num_programs(0) // 2

    def product(d):
        spot = spot_of(starts_ref, d, t)
        if count == 1:
            return dot_nn(grads[0][spot, :], w_ref[0].reshape(nc * rows, width)).astype(BF)
        return sum(dot_nn(grads[c][spot, :], w_ref[0, c]) for c in range(count)).astype(BF)

    @pl.when(in_low)
    def _():
        for d in range(4):
            (low_out if d // 2 else low_keep)[d % 2, 0] = product(d)

    @pl.when(jnp.logical_not(in_low))
    def _():
        for d in range(4):
            (high_out if d % 2 else high_keep)[d // 2, 0] = product(d)


def mm_nn(grads, w, first, rows, starts):
    total = grads[0].shape[0]
    nz, nc, _, width = w.shape
    skip, half, t = first // rows, nz // 2, total // 4
    low = pl.BlockSpec((2, 1, t, width), lambda z: (0, jnp.minimum(z, half - 1), 0, 0))
    high = pl.BlockSpec((2, 1, t, width), lambda z: (0, jnp.maximum(z - half, 0), 0, 0))
    return pl.pallas_call(
        functools.partial(nn_kernel, len(grads)),
        grid=(nz,),
        in_specs=[pl.BlockSpec(memory_space=pltpu.SMEM)]
        + [pl.BlockSpec(grad.shape, lambda z: (0, 0)) for grad in grads]
        + [pl.BlockSpec((1, nc, rows, width), lambda z: (z, 0, skip, 0))],
        out_specs=[low, low, high, high],
        out_shape=[jax.ShapeDtypeStruct((2, half, t, width), BF)] * 4,
        compiler_params=params(1),
        cost_estimate=cost(
            2 * nz * total * width * nc * rows, 2 * nz * width * (total + nc * rows) + 2 * total * nc * rows
        ),
        name="product_nn",
    )(starts, *grads, w)


def tn_kernel(count, starts_ref, *refs):
    grads, pieces, out_ref = refs[:count], refs[count:-1], refs[-1]
    half, t, _ = pieces[0].shape

    def one(grad_ref):
        turned = [grad_ref[spot_of(starts_ref, d, t), :].T for d in range(4)]
        for z in range(2 * half):
            acc = dot_nn(turned[0], pieces[4 * (z // half)][z % half])
            for d in range(1, 4):
                acc += dot_nn(turned[d], pieces[4 * (z // half) + d][z % half])
            out_ref[z] = acc.astype(BF)

    if count == 1:
        one(grads[0])
    else:
        for c in range(count):

            @pl.when(pl.program_id(0) // (pl.num_programs(0) // count) == c)
            def _():
                one(grads[c])


def mm_tn(grads, pieces, starts):
    total, rows = grads[0].shape
    half, _, width = pieces[0].shape
    nz, count = 2 * half, len(grads)
    block = next(b for b in (640, 384, 256) if rows % b == 0)
    steps = rows // block

    def spec(c):
        return pl.BlockSpec((total, block), lambda i: (0, jnp.clip(i - c * steps, 0, steps - 1)))

    return pl.pallas_call(
        functools.partial(tn_kernel, count),
        grid=(count * steps,),
        in_specs=[pl.BlockSpec(memory_space=pltpu.SMEM)]
        + [spec(c) for c in range(count)]
        + piece_specs(pieces),
        out_specs=pl.BlockSpec((nz, block, width), lambda i: (0, i, 0)),
        out_shape=jax.ShapeDtypeStruct((nz, count * rows, width), BF),
        compiler_params=params(1),
        cost_estimate=cost(
            2 * nz * total * width * count * rows, 2 * nz * width * (total + count * rows) + 2 * total * count * rows
        ),
        name="product_tn",
    )(starts, *grads, *pieces)


def gelu_parts(gate):
    curve = jnp.tanh(gelu_a * (gate + gelu_b * gate * gate * gate))
    value = 0.5 * gate * (1.0 + curve)
    slope = 0.5 * (1.0 + curve) + 0.5 * gate * (1.0 - curve * curve) * gelu_a * (
        1.0 + 3.0 * gelu_b * gate * gate
    )
    return value, slope


def ffn_in_kernel(starts_ref, *refs):
    pieces, (w_ref, gate_ref, up_ref, active_ref) = refs[:8], refs[8:]
    _, _, _, block, width = w_ref.shape
    for d in range(4):
        acc = nt_sum(pieces, d, lambda z: w_ref[z, 0].reshape(2 * block, width))
        spot = spot_of(starts_ref, d, acc.shape[0])
        gate, up = acc[:, :block], acc[:, block:]
        value = 0.5 * gate * (1.0 + jnp.tanh(gelu_a * (gate + gelu_b * gate * gate * gate)))
        gate_ref[spot, :] = gate.astype(BF)
        up_ref[spot, :] = up.astype(BF)
        active_ref[spot, :] = (value * up).astype(BF)


def ffn_in(pieces, w, starts):
    nz, nc, rows, width = w.shape
    half, total = rows // 2, 4 * pieces[0].shape[1]
    count = half // 128
    block = pl.BlockSpec((total, 128), lambda c, i: (0, c * count + i))
    return pl.pallas_call(
        ffn_in_kernel,
        grid=(nc, count),
        in_specs=[pl.BlockSpec(memory_space=pltpu.SMEM)]
        + piece_specs(pieces)
        + [pl.BlockSpec((nz, 1, 2, 128, width), lambda c, i: (0, c, 0, i, 0))],
        out_specs=[block, block, block],
        out_shape=[jax.ShapeDtypeStruct((total, nc * half), BF)] * 3,
        compiler_params=params(2),
        cost_estimate=cost(
            2 * nz * total * width * nc * rows, 2 * nz * width * (total + nc * rows) + 3 * total * nc * rows
        ),
        name="ffn_in",
    )(starts, *pieces, w.reshape(nz, nc, 2, half, width))


def ffn_back_kernel(starts_ref, *refs):
    pieces, (w_ref, gate_ref, up_ref, out_ref) = refs[:8], refs[8:]
    half = w_ref.shape[2]
    for d in range(4):
        acc = nt_sum(pieces, d, lambda z: w_ref[z, 0])
        spot = spot_of(starts_ref, d, acc.shape[0])
        value, slope = gelu_parts(gate_ref[spot, :].astype(F32))
        out_ref[spot, :half] = (acc * up_ref[spot, :].astype(F32) * slope).astype(BF)
        out_ref[spot, half:] = (acc * value).astype(BF)


def ffn_back(pieces, w, gate, up, starts):
    nz, nc, half, width = w.shape
    total = gate.shape[0]
    kept = pl.BlockSpec((total, half), lambda c: (0, c))
    return pl.pallas_call(
        ffn_back_kernel,
        grid=(nc,),
        in_specs=[pl.BlockSpec(memory_space=pltpu.SMEM)]
        + piece_specs(pieces)
        + [pl.BlockSpec((nz, 1, half, width), lambda c: (0, c, 0, 0)), kept, kept],
        out_specs=pl.BlockSpec((total, 2 * half), lambda c: (0, c)),
        out_shape=jax.ShapeDtypeStruct((total, nc * 2 * half), BF),
        compiler_params=params(1),
        cost_estimate=cost(
            2 * nz * total * width * nc * half, 2 * nz * width * (total + nc * half) + 8 * total * nc * half
        ),
        name="ffn_back",
    )(starts, *pieces, w, gate, up)


def mm_nt_plain(act, w, first, rows, starts):
    part = lax.slice_in_dim(w, first, first + rows, axis=2)
    out = jnp.einsum("ztf,zcrf->tcr", act, part, preferred_element_type=F32)
    return out.astype(BF).reshape(act.shape[1], -1)


def mm_nn_plain(grads, w, first, rows, starts):
    grad = grads[0]
    part = lax.slice_in_dim(w, first, first + rows, axis=2)
    split = grad.reshape(grad.shape[0], w.shape[1], rows)
    out = jnp.einsum("tcr,zcrf->ztf", split, part, preferred_element_type=F32)
    return [out.astype(BF)]


def mm_tn_plain(grads, act, starts):
    return jnp.einsum("tr,ztf->zrf", grads[0], act, preferred_element_type=F32).astype(BF)


def ffn_in_plain(act, w, starts):
    _, nc, rows, _ = w.shape
    total = act.shape[1]
    both = jnp.einsum("ztf,zcrf->tcr", act, w, preferred_element_type=F32)
    gate, up = both[:, :, : rows // 2], both[:, :, rows // 2 :]
    value, _ = gelu_parts(gate)
    return [part.astype(BF).reshape(total, -1) for part in (gate, up, value * up)]


def ffn_back_plain(act, w, gate, up, starts):
    total, nc = gate.shape[0], w.shape[1]
    grad = jnp.einsum("ztf,zcrf->tcr", act, w, preferred_element_type=F32)
    value, slope = gelu_parts(gate.astype(F32).reshape(grad.shape))
    both = [grad * up.astype(F32).reshape(grad.shape) * slope, grad * value]
    return jnp.concatenate(both, axis=2).astype(BF).reshape(total, -1)


def near_buckets(tile, total):
    first = (total // LB - 2 + tile) * LB
    rows = lax.broadcasted_iota(jnp.int32, (LB, LB), 0)
    lanes = lax.broadcasted_iota(jnp.int32, (LB, LB), 1)
    return bucket_index(first + rows - (total - LB) - lanes)


def near_kernel(total, table_ref, out_ref):
    heads = out_ref.shape[0]

    def one_tile(tile, _):
        index = near_buckets(tile, total)
        vals = [jnp.full((LB, LB), table_ref[h, 0], F32) for h in range(heads)]
        for b in range(1, 32):
            hit = index == b
            vals = [jnp.where(hit, table_ref[h, b], vals[h]) for h in range(heads)]
        for h in range(heads):
            out_ref[h, pl.ds(pl.multiple_of(tile * LB, LB), LB)] = vals[h]
        return 0

    lax.fori_loop(0, 3, one_tile, 0)


def near_bias(table, total):
    heads = table.shape[0]
    return pl.pallas_call(
        functools.partial(near_kernel, total),
        in_specs=[pl.BlockSpec(memory_space=pltpu.SMEM)],
        out_specs=pl.BlockSpec((heads, 3 * LB, LB), lambda: (0, 0, 0)),
        out_shape=jax.ShapeDtypeStruct((heads, 3 * LB, LB), F32),
        compiler_params=params(0),
        cost_estimate=cost(0, heads * LB * LB),
        name="near_bias",
    )(table)


def build_strips(table_ref, near_ref, strip_ref, total, group):
    heads = strip_ref.shape[0]
    near = (total // LB - 2) * LB
    for h in range(heads):
        head = group * heads + h
        strip_ref[h, :near] = jnp.full((near, LB), table_ref[head, 15], F32)
        strip_ref[h, near : near + 3 * LB] = near_ref[h]
        strip_ref[h, near + 3 * LB :] = jnp.full((near, LB), table_ref[head, 31], F32)


def table_kernel(total, *refs):
    parts, out_ref = refs[:-1], refs[-1]
    index = [near_buckets(tile, total) for tile in range(3)]
    buckets = [range(1, 16), [b for b in range(32) if b != 16], range(17, 32)]
    for g, part_ref in enumerate(parts):
        heads = part_ref.shape[0]

        def one_head(h, _):
            here = g * heads + h
            out_ref[here] = jnp.zeros((32, LB), F32)
            out_ref[here, 15:16] = part_ref[h, 3 * LB : 3 * LB + 1]
            out_ref[here, 31:32] = part_ref[h, 3 * LB + 8 : 3 * LB + 9]
            for tile in range(3):
                grads = part_ref[h, tile * LB : (tile + 1) * LB]
                for b in buckets[tile]:
                    picked = jnp.where(index[tile] == b, grads, 0.0)
                    out_ref[here, b : b + 1] += jnp.sum(picked, axis=0, keepdims=True)
            return 0

        lax.fori_loop(0, heads, one_head, 0)


def table_sums(parts, total):
    heads = len(parts) * parts[0].shape[0]
    out = pl.pallas_call(
        functools.partial(table_kernel, total),
        in_specs=[pl.BlockSpec(part.shape, lambda: (0, 0, 0)) for part in parts],
        out_specs=pl.BlockSpec((heads, 32, LB), lambda: (0, 0, 0)),
        out_shape=jax.ShapeDtypeStruct((heads, 32, LB), F32),
        compiler_params=params(0),
        cost_estimate=cost(0, heads * LB * LB),
        name="table_sums",
    )(*parts)
    return jnp.sum(out, axis=2)


def head_lanes(shape, h):
    lanes = lax.broadcasted_iota(jnp.int32, shape, 1)
    return lanes // 64 == h, lanes == ((h + 1) % 4) * 64


def mask_keys(keys, length, h):
    own, spare = head_lanes(keys.shape, h)
    dead = lax.broadcasted_iota(jnp.int32, keys.shape, 0) >= length
    mask = jnp.where(jnp.logical_and(spare, dead), masked_score, 0.0)
    return jnp.where(own, keys.astype(F32), mask).astype(BF)


def with_one(queries, h):
    _, spare = head_lanes(queries.shape, h)
    return jnp.where(spare, 1.0, queries.astype(F32)).astype(BF)


def own_lanes(values, h):
    own, _ = head_lanes(values.shape, h)
    return jnp.where(own, values.astype(F32), 0.0).astype(BF)


def block_bias(strip_ref, h, block, total):
    first = total - LB - 2 * block * LB
    left = strip_ref[h, pl.ds(pl.multiple_of(first, LB), total)]
    right = strip_ref[h, pl.ds(pl.multiple_of(first - LB, LB), total)]
    return jnp.concatenate([left, right], axis=1)


def attend_kernel(group, length_ref, table_ref, near_ref, q_ref, k_ref, v_ref, out_ref, lse_ref, strip, heads_k, turned_v, turned_out):
    total = q_ref.shape[0]
    heads = strip.shape[0]
    build_strips(table_ref, near_ref, strip, total, group)
    turned_v[...] = v_ref[...].astype(F32).T.astype(BF)
    for h in range(heads):
        heads_k[h] = mask_keys(k_ref[...], length_ref[0], h)

    def one_block(block, _):
        spot = pl.ds(pl.multiple_of(block * 256, 256), 256)
        queries = q_ref[spot]
        for h in range(heads):
            scores = dot_nt(heads_k[h], with_one(queries, h)) + block_bias(strip, h, block, total)
            largest = jnp.max(scores, axis=0, keepdims=True)
            raised = jnp.exp(scores - largest)
            totals = jnp.sum(raised, axis=0, keepdims=True)
            out = dot_nn(turned_v[h * 64 : (h + 1) * 64], raised.astype(BF))
            turned_out[h * 64 : (h + 1) * 64, spot] = out * (1.0 / totals)
            lse_ref[h : h + 1, spot] = largest + jnp.log(totals)
        return 0

    lax.fori_loop(0, total // 256, one_block, 0)
    out_ref[...] = turned_out[...].T.astype(BF)


def attend_back_kernel(
    group, length_ref, table_ref, near_ref, q_ref, k_ref, v_ref, grad_ref, lse_ref, out_ref, table_grad_ref,
    strip, strip_grad, heads_k, turned_k, turned_q, ds_ref, p_ref, dk_ref, dv_ref,
):
    total = q_ref.shape[0]
    heads = strip.shape[0]
    build_strips(table_ref, near_ref, strip, total, group)
    strip_grad[...] = jnp.zeros_like(strip_grad)
    dk_ref[...] = jnp.zeros_like(dk_ref)
    dv_ref[...] = jnp.zeros_like(dv_ref)
    turned_k[...] = k_ref[...].astype(F32).T.astype(BF)
    for h in range(heads):
        heads_k[h] = mask_keys(k_ref[...], length_ref[0], h)

    def one_block(block, _):
        spot = pl.ds(pl.multiple_of(block * 256, 256), 256)
        queries, grads = q_ref[spot], grad_ref[spot]
        own_q, own_g = [], []
        for h in range(heads):
            own_q.append(own_lanes(queries, h))
            own_g.append(own_lanes(grads, h))
            scores = dot_nt(heads_k[h], with_one(queries, h)) + block_bias(strip, h, block, total)
            probs = jnp.exp(scores - lse_ref[h : h + 1, spot])
            weighed = probs * dot_nt(v_ref[...], own_g[h])
            delta = jnp.sum(weighed, axis=0, keepdims=True)
            grad_scores = weighed - probs * delta
            first = total - LB - 2 * block * LB
            left = pl.ds(pl.multiple_of(first, LB), total)
            right = pl.ds(pl.multiple_of(first - LB, LB), total)
            strip_grad[h, left] += grad_scores[:, :LB]
            strip_grad[h, right] += grad_scores[:, LB:]
            rounded = grad_scores.astype(BF)
            ds_ref[:, h * 256 : (h + 1) * 256] = rounded
            p_ref[:, h * 256 : (h + 1) * 256] = probs.astype(BF)
            turned_q[h * 64 : (h + 1) * 64, spot] = dot_nn(turned_k[h * 64 : (h + 1) * 64], rounded)
        dk_ref[...] += dot_nn(ds_ref[...], jnp.concatenate(own_q, axis=0))
        dv_ref[...] += dot_nn(p_ref[...], jnp.concatenate(own_g, axis=0))
        return 0

    lax.fori_loop(0, total // 256, one_block, 0)
    out_ref[:, :256] = turned_q[...].T.astype(BF)
    out_ref[:, 256:512] = dk_ref[...].astype(BF)
    out_ref[:, 512:] = dv_ref[...].astype(BF)

    near = (total // LB - 2) * LB
    for h in range(heads):
        table_grad_ref[h, : 3 * LB] = strip_grad[h, near : near + 3 * LB]
        left = jnp.sum(strip_grad[h, :near], axis=0, keepdims=True)
        right = jnp.sum(strip_grad[h, near + 3 * LB :], axis=0, keepdims=True)
        table_grad_ref[h, 3 * LB : 3 * LB + 8] = jnp.broadcast_to(left, (8, LB))
        table_grad_ref[h, 3 * LB + 8 :] = jnp.broadcast_to(right, (8, LB))


def block_specs(total, group):
    def spec(i):
        return pl.BlockSpec((total, 256), lambda _: (0, 3 * group + i))

    smem = pl.BlockSpec(memory_space=pltpu.SMEM)
    near = pl.BlockSpec((4, 3 * LB, LB), lambda _: (group, 0, 0))
    return [smem, smem, near, spec(0), spec(1), spec(2)]


def attend(group, projected, length, table, near):
    total = projected.shape[0]
    heads = 4
    return pl.pallas_call(
        functools.partial(attend_kernel, group),
        grid=(1,),
        in_specs=block_specs(total, group),
        out_specs=[
            pl.BlockSpec((total, 256), lambda _: (0, 0)),
            pl.BlockSpec((8, total), lambda _: (0, 0)),
        ],
        out_shape=[
            jax.ShapeDtypeStruct((total, 256), BF),
            jax.ShapeDtypeStruct((8, total), F32),
        ],
        scratch_shapes=[
            pltpu.VMEM((heads, 2 * total - LB, LB), F32),
            pltpu.VMEM((heads, total, 256), BF),
            pltpu.VMEM((256, total), BF),
            pltpu.VMEM((256, total), F32),
        ],
        compiler_params=params(1),
        cost_estimate=cost(heads * total * total * 2 * 256 * 2, 4 * total * 256 * 2),
        name="attend",
    )(length, table, near, projected, projected, projected)


def attend_back(group, projected, length, table, near, grad_out, lse):
    total = projected.shape[0]
    heads = 4
    return pl.pallas_call(
        functools.partial(attend_back_kernel, group),
        grid=(1,),
        in_specs=block_specs(total, group)
        + [
            pl.BlockSpec((total, 256), lambda _: (0, group)),
            pl.BlockSpec((8, total), lambda _: (0, 0)),
        ],
        out_specs=[
            pl.BlockSpec((total, 768), lambda _: (0, 0)),
            pl.BlockSpec((heads, 3 * LB + 16, LB), lambda _: (0, 0, 0)),
        ],
        out_shape=[
            jax.ShapeDtypeStruct((total, 768), BF),
            jax.ShapeDtypeStruct((heads, 3 * LB + 16, LB), F32),
        ],
        scratch_shapes=[
            pltpu.VMEM((heads, 2 * total - LB, LB), F32),
            pltpu.VMEM((heads, 2 * total - LB, LB), F32),
            pltpu.VMEM((heads, total, 256), BF),
            pltpu.VMEM((256, total), BF),
            pltpu.VMEM((256, total), F32),
            pltpu.VMEM((total, heads * 256), BF),
            pltpu.VMEM((total, heads * 256), BF),
            pltpu.VMEM((total, 256), F32),
            pltpu.VMEM((total, 256), F32),
        ],
        compiler_params=params(1),
        cost_estimate=cost(heads * total * total * 2 * 256 * 5, 8 * total * 256 * 2),
        name="attend_back",
    )(length, table, near, projected, projected, projected, grad_out, lse)


def split_heads(projected, groups, heads):
    parts = projected.reshape(projected.shape[0], groups, 3, heads, 64)
    return [parts[:, :, i].reshape(projected.shape[0], groups * heads, 64) for i in range(3)]


def plain_scores(queries, keys, length, table):
    slots = jnp.arange(keys.shape[0], dtype=jnp.int32)
    picked = (bucket_index(slots[None, :] - slots[:, None])[:, :, None] == jnp.arange(32)).astype(F32)
    bias = jnp.einsum("qkb,hb->hqk", picked, table, precision=lax.Precision.HIGHEST)
    scores = jnp.einsum("qhs,khs->hqk", queries, keys, preferred_element_type=F32) + bias
    return jnp.where(slots < length[0], scores, masked_score), picked


def attend_plain(projected, length, table, groups, heads):
    queries, keys, values = split_heads(projected, groups, heads)
    scores, _ = plain_scores(queries, keys, length, table)
    lse = jax.nn.logsumexp(scores, axis=2)
    probs = jnp.exp(scores - lse[:, :, None]).astype(BF)
    out = jnp.einsum("hqk,khs->qhs", probs, values, preferred_element_type=F32)
    return out.astype(BF).reshape(projected.shape[0], -1), lse


def attend_back_plain(projected, length, table, grad_out, lse, groups, heads):
    total = projected.shape[0]
    queries, keys, values = split_heads(projected, groups, heads)
    grads = grad_out.reshape(queries.shape)
    scores, picked = plain_scores(queries, keys, length, table)
    probs = jnp.exp(scores - lse[:, :, None])
    weighed = probs * jnp.einsum("qhs,khs->hqk", grads, values, preferred_element_type=F32)
    wide = weighed - probs * jnp.sum(weighed, axis=2, keepdims=True)
    rounded = wide.astype(BF)
    parts = [
        jnp.einsum("hqk,khs->qhs", rounded, keys, preferred_element_type=F32),
        jnp.einsum("hqk,qhs->khs", rounded, queries, preferred_element_type=F32),
        jnp.einsum("hqk,qhs->khs", probs.astype(BF), grads, preferred_element_type=F32),
    ]
    parts = [part.astype(BF).reshape(total, groups, 1, heads * 64) for part in parts]
    table_grad = jnp.einsum("hqk,qkb->hb", wide, picked, precision=lax.Precision.HIGHEST)
    return (
        jnp.concatenate(parts, axis=2).reshape(total, -1),
        table_grad.reshape(groups * heads, 32, 1),
    )


def hop(value, axis):
    return lax.ppermute(value, axis, swap)


def pick(value, index, axis):
    return lax.dynamic_index_in_dim(value, index, axis, keepdims=False)


def paired(mine, other, axis, place=0):
    return jnp.where(
        lax.axis_index(axis) == 0,
        jnp.stack([mine, other], axis=place),
        jnp.stack([other, mine], axis=place),
    )


def after(value, *others):
    return lax.optimization_barrier((value, *others))[0]


def gather_plain(part, *beside):
    return lax.all_gather(part, ("x", "y"), axis=1, tiled=True), (), ()


def gather_tokens(part, *beside):
    half = part.shape[0] // 2
    low, high = part[:half], part[half:]
    low_x, high_y = hop(low, "x"), hop(high, "y")
    if beside:
        low_x, high_y = after(low_x, *beside), after(high_y, *beside)
    low_y, high_x = hop(low, "y"), hop(high, "x")
    low_xy, high_xy = hop(low_x, "y"), hop(high_y, "x")
    pieces = [low, low_y, low_x, low_xy, high, high_y, high_x, high_xy]
    return pieces, (low_x, high_y), (low_y, low_xy, high_x, high_xy)


def scatter_plain(parts, beside=(), beside_last=()):
    whole = parts[0].astype(F32)
    return lax.psum_scatter(whole, ("x", "y"), scatter_dimension=1, tiled=True), (), ()


def scatter_tokens(parts, beside=(), beside_last=()):
    low_out, low_keep, high_out, high_keep = parts
    low_in, high_in = hop(low_out, "x"), hop(high_out, "y")
    if beside:
        low_in, high_in = after(low_in, *beside), after(high_in, *beside)

    def add(keep, arrived, index):
        return keep[index].astype(F32) + arrived[index].astype(F32)

    low_last = hop(add(low_keep, low_in, 1).astype(BF), "y")
    high_last = hop(add(high_keep, high_in, 1).astype(BF), "x")
    if beside_last:
        low_last, high_last = after(low_last, *beside_last), after(high_last, *beside_last)
    low = add(low_keep, low_in, 0) + low_last.astype(F32)
    high = add(high_keep, high_in, 0) + high_last.astype(F32)
    return jnp.concatenate([low, high], axis=0), (low_in, high_in), (low_last, high_last)


def place_kernel(write, here_ref, *refs):
    pieces, outs = refs[:4], refs[4:]
    step = pl.program_id(0)
    for near in range(4):
        y = here_ref[0] if near < 2 else 1 - here_ref[0]
        c = here_ref[1] if near % 2 == 0 else 1 - here_ref[1]

        @pl.when(step == 2 * y + c)
        def _():
            write(pieces[near], outs)


def place(pieces, here, shapes, write):
    return pl.pallas_call(
        functools.partial(place_kernel, write),
        grid=(4,),
        in_specs=[pl.BlockSpec(memory_space=pltpu.SMEM)]
        + [pl.BlockSpec(piece.shape, lambda q: (0, 0)) for piece in pieces],
        out_specs=[
            pl.BlockSpec(shape, lambda q, rank=len(shape): (q,) + (0,) * (rank - 1)) for shape in shapes
        ],
        out_shape=[jax.ShapeDtypeStruct((4 * shape[0], *shape[1:]), F32) for shape in shapes],
        compiler_params=params(1),
        cost_estimate=cost(0, pieces[0].size),
        name="place",
    )(here, *pieces)


def share(part, *beside):
    over_y = hop(part, "y")
    if beside:
        over_y = after(over_y, *beside)
    return [part, hop(part, "c"), over_y, hop(over_y, "c")], over_y


def share_plain(part):
    return lax.all_gather(part, ("y", "c"), axis=0), part


def to_groups(halves, other, extra):
    count, _, t, width = halves.shape
    both = paired(pick(halves, lax.axis_index("y"), 1), other, "y").reshape(2 * count, t, width)
    if extra is not None:
        wide = jnp.broadcast_to(extra[None], (2 * count, *extra.shape))
        both = jnp.concatenate([both, wide], axis=1)
    return lax.all_to_all(both, "z", 0, 0, tiled=True)


def from_groups(mine):
    nz, t, width = mine.shape
    back = lax.all_to_all(mine, "z", 0, 0, tiled=True).reshape(2, nz // 2, t, width)
    leaving = pick(back, 1 - lax.axis_index("y"), 0)
    return (back, hop(leaving, "y")), leaving


def settle_kernel(y_ref, back_ref, other_ref, out_ref):
    j, y = pl.program_id(0), pl.program_id(1)

    @pl.when(y == y_ref[0])
    def _():
        out_ref[0, 0] = back_ref[y, j].astype(out_ref.dtype)

    @pl.when(y != y_ref[0])
    def _():
        out_ref[0, 0] = other_ref[j].astype(out_ref.dtype)


def settle(arrived, dtype):
    back, other = arrived
    _, count, t, width = back.shape
    y = lax.axis_index("y").astype(jnp.int32).reshape(1)
    out = pl.pallas_call(
        settle_kernel,
        grid=(count, 2),
        in_specs=[
            pl.BlockSpec(memory_space=pltpu.SMEM),
            pl.BlockSpec(back.shape, lambda j, y: (0, 0, 0, 0)),
            pl.BlockSpec(other.shape, lambda j, y: (0, 0, 0)),
        ],
        out_specs=pl.BlockSpec((1, 1, t, width), lambda j, y: (j, y, 0, 0)),
        out_shape=jax.ShapeDtypeStruct((count, 2, t, width), dtype),
        compiler_params=params(2),
        cost_estimate=cost(0, count * t * width),
        name="settle",
    )(y, back, other)
    return out.reshape(count, 2 * t, width)


def settle_plain(arrived, dtype):
    back, other = arrived
    _, count, t, width = back.shape
    both = paired(pick(back, lax.axis_index("y"), 0), other, "y")
    return both.transpose(1, 0, 2, 3).reshape(count, 2 * t, width).astype(dtype)


def sum_plane(value, nx, *earlier):
    value = value + after(hop(value, "c"), *earlier)
    value = value + hop(value, "x") if nx == 2 else lax.psum(value, "x")
    return value + hop(value, "y")


def sum_line(value, nz):
    step = 1
    while step < nz:
        value = value + lax.ppermute(value, "z", [(i, i ^ step) for i in range(nz)])
        step *= 2
    return value


def body(
    nx, nz, nc, inputs, lengths, attn_gain, ffn_gain, query_key, value_proj, out_proj, gate_up, down_proj, bias_table, cotangent
):
    x, y = lax.axis_index("x"), lax.axis_index("y")
    c, z = lax.axis_index("c"), lax.axis_index("z")
    width = inputs.shape[2]
    features = nz * width
    quarter = y * nc + c
    parts = 2 * nc
    buckets, mine = bias_table.shape
    count = inputs.shape[1] // 2

    stored_in = inputs.reshape(inputs.shape[0], 2, count, width)
    stored_cot = cotangent.reshape(stored_in.shape)
    small = jnp.concatenate(
        [attn_gain[None], ffn_gain[None], jnp.pad(bias_table.reshape(1, -1), ((0, 0), (0, width - buckets * mine)))]
    )
    small = jnp.pad(small, ((0, 5), (0, 0)))
    leaving = pick(stored_in, 1 - y, 1)

    query_key_rows = jnp.transpose(query_key, (1, 2, 3, 0))
    value_rows = jnp.transpose(value_proj, (1, 2, 0))
    gate_up_rows = jnp.transpose(gate_up, (1, 2, 3, 0))
    heads = value_rows.shape[0] // parts
    units = gate_up_rows.shape[0] // parts
    unit = gate_up_rows.shape[2]
    local_heads = nc * heads

    def own(rows, size):
        return lax.dynamic_slice_in_dim(rows, quarter * size, size, 0)

    def flat(rows):
        return rows.reshape(-1, width)

    def spread(rows):
        gathered = lax.all_gather(rows, ("z", "c"), axis=0, tiled=True)
        return gathered.reshape(nz, nc, rows.shape[0], width)

    own_pair = own(query_key_rows, heads)
    own_attn = [own_pair[:, 0], own_pair[:, 1], own(value_rows, heads), own(out_proj, heads)]
    own_attn = jnp.concatenate([flat(rows) for rows in own_attn])
    w_attn = spread(own_attn)
    other = after(hop(leaving, "y"), own_attn)
    own_pair = own(after(gate_up_rows, other), units)
    own_gate_up = jnp.concatenate([flat(own_pair[:, 0]), flat(own_pair[:, 1])])
    w_gate_up = spread(own_gate_up)
    own_down = flat(own(after(down_proj, other), units))
    w_down = spread(own_down)
    qkv_count, out_count = 3 * heads * 64, heads * 64

    both_lengths = jnp.stack([lengths, lax.ppermute(lengths, "y", swap)])
    both_lengths = jnp.where(y == 0, both_lengths, both_lengths[::-1]).reshape(-1)
    length = lax.dynamic_slice_in_dim(both_lengths, z, 1, 0)
    slots = (x * 2 + y) * count + jnp.arange(count, dtype=jnp.int32)
    near_x, near_y = jnp.array([0, 0, 1, 1]) ^ x, jnp.array([0, 1, 0, 1]) ^ y
    starts = ((near_x * 2 + near_y) * count).astype(jnp.int32)
    arrived = after(to_groups(stored_in, other, small), own_gate_up, own_down, length, starts)
    tokens = arrived[:, :count].astype(F32)
    small = arrived[:, count:]
    gain_one = small[:, :1].astype(F32)
    gain_two = small[:, 1:2].astype(F32)
    table = small[:, 2, : buckets * mine].reshape(nz, buckets, mine).transpose(0, 2, 1)
    table = table.reshape(-1, buckets).astype(F32)
    table = lax.dynamic_slice_in_dim(table, y * local_heads, local_heads, 0)

    live = (slots < length).astype(F32)[None, :, None]

    def scale_of(values):
        squares = jnp.sum(values * values, axis=(0, 2), keepdims=True)
        return lax.rsqrt(squares / features + norm_eps)

    def norm_back(values, scale, gain, grad):
        inner = jnp.sum(values * gain * grad, axis=(0, 2), keepdims=True)
        out = scale * gain * grad - values * (scale * scale * scale) * inner / features
        return out, jnp.sum(values * scale * grad, axis=1)

    def reduce(partial):
        rows = partial.reshape(nz * partial.shape[1], width)
        return lax.psum_scatter(rows, ("z", "c"), scatter_dimension=0, tiled=True)

    fits = nx == 2 and heads == 4 and count == 256 and units * unit % 640 == 0 and nz % 2 == 0
    if fits:
        forward, backward, gather, scatter = attend, attend_back, gather_tokens, scatter_tokens
        nt, nn, tn, ffn_one, ffn_two = mm_nt, mm_nn, mm_tn, ffn_in, ffn_back
        shared, stored_from = share, settle
    else:
        forward, backward, gather, scatter = attend_plain, attend_back_plain, gather_plain, scatter_plain
        nt, nn, tn, ffn_one, ffn_two = mm_nt_plain, mm_nn_plain, mm_tn_plain, ffn_in_plain, ffn_back_plain
        shared, stored_from = share_plain, settle_plain
    def attend_back_all(grad, *last):
        if not fits:
            grads, table_grad = backward(projected, length, table, grad, lse, nc, heads)
            return (grads,), table_grad[:, :, 0]
        first = backward(0, projected, length, table, near, grad, lse[0])
        second = backward(1, after(projected, first[0], *last), length, table, near, grad, lse[1])
        return (first[0], second[0]), (first[1], second[1])

    scale_one = scale_of(tokens)
    near = near_bias(table, 4 * count) if fits else table
    normed, _, _ = gather((tokens * scale_one * gain_one).astype(BF), near, live)
    cot_other = hop(pick(stored_cot, 1 - y, 1), "y")
    upstream = live * to_groups(stored_cot, after(cot_other, arrived), None).astype(F32)
    upstream_rounded = after(upstream.astype(BF), w_attn)
    projected = nt(normed, w_attn, 0, qkv_count, starts)
    if fits:
        first = forward(0, projected, length, table, near)
        grad_ffn, cot_first, cot_last = gather(upstream_rounded, first[0])
        second = forward(1, after(projected, first[0], *cot_first), length, table, near)
        attended, lse = (first[0], second[0]), (first[1], second[1])
    else:
        grad_ffn, _, cot_last = gather(upstream_rounded)
        attended, lse = forward(projected, length, table, nc, heads)
        attended = (attended,)
    heads_out = [after(attended[0], *cot_last), *attended[1:]]
    hidden = tokens + scatter(nn(heads_out, w_attn, qkv_count, out_count, starts))[0]
    scale_two = scale_of(hidden)
    normed_two, _, _ = gather((hidden * scale_two * gain_two).astype(BF))
    gate, up, activated = ffn_one(normed_two, w_gate_up, starts)

    down_partial = tn([activated], grad_ffn, starts)
    down_part = reduce(down_partial)
    grad_gate_up = ffn_two(grad_ffn, w_down, after(gate, down_partial), up, starts)
    two_parts = nn([grad_gate_up], w_gate_up, 0, 2 * units * unit, starts)
    grad_two, two_first, _ = scatter(two_parts)
    gate_up_partial = tn([after(grad_gate_up, two_parts[0])], normed_two, starts)
    gate_up_part = reduce(after(gate_up_partial, down_part, *two_first))
    branch_parts = nn([after(activated, gate_up_partial)], w_down, 0, units * unit, starts)
    through, ffn_gain_part = norm_back(hidden, scale_two, gain_two, grad_two)
    grad_hidden = upstream + through
    grad_branch, _, branch_here = gather(after(grad_hidden.astype(BF), branch_parts[0]))
    grad_attended = nt(grad_branch, w_attn, qkv_count, out_count, starts)
    out_partial = tn(attended, grad_branch, starts)
    branch_parts = [after(part, *branch_here) for part in branch_parts]
    branch, branch_first, branch_last = scatter(branch_parts)
    down_pieces, down_last = shared(after(down_part, *branch_here))
    grad_projected, table_part = attend_back_all(after(grad_attended, out_partial), *branch_first)
    out_part = reduce(after(out_partial, gate_up_part, grad_projected[0], *branch_first, down_last))
    outputs = (live * (hidden + branch)).astype(BF)
    outputs, _ = from_groups(outputs)
    qkv_partial = tn(grad_projected, normed, starts)
    gate_up_pieces, gate_up_last = shared(after(gate_up_part, grad_projected[0]))
    qkv_part = reduce(after(qkv_partial, out_part, *branch_last, gate_up_last))
    one_parts = nn(grad_projected, w_attn, 0, qkv_count, starts)
    if fits:
        here = jnp.stack([y, c]).astype(jnp.int32)

        def write_rows(source, outs):
            outs[0][...] = source[...].astype(F32)

        def write_qkv(source, outs):
            for h in range(heads):
                for i in range(3):
                    value = source[(i * heads + h) * 64 : (i * heads + h + 1) * 64, :].astype(F32)
                    if i == 2:
                        outs[1][h] = value
                    else:
                        outs[0][h, i] = value

        def write_gate_up(source, outs):
            for u in range(units):
                for i in range(2):
                    first = (i * units + u) * unit
                    outs[0][u, i] = source[first : first + unit, :].astype(F32)

        (down_all,) = place(down_pieces, here, [(units * unit, width)], write_rows)
        (gate_up_all,) = place(gate_up_pieces, here, [(units, 2, unit, width)], write_gate_up)
    beside = (down_all, gate_up_all) if fits else ()
    table_part = table_sums(table_part, 4 * count) if fits else table_part
    grad_one, _, one_last = scatter(one_parts, beside, (table_part, outputs[0]))
    through, attn_gain_part = norm_back(tokens, scale_one, gain_one, grad_one)
    input_grad, input_leaves = from_groups((grad_hidden + through).astype(BF))

    out_pieces, out_last = shared(out_part)

    every = jnp.zeros((nx * 2 * local_heads, table_part.shape[1]), F32)
    every = lax.dynamic_update_slice_in_dim(every, table_part, (x * 2 + y) * local_heads, 0)
    spare = -every.size % width
    every = jnp.pad(every.reshape(-1), (0, spare)).reshape(-1, width)
    sums = sum_plane(jnp.concatenate([attn_gain_part, ffn_gain_part, every]), nx, out_last, outputs[1])
    all_sums = sum_line(after(sums, input_leaves), nz)
    attn_gain_grad, ffn_gain_grad = all_sums[:nz], all_sums[nz : 2 * nz]
    every = all_sums[2 * nz :].reshape(-1)[: nx * 2 * local_heads * buckets].reshape(-1, buckets)

    outputs = stored_from(outputs, BF)
    if fits:
        (out_all,) = place(out_pieces, here, [(heads * 64, width)], write_rows)
        qkv_pieces, _ = shared(after(qkv_part, sums, *one_last), out_all, outputs, input_leaves)
        query_key_all, value_all = place(
            qkv_pieces, here, [(heads, 2, 64, width), (heads, 64, width)], write_qkv
        )
    else:
        down_all, out_all = down_pieces.astype(F32), out_pieces.astype(F32)
        gate_up_all = gate_up_pieces.astype(F32).reshape(parts, 2, units, unit, width)
        gate_up_all = gate_up_all.transpose(0, 2, 1, 3, 4).reshape(-1, 2, unit, width)
        qkv_all = shared(qkv_part)[0].astype(F32).reshape(parts, 3, heads, 64, width)
        qkv_all = qkv_all.transpose(0, 2, 1, 3, 4).reshape(-1, 3, 64, width)
        query_key_all, value_all = qkv_all[:, :2], qkv_all[:, 2]
    input_grad = stored_from(input_grad, F32)
    down_all, out_all = down_all.reshape(down_proj.shape), out_all.reshape(out_proj.shape)

    table_grad = lax.dynamic_slice_in_dim(every, (x * nz + z) * mine, mine, 0).T
    return (
        outputs,
        input_grad,
        pick(attn_gain_grad, z, 0),
        pick(ffn_gain_grad, z, 0),
        query_key_all.transpose(3, 0, 1, 2),
        value_all.transpose(2, 0, 1),
        out_all,
        gate_up_all.transpose(3, 0, 1, 2),
        down_all,
        table_grad,
    )


def solution(mesh):
    dp, nx, nz = (mesh.shape[name] for name in ("dp", "gx", "gy"))
    nc = dp // 2
    split = Mesh(mesh.devices.reshape(2, nc, nx, nz), ("y", "c", "x", "z"))
    seq = ("y", "c")
    return jax.shard_map(
        functools.partial(body, nx, nz, nc),
        mesh=split,
        in_specs=(
            P(seq, "x", "z"),
            P(seq),
            P("z"),
            P("z"),
            P("z", "x", None, None),
            P("z", "x", None),
            P("x", None, "z"),
            P("z", "x", None, None),
            P("x", None, "z"),
            P(None, ("x", "z")),
            P(seq, "x", "z"),
        ),
        out_specs=(
            P(seq, "x", "z"),
            P(seq, "x", "z"),
            P("z"),
            P("z"),
            P("z", "x", None, None),
            P("z", "x", None),
            P("x", None, "z"),
            P("z", "x", None, None),
            P("x", None, "z"),
            P(None, ("x", "z")),
        ),
        check_vma=False,
    )
```

```python
import functools
import math

import jax
import jax.numpy as jnp
from jax import lax
from jax.experimental import pallas as pl
from jax.experimental.pallas import tpu as pltpu
from jax.sharding import Mesh
from jax.sharding import PartitionSpec as P

norm_eps = 1e-06
masked_score = -1e30
bucket_edges = (12, 16, 23, 32, 46, 64, 91)
BF = jnp.bfloat16
F32 = jnp.float32
LB = 128
VMEM = 60 * 1024 * 1024
swap = [(0, 1), (1, 0)]
gelu_a = math.sqrt(2.0 / math.pi)
gelu_b = 0.044715


def bucket_index(offset):
    magnitude = jnp.abs(offset)
    far_bucket = 8 + sum(((magnitude >= boundary).astype(jnp.int32) for boundary in bucket_edges))
    near_bucket = jnp.where(magnitude < 8, magnitude, far_bucket)
    return near_bucket + 16 * (offset > 0).astype(jnp.int32)


def cost(flops, moved):
    return pl.CostEstimate(flops=int(flops) // 16, bytes_accessed=int(moved) // 16, transcendentals=0)


def params(steps):
    return pltpu.CompilerParams(
        dimension_semantics=("arbitrary",) * steps, vmem_limit_bytes=VMEM
    )


def dot_nt(a, b):
    return lax.dot_general(a, b, (((1,), (1,)), ((), ())), preferred_element_type=F32)


def dot_nn(a, b):
    return lax.dot_general(a, b, (((1,), (0,)), ((), ())), preferred_element_type=F32)


def spot_of(starts_ref, d, count):
    return pl.ds(pl.multiple_of(starts_ref[d], 256), count)


def piece_specs(pieces):
    shape = pieces[0].shape
    return [pl.BlockSpec(shape, lambda *_: (0, 0, 0)) for _ in pieces]


def nt_sum(piece_refs, d, w_of):
    half = piece_refs[0].shape[0]
    acc = None
    for z in range(2 * half):
        part = dot_nt(piece_refs[4 * (z // half) + d][z % half], w_of(z))
        acc = part if acc is None else acc + part
    return acc


def nt_kernel(starts_ref, *refs):
    pieces, (w_ref, out_ref) = refs[:8], refs[8:]
    for d in range(4):
        acc = nt_sum(pieces, d, lambda z: w_ref[z, 0])
        out_ref[spot_of(starts_ref, d, acc.shape[0]), :] = acc.astype(BF)


def mm_nt(pieces, w, first, rows, starts):
    nz, nc, _, width = w.shape
    total = 4 * pieces[0].shape[1]
    count, skip = rows // 256, first // 256
    return pl.pallas_call(
        nt_kernel,
        grid=(nc, count),
        in_specs=[pl.BlockSpec(memory_space=pltpu.SMEM)]
        + piece_specs(pieces)
        + [pl.BlockSpec((nz, 1, 256, width), lambda c, i: (0, c, skip + i, 0))],
        out_specs=pl.BlockSpec((total, 256), lambda c, i: (0, c * count + i)),
        out_shape=jax.ShapeDtypeStruct((total, nc * rows), BF),
        compiler_params=params(2),
        cost_estimate=cost(
            2 * nz * total * width * nc * rows, 2 * nz * width * (total + nc * rows) + 2 * total * nc * rows
        ),
        name="product_nt",
    )(starts, *pieces, w)


def nn_kernel(count, starts_ref, *refs):
    grads, (w_ref, low_out, low_keep, high_out, high_keep) = refs[:count], refs[count:]
    nc, rows, width = w_ref.shape[1:]
    t = grads[0].shape[0] // 4
    in_low = pl.program_id(0) < pl.num_programs(0) // 2

    def product(d):
        spot = spot_of(starts_ref, d, t)
        if count == 1:
            return dot_nn(grads[0][spot, :], w_ref[0].reshape(nc * rows, width)).astype(BF)
        return sum(dot_nn(grads[c][spot, :], w_ref[0, c]) for c in range(count)).astype(BF)

    @pl.when(in_low)
    def _():
        for d in range(4):
            (low_out if d // 2 else low_keep)[d % 2, 0] = product(d)

    @pl.when(jnp.logical_not(in_low))
    def _():
        for d in range(4):
            (high_out if d % 2 else high_keep)[d // 2, 0] = product(d)


def mm_nn(grads, w, first, rows, starts):
    total = grads[0].shape[0]
    nz, nc, _, width = w.shape
    skip, half, t = first // rows, nz // 2, total // 4
    low = pl.BlockSpec((2, 1, t, width), lambda z: (0, jnp.minimum(z, half - 1), 0, 0))
    high = pl.BlockSpec((2, 1, t, width), lambda z: (0, jnp.maximum(z - half, 0), 0, 0))
    return pl.pallas_call(
        functools.partial(nn_kernel, len(grads)),
        grid=(nz,),
        in_specs=[pl.BlockSpec(memory_space=pltpu.SMEM)]
        + [pl.BlockSpec(grad.shape, lambda z: (0, 0)) for grad in grads]
        + [pl.BlockSpec((1, nc, rows, width), lambda z: (z, 0, skip, 0))],
        out_specs=[low, low, high, high],
        out_shape=[jax.ShapeDtypeStruct((2, half, t, width), BF)] * 4,
        compiler_params=params(1),
        cost_estimate=cost(
            2 * nz * total * width * nc * rows, 2 * nz * width * (total + nc * rows) + 2 * total * nc * rows
        ),
        name="product_nn",
    )(starts, *grads, w)


def tn_kernel(count, starts_ref, *refs):
    grads, pieces, out_ref = refs[:count], refs[count:-1], refs[-1]
    half, t, _ = pieces[0].shape

    def one(grad_ref):
        turned = [grad_ref[spot_of(starts_ref, d, t), :].T for d in range(4)]
        for z in range(2 * half):
            acc = dot_nn(turned[0], pieces[4 * (z // half)][z % half])
            for d in range(1, 4):
                acc += dot_nn(turned[d], pieces[4 * (z // half) + d][z % half])
            out_ref[z] = acc.astype(BF)

    if count == 1:
        one(grads[0])
    else:
        for c in range(count):

            @pl.when(pl.program_id(0) // (pl.num_programs(0) // count) == c)
            def _():
                one(grads[c])


def mm_tn(grads, pieces, starts):
    total, rows = grads[0].shape
    half, _, width = pieces[0].shape
    nz, count = 2 * half, len(grads)
    block = next(b for b in (640, 384, 256) if rows % b == 0)
    steps = rows // block

    def spec(c):
        return pl.BlockSpec((total, block), lambda i: (0, jnp.clip(i - c * steps, 0, steps - 1)))

    return pl.pallas_call(
        functools.partial(tn_kernel, count),
        grid=(count * steps,),
        in_specs=[pl.BlockSpec(memory_space=pltpu.SMEM)]
        + [spec(c) for c in range(count)]
        + piece_specs(pieces),
        out_specs=pl.BlockSpec((nz, block, width), lambda i: (0, i, 0)),
        out_shape=jax.ShapeDtypeStruct((nz, count * rows, width), BF),
        compiler_params=params(1),
        cost_estimate=cost(
            2 * nz * total * width * count * rows, 2 * nz * width * (total + count * rows) + 2 * total * count * rows
        ),
        name="product_tn",
    )(starts, *grads, *pieces)


def gelu_parts(gate):
    curve = jnp.tanh(gelu_a * (gate + gelu_b * gate * gate * gate))
    value = 0.5 * gate * (1.0 + curve)
    slope = 0.5 * (1.0 + curve) + 0.5 * gate * (1.0 - curve * curve) * gelu_a * (
        1.0 + 3.0 * gelu_b * gate * gate
    )
    return value, slope


def ffn_in_kernel(starts_ref, *refs):
    pieces, (w_ref, gate_ref, up_ref, active_ref) = refs[:8], refs[8:]
    _, _, _, block, width = w_ref.shape
    for d in range(4):
        acc = nt_sum(pieces, d, lambda z: w_ref[z, 0].reshape(2 * block, width))
        spot = spot_of(starts_ref, d, acc.shape[0])
        gate, up = acc[:, :block], acc[:, block:]
        value = 0.5 * gate * (1.0 + jnp.tanh(gelu_a * (gate + gelu_b * gate * gate * gate)))
        gate_ref[spot, :] = gate.astype(BF)
        up_ref[spot, :] = up.astype(BF)
        active_ref[spot, :] = (value * up).astype(BF)


def ffn_in(pieces, w, starts):
    nz, nc, rows, width = w.shape
    half, total = rows // 2, 4 * pieces[0].shape[1]
    count = half // 128
    block = pl.BlockSpec((total, 128), lambda c, i: (0, c * count + i))
    return pl.pallas_call(
        ffn_in_kernel,
        grid=(nc, count),
        in_specs=[pl.BlockSpec(memory_space=pltpu.SMEM)]
        + piece_specs(pieces)
        + [pl.BlockSpec((nz, 1, 2, 128, width), lambda c, i: (0, c, 0, i, 0))],
        out_specs=[block, block, block],
        out_shape=[jax.ShapeDtypeStruct((total, nc * half), BF)] * 3,
        compiler_params=params(2),
        cost_estimate=cost(
            2 * nz * total * width * nc * rows, 2 * nz * width * (total + nc * rows) + 3 * total * nc * rows
        ),
        name="ffn_in",
    )(starts, *pieces, w.reshape(nz, nc, 2, half, width))


def ffn_back_kernel(starts_ref, *refs):
    pieces, (w_ref, gate_ref, up_ref, out_ref) = refs[:8], refs[8:]
    half = w_ref.shape[2]
    for d in range(4):
        acc = nt_sum(pieces, d, lambda z: w_ref[z, 0])
        spot = spot_of(starts_ref, d, acc.shape[0])
        value, slope = gelu_parts(gate_ref[spot, :].astype(F32))
        out_ref[spot, :half] = (acc * up_ref[spot, :].astype(F32) * slope).astype(BF)
        out_ref[spot, half:] = (acc * value).astype(BF)


def ffn_back(pieces, w, gate, up, starts):
    nz, nc, half, width = w.shape
    total = gate.shape[0]
    kept = pl.BlockSpec((total, half), lambda c: (0, c))
    return pl.pallas_call(
        ffn_back_kernel,
        grid=(nc,),
        in_specs=[pl.BlockSpec(memory_space=pltpu.SMEM)]
        + piece_specs(pieces)
        + [pl.BlockSpec((nz, 1, half, width), lambda c: (0, c, 0, 0)), kept, kept],
        out_specs=pl.BlockSpec((total, 2 * half), lambda c: (0, c)),
        out_shape=jax.ShapeDtypeStruct((total, nc * 2 * half), BF),
        compiler_params=params(1),
        cost_estimate=cost(
            2 * nz * total * width * nc * half, 2 * nz * width * (total + nc * half) + 8 * total * nc * half
        ),
        name="ffn_back",
    )(starts, *pieces, w, gate, up)


def mm_nt_plain(act, w, first, rows, starts):
    part = lax.slice_in_dim(w, first, first + rows, axis=2)
    out = jnp.einsum("ztf,zcrf->tcr", act, part, preferred_element_type=F32)
    return out.astype(BF).reshape(act.shape[1], -1)


def mm_nn_plain(grads, w, first, rows, starts):
    grad = grads[0]
    part = lax.slice_in_dim(w, first, first + rows, axis=2)
    split = grad.reshape(grad.shape[0], w.shape[1], rows)
    out = jnp.einsum("tcr,zcrf->ztf", split, part, preferred_element_type=F32)
    return [out.astype(BF)]


def mm_tn_plain(grads, act, starts):
    return jnp.einsum("tr,ztf->zrf", grads[0], act, preferred_element_type=F32).astype(BF)


def ffn_in_plain(act, w, starts):
    _, nc, rows, _ = w.shape
    total = act.shape[1]
    both = jnp.einsum("ztf,zcrf->tcr", act, w, preferred_element_type=F32)
    gate, up = both[:, :, : rows // 2], both[:, :, rows // 2 :]
    value, _ = gelu_parts(gate)
    return [part.astype(BF).reshape(total, -1) for part in (gate, up, value * up)]


def ffn_back_plain(act, w, gate, up, starts):
    total, nc = gate.shape[0], w.shape[1]
    grad = jnp.einsum("ztf,zcrf->tcr", act, w, preferred_element_type=F32)
    value, slope = gelu_parts(gate.astype(F32).reshape(grad.shape))
    both = [grad * up.astype(F32).reshape(grad.shape) * slope, grad * value]
    return jnp.concatenate(both, axis=2).astype(BF).reshape(total, -1)


def near_buckets(tile, total):
    first = (total // LB - 2 + tile) * LB
    rows = lax.broadcasted_iota(jnp.int32, (LB, LB), 0)
    lanes = lax.broadcasted_iota(jnp.int32, (LB, LB), 1)
    return bucket_index(first + rows - (total - LB) - lanes)


def near_kernel(total, table_ref, out_ref):
    heads = out_ref.shape[0]

    def one_tile(tile, _):
        index = near_buckets(tile, total)
        vals = [jnp.full((LB, LB), table_ref[h, 0], F32) for h in range(heads)]
        for b in range(1, 32):
            hit = index == b
            vals = [jnp.where(hit, table_ref[h, b], vals[h]) for h in range(heads)]
        for h in range(heads):
            out_ref[h, pl.ds(pl.multiple_of(tile * LB, LB), LB)] = vals[h]
        return 0

    lax.fori_loop(0, 3, one_tile, 0)


def near_bias(table, total):
    heads = table.shape[0]
    return pl.pallas_call(
        functools.partial(near_kernel, total),
        in_specs=[pl.BlockSpec(memory_space=pltpu.SMEM)],
        out_specs=pl.BlockSpec((heads, 3 * LB, LB), lambda: (0, 0, 0)),
        out_shape=jax.ShapeDtypeStruct((heads, 3 * LB, LB), F32),
        compiler_params=params(0),
        cost_estimate=cost(0, heads * LB * LB),
        name="near_bias",
    )(table)


def build_strips(table_ref, near_ref, strip_ref, total, group):
    heads = strip_ref.shape[0]
    near = (total // LB - 2) * LB
    for h in range(heads):
        head = group * heads + h
        strip_ref[h, :near] = jnp.full((near, LB), table_ref[head, 15], F32)
        strip_ref[h, near : near + 3 * LB] = near_ref[h]
        strip_ref[h, near + 3 * LB :] = jnp.full((near, LB), table_ref[head, 31], F32)


def table_kernel(total, *refs):
    parts, out_ref = refs[:-1], refs[-1]
    index = [near_buckets(tile, total) for tile in range(3)]
    buckets = [range(1, 16), [b for b in range(32) if b != 16], range(17, 32)]
    for g, part_ref in enumerate(parts):
        heads = part_ref.shape[0]

        def one_head(h, _):
            here = g * heads + h
            out_ref[here] = jnp.zeros((32, LB), F32)
            out_ref[here, 15:16] = part_ref[h, 3 * LB : 3 * LB + 1]
            out_ref[here, 31:32] = part_ref[h, 3 * LB + 8 : 3 * LB + 9]
            for tile in range(3):
                grads = part_ref[h, tile * LB : (tile + 1) * LB]
                for b in buckets[tile]:
                    picked = jnp.where(index[tile] == b, grads, 0.0)
                    out_ref[here, b : b + 1] += jnp.sum(picked, axis=0, keepdims=True)
            return 0

        lax.fori_loop(0, heads, one_head, 0)


def table_sums(parts, total):
    heads = len(parts) * parts[0].shape[0]
    out = pl.pallas_call(
        functools.partial(table_kernel, total),
        in_specs=[pl.BlockSpec(part.shape, lambda: (0, 0, 0)) for part in parts],
        out_specs=pl.BlockSpec((heads, 32, LB), lambda: (0, 0, 0)),
        out_shape=jax.ShapeDtypeStruct((heads, 32, LB), F32),
        compiler_params=params(0),
        cost_estimate=cost(0, heads * LB * LB),
        name="table_sums",
    )(*parts)
    return jnp.sum(out, axis=2)


def head_lanes(shape, h):
    lanes = lax.broadcasted_iota(jnp.int32, shape, 1)
    return lanes // 64 == h, lanes == ((h + 1) % 4) * 64


def mask_keys(keys, length, h):
    own, spare = head_lanes(keys.shape, h)
    dead = lax.broadcasted_iota(jnp.int32, keys.shape, 0) >= length
    mask = jnp.where(jnp.logical_and(spare, dead), masked_score, 0.0)
    return jnp.where(own, keys.astype(F32), mask).astype(BF)


def with_one(queries, h):
    _, spare = head_lanes(queries.shape, h)
    return jnp.where(spare, 1.0, queries.astype(F32)).astype(BF)


def own_lanes(values, h):
    own, _ = head_lanes(values.shape, h)
    return jnp.where(own, values.astype(F32), 0.0).astype(BF)


def block_bias(strip_ref, h, block, total):
    first = total - LB - 2 * block * LB
    left = strip_ref[h, pl.ds(pl.multiple_of(first, LB), total)]
    right = strip_ref[h, pl.ds(pl.multiple_of(first - LB, LB), total)]
    return jnp.concatenate([left, right], axis=1)


def attend_kernel(group, length_ref, table_ref, near_ref, q_ref, k_ref, v_ref, out_ref, lse_ref, strip, heads_k, turned_v, turned_out):
    total = q_ref.shape[0]
    heads = strip.shape[0]
    build_strips(table_ref, near_ref, strip, total, group)
    turned_v[...] = v_ref[...].astype(F32).T.astype(BF)
    for h in range(heads):
        heads_k[h] = mask_keys(k_ref[...], length_ref[0], h)

    def one_block(block, _):
        spot = pl.ds(pl.multiple_of(block * 256, 256), 256)
        queries = q_ref[spot]
        for h in range(heads):
            scores = dot_nt(heads_k[h], with_one(queries, h)) + block_bias(strip, h, block, total)
            largest = jnp.max(scores, axis=0, keepdims=True)
            raised = jnp.exp(scores - largest)
            totals = jnp.sum(raised, axis=0, keepdims=True)
            out = dot_nn(turned_v[h * 64 : (h + 1) * 64], raised.astype(BF))
            turned_out[h * 64 : (h + 1) * 64, spot] = out * (1.0 / totals)
            lse_ref[h : h + 1, spot] = largest + jnp.log(totals)
        return 0

    lax.fori_loop(0, total // 256, one_block, 0)
    out_ref[...] = turned_out[...].T.astype(BF)


def attend_back_kernel(
    group, length_ref, table_ref, near_ref, q_ref, k_ref, v_ref, grad_ref, lse_ref, out_ref, table_grad_ref,
    strip, strip_grad, heads_k, turned_k, turned_q, ds_ref, p_ref, dk_ref, dv_ref,
):
    total = q_ref.shape[0]
    heads = strip.shape[0]
    build_strips(table_ref, near_ref, strip, total, group)
    strip_grad[...] = jnp.zeros_like(strip_grad)
    dk_ref[...] = jnp.zeros_like(dk_ref)
    dv_ref[...] = jnp.zeros_like(dv_ref)
    turned_k[...] = k_ref[...].astype(F32).T.astype(BF)
    for h in range(heads):
        heads_k[h] = mask_keys(k_ref[...], length_ref[0], h)

    def one_block(block, _):
        spot = pl.ds(pl.multiple_of(block * 256, 256), 256)
        queries, grads = q_ref[spot], grad_ref[spot]
        own_q, own_g = [], []
        for h in range(heads):
            own_q.append(own_lanes(queries, h))
            own_g.append(own_lanes(grads, h))
            scores = dot_nt(heads_k[h], with_one(queries, h)) + block_bias(strip, h, block, total)
            probs = jnp.exp(scores - lse_ref[h : h + 1, spot])
            weighed = probs * dot_nt(v_ref[...], own_g[h])
            delta = jnp.sum(weighed, axis=0, keepdims=True)
            grad_scores = weighed - probs * delta
            first = total - LB - 2 * block * LB
            left = pl.ds(pl.multiple_of(first, LB), total)
            right = pl.ds(pl.multiple_of(first - LB, LB), total)
            strip_grad[h, left] += grad_scores[:, :LB]
            strip_grad[h, right] += grad_scores[:, LB:]
            rounded = grad_scores.astype(BF)
            ds_ref[:, h * 256 : (h + 1) * 256] = rounded
            p_ref[:, h * 256 : (h + 1) * 256] = probs.astype(BF)
            turned_q[h * 64 : (h + 1) * 64, spot] = dot_nn(turned_k[h * 64 : (h + 1) * 64], rounded)
        dk_ref[...] += dot_nn(ds_ref[...], jnp.concatenate(own_q, axis=0))
        dv_ref[...] += dot_nn(p_ref[...], jnp.concatenate(own_g, axis=0))
        return 0

    lax.fori_loop(0, total // 256, one_block, 0)
    out_ref[:, :256] = turned_q[...].T.astype(BF)
    out_ref[:, 256:512] = dk_ref[...].astype(BF)
    out_ref[:, 512:] = dv_ref[...].astype(BF)

    near = (total // LB - 2) * LB
    for h in range(heads):
        table_grad_ref[h, : 3 * LB] = strip_grad[h, near : near + 3 * LB]
        left = jnp.sum(strip_grad[h, :near], axis=0, keepdims=True)
        right = jnp.sum(strip_grad[h, near + 3 * LB :], axis=0, keepdims=True)
        table_grad_ref[h, 3 * LB : 3 * LB + 8] = jnp.broadcast_to(left, (8, LB))
        table_grad_ref[h, 3 * LB + 8 :] = jnp.broadcast_to(right, (8, LB))


def block_specs(total, group):
    def spec(i):
        return pl.BlockSpec((total, 256), lambda _: (0, 3 * group + i))

    smem = pl.BlockSpec(memory_space=pltpu.SMEM)
    near = pl.BlockSpec((4, 3 * LB, LB), lambda _: (group, 0, 0))
    return [smem, smem, near, spec(0), spec(1), spec(2)]


def attend(group, projected, length, table, near):
    total = projected.shape[0]
    heads = 4
    return pl.pallas_call(
        functools.partial(attend_kernel, group),
        grid=(1,),
        in_specs=block_specs(total, group),
        out_specs=[
            pl.BlockSpec((total, 256), lambda _: (0, 0)),
            pl.BlockSpec((8, total), lambda _: (0, 0)),
        ],
        out_shape=[
            jax.ShapeDtypeStruct((total, 256), BF),
            jax.ShapeDtypeStruct((8, total), F32),
        ],
        scratch_shapes=[
            pltpu.VMEM((heads, 2 * total - LB, LB), F32),
            pltpu.VMEM((heads, total, 256), BF),
            pltpu.VMEM((256, total), BF),
            pltpu.VMEM((256, total), F32),
        ],
        compiler_params=params(1),
        cost_estimate=cost(heads * total * total * 2 * 256 * 2, 4 * total * 256 * 2),
        name="attend",
    )(length, table, near, projected, projected, projected)


def attend_back(group, projected, length, table, near, grad_out, lse):
    total = projected.shape[0]
    heads = 4
    return pl.pallas_call(
        functools.partial(attend_back_kernel, group),
        grid=(1,),
        in_specs=block_specs(total, group)
        + [
            pl.BlockSpec((total, 256), lambda _: (0, group)),
            pl.BlockSpec((8, total), lambda _: (0, 0)),
        ],
        out_specs=[
            pl.BlockSpec((total, 768), lambda _: (0, 0)),
            pl.BlockSpec((heads, 3 * LB + 16, LB), lambda _: (0, 0, 0)),
        ],
        out_shape=[
            jax.ShapeDtypeStruct((total, 768), BF),
            jax.ShapeDtypeStruct((heads, 3 * LB + 16, LB), F32),
        ],
        scratch_shapes=[
            pltpu.VMEM((heads, 2 * total - LB, LB), F32),
            pltpu.VMEM((heads, 2 * total - LB, LB), F32),
            pltpu.VMEM((heads, total, 256), BF),
            pltpu.VMEM((256, total), BF),
            pltpu.VMEM((256, total), F32),
            pltpu.VMEM((total, heads * 256), BF),
            pltpu.VMEM((total, heads * 256), BF),
            pltpu.VMEM((total, 256), F32),
            pltpu.VMEM((total, 256), F32),
        ],
        compiler_params=params(1),
        cost_estimate=cost(heads * total * total * 2 * 256 * 5, 8 * total * 256 * 2),
        name="attend_back",
    )(length, table, near, projected, projected, projected, grad_out, lse)


def split_heads(projected, groups, heads):
    parts = projected.reshape(projected.shape[0], groups, 3, heads, 64)
    return [parts[:, :, i].reshape(projected.shape[0], groups * heads, 64) for i in range(3)]


def plain_scores(queries, keys, length, table):
    slots = jnp.arange(keys.shape[0], dtype=jnp.int32)
    picked = (bucket_index(slots[None, :] - slots[:, None])[:, :, None] == jnp.arange(32)).astype(F32)
    bias = jnp.einsum("qkb,hb->hqk", picked, table, precision=lax.Precision.HIGHEST)
    scores = jnp.einsum("qhs,khs->hqk", queries, keys, preferred_element_type=F32) + bias
    return jnp.where(slots < length[0], scores, masked_score), picked


def attend_plain(projected, length, table, groups, heads):
    queries, keys, values = split_heads(projected, groups, heads)
    scores, _ = plain_scores(queries, keys, length, table)
    lse = jax.nn.logsumexp(scores, axis=2)
    probs = jnp.exp(scores - lse[:, :, None]).astype(BF)
    out = jnp.einsum("hqk,khs->qhs", probs, values, preferred_element_type=F32)
    return out.astype(BF).reshape(projected.shape[0], -1), lse


def attend_back_plain(projected, length, table, grad_out, lse, groups, heads):
    total = projected.shape[0]
    queries, keys, values = split_heads(projected, groups, heads)
    grads = grad_out.reshape(queries.shape)
    scores, picked = plain_scores(queries, keys, length, table)
    probs = jnp.exp(scores - lse[:, :, None])
    weighed = probs * jnp.einsum("qhs,khs->hqk", grads, values, preferred_element_type=F32)
    wide = weighed - probs * jnp.sum(weighed, axis=2, keepdims=True)
    rounded = wide.astype(BF)
    parts = [
        jnp.einsum("hqk,khs->qhs", rounded, keys, preferred_element_type=F32),
        jnp.einsum("hqk,qhs->khs", rounded, queries, preferred_element_type=F32),
        jnp.einsum("hqk,qhs->khs", probs.astype(BF), grads, preferred_element_type=F32),
    ]
    parts = [part.astype(BF).reshape(total, groups, 1, heads * 64) for part in parts]
    table_grad = jnp.einsum("hqk,qkb->hb", wide, picked, precision=lax.Precision.HIGHEST)
    return (
        jnp.concatenate(parts, axis=2).reshape(total, -1),
        table_grad.reshape(groups * heads, 32, 1),
    )


def hop(value, axis):
    return lax.ppermute(value, axis, swap)


def pick(value, index, axis):
    return lax.dynamic_index_in_dim(value, index, axis, keepdims=False)


def paired(mine, other, axis, place=0):
    return jnp.where(
        lax.axis_index(axis) == 0,
        jnp.stack([mine, other], axis=place),
        jnp.stack([other, mine], axis=place),
    )


def after(value, *others):
    return lax.optimization_barrier((value, *others))[0]


def gather_plain(part, *beside):
    return lax.all_gather(part, ("x", "y"), axis=1, tiled=True), (), ()


def gather_tokens(part, *beside):
    half = part.shape[0] // 2
    low, high = part[:half], part[half:]
    low_x, high_y = hop(low, "x"), hop(high, "y")
    if beside:
        low_x, high_y = after(low_x, *beside), after(high_y, *beside)
    low_y, high_x = hop(low, "y"), hop(high, "x")
    low_xy, high_xy = hop(low_x, "y"), hop(high_y, "x")
    pieces = [low, low_y, low_x, low_xy, high, high_y, high_x, high_xy]
    return pieces, (low_x, high_y), (low_y, low_xy, high_x, high_xy)


def scatter_plain(parts, beside=(), beside_last=()):
    whole = parts[0].astype(F32)
    return lax.psum_scatter(whole, ("x", "y"), scatter_dimension=1, tiled=True), (), ()


def scatter_tokens(parts, beside=(), beside_last=()):
    low_out, low_keep, high_out, high_keep = parts
    low_in, high_in = hop(low_out, "x"), hop(high_out, "y")
    if beside:
        low_in, high_in = after(low_in, *beside), after(high_in, *beside)

    def add(keep, arrived, index):
        return keep[index].astype(F32) + arrived[index].astype(F32)

    low_last = hop(add(low_keep, low_in, 1).astype(BF), "y")
    high_last = hop(add(high_keep, high_in, 1).astype(BF), "x")
    if beside_last:
        low_last, high_last = after(low_last, *beside_last), after(high_last, *beside_last)
    low = add(low_keep, low_in, 0) + low_last.astype(F32)
    high = add(high_keep, high_in, 0) + high_last.astype(F32)
    return jnp.concatenate([low, high], axis=0), (low_in, high_in), (low_last, high_last)


def place_kernel(write, here_ref, *refs):
    pieces, outs = refs[:4], refs[4:]
    step = pl.program_id(0)
    for near in range(4):
        y = here_ref[0] if near < 2 else 1 - here_ref[0]
        c = here_ref[1] if near % 2 == 0 else 1 - here_ref[1]

        @pl.when(step == 2 * y + c)
        def _():
            write(pieces[near], outs)


def place(pieces, here, shapes, write):
    return pl.pallas_call(
        functools.partial(place_kernel, write),
        grid=(4,),
        in_specs=[pl.BlockSpec(memory_space=pltpu.SMEM)]
        + [pl.BlockSpec(piece.shape, lambda q: (0, 0)) for piece in pieces],
        out_specs=[
            pl.BlockSpec(shape, lambda q, rank=len(shape): (q,) + (0,) * (rank - 1)) for shape in shapes
        ],
        out_shape=[jax.ShapeDtypeStruct((4 * shape[0], *shape[1:]), F32) for shape in shapes],
        compiler_params=params(1),
        cost_estimate=cost(0, pieces[0].size),
        name="place",
    )(here, *pieces)


def share(part, *beside):
    over_y = hop(part, "y")
    if beside:
        over_y = after(over_y, *beside)
    return [part, hop(part, "c"), over_y, hop(over_y, "c")], over_y


def share_plain(part, *beside):
    return lax.all_gather(part, ("y", "c"), axis=0), part


def to_groups(halves, other, extra):
    count, _, t, width = halves.shape
    both = paired(pick(halves, lax.axis_index("y"), 1), other, "y").reshape(2 * count, t, width)
    if extra is not None:
        wide = jnp.broadcast_to(extra[None], (2 * count, *extra.shape))
        both = jnp.concatenate([both, wide], axis=1)
    return lax.all_to_all(both, "z", 0, 0, tiled=True)


def from_groups(mine):
    nz, t, width = mine.shape
    back = lax.all_to_all(mine, "z", 0, 0, tiled=True).reshape(2, nz // 2, t, width)
    leaving = pick(back, 1 - lax.axis_index("y"), 0)
    return (back, hop(leaving, "y")), leaving


def settle_kernel(y_ref, back_ref, other_ref, out_ref):
    j, y = pl.program_id(0), pl.program_id(1)

    @pl.when(y == y_ref[0])
    def _():
        out_ref[0, 0] = back_ref[y, j].astype(out_ref.dtype)

    @pl.when(y != y_ref[0])
    def _():
        out_ref[0, 0] = other_ref[j].astype(out_ref.dtype)


def settle(arrived, dtype):
    back, other = arrived
    _, count, t, width = back.shape
    y = lax.axis_index("y").astype(jnp.int32).reshape(1)
    out = pl.pallas_call(
        settle_kernel,
        grid=(count, 2),
        in_specs=[
            pl.BlockSpec(memory_space=pltpu.SMEM),
            pl.BlockSpec(back.shape, lambda j, y: (0, 0, 0, 0)),
            pl.BlockSpec(other.shape, lambda j, y: (0, 0, 0)),
        ],
        out_specs=pl.BlockSpec((1, 1, t, width), lambda j, y: (j, y, 0, 0)),
        out_shape=jax.ShapeDtypeStruct((count, 2, t, width), dtype),
        compiler_params=params(2),
        cost_estimate=cost(0, count * t * width),
        name="settle",
    )(y, back, other)
    return out.reshape(count, 2 * t, width)


def settle_plain(arrived, dtype):
    back, other = arrived
    _, count, t, width = back.shape
    both = paired(pick(back, lax.axis_index("y"), 0), other, "y")
    return both.transpose(1, 0, 2, 3).reshape(count, 2 * t, width).astype(dtype)


def sum_plane(value, nx, *earlier):
    value = value + after(hop(value, "c"), *earlier)
    value = value + hop(value, "x") if nx == 2 else lax.psum(value, "x")
    return value + hop(value, "y")


def sum_line(value, nz):
    step = 1
    while step < nz:
        value = value + lax.ppermute(value, "z", [(i, i ^ step) for i in range(nz)])
        step *= 2
    return value


def body(
    nx, nz, nc, inputs, lengths, attn_gain, ffn_gain, query_key, value_proj, out_proj, gate_up, down_proj, bias_table, cotangent
):
    x, y = lax.axis_index("x"), lax.axis_index("y")
    c, z = lax.axis_index("c"), lax.axis_index("z")
    width = inputs.shape[2]
    features = nz * width
    quarter = y * nc + c
    parts = 2 * nc
    buckets, mine = bias_table.shape
    count = inputs.shape[1] // 2

    stored_in = inputs.reshape(inputs.shape[0], 2, count, width)
    stored_cot = cotangent.reshape(stored_in.shape)
    small = jnp.concatenate(
        [attn_gain[None], ffn_gain[None], jnp.pad(bias_table.reshape(1, -1), ((0, 0), (0, width - buckets * mine)))]
    )
    small = jnp.pad(small, ((0, 5), (0, 0)))
    leaving = pick(stored_in, 1 - y, 1)

    query_key_rows = jnp.transpose(query_key, (1, 2, 3, 0))
    value_rows = jnp.transpose(value_proj, (1, 2, 0))
    gate_up_rows = jnp.transpose(gate_up, (1, 2, 3, 0))
    heads = value_rows.shape[0] // parts
    units = gate_up_rows.shape[0] // parts
    unit = gate_up_rows.shape[2]
    local_heads = nc * heads

    def own(rows, size):
        return lax.dynamic_slice_in_dim(rows, quarter * size, size, 0)

    def flat(rows):
        return rows.reshape(-1, width)

    def spread(rows):
        gathered = lax.all_gather(rows, ("z", "c"), axis=0, tiled=True)
        return gathered.reshape(nz, nc, rows.shape[0], width)

    own_pair = own(query_key_rows, heads)
    own_attn = [own_pair[:, 0], own_pair[:, 1], own(value_rows, heads), own(out_proj, heads)]
    own_attn = jnp.concatenate([flat(rows) for rows in own_attn])
    w_attn = spread(own_attn)
    other = after(hop(leaving, "y"), own_attn)
    own_pair = own(after(gate_up_rows, other), units)
    own_gate_up = jnp.concatenate([flat(own_pair[:, 0]), flat(own_pair[:, 1])])
    w_gate_up = spread(own_gate_up)
    own_down = flat(own(after(down_proj, other), units))
    w_down = spread(own_down)
    qkv_count, out_count = 3 * heads * 64, heads * 64

    both_lengths = jnp.stack([lengths, lax.ppermute(lengths, "y", swap)])
    both_lengths = jnp.where(y == 0, both_lengths, both_lengths[::-1]).reshape(-1)
    length = lax.dynamic_slice_in_dim(both_lengths, z, 1, 0)
    slots = (x * 2 + y) * count + jnp.arange(count, dtype=jnp.int32)
    near_x, near_y = jnp.array([0, 0, 1, 1]) ^ x, jnp.array([0, 1, 0, 1]) ^ y
    starts = ((near_x * 2 + near_y) * count).astype(jnp.int32)
    arrived = after(to_groups(stored_in, other, small), own_gate_up, own_down, length, starts)
    tokens = arrived[:, :count].astype(F32)
    small = arrived[:, count:]
    gain_one = small[:, :1].astype(F32)
    gain_two = small[:, 1:2].astype(F32)
    table = small[:, 2, : buckets * mine].reshape(nz, buckets, mine).transpose(0, 2, 1)
    table = table.reshape(-1, buckets).astype(F32)
    table = lax.dynamic_slice_in_dim(table, y * local_heads, local_heads, 0)

    live = (slots < length).astype(F32)[None, :, None]

    def scale_of(values):
        squares = jnp.sum(values * values, axis=(0, 2), keepdims=True)
        return lax.rsqrt(squares / features + norm_eps)

    def norm_back(values, scale, gain, grad):
        inner = jnp.sum(values * gain * grad, axis=(0, 2), keepdims=True)
        out = scale * gain * grad - values * (scale * scale * scale) * inner / features
        return out, jnp.sum(values * scale * grad, axis=1)

    def reduce(partial):
        rows = partial.reshape(nz * partial.shape[1], width)
        return lax.psum_scatter(rows, ("z", "c"), scatter_dimension=0, tiled=True)

    fits = nx == 2 and heads == 4 and count == 256 and units * unit % 640 == 0 and nz % 2 == 0
    if fits:
        forward, backward, gather, scatter = attend, attend_back, gather_tokens, scatter_tokens
        nt, nn, tn, ffn_one, ffn_two = mm_nt, mm_nn, mm_tn, ffn_in, ffn_back
        shared, stored_from = share, settle
    else:
        forward, backward, gather, scatter = attend_plain, attend_back_plain, gather_plain, scatter_plain
        nt, nn, tn, ffn_one, ffn_two = mm_nt_plain, mm_nn_plain, mm_tn_plain, ffn_in_plain, ffn_back_plain
        shared, stored_from = share_plain, settle_plain
    scale_one = scale_of(tokens)
    near = near_bias(table, 4 * count) if fits else table
    normed, _, _ = gather((tokens * scale_one * gain_one).astype(BF), near, live)
    cot_other = hop(pick(stored_cot, 1 - y, 1), "y")
    upstream = live * to_groups(stored_cot, after(cot_other, arrived), None).astype(F32)
    upstream_rounded = after(upstream.astype(BF), w_attn)
    projected = nt(normed, w_attn, 0, qkv_count, starts)
    if fits:
        first = forward(0, projected, length, table, near)
        grad_ffn, cot_first, cot_last = gather(upstream_rounded, first[0])
        second = forward(1, after(projected, first[0], *cot_first), length, table, near)
        attended, lse = (first[0], second[0]), (first[1], second[1])
    else:
        grad_ffn, _, cot_last = gather(upstream_rounded)
        attended, lse = forward(projected, length, table, nc, heads)
        attended = (attended,)
    heads_out = [after(attended[0], *cot_last), *attended[1:]]
    hidden = tokens + scatter(nn(heads_out, w_attn, qkv_count, out_count, starts))[0]
    scale_two = scale_of(hidden)
    normed_two, _, _ = gather((hidden * scale_two * gain_two).astype(BF))
    gate, up, activated = ffn_one(normed_two, w_gate_up, starts)

    down_partial = tn([activated], grad_ffn, starts)
    down_part = reduce(down_partial)
    grad_gate_up = ffn_two(grad_ffn, w_down, after(gate, down_partial), up, starts)
    two_parts = nn([grad_gate_up], w_gate_up, 0, 2 * units * unit, starts)
    grad_two, two_first, _ = scatter(two_parts)
    gate_up_partial = tn([after(grad_gate_up, two_parts[0])], normed_two, starts)
    gate_up_part = reduce(after(gate_up_partial, down_part, *two_first))
    branch_parts = nn([after(activated, gate_up_partial)], w_down, 0, units * unit, starts)
    through, ffn_gain_part = norm_back(hidden, scale_two, gain_two, grad_two)
    grad_hidden = upstream + through
    grad_branch, _, branch_here = gather(after(grad_hidden.astype(BF), branch_parts[0]))
    grad_attended = nt(grad_branch, w_attn, qkv_count, out_count, starts)
    out_partial = tn(attended, grad_branch, starts)
    grad_attended = after(grad_attended, out_partial)
    branch_parts = [after(part, *branch_here) for part in branch_parts]
    if fits:
        first = backward(0, projected, length, table, near, grad_attended, lse[0])
        branch, branch_first, branch_last = scatter(branch_parts, (first[0],))
    else:
        branch, branch_first, branch_last = scatter(branch_parts)
    down_pieces, down_last = shared(after(down_part, *branch_here))
    if fits:
        second = backward(
            1, after(projected, first[0], *branch_first), length, table, near, grad_attended, lse[1]
        )
        grad_projected, table_part = (first[0], second[0]), (first[1], second[1])
    else:
        grads, table_part = backward(projected, length, table, grad_attended, lse, nc, heads)
        grad_projected, table_part = (grads,), table_part[:, :, 0]
    out_part = reduce(after(out_partial, gate_up_part, grad_projected[-1], *branch_last, down_last))
    outputs = (live * (hidden + branch)).astype(BF)
    outputs, _ = from_groups(outputs)
    one_parts = nn(grad_projected, w_attn, 0, qkv_count, starts)
    last = after(grad_projected[-1], one_parts[0])
    qkv_partial = tn([*grad_projected[:-1], last], normed, starts)
    if fits:
        here = jnp.stack([y, c]).astype(jnp.int32)

        def write_rows(source, outs):
            outs[0][...] = source[...].astype(F32)

        def write_qkv(source, outs):
            for h in range(heads):
                for i in range(3):
                    value = source[(i * heads + h) * 64 : (i * heads + h + 1) * 64, :].astype(F32)
                    if i == 2:
                        outs[1][h] = value
                    else:
                        outs[0][h, i] = value

        def write_gate_up(source, outs):
            for u in range(units):
                for i in range(2):
                    first = (i * units + u) * unit
                    outs[0][u, i] = source[first : first + unit, :].astype(F32)

        (down_all,) = place(down_pieces, here, [(units * unit, width)], write_rows)
    beside = (qkv_partial, down_all, outputs[0]) if fits else ()
    table_part = table_sums(table_part, 4 * count) if fits else table_part
    grad_one, one_first, one_last = scatter(one_parts, beside, (table_part,))
    qkv_part = reduce(after(qkv_partial, gate_up_part, *one_first))
    through, attn_gain_part = norm_back(tokens, scale_one, gain_one, grad_one)
    input_grad, input_leaves = from_groups((grad_hidden + through).astype(BF))

    out_pieces, out_last = shared(out_part)
    gate_up_pieces, _ = shared(after(gate_up_part, *one_first), input_leaves)

    every = jnp.zeros((nx * 2 * local_heads, table_part.shape[1]), F32)
    every = lax.dynamic_update_slice_in_dim(every, table_part, (x * 2 + y) * local_heads, 0)
    spare = -every.size % width
    every = jnp.pad(every.reshape(-1), (0, spare)).reshape(-1, width)
    sums = sum_plane(jnp.concatenate([attn_gain_part, ffn_gain_part, every]), nx, out_last, outputs[1], input_grad[1])
    all_sums = sum_line(after(sums, input_leaves), nz)
    attn_gain_grad, ffn_gain_grad = all_sums[:nz], all_sums[nz : 2 * nz]
    every = all_sums[2 * nz :].reshape(-1)[: nx * 2 * local_heads * buckets].reshape(-1, buckets)

    outputs = stored_from(outputs, BF)
    if fits:
        (gate_up_all,) = place(gate_up_pieces, here, [(units, 2, unit, width)], write_gate_up)
        (out_all,) = place(out_pieces, here, [(heads * 64, width)], write_rows)
        qkv_pieces, _ = shared(after(qkv_part, sums, *one_last), out_all, gate_up_all, outputs, input_leaves)
        query_key_all, value_all = place(
            qkv_pieces, here, [(heads, 2, 64, width), (heads, 64, width)], write_qkv
        )
    else:
        down_all, out_all = down_pieces.astype(F32), out_pieces.astype(F32)
        gate_up_all = gate_up_pieces.astype(F32).reshape(parts, 2, units, unit, width)
        gate_up_all = gate_up_all.transpose(0, 2, 1, 3, 4).reshape(-1, 2, unit, width)
        qkv_all = shared(qkv_part)[0].astype(F32).reshape(parts, 3, heads, 64, width)
        qkv_all = qkv_all.transpose(0, 2, 1, 3, 4).reshape(-1, 3, 64, width)
        query_key_all, value_all = qkv_all[:, :2], qkv_all[:, 2]
    input_grad = stored_from(input_grad, F32)
    down_all, out_all = down_all.reshape(down_proj.shape), out_all.reshape(out_proj.shape)

    table_grad = lax.dynamic_slice_in_dim(every, (x * nz + z) * mine, mine, 0).T
    return (
        outputs,
        input_grad,
        pick(attn_gain_grad, z, 0),
        pick(ffn_gain_grad, z, 0),
        query_key_all.transpose(3, 0, 1, 2),
        value_all.transpose(2, 0, 1),
        out_all,
        gate_up_all.transpose(3, 0, 1, 2),
        down_all,
        table_grad,
    )


def solution(mesh):
    dp, nx, nz = (mesh.shape[name] for name in ("dp", "gx", "gy"))
    nc = dp // 2
    split = Mesh(mesh.devices.reshape(2, nc, nx, nz), ("y", "c", "x", "z"))
    seq = ("y", "c")
    return jax.shard_map(
        functools.partial(body, nx, nz, nc),
        mesh=split,
        in_specs=(
            P(seq, "x", "z"),
            P(seq),
            P("z"),
            P("z"),
            P("z", "x", None, None),
            P("z", "x", None),
            P("x", None, "z"),
            P("z", "x", None, None),
            P("x", None, "z"),
            P(None, ("x", "z")),
            P(seq, "x", "z"),
        ),
        out_specs=(
            P(seq, "x", "z"),
            P(seq, "x", "z"),
            P("z"),
            P("z"),
            P("z", "x", None, None),
            P("z", "x", None),
            P("x", None, "z"),
            P("z", "x", None, None),
            P("x", None, "z"),
            P(None, ("x", "z")),
        ),
        check_vma=False,
    )
```

```python
import functools
import math

import jax
import jax.numpy as jnp
from jax import lax
from jax.experimental import pallas as pl
from jax.experimental.pallas import tpu as pltpu
from jax.sharding import Mesh
from jax.sharding import PartitionSpec as P

norm_eps = 1e-06
masked_score = -1e30
bucket_edges = (12, 16, 23, 32, 46, 64, 91)
BF = jnp.bfloat16
F32 = jnp.float32
LB = 128
VMEM = 60 * 1024 * 1024
swap = [(0, 1), (1, 0)]
gelu_a = math.sqrt(2.0 / math.pi)
gelu_b = 0.044715


def bucket_index(offset):
    magnitude = jnp.abs(offset)
    far_bucket = 8 + sum(((magnitude >= boundary).astype(jnp.int32) for boundary in bucket_edges))
    near_bucket = jnp.where(magnitude < 8, magnitude, far_bucket)
    return near_bucket + 16 * (offset > 0).astype(jnp.int32)


def cost(flops, moved):
    return pl.CostEstimate(flops=int(flops) // 16, bytes_accessed=int(moved) // 16, transcendentals=0)


def params(steps):
    return pltpu.CompilerParams(
        dimension_semantics=("arbitrary",) * steps, vmem_limit_bytes=VMEM
    )


def dot_nt(a, b):
    return lax.dot_general(a, b, (((1,), (1,)), ((), ())), preferred_element_type=F32)


def dot_nn(a, b):
    return lax.dot_general(a, b, (((1,), (0,)), ((), ())), preferred_element_type=F32)


def spot_of(starts_ref, d, count):
    return pl.ds(pl.multiple_of(starts_ref[d], 256), count)


def piece_specs(pieces):
    shape = pieces[0].shape
    return [pl.BlockSpec(shape, lambda *_: (0, 0, 0)) for _ in pieces]


def nt_sum(piece_refs, d, w_of):
    half = piece_refs[0].shape[0]
    acc = None
    for z in range(2 * half):
        part = dot_nt(piece_refs[4 * (z // half) + d][z % half], w_of(z))
        acc = part if acc is None else acc + part
    return acc


def nt_kernel(starts_ref, *refs):
    pieces, (w_ref, out_ref) = refs[:8], refs[8:]
    for d in range(4):
        acc = nt_sum(pieces, d, lambda z: w_ref[z, 0])
        out_ref[spot_of(starts_ref, d, acc.shape[0]), :] = acc.astype(BF)


def mm_nt(pieces, w, first, rows, starts):
    nz, nc, _, width = w.shape
    total = 4 * pieces[0].shape[1]
    count, skip = rows // 256, first // 256
    return pl.pallas_call(
        nt_kernel,
        grid=(nc, count),
        in_specs=[pl.BlockSpec(memory_space=pltpu.SMEM)]
        + piece_specs(pieces)
        + [pl.BlockSpec((nz, 1, 256, width), lambda c, i: (0, c, skip + i, 0))],
        out_specs=pl.BlockSpec((total, 256), lambda c, i: (0, c * count + i)),
        out_shape=jax.ShapeDtypeStruct((total, nc * rows), BF),
        compiler_params=params(2),
        cost_estimate=cost(
            2 * nz * total * width * nc * rows, 2 * nz * width * (total + nc * rows) + 2 * total * nc * rows
        ),
        name="product_nt",
    )(starts, *pieces, w)


def nn_kernel(count, starts_ref, *refs):
    grads, (w_ref, low_out, low_keep, high_out, high_keep) = refs[:count], refs[count:]
    nc, rows, width = w_ref.shape[1:]
    t = grads[0].shape[0] // 4
    in_low = pl.program_id(0) < pl.num_programs(0) // 2

    def product(d):
        spot = spot_of(starts_ref, d, t)
        if count == 1:
            return dot_nn(grads[0][spot, :], w_ref[0].reshape(nc * rows, width)).astype(BF)
        return sum(dot_nn(grads[c][spot, :], w_ref[0, c]) for c in range(count)).astype(BF)

    @pl.when(in_low)
    def _():
        for d in range(4):
            (low_out if d // 2 else low_keep)[d % 2, 0] = product(d)

    @pl.when(jnp.logical_not(in_low))
    def _():
        for d in range(4):
            (high_out if d % 2 else high_keep)[d // 2, 0] = product(d)


def mm_nn(grads, w, first, rows, starts):
    total = grads[0].shape[0]
    nz, nc, _, width = w.shape
    skip, half, t = first // rows, nz // 2, total // 4
    low = pl.BlockSpec((2, 1, t, width), lambda z: (0, jnp.minimum(z, half - 1), 0, 0))
    high = pl.BlockSpec((2, 1, t, width), lambda z: (0, jnp.maximum(z - half, 0), 0, 0))
    return pl.pallas_call(
        functools.partial(nn_kernel, len(grads)),
        grid=(nz,),
        in_specs=[pl.BlockSpec(memory_space=pltpu.SMEM)]
        + [pl.BlockSpec(grad.shape, lambda z: (0, 0)) for grad in grads]
        + [pl.BlockSpec((1, nc, rows, width), lambda z: (z, 0, skip, 0))],
        out_specs=[low, low, high, high],
        out_shape=[jax.ShapeDtypeStruct((2, half, t, width), BF)] * 4,
        compiler_params=params(1),
        cost_estimate=cost(
            2 * nz * total * width * nc * rows, 2 * nz * width * (total + nc * rows) + 2 * total * nc * rows
        ),
        name="product_nn",
    )(starts, *grads, w)


def tn_kernel(count, starts_ref, *refs):
    grads, pieces, out_ref = refs[:count], refs[count:-1], refs[-1]
    half, t, _ = pieces[0].shape

    def one(grad_ref):
        turned = [grad_ref[spot_of(starts_ref, d, t), :].T for d in range(4)]
        for z in range(2 * half):
            acc = dot_nn(turned[0], pieces[4 * (z // half)][z % half])
            for d in range(1, 4):
                acc += dot_nn(turned[d], pieces[4 * (z // half) + d][z % half])
            out_ref[z] = acc.astype(BF)

    if count == 1:
        one(grads[0])
    else:
        for c in range(count):

            @pl.when(pl.program_id(0) // (pl.num_programs(0) // count) == c)
            def _():
                one(grads[c])


def mm_tn(grads, pieces, starts):
    total, rows = grads[0].shape
    half, _, width = pieces[0].shape
    nz, count = 2 * half, len(grads)
    block = next(b for b in (640, 384, 256) if rows % b == 0)
    steps = rows // block

    def spec(c):
        return pl.BlockSpec((total, block), lambda i: (0, jnp.clip(i - c * steps, 0, steps - 1)))

    return pl.pallas_call(
        functools.partial(tn_kernel, count),
        grid=(count * steps,),
        in_specs=[pl.BlockSpec(memory_space=pltpu.SMEM)]
        + [spec(c) for c in range(count)]
        + piece_specs(pieces),
        out_specs=pl.BlockSpec((nz, block, width), lambda i: (0, i, 0)),
        out_shape=jax.ShapeDtypeStruct((nz, count * rows, width), BF),
        compiler_params=params(1),
        cost_estimate=cost(
            2 * nz * total * width * count * rows, 2 * nz * width * (total + count * rows) + 2 * total * count * rows
        ),
        name="product_tn",
    )(starts, *grads, *pieces)


def gelu_parts(gate):
    curve = jnp.tanh(gelu_a * (gate + gelu_b * gate * gate * gate))
    value = 0.5 * gate * (1.0 + curve)
    slope = 0.5 * (1.0 + curve) + 0.5 * gate * (1.0 - curve * curve) * gelu_a * (
        1.0 + 3.0 * gelu_b * gate * gate
    )
    return value, slope


def ffn_in_kernel(starts_ref, *refs):
    pieces, (w_ref, gate_ref, up_ref, active_ref) = refs[:8], refs[8:]
    _, _, _, block, width = w_ref.shape
    for d in range(4):
        acc = nt_sum(pieces, d, lambda z: w_ref[z, 0].reshape(2 * block, width))
        spot = spot_of(starts_ref, d, acc.shape[0])
        gate, up = acc[:, :block], acc[:, block:]
        value = 0.5 * gate * (1.0 + jnp.tanh(gelu_a * (gate + gelu_b * gate * gate * gate)))
        gate_ref[spot, :] = gate.astype(BF)
        up_ref[spot, :] = up.astype(BF)
        active_ref[spot, :] = (value * up).astype(BF)


def ffn_in(pieces, w, starts):
    nz, nc, rows, width = w.shape
    half, total = rows // 2, 4 * pieces[0].shape[1]
    count = half // 128
    block = pl.BlockSpec((total, 128), lambda c, i: (0, c * count + i))
    return pl.pallas_call(
        ffn_in_kernel,
        grid=(nc, count),
        in_specs=[pl.BlockSpec(memory_space=pltpu.SMEM)]
        + piece_specs(pieces)
        + [pl.BlockSpec((nz, 1, 2, 128, width), lambda c, i: (0, c, 0, i, 0))],
        out_specs=[block, block, block],
        out_shape=[jax.ShapeDtypeStruct((total, nc * half), BF)] * 3,
        compiler_params=params(2),
        cost_estimate=cost(
            2 * nz * total * width * nc * rows, 2 * nz * width * (total + nc * rows) + 3 * total * nc * rows
        ),
        name="ffn_in",
    )(starts, *pieces, w.reshape(nz, nc, 2, half, width))


def ffn_back_kernel(starts_ref, *refs):
    pieces, (w_ref, gate_ref, up_ref, out_ref) = refs[:8], refs[8:]
    half = w_ref.shape[2]
    for d in range(4):
        acc = nt_sum(pieces, d, lambda z: w_ref[z, 0])
        spot = spot_of(starts_ref, d, acc.shape[0])
        value, slope = gelu_parts(gate_ref[spot, :].astype(F32))
        out_ref[spot, :half] = (acc * up_ref[spot, :].astype(F32) * slope).astype(BF)
        out_ref[spot, half:] = (acc * value).astype(BF)


def ffn_back(pieces, w, gate, up, starts):
    nz, nc, half, width = w.shape
    total = gate.shape[0]
    kept = pl.BlockSpec((total, half), lambda c: (0, c))
    return pl.pallas_call(
        ffn_back_kernel,
        grid=(nc,),
        in_specs=[pl.BlockSpec(memory_space=pltpu.SMEM)]
        + piece_specs(pieces)
        + [pl.BlockSpec((nz, 1, half, width), lambda c: (0, c, 0, 0)), kept, kept],
        out_specs=pl.BlockSpec((total, 2 * half), lambda c: (0, c)),
        out_shape=jax.ShapeDtypeStruct((total, nc * 2 * half), BF),
        compiler_params=params(1),
        cost_estimate=cost(
            2 * nz * total * width * nc * half, 2 * nz * width * (total + nc * half) + 8 * total * nc * half
        ),
        name="ffn_back",
    )(starts, *pieces, w, gate, up)


def mm_nt_plain(act, w, first, rows, starts):
    part = lax.slice_in_dim(w, first, first + rows, axis=2)
    out = jnp.einsum("ztf,zcrf->tcr", act, part, preferred_element_type=F32)
    return out.astype(BF).reshape(act.shape[1], -1)


def mm_nn_plain(grads, w, first, rows, starts):
    grad = grads[0]
    part = lax.slice_in_dim(w, first, first + rows, axis=2)
    split = grad.reshape(grad.shape[0], w.shape[1], rows)
    out = jnp.einsum("tcr,zcrf->ztf", split, part, preferred_element_type=F32)
    return [out.astype(BF)]


def mm_tn_plain(grads, act, starts):
    return jnp.einsum("tr,ztf->zrf", grads[0], act, preferred_element_type=F32).astype(BF)


def ffn_in_plain(act, w, starts):
    _, nc, rows, _ = w.shape
    total = act.shape[1]
    both = jnp.einsum("ztf,zcrf->tcr", act, w, preferred_element_type=F32)
    gate, up = both[:, :, : rows // 2], both[:, :, rows // 2 :]
    value, _ = gelu_parts(gate)
    return [part.astype(BF).reshape(total, -1) for part in (gate, up, value * up)]


def ffn_back_plain(act, w, gate, up, starts):
    total, nc = gate.shape[0], w.shape[1]
    grad = jnp.einsum("ztf,zcrf->tcr", act, w, preferred_element_type=F32)
    value, slope = gelu_parts(gate.astype(F32).reshape(grad.shape))
    both = [grad * up.astype(F32).reshape(grad.shape) * slope, grad * value]
    return jnp.concatenate(both, axis=2).astype(BF).reshape(total, -1)


def near_buckets(tile, total):
    first = (total // LB - 2 + tile) * LB
    rows = lax.broadcasted_iota(jnp.int32, (LB, LB), 0)
    lanes = lax.broadcasted_iota(jnp.int32, (LB, LB), 1)
    return bucket_index(first + rows - (total - LB) - lanes)


def near_kernel(total, table_ref, out_ref):
    heads = out_ref.shape[0]

    def one_tile(tile, _):
        index = near_buckets(tile, total)
        vals = [jnp.full((LB, LB), table_ref[h, 0], F32) for h in range(heads)]
        for b in range(1, 32):
            hit = index == b
            vals = [jnp.where(hit, table_ref[h, b], vals[h]) for h in range(heads)]
        for h in range(heads):
            out_ref[h, pl.ds(pl.multiple_of(tile * LB, LB), LB)] = vals[h]
        return 0

    lax.fori_loop(0, 3, one_tile, 0)


def near_bias(table, total):
    heads = table.shape[0]
    return pl.pallas_call(
        functools.partial(near_kernel, total),
        in_specs=[pl.BlockSpec(memory_space=pltpu.SMEM)],
        out_specs=pl.BlockSpec((heads, 3 * LB, LB), lambda: (0, 0, 0)),
        out_shape=jax.ShapeDtypeStruct((heads, 3 * LB, LB), F32),
        compiler_params=params(0),
        cost_estimate=cost(0, heads * LB * LB),
        name="near_bias",
    )(table)


def build_strips(table_ref, near_ref, strip_ref, total, group):
    heads = strip_ref.shape[0]
    near = (total // LB - 2) * LB
    for h in range(heads):
        head = group * heads + h
        strip_ref[h, :near] = jnp.full((near, LB), table_ref[head, 15], F32)
        strip_ref[h, near : near + 3 * LB] = near_ref[h]
        strip_ref[h, near + 3 * LB :] = jnp.full((near, LB), table_ref[head, 31], F32)


def table_kernel(total, *refs):
    parts, out_ref = refs[:-1], refs[-1]
    index = [near_buckets(tile, total) for tile in range(3)]
    buckets = [range(1, 16), [b for b in range(32) if b != 16], range(17, 32)]
    for g, part_ref in enumerate(parts):
        heads = part_ref.shape[0]

        def one_head(h, _):
            here = g * heads + h
            out_ref[here] = jnp.zeros((32, LB), F32)
            out_ref[here, 15:16] = part_ref[h, 3 * LB : 3 * LB + 1]
            out_ref[here, 31:32] = part_ref[h, 3 * LB + 8 : 3 * LB + 9]
            for tile in range(3):
                grads = part_ref[h, tile * LB : (tile + 1) * LB]
                for b in buckets[tile]:
                    picked = jnp.where(index[tile] == b, grads, 0.0)
                    out_ref[here, b : b + 1] += jnp.sum(picked, axis=0, keepdims=True)
            return 0

        lax.fori_loop(0, heads, one_head, 0)


def table_sums(parts, total):
    heads = len(parts) * parts[0].shape[0]
    out = pl.pallas_call(
        functools.partial(table_kernel, total),
        in_specs=[pl.BlockSpec(part.shape, lambda: (0, 0, 0)) for part in parts],
        out_specs=pl.BlockSpec((heads, 32, LB), lambda: (0, 0, 0)),
        out_shape=jax.ShapeDtypeStruct((heads, 32, LB), F32),
        compiler_params=params(0),
        cost_estimate=cost(0, heads * LB * LB),
        name="table_sums",
    )(*parts)
    return jnp.sum(out, axis=2)


def head_lanes(shape, h):
    lanes = lax.broadcasted_iota(jnp.int32, shape, 1)
    return lanes // 64 == h, lanes == ((h + 1) % 4) * 64


def mask_keys(keys, length, h):
    own, spare = head_lanes(keys.shape, h)
    dead = lax.broadcasted_iota(jnp.int32, keys.shape, 0) >= length
    mask = jnp.where(jnp.logical_and(spare, dead), masked_score, 0.0)
    return jnp.where(own, keys.astype(F32), mask).astype(BF)


def with_one(queries, h):
    _, spare = head_lanes(queries.shape, h)
    return jnp.where(spare, 1.0, queries.astype(F32)).astype(BF)


def own_lanes(values, h):
    own, _ = head_lanes(values.shape, h)
    return jnp.where(own, values.astype(F32), 0.0).astype(BF)


def block_bias(strip_ref, h, block, total):
    first = total - LB - 2 * block * LB
    left = strip_ref[h, pl.ds(pl.multiple_of(first, LB), total)]
    right = strip_ref[h, pl.ds(pl.multiple_of(first - LB, LB), total)]
    return jnp.concatenate([left, right], axis=1)


def attend_kernel(group, length_ref, table_ref, near_ref, q_ref, k_ref, v_ref, out_ref, lse_ref, strip, heads_k, turned_v, turned_out):
    total = q_ref.shape[0]
    heads = strip.shape[0]
    build_strips(table_ref, near_ref, strip, total, group)
    turned_v[...] = v_ref[...].astype(F32).T.astype(BF)
    for h in range(heads):
        heads_k[h] = mask_keys(k_ref[...], length_ref[0], h)

    def one_block(block, _):
        spot = pl.ds(pl.multiple_of(block * 256, 256), 256)
        queries = q_ref[spot]
        for h in range(heads):
            scores = dot_nt(heads_k[h], with_one(queries, h)) + block_bias(strip, h, block, total)
            largest = jnp.max(scores, axis=0, keepdims=True)
            raised = jnp.exp(scores - largest)
            totals = jnp.sum(raised, axis=0, keepdims=True)
            out = dot_nn(turned_v[h * 64 : (h + 1) * 64], raised.astype(BF))
            turned_out[h * 64 : (h + 1) * 64, spot] = out * (1.0 / totals)
            lse_ref[h : h + 1, spot] = largest + jnp.log(totals)
        return 0

    lax.fori_loop(0, total // 256, one_block, 0)
    out_ref[...] = turned_out[...].T.astype(BF)


def attend_back_kernel(
    group, length_ref, table_ref, near_ref, q_ref, k_ref, v_ref, grad_ref, lse_ref, out_ref, table_grad_ref,
    strip, strip_grad, heads_k, turned_k, turned_q, ds_ref, p_ref, dk_ref, dv_ref,
):
    total = q_ref.shape[0]
    heads = strip.shape[0]
    build_strips(table_ref, near_ref, strip, total, group)
    strip_grad[...] = jnp.zeros_like(strip_grad)
    dk_ref[...] = jnp.zeros_like(dk_ref)
    dv_ref[...] = jnp.zeros_like(dv_ref)
    turned_k[...] = k_ref[...].astype(F32).T.astype(BF)
    for h in range(heads):
        heads_k[h] = mask_keys(k_ref[...], length_ref[0], h)

    def one_block(block, _):
        spot = pl.ds(pl.multiple_of(block * 256, 256), 256)
        queries, grads = q_ref[spot], grad_ref[spot]
        own_q, own_g = [], []
        for h in range(heads):
            own_q.append(own_lanes(queries, h))
            own_g.append(own_lanes(grads, h))
            scores = dot_nt(heads_k[h], with_one(queries, h)) + block_bias(strip, h, block, total)
            probs = jnp.exp(scores - lse_ref[h : h + 1, spot])
            weighed = probs * dot_nt(v_ref[...], own_g[h])
            delta = jnp.sum(weighed, axis=0, keepdims=True)
            grad_scores = weighed - probs * delta
            first = total - LB - 2 * block * LB
            left = pl.ds(pl.multiple_of(first, LB), total)
            right = pl.ds(pl.multiple_of(first - LB, LB), total)
            strip_grad[h, left] += grad_scores[:, :LB]
            strip_grad[h, right] += grad_scores[:, LB:]
            rounded = grad_scores.astype(BF)
            ds_ref[:, h * 256 : (h + 1) * 256] = rounded
            p_ref[:, h * 256 : (h + 1) * 256] = probs.astype(BF)
            turned_q[h * 64 : (h + 1) * 64, spot] = dot_nn(turned_k[h * 64 : (h + 1) * 64], rounded)
        dk_ref[...] += dot_nn(ds_ref[...], jnp.concatenate(own_q, axis=0))
        dv_ref[...] += dot_nn(p_ref[...], jnp.concatenate(own_g, axis=0))
        return 0

    lax.fori_loop(0, total // 256, one_block, 0)
    out_ref[:, :256] = turned_q[...].T.astype(BF)
    out_ref[:, 256:512] = dk_ref[...].astype(BF)
    out_ref[:, 512:] = dv_ref[...].astype(BF)

    near = (total // LB - 2) * LB
    for h in range(heads):
        table_grad_ref[h, : 3 * LB] = strip_grad[h, near : near + 3 * LB]
        left = jnp.sum(strip_grad[h, :near], axis=0, keepdims=True)
        right = jnp.sum(strip_grad[h, near + 3 * LB :], axis=0, keepdims=True)
        table_grad_ref[h, 3 * LB : 3 * LB + 8] = jnp.broadcast_to(left, (8, LB))
        table_grad_ref[h, 3 * LB + 8 :] = jnp.broadcast_to(right, (8, LB))


def block_specs(total, group):
    def spec(i):
        return pl.BlockSpec((total, 256), lambda _: (0, 3 * group + i))

    smem = pl.BlockSpec(memory_space=pltpu.SMEM)
    near = pl.BlockSpec((4, 3 * LB, LB), lambda _: (group, 0, 0))
    return [smem, smem, near, spec(0), spec(1), spec(2)]


def attend(group, projected, length, table, near):
    total = projected.shape[0]
    heads = 4
    return pl.pallas_call(
        functools.partial(attend_kernel, group),
        grid=(1,),
        in_specs=block_specs(total, group),
        out_specs=[
            pl.BlockSpec((total, 256), lambda _: (0, 0)),
            pl.BlockSpec((8, total), lambda _: (0, 0)),
        ],
        out_shape=[
            jax.ShapeDtypeStruct((total, 256), BF),
            jax.ShapeDtypeStruct((8, total), F32),
        ],
        scratch_shapes=[
            pltpu.VMEM((heads, 2 * total - LB, LB), F32),
            pltpu.VMEM((heads, total, 256), BF),
            pltpu.VMEM((256, total), BF),
            pltpu.VMEM((256, total), F32),
        ],
        compiler_params=params(1),
        cost_estimate=cost(heads * total * total * 2 * 256 * 2, 4 * total * 256 * 2),
        name="attend",
    )(length, table, near, projected, projected, projected)


def attend_back(group, projected, length, table, near, grad_out, lse):
    total = projected.shape[0]
    heads = 4
    return pl.pallas_call(
        functools.partial(attend_back_kernel, group),
        grid=(1,),
        in_specs=block_specs(total, group)
        + [
            pl.BlockSpec((total, 256), lambda _: (0, group)),
            pl.BlockSpec((8, total), lambda _: (0, 0)),
        ],
        out_specs=[
            pl.BlockSpec((total, 768), lambda _: (0, 0)),
            pl.BlockSpec((heads, 3 * LB + 16, LB), lambda _: (0, 0, 0)),
        ],
        out_shape=[
            jax.ShapeDtypeStruct((total, 768), BF),
            jax.ShapeDtypeStruct((heads, 3 * LB + 16, LB), F32),
        ],
        scratch_shapes=[
            pltpu.VMEM((heads, 2 * total - LB, LB), F32),
            pltpu.VMEM((heads, 2 * total - LB, LB), F32),
            pltpu.VMEM((heads, total, 256), BF),
            pltpu.VMEM((256, total), BF),
            pltpu.VMEM((256, total), F32),
            pltpu.VMEM((total, heads * 256), BF),
            pltpu.VMEM((total, heads * 256), BF),
            pltpu.VMEM((total, 256), F32),
            pltpu.VMEM((total, 256), F32),
        ],
        compiler_params=params(1),
        cost_estimate=cost(heads * total * total * 2 * 256 * 5, 8 * total * 256 * 2),
        name="attend_back",
    )(length, table, near, projected, projected, projected, grad_out, lse)


def split_heads(projected, groups, heads):
    parts = projected.reshape(projected.shape[0], groups, 3, heads, 64)
    return [parts[:, :, i].reshape(projected.shape[0], groups * heads, 64) for i in range(3)]


def plain_scores(queries, keys, length, table):
    slots = jnp.arange(keys.shape[0], dtype=jnp.int32)
    picked = (bucket_index(slots[None, :] - slots[:, None])[:, :, None] == jnp.arange(32)).astype(F32)
    bias = jnp.einsum("qkb,hb->hqk", picked, table, precision=lax.Precision.HIGHEST)
    scores = jnp.einsum("qhs,khs->hqk", queries, keys, preferred_element_type=F32) + bias
    return jnp.where(slots < length[0], scores, masked_score), picked


def attend_plain(projected, length, table, groups, heads):
    queries, keys, values = split_heads(projected, groups, heads)
    scores, _ = plain_scores(queries, keys, length, table)
    lse = jax.nn.logsumexp(scores, axis=2)
    probs = jnp.exp(scores - lse[:, :, None]).astype(BF)
    out = jnp.einsum("hqk,khs->qhs", probs, values, preferred_element_type=F32)
    return out.astype(BF).reshape(projected.shape[0], -1), lse


def attend_back_plain(projected, length, table, grad_out, lse, groups, heads):
    total = projected.shape[0]
    queries, keys, values = split_heads(projected, groups, heads)
    grads = grad_out.reshape(queries.shape)
    scores, picked = plain_scores(queries, keys, length, table)
    probs = jnp.exp(scores - lse[:, :, None])
    weighed = probs * jnp.einsum("qhs,khs->hqk", grads, values, preferred_element_type=F32)
    wide = weighed - probs * jnp.sum(weighed, axis=2, keepdims=True)
    rounded = wide.astype(BF)
    parts = [
        jnp.einsum("hqk,khs->qhs", rounded, keys, preferred_element_type=F32),
        jnp.einsum("hqk,qhs->khs", rounded, queries, preferred_element_type=F32),
        jnp.einsum("hqk,qhs->khs", probs.astype(BF), grads, preferred_element_type=F32),
    ]
    parts = [part.astype(BF).reshape(total, groups, 1, heads * 64) for part in parts]
    table_grad = jnp.einsum("hqk,qkb->hb", wide, picked, precision=lax.Precision.HIGHEST)
    return (
        jnp.concatenate(parts, axis=2).reshape(total, -1),
        table_grad.reshape(groups * heads, 32, 1),
    )


def hop(value, axis):
    return lax.ppermute(value, axis, swap)


def pick(value, index, axis):
    return lax.dynamic_index_in_dim(value, index, axis, keepdims=False)


def paired(mine, other, axis, place=0):
    return jnp.where(
        lax.axis_index(axis) == 0,
        jnp.stack([mine, other], axis=place),
        jnp.stack([other, mine], axis=place),
    )


def after(value, *others):
    return lax.optimization_barrier((value, *others))[0]


def gather_plain(part, *beside):
    return lax.all_gather(part, ("x", "y"), axis=1, tiled=True), (), ()


def gather_tokens(part, *beside):
    half = part.shape[0] // 2
    low, high = part[:half], part[half:]
    low_x, high_y = hop(low, "x"), hop(high, "y")
    if beside:
        low_x, high_y = after(low_x, *beside), after(high_y, *beside)
    low_y, high_x = hop(low, "y"), hop(high, "x")
    low_xy, high_xy = hop(low_x, "y"), hop(high_y, "x")
    pieces = [low, low_y, low_x, low_xy, high, high_y, high_x, high_xy]
    return pieces, (low_x, high_y), (low_y, low_xy, high_x, high_xy)


def scatter_plain(parts, beside=(), beside_last=()):
    whole = parts[0].astype(F32)
    return lax.psum_scatter(whole, ("x", "y"), scatter_dimension=1, tiled=True), (), ()


def scatter_tokens(parts, beside=(), beside_last=()):
    low_out, low_keep, high_out, high_keep = parts
    low_in, high_in = hop(low_out, "x"), hop(high_out, "y")
    if beside:
        low_in, high_in = after(low_in, *beside), after(high_in, *beside)

    def add(keep, arrived, index):
        return keep[index].astype(F32) + arrived[index].astype(F32)

    low_last = hop(add(low_keep, low_in, 1).astype(BF), "y")
    high_last = hop(add(high_keep, high_in, 1).astype(BF), "x")
    if beside_last:
        low_last, high_last = after(low_last, *beside_last), after(high_last, *beside_last)
    low = add(low_keep, low_in, 0) + low_last.astype(F32)
    high = add(high_keep, high_in, 0) + high_last.astype(F32)
    return jnp.concatenate([low, high], axis=0), (low_in, high_in), (low_last, high_last)


def place_kernel(write, here_ref, *refs):
    pieces, outs = refs[:4], refs[4:]
    step = pl.program_id(0)
    for near in range(4):
        y = here_ref[0] if near < 2 else 1 - here_ref[0]
        c = here_ref[1] if near % 2 == 0 else 1 - here_ref[1]

        @pl.when(step == 2 * y + c)
        def _():
            write(pieces[near], outs)


def place(pieces, here, shapes, write):
    return pl.pallas_call(
        functools.partial(place_kernel, write),
        grid=(4,),
        in_specs=[pl.BlockSpec(memory_space=pltpu.SMEM)]
        + [pl.BlockSpec(piece.shape, lambda q: (0, 0)) for piece in pieces],
        out_specs=[
            pl.BlockSpec(shape, lambda q, rank=len(shape): (q,) + (0,) * (rank - 1)) for shape in shapes
        ],
        out_shape=[jax.ShapeDtypeStruct((4 * shape[0], *shape[1:]), F32) for shape in shapes],
        compiler_params=params(1),
        cost_estimate=cost(0, pieces[0].size),
        name="place",
    )(here, *pieces)


def share(part, *beside):
    over_y = hop(part, "y")
    if beside:
        over_y = after(over_y, *beside)
    return [part, hop(part, "c"), over_y, hop(over_y, "c")], over_y


def share_plain(part):
    return lax.all_gather(part, ("y", "c"), axis=0), part


def to_groups(halves, other, extra):
    count, _, t, width = halves.shape
    both = paired(pick(halves, lax.axis_index("y"), 1), other, "y").reshape(2 * count, t, width)
    if extra is not None:
        wide = jnp.broadcast_to(extra[None], (2 * count, *extra.shape))
        both = jnp.concatenate([both, wide], axis=1)
    return lax.all_to_all(both, "z", 0, 0, tiled=True)


def from_groups(mine):
    nz, t, width = mine.shape
    back = lax.all_to_all(mine, "z", 0, 0, tiled=True).reshape(2, nz // 2, t, width)
    leaving = pick(back, 1 - lax.axis_index("y"), 0)
    return (back, hop(leaving, "y")), leaving


def settle_kernel(y_ref, back_ref, other_ref, out_ref):
    j, y = pl.program_id(0), pl.program_id(1)

    @pl.when(y == y_ref[0])
    def _():
        out_ref[0, 0] = back_ref[y, j].astype(out_ref.dtype)

    @pl.when(y != y_ref[0])
    def _():
        out_ref[0, 0] = other_ref[j].astype(out_ref.dtype)


def settle(arrived, dtype):
    back, other = arrived
    _, count, t, width = back.shape
    y = lax.axis_index("y").astype(jnp.int32).reshape(1)
    out = pl.pallas_call(
        settle_kernel,
        grid=(count, 2),
        in_specs=[
            pl.BlockSpec(memory_space=pltpu.SMEM),
            pl.BlockSpec(back.shape, lambda j, y: (0, 0, 0, 0)),
            pl.BlockSpec(other.shape, lambda j, y: (0, 0, 0)),
        ],
        out_specs=pl.BlockSpec((1, 1, t, width), lambda j, y: (j, y, 0, 0)),
        out_shape=jax.ShapeDtypeStruct((count, 2, t, width), dtype),
        compiler_params=params(2),
        cost_estimate=cost(0, count * t * width),
        name="settle",
    )(y, back, other)
    return out.reshape(count, 2 * t, width)


def settle_plain(arrived, dtype):
    back, other = arrived
    _, count, t, width = back.shape
    both = paired(pick(back, lax.axis_index("y"), 0), other, "y")
    return both.transpose(1, 0, 2, 3).reshape(count, 2 * t, width).astype(dtype)


def sum_plane(value, nx, *earlier):
    value = value + after(hop(value, "c"), *earlier)
    value = value + hop(value, "x") if nx == 2 else lax.psum(value, "x")
    return value + hop(value, "y")


def sum_line(value, nz):
    step = 1
    while step < nz:
        value = value + lax.ppermute(value, "z", [(i, i ^ step) for i in range(nz)])
        step *= 2
    return value


def body(
    nx, nz, nc, inputs, lengths, attn_gain, ffn_gain, query_key, value_proj, out_proj, gate_up, down_proj, bias_table, cotangent
):
    x, y = lax.axis_index("x"), lax.axis_index("y")
    c, z = lax.axis_index("c"), lax.axis_index("z")
    width = inputs.shape[2]
    features = nz * width
    quarter = y * nc + c
    parts = 2 * nc
    buckets, mine = bias_table.shape
    count = inputs.shape[1] // 2

    stored_in = inputs.reshape(inputs.shape[0], 2, count, width)
    stored_cot = cotangent.reshape(stored_in.shape)
    small = jnp.concatenate(
        [attn_gain[None], ffn_gain[None], jnp.pad(bias_table.reshape(1, -1), ((0, 0), (0, width - buckets * mine)))]
    )
    small = jnp.pad(small, ((0, 5), (0, 0)))
    leaving = pick(stored_in, 1 - y, 1)

    query_key_rows = jnp.transpose(query_key, (1, 2, 3, 0))
    value_rows = jnp.transpose(value_proj, (1, 2, 0))
    gate_up_rows = jnp.transpose(gate_up, (1, 2, 3, 0))
    heads = value_rows.shape[0] // parts
    units = gate_up_rows.shape[0] // parts
    unit = gate_up_rows.shape[2]
    local_heads = nc * heads

    def own(rows, size):
        return lax.dynamic_slice_in_dim(rows, quarter * size, size, 0)

    def flat(rows):
        return rows.reshape(-1, width)

    def spread(rows):
        gathered = lax.all_gather(rows, ("z", "c"), axis=0, tiled=True)
        return gathered.reshape(nz, nc, rows.shape[0], width)

    own_pair = own(query_key_rows, heads)
    own_attn = [own_pair[:, 0], own_pair[:, 1], own(value_rows, heads), own(out_proj, heads)]
    own_attn = jnp.concatenate([flat(rows) for rows in own_attn])
    w_attn = spread(own_attn)
    other = after(hop(leaving, "y"), own_attn)
    own_pair = own(after(gate_up_rows, other), units)
    own_gate_up = jnp.concatenate([flat(own_pair[:, 0]), flat(own_pair[:, 1])])
    w_gate_up = spread(own_gate_up)
    own_down = flat(own(after(down_proj, other), units))
    w_down = spread(own_down)
    qkv_count, out_count = 3 * heads * 64, heads * 64

    both_lengths = jnp.stack([lengths, lax.ppermute(lengths, "y", swap)])
    both_lengths = jnp.where(y == 0, both_lengths, both_lengths[::-1]).reshape(-1)
    length = lax.dynamic_slice_in_dim(both_lengths, z, 1, 0)
    slots = (x * 2 + y) * count + jnp.arange(count, dtype=jnp.int32)
    near_x, near_y = jnp.array([0, 0, 1, 1]) ^ x, jnp.array([0, 1, 0, 1]) ^ y
    starts = ((near_x * 2 + near_y) * count).astype(jnp.int32)
    arrived = after(to_groups(stored_in, other, small), own_gate_up, own_down, length, starts)
    tokens = arrived[:, :count].astype(F32)
    small = arrived[:, count:]
    gain_one = small[:, :1].astype(F32)
    gain_two = small[:, 1:2].astype(F32)
    table = small[:, 2, : buckets * mine].reshape(nz, buckets, mine).transpose(0, 2, 1)
    table = table.reshape(-1, buckets).astype(F32)
    table = lax.dynamic_slice_in_dim(table, y * local_heads, local_heads, 0)

    live = (slots < length).astype(F32)[None, :, None]

    def scale_of(values):
        squares = jnp.sum(values * values, axis=(0, 2), keepdims=True)
        return lax.rsqrt(squares / features + norm_eps)

    def norm_back(values, scale, gain, grad):
        inner = jnp.sum(values * gain * grad, axis=(0, 2), keepdims=True)
        out = scale * gain * grad - values * (scale * scale * scale) * inner / features
        return out, jnp.sum(values * scale * grad, axis=1)

    def reduce(partial):
        rows = partial.reshape(nz * partial.shape[1], width)
        return lax.psum_scatter(rows, ("z", "c"), scatter_dimension=0, tiled=True)

    fits = nx == 2 and heads == 4 and count == 256 and units * unit % 640 == 0 and nz % 2 == 0
    if fits:
        forward, backward, gather, scatter = attend, attend_back, gather_tokens, scatter_tokens
        nt, nn, tn, ffn_one, ffn_two = mm_nt, mm_nn, mm_tn, ffn_in, ffn_back
        shared, stored_from = share, settle
    else:
        forward, backward, gather, scatter = attend_plain, attend_back_plain, gather_plain, scatter_plain
        nt, nn, tn, ffn_one, ffn_two = mm_nt_plain, mm_nn_plain, mm_tn_plain, ffn_in_plain, ffn_back_plain
        shared, stored_from = share_plain, settle_plain
    scale_one = scale_of(tokens)
    near = near_bias(table, 4 * count) if fits else table
    normed, _, _ = gather((tokens * scale_one * gain_one).astype(BF), near, live)
    cot_other = hop(pick(stored_cot, 1 - y, 1), "y")
    upstream = live * to_groups(stored_cot, after(cot_other, arrived), None).astype(F32)
    upstream_rounded = after(upstream.astype(BF), w_attn)
    projected = nt(normed, w_attn, 0, qkv_count, starts)
    if fits:
        first = forward(0, projected, length, table, near)
        grad_ffn, cot_first, cot_last = gather(upstream_rounded, first[0])
        second = forward(1, after(projected, first[0], *cot_first), length, table, near)
        attended, lse = (first[0], second[0]), (first[1], second[1])
    else:
        grad_ffn, _, cot_last = gather(upstream_rounded)
        attended, lse = forward(projected, length, table, nc, heads)
        attended = (attended,)
    heads_out = [after(attended[0], *cot_last), *attended[1:]]
    hidden = tokens + scatter(nn(heads_out, w_attn, qkv_count, out_count, starts))[0]
    scale_two = scale_of(hidden)
    normed_two, _, _ = gather((hidden * scale_two * gain_two).astype(BF))
    gate, up, activated = ffn_one(normed_two, w_gate_up, starts)

    down_partial = tn([activated], grad_ffn, starts)
    down_part = reduce(down_partial)
    grad_gate_up = ffn_two(grad_ffn, w_down, after(gate, down_partial), up, starts)
    two_parts = nn([grad_gate_up], w_gate_up, 0, 2 * units * unit, starts)
    grad_two, two_first, _ = scatter(two_parts)
    gate_up_partial = tn([after(grad_gate_up, two_parts[0])], normed_two, starts)
    gate_up_part = reduce(after(gate_up_partial, down_part, *two_first))
    branch_parts = nn([after(activated, gate_up_partial)], w_down, 0, units * unit, starts)
    through, ffn_gain_part = norm_back(hidden, scale_two, gain_two, grad_two)
    grad_hidden = upstream + through
    grad_branch, _, branch_here = gather(after(grad_hidden.astype(BF), branch_parts[0]))
    grad_attended = nt(grad_branch, w_attn, qkv_count, out_count, starts)
    out_partial = tn(attended, grad_branch, starts)
    grad_attended = after(grad_attended, out_partial)
    branch_parts = [after(part, *branch_here) for part in branch_parts]
    down_pieces, down_last = shared(after(down_part, *branch_here))
    if fits:
        first = backward(0, projected, length, table, near, grad_attended, lse[0])
        branch, branch_first, branch_last = scatter(branch_parts, (first[0], down_last))
    else:
        branch, branch_first, branch_last = scatter(branch_parts)
    if fits:
        second = backward(
            1, after(projected, first[0], *branch_last), length, table, near, grad_attended, lse[1]
        )
        grad_projected, table_part = (first[0], second[0]), (first[1], second[1])
    else:
        grads, table_part = backward(projected, length, table, grad_attended, lse, nc, heads)
        grad_projected, table_part = (grads,), table_part[:, :, 0]
    out_part = reduce(after(out_partial, gate_up_part, grad_projected[0], *branch_last))
    outputs = (live * (hidden + branch)).astype(BF)
    outputs, _ = from_groups(outputs)
    qkv_partial = tn(grad_projected, normed, starts)
    gate_up_pieces, gate_up_last = shared(after(gate_up_part, grad_projected[0]))
    qkv_part = reduce(after(qkv_partial, out_part, gate_up_last, outputs[0]))
    one_parts = nn(grad_projected, w_attn, 0, qkv_count, starts)
    if fits:
        here = jnp.stack([y, c]).astype(jnp.int32)

        def write_rows(source, outs):
            outs[0][...] = source[...].astype(F32)

        def write_qkv(source, outs):
            for h in range(heads):
                for i in range(3):
                    value = source[(i * heads + h) * 64 : (i * heads + h + 1) * 64, :].astype(F32)
                    if i == 2:
                        outs[1][h] = value
                    else:
                        outs[0][h, i] = value

        def write_gate_up(source, outs):
            for u in range(units):
                for i in range(2):
                    first = (i * units + u) * unit
                    outs[0][u, i] = source[first : first + unit, :].astype(F32)

        (down_all,) = place(down_pieces, here, [(units * unit, width)], write_rows)
        (gate_up_all,) = place(gate_up_pieces, here, [(units, 2, unit, width)], write_gate_up)
    beside = (down_all, gate_up_all, outputs[0]) if fits else ()
    table_part = table_sums(table_part, 4 * count) if fits else table_part
    grad_one, _, one_last = scatter(one_parts, beside, (table_part,))
    through, attn_gain_part = norm_back(tokens, scale_one, gain_one, grad_one)
    input_grad, input_leaves = from_groups((grad_hidden + through).astype(BF))

    out_pieces, out_last = shared(out_part)

    every = jnp.zeros((nx * 2 * local_heads, table_part.shape[1]), F32)
    every = lax.dynamic_update_slice_in_dim(every, table_part, (x * 2 + y) * local_heads, 0)
    spare = -every.size % width
    every = jnp.pad(every.reshape(-1), (0, spare)).reshape(-1, width)
    sums = sum_plane(jnp.concatenate([attn_gain_part, ffn_gain_part, every]), nx, out_last, outputs[1])
    all_sums = sum_line(after(sums, input_leaves), nz)
    attn_gain_grad, ffn_gain_grad = all_sums[:nz], all_sums[nz : 2 * nz]
    every = all_sums[2 * nz :].reshape(-1)[: nx * 2 * local_heads * buckets].reshape(-1, buckets)

    outputs = stored_from(outputs, BF)
    if fits:
        (out_all,) = place(out_pieces, here, [(heads * 64, width)], write_rows)
        qkv_pieces, _ = shared(after(qkv_part, sums, *one_last), out_all, outputs, input_leaves)
        query_key_all, value_all = place(
            qkv_pieces, here, [(heads, 2, 64, width), (heads, 64, width)], write_qkv
        )
    else:
        down_all, out_all = down_pieces.astype(F32), out_pieces.astype(F32)
        gate_up_all = gate_up_pieces.astype(F32).reshape(parts, 2, units, unit, width)
        gate_up_all = gate_up_all.transpose(0, 2, 1, 3, 4).reshape(-1, 2, unit, width)
        qkv_all = shared(qkv_part)[0].astype(F32).reshape(parts, 3, heads, 64, width)
        qkv_all = qkv_all.transpose(0, 2, 1, 3, 4).reshape(-1, 3, 64, width)
        query_key_all, value_all = qkv_all[:, :2], qkv_all[:, 2]
    input_grad = stored_from(input_grad, F32)
    down_all, out_all = down_all.reshape(down_proj.shape), out_all.reshape(out_proj.shape)

    table_grad = lax.dynamic_slice_in_dim(every, (x * nz + z) * mine, mine, 0).T
    return (
        outputs,
        input_grad,
        pick(attn_gain_grad, z, 0),
        pick(ffn_gain_grad, z, 0),
        query_key_all.transpose(3, 0, 1, 2),
        value_all.transpose(2, 0, 1),
        out_all,
        gate_up_all.transpose(3, 0, 1, 2),
        down_all,
        table_grad,
    )


def solution(mesh):
    dp, nx, nz = (mesh.shape[name] for name in ("dp", "gx", "gy"))
    nc = dp // 2
    split = Mesh(mesh.devices.reshape(2, nc, nx, nz), ("y", "c", "x", "z"))
    seq = ("y", "c")
    return jax.shard_map(
        functools.partial(body, nx, nz, nc),
        mesh=split,
        in_specs=(
            P(seq, "x", "z"),
            P(seq),
            P("z"),
            P("z"),
            P("z", "x", None, None),
            P("z", "x", None),
            P("x", None, "z"),
            P("z", "x", None, None),
            P("x", None, "z"),
            P(None, ("x", "z")),
            P(seq, "x", "z"),
        ),
        out_specs=(
            P(seq, "x", "z"),
            P(seq, "x", "z"),
            P("z"),
            P("z"),
            P("z", "x", None, None),
            P("z", "x", None),
            P("x", None, "z"),
            P("z", "x", None, None),
            P("x", None, "z"),
            P(None, ("x", "z")),
        ),
        check_vma=False,
    )
```

```python
import functools
import math

import jax
import jax.numpy as jnp
from jax import lax
from jax.experimental import pallas as pl
from jax.experimental.pallas import tpu as pltpu
from jax.sharding import Mesh
from jax.sharding import PartitionSpec as P

norm_eps = 1e-06
masked_score = -1e30
bucket_edges = (12, 16, 23, 32, 46, 64, 91)
BF = jnp.bfloat16
F32 = jnp.float32
LB = 128
VMEM = 60 * 1024 * 1024
swap = [(0, 1), (1, 0)]
gelu_a = math.sqrt(2.0 / math.pi)
gelu_b = 0.044715


def bucket_index(offset):
    magnitude = jnp.abs(offset)
    far_bucket = 8 + sum(((magnitude >= boundary).astype(jnp.int32) for boundary in bucket_edges))
    near_bucket = jnp.where(magnitude < 8, magnitude, far_bucket)
    return near_bucket + 16 * (offset > 0).astype(jnp.int32)


def cost(flops, moved):
    return pl.CostEstimate(flops=int(flops) // 16, bytes_accessed=int(moved) // 16, transcendentals=0)


def params(steps):
    return pltpu.CompilerParams(
        dimension_semantics=("arbitrary",) * steps, vmem_limit_bytes=VMEM
    )


def dot_nt(a, b):
    return lax.dot_general(a, b, (((1,), (1,)), ((), ())), preferred_element_type=F32)


def dot_nn(a, b):
    return lax.dot_general(a, b, (((1,), (0,)), ((), ())), preferred_element_type=F32)


def spot_of(starts_ref, d, count):
    return pl.ds(pl.multiple_of(starts_ref[d], 256), count)


def piece_specs(pieces):
    shape = pieces[0].shape
    return [pl.BlockSpec(shape, lambda *_: (0, 0, 0)) for _ in pieces]


def nt_sum(piece_refs, d, w_of):
    half = piece_refs[0].shape[0]
    acc = None
    for z in range(2 * half):
        part = dot_nt(piece_refs[4 * (z // half) + d][z % half], w_of(z))
        acc = part if acc is None else acc + part
    return acc


def nt_kernel(starts_ref, *refs):
    pieces, (w_ref, out_ref) = refs[:8], refs[8:]
    for d in range(4):
        acc = nt_sum(pieces, d, lambda z: w_ref[z, 0])
        out_ref[spot_of(starts_ref, d, acc.shape[0]), :] = acc.astype(BF)


def mm_nt(pieces, w, first, rows, starts):
    nz, nc, _, width = w.shape
    total = 4 * pieces[0].shape[1]
    count, skip = rows // 256, first // 256
    return pl.pallas_call(
        nt_kernel,
        grid=(nc, count),
        in_specs=[pl.BlockSpec(memory_space=pltpu.SMEM)]
        + piece_specs(pieces)
        + [pl.BlockSpec((nz, 1, 256, width), lambda c, i: (0, c, skip + i, 0))],
        out_specs=pl.BlockSpec((total, 256), lambda c, i: (0, c * count + i)),
        out_shape=jax.ShapeDtypeStruct((total, nc * rows), BF),
        compiler_params=params(2),
        cost_estimate=cost(
            2 * nz * total * width * nc * rows, 2 * nz * width * (total + nc * rows) + 2 * total * nc * rows
        ),
        name="product_nt",
    )(starts, *pieces, w)


def nn_kernel(count, starts_ref, *refs):
    grads, (w_ref, low_out, low_keep, high_out, high_keep) = refs[:count], refs[count:]
    nc, rows, width = w_ref.shape[1:]
    t = grads[0].shape[0] // 4
    in_low = pl.program_id(0) < pl.num_programs(0) // 2

    def product(d):
        spot = spot_of(starts_ref, d, t)
        if count == 1:
            return dot_nn(grads[0][spot, :], w_ref[0].reshape(nc * rows, width)).astype(BF)
        return sum(dot_nn(grads[c][spot, :], w_ref[0, c]) for c in range(count)).astype(BF)

    @pl.when(in_low)
    def _():
        for d in range(4):
            (low_out if d // 2 else low_keep)[d % 2, 0] = product(d)

    @pl.when(jnp.logical_not(in_low))
    def _():
        for d in range(4):
            (high_out if d % 2 else high_keep)[d // 2, 0] = product(d)


def mm_nn(grads, w, first, rows, starts):
    total = grads[0].shape[0]
    nz, nc, _, width = w.shape
    skip, half, t = first // rows, nz // 2, total // 4
    low = pl.BlockSpec((2, 1, t, width), lambda z: (0, jnp.minimum(z, half - 1), 0, 0))
    high = pl.BlockSpec((2, 1, t, width), lambda z: (0, jnp.maximum(z - half, 0), 0, 0))
    return pl.pallas_call(
        functools.partial(nn_kernel, len(grads)),
        grid=(nz,),
        in_specs=[pl.BlockSpec(memory_space=pltpu.SMEM)]
        + [pl.BlockSpec(grad.shape, lambda z: (0, 0)) for grad in grads]
        + [pl.BlockSpec((1, nc, rows, width), lambda z: (z, 0, skip, 0))],
        out_specs=[low, low, high, high],
        out_shape=[jax.ShapeDtypeStruct((2, half, t, width), BF)] * 4,
        compiler_params=params(1),
        cost_estimate=cost(
            2 * nz * total * width * nc * rows, 2 * nz * width * (total + nc * rows) + 2 * total * nc * rows
        ),
        name="product_nn",
    )(starts, *grads, w)


def tn_kernel(count, starts_ref, *refs):
    grads, pieces, out_ref = refs[:count], refs[count:-1], refs[-1]
    half, t, _ = pieces[0].shape

    def one(grad_ref):
        turned = [grad_ref[spot_of(starts_ref, d, t), :].T for d in range(4)]
        for z in range(2 * half):
            acc = dot_nn(turned[0], pieces[4 * (z // half)][z % half])
            for d in range(1, 4):
                acc += dot_nn(turned[d], pieces[4 * (z // half) + d][z % half])
            out_ref[z] = acc.astype(BF)

    if count == 1:
        one(grads[0])
    else:
        for c in range(count):

            @pl.when(pl.program_id(0) // (pl.num_programs(0) // count) == c)
            def _():
                one(grads[c])


def mm_tn(grads, pieces, starts):
    total, rows = grads[0].shape
    half, _, width = pieces[0].shape
    nz, count = 2 * half, len(grads)
    block = next(b for b in (640, 384, 256) if rows % b == 0)
    steps = rows // block

    def spec(c):
        return pl.BlockSpec((total, block), lambda i: (0, jnp.clip(i - c * steps, 0, steps - 1)))

    return pl.pallas_call(
        functools.partial(tn_kernel, count),
        grid=(count * steps,),
        in_specs=[pl.BlockSpec(memory_space=pltpu.SMEM)]
        + [spec(c) for c in range(count)]
        + piece_specs(pieces),
        out_specs=pl.BlockSpec((nz, block, width), lambda i: (0, i, 0)),
        out_shape=jax.ShapeDtypeStruct((nz, count * rows, width), BF),
        compiler_params=params(1),
        cost_estimate=cost(
            2 * nz * total * width * count * rows, 2 * nz * width * (total + count * rows) + 2 * total * count * rows
        ),
        name="product_tn",
    )(starts, *grads, *pieces)


def gelu_parts(gate):
    curve = jnp.tanh(gelu_a * (gate + gelu_b * gate * gate * gate))
    value = 0.5 * gate * (1.0 + curve)
    slope = 0.5 * (1.0 + curve) + 0.5 * gate * (1.0 - curve * curve) * gelu_a * (
        1.0 + 3.0 * gelu_b * gate * gate
    )
    return value, slope


def ffn_in_kernel(starts_ref, *refs):
    pieces, (w_ref, gate_ref, up_ref, active_ref) = refs[:8], refs[8:]
    _, _, _, block, width = w_ref.shape
    for d in range(4):
        acc = nt_sum(pieces, d, lambda z: w_ref[z, 0].reshape(2 * block, width))
        spot = spot_of(starts_ref, d, acc.shape[0])
        gate, up = acc[:, :block], acc[:, block:]
        value = 0.5 * gate * (1.0 + jnp.tanh(gelu_a * (gate + gelu_b * gate * gate * gate)))
        gate_ref[spot, :] = gate.astype(BF)
        up_ref[spot, :] = up.astype(BF)
        active_ref[spot, :] = (value * up).astype(BF)


def ffn_in(pieces, w, starts):
    nz, nc, rows, width = w.shape
    half, total = rows // 2, 4 * pieces[0].shape[1]
    count = half // 128
    block = pl.BlockSpec((total, 128), lambda c, i: (0, c * count + i))
    return pl.pallas_call(
        ffn_in_kernel,
        grid=(nc, count),
        in_specs=[pl.BlockSpec(memory_space=pltpu.SMEM)]
        + piece_specs(pieces)
        + [pl.BlockSpec((nz, 1, 2, 128, width), lambda c, i: (0, c, 0, i, 0))],
        out_specs=[block, block, block],
        out_shape=[jax.ShapeDtypeStruct((total, nc * half), BF)] * 3,
        compiler_params=params(2),
        cost_estimate=cost(
            2 * nz * total * width * nc * rows, 2 * nz * width * (total + nc * rows) + 3 * total * nc * rows
        ),
        name="ffn_in",
    )(starts, *pieces, w.reshape(nz, nc, 2, half, width))


def ffn_back_kernel(starts_ref, *refs):
    pieces, (w_ref, gate_ref, up_ref, out_ref) = refs[:8], refs[8:]
    half = w_ref.shape[2]
    for d in range(4):
        acc = nt_sum(pieces, d, lambda z: w_ref[z, 0])
        spot = spot_of(starts_ref, d, acc.shape[0])
        value, slope = gelu_parts(gate_ref[spot, :].astype(F32))
        out_ref[spot, :half] = (acc * up_ref[spot, :].astype(F32) * slope).astype(BF)
        out_ref[spot, half:] = (acc * value).astype(BF)


def ffn_back(pieces, w, gate, up, starts):
    nz, nc, half, width = w.shape
    total = gate.shape[0]
    kept = pl.BlockSpec((total, half), lambda c: (0, c))
    return pl.pallas_call(
        ffn_back_kernel,
        grid=(nc,),
        in_specs=[pl.BlockSpec(memory_space=pltpu.SMEM)]
        + piece_specs(pieces)
        + [pl.BlockSpec((nz, 1, half, width), lambda c: (0, c, 0, 0)), kept, kept],
        out_specs=pl.BlockSpec((total, 2 * half), lambda c: (0, c)),
        out_shape=jax.ShapeDtypeStruct((total, nc * 2 * half), BF),
        compiler_params=params(1),
        cost_estimate=cost(
            2 * nz * total * width * nc * half, 2 * nz * width * (total + nc * half) + 8 * total * nc * half
        ),
        name="ffn_back",
    )(starts, *pieces, w, gate, up)


def mm_nt_plain(act, w, first, rows, starts):
    part = lax.slice_in_dim(w, first, first + rows, axis=2)
    out = jnp.einsum("ztf,zcrf->tcr", act, part, preferred_element_type=F32)
    return out.astype(BF).reshape(act.shape[1], -1)


def mm_nn_plain(grads, w, first, rows, starts):
    grad = grads[0]
    part = lax.slice_in_dim(w, first, first + rows, axis=2)
    split = grad.reshape(grad.shape[0], w.shape[1], rows)
    out = jnp.einsum("tcr,zcrf->ztf", split, part, preferred_element_type=F32)
    return [out.astype(BF)]


def mm_tn_plain(grads, act, starts):
    return jnp.einsum("tr,ztf->zrf", grads[0], act, preferred_element_type=F32).astype(BF)


def ffn_in_plain(act, w, starts):
    _, nc, rows, _ = w.shape
    total = act.shape[1]
    both = jnp.einsum("ztf,zcrf->tcr", act, w, preferred_element_type=F32)
    gate, up = both[:, :, : rows // 2], both[:, :, rows // 2 :]
    value, _ = gelu_parts(gate)
    return [part.astype(BF).reshape(total, -1) for part in (gate, up, value * up)]


def ffn_back_plain(act, w, gate, up, starts):
    total, nc = gate.shape[0], w.shape[1]
    grad = jnp.einsum("ztf,zcrf->tcr", act, w, preferred_element_type=F32)
    value, slope = gelu_parts(gate.astype(F32).reshape(grad.shape))
    both = [grad * up.astype(F32).reshape(grad.shape) * slope, grad * value]
    return jnp.concatenate(both, axis=2).astype(BF).reshape(total, -1)


def near_buckets(tile, total):
    first = (total // LB - 2 + tile) * LB
    rows = lax.broadcasted_iota(jnp.int32, (LB, LB), 0)
    lanes = lax.broadcasted_iota(jnp.int32, (LB, LB), 1)
    return bucket_index(first + rows - (total - LB) - lanes)


def near_kernel(total, table_ref, out_ref):
    heads = out_ref.shape[0]

    def one_tile(tile, _):
        index = near_buckets(tile, total)
        vals = [jnp.full((LB, LB), table_ref[h, 0], F32) for h in range(heads)]
        for b in range(1, 32):
            hit = index == b
            vals = [jnp.where(hit, table_ref[h, b], vals[h]) for h in range(heads)]
        for h in range(heads):
            out_ref[h, pl.ds(pl.multiple_of(tile * LB, LB), LB)] = vals[h]
        return 0

    lax.fori_loop(0, 3, one_tile, 0)


def near_bias(table, total):
    heads = table.shape[0]
    return pl.pallas_call(
        functools.partial(near_kernel, total),
        in_specs=[pl.BlockSpec(memory_space=pltpu.SMEM)],
        out_specs=pl.BlockSpec((heads, 3 * LB, LB), lambda: (0, 0, 0)),
        out_shape=jax.ShapeDtypeStruct((heads, 3 * LB, LB), F32),
        compiler_params=params(0),
        cost_estimate=cost(0, heads * LB * LB),
        name="near_bias",
    )(table)


def build_strips(table_ref, near_ref, strip_ref, total, group):
    heads = strip_ref.shape[0]
    near = (total // LB - 2) * LB
    for h in range(heads):
        head = group * heads + h
        strip_ref[h, :near] = jnp.full((near, LB), table_ref[head, 15], F32)
        strip_ref[h, near : near + 3 * LB] = near_ref[h]
        strip_ref[h, near + 3 * LB :] = jnp.full((near, LB), table_ref[head, 31], F32)


def table_kernel(total, *refs):
    parts, out_ref = refs[:-1], refs[-1]
    index = [near_buckets(tile, total) for tile in range(3)]
    buckets = [range(1, 16), [b for b in range(32) if b != 16], range(17, 32)]
    for g, part_ref in enumerate(parts):
        heads = part_ref.shape[0]

        def one_head(h, _):
            here = g * heads + h
            out_ref[here] = jnp.zeros((32, LB), F32)
            out_ref[here, 15:16] = part_ref[h, 3 * LB : 3 * LB + 1]
            out_ref[here, 31:32] = part_ref[h, 3 * LB + 8 : 3 * LB + 9]
            for tile in range(3):
                grads = part_ref[h, tile * LB : (tile + 1) * LB]
                for b in buckets[tile]:
                    picked = jnp.where(index[tile] == b, grads, 0.0)
                    out_ref[here, b : b + 1] += jnp.sum(picked, axis=0, keepdims=True)
            return 0

        lax.fori_loop(0, heads, one_head, 0)


def table_sums(parts, total):
    heads = len(parts) * parts[0].shape[0]
    out = pl.pallas_call(
        functools.partial(table_kernel, total),
        in_specs=[pl.BlockSpec(part.shape, lambda: (0, 0, 0)) for part in parts],
        out_specs=pl.BlockSpec((heads, 32, LB), lambda: (0, 0, 0)),
        out_shape=jax.ShapeDtypeStruct((heads, 32, LB), F32),
        compiler_params=params(0),
        cost_estimate=cost(0, heads * LB * LB),
        name="table_sums",
    )(*parts)
    return jnp.sum(out, axis=2)


def head_lanes(shape, h):
    lanes = lax.broadcasted_iota(jnp.int32, shape, 1)
    return lanes // 64 == h, lanes == ((h + 1) % 4) * 64


def mask_keys(keys, length, h):
    own, spare = head_lanes(keys.shape, h)
    dead = lax.broadcasted_iota(jnp.int32, keys.shape, 0) >= length
    mask = jnp.where(jnp.logical_and(spare, dead), masked_score, 0.0)
    return jnp.where(own, keys.astype(F32), mask).astype(BF)


def with_one(queries, h):
    _, spare = head_lanes(queries.shape, h)
    return jnp.where(spare, 1.0, queries.astype(F32)).astype(BF)


def own_lanes(values, h):
    own, _ = head_lanes(values.shape, h)
    return jnp.where(own, values.astype(F32), 0.0).astype(BF)


def block_bias(strip_ref, h, block, total):
    first = total - LB - 2 * block * LB
    left = strip_ref[h, pl.ds(pl.multiple_of(first, LB), total)]
    right = strip_ref[h, pl.ds(pl.multiple_of(first - LB, LB), total)]
    return jnp.concatenate([left, right], axis=1)


def attend_kernel(group, length_ref, table_ref, near_ref, q_ref, k_ref, v_ref, out_ref, lse_ref, strip, heads_k, turned_v, turned_out):
    total = q_ref.shape[0]
    heads = strip.shape[0]
    build_strips(table_ref, near_ref, strip, total, group)
    turned_v[...] = v_ref[...].astype(F32).T.astype(BF)
    for h in range(heads):
        heads_k[h] = mask_keys(k_ref[...], length_ref[0], h)

    def one_block(block, _):
        spot = pl.ds(pl.multiple_of(block * 256, 256), 256)
        queries = q_ref[spot]
        for h in range(heads):
            scores = dot_nt(heads_k[h], with_one(queries, h)) + block_bias(strip, h, block, total)
            largest = jnp.max(scores, axis=0, keepdims=True)
            raised = jnp.exp(scores - largest)
            totals = jnp.sum(raised, axis=0, keepdims=True)
            out = dot_nn(turned_v[h * 64 : (h + 1) * 64], raised.astype(BF))
            turned_out[h * 64 : (h + 1) * 64, spot] = out * (1.0 / totals)
            lse_ref[h : h + 1, spot] = largest + jnp.log(totals)
        return 0

    lax.fori_loop(0, total // 256, one_block, 0)
    out_ref[...] = turned_out[...].T.astype(BF)


def attend_back_kernel(
    group, length_ref, table_ref, near_ref, q_ref, k_ref, v_ref, grad_ref, lse_ref, out_ref, table_grad_ref,
    strip, strip_grad, heads_k, turned_k, turned_q, ds_ref, p_ref, dk_ref, dv_ref,
):
    total = q_ref.shape[0]
    heads = strip.shape[0]
    build_strips(table_ref, near_ref, strip, total, group)
    strip_grad[...] = jnp.zeros_like(strip_grad)
    dk_ref[...] = jnp.zeros_like(dk_ref)
    dv_ref[...] = jnp.zeros_like(dv_ref)
    turned_k[...] = k_ref[...].astype(F32).T.astype(BF)
    for h in range(heads):
        heads_k[h] = mask_keys(k_ref[...], length_ref[0], h)

    def one_block(block, _):
        spot = pl.ds(pl.multiple_of(block * 256, 256), 256)
        queries, grads = q_ref[spot], grad_ref[spot]
        own_q, own_g = [], []
        for h in range(heads):
            own_q.append(own_lanes(queries, h))
            own_g.append(own_lanes(grads, h))
            scores = dot_nt(heads_k[h], with_one(queries, h)) + block_bias(strip, h, block, total)
            probs = jnp.exp(scores - lse_ref[h : h + 1, spot])
            weighed = probs * dot_nt(v_ref[...], own_g[h])
            delta = jnp.sum(weighed, axis=0, keepdims=True)
            grad_scores = weighed - probs * delta
            first = total - LB - 2 * block * LB
            left = pl.ds(pl.multiple_of(first, LB), total)
            right = pl.ds(pl.multiple_of(first - LB, LB), total)
            strip_grad[h, left] += grad_scores[:, :LB]
            strip_grad[h, right] += grad_scores[:, LB:]
            rounded = grad_scores.astype(BF)
            ds_ref[:, h * 256 : (h + 1) * 256] = rounded
            p_ref[:, h * 256 : (h + 1) * 256] = probs.astype(BF)
            turned_q[h * 64 : (h + 1) * 64, spot] = dot_nn(turned_k[h * 64 : (h + 1) * 64], rounded)
        dk_ref[...] += dot_nn(ds_ref[...], jnp.concatenate(own_q, axis=0))
        dv_ref[...] += dot_nn(p_ref[...], jnp.concatenate(own_g, axis=0))
        return 0

    lax.fori_loop(0, total // 256, one_block, 0)
    out_ref[:, :256] = turned_q[...].T.astype(BF)
    out_ref[:, 256:512] = dk_ref[...].astype(BF)
    out_ref[:, 512:] = dv_ref[...].astype(BF)

    near = (total // LB - 2) * LB
    for h in range(heads):
        table_grad_ref[h, : 3 * LB] = strip_grad[h, near : near + 3 * LB]
        left = jnp.sum(strip_grad[h, :near], axis=0, keepdims=True)
        right = jnp.sum(strip_grad[h, near + 3 * LB :], axis=0, keepdims=True)
        table_grad_ref[h, 3 * LB : 3 * LB + 8] = jnp.broadcast_to(left, (8, LB))
        table_grad_ref[h, 3 * LB + 8 :] = jnp.broadcast_to(right, (8, LB))


def block_specs(total, group):
    def spec(i):
        return pl.BlockSpec((total, 256), lambda _: (0, 3 * group + i))

    smem = pl.BlockSpec(memory_space=pltpu.SMEM)
    near = pl.BlockSpec((4, 3 * LB, LB), lambda _: (group, 0, 0))
    return [smem, smem, near, spec(0), spec(1), spec(2)]


def attend(group, projected, length, table, near):
    total = projected.shape[0]
    heads = 4
    return pl.pallas_call(
        functools.partial(attend_kernel, group),
        grid=(1,),
        in_specs=block_specs(total, group),
        out_specs=[
            pl.BlockSpec((total, 256), lambda _: (0, 0)),
            pl.BlockSpec((8, total), lambda _: (0, 0)),
        ],
        out_shape=[
            jax.ShapeDtypeStruct((total, 256), BF),
            jax.ShapeDtypeStruct((8, total), F32),
        ],
        scratch_shapes=[
            pltpu.VMEM((heads, 2 * total - LB, LB), F32),
            pltpu.VMEM((heads, total, 256), BF),
            pltpu.VMEM((256, total), BF),
            pltpu.VMEM((256, total), F32),
        ],
        compiler_params=params(1),
        cost_estimate=cost(heads * total * total * 2 * 256 * 2, 4 * total * 256 * 2),
        name="attend",
    )(length, table, near, projected, projected, projected)


def attend_back(group, projected, length, table, near, grad_out, lse):
    total = projected.shape[0]
    heads = 4
    return pl.pallas_call(
        functools.partial(attend_back_kernel, group),
        grid=(1,),
        in_specs=block_specs(total, group)
        + [
            pl.BlockSpec((total, 256), lambda _: (0, group)),
            pl.BlockSpec((8, total), lambda _: (0, 0)),
        ],
        out_specs=[
            pl.BlockSpec((total, 768), lambda _: (0, 0)),
            pl.BlockSpec((heads, 3 * LB + 16, LB), lambda _: (0, 0, 0)),
        ],
        out_shape=[
            jax.ShapeDtypeStruct((total, 768), BF),
            jax.ShapeDtypeStruct((heads, 3 * LB + 16, LB), F32),
        ],
        scratch_shapes=[
            pltpu.VMEM((heads, 2 * total - LB, LB), F32),
            pltpu.VMEM((heads, 2 * total - LB, LB), F32),
            pltpu.VMEM((heads, total, 256), BF),
            pltpu.VMEM((256, total), BF),
            pltpu.VMEM((256, total), F32),
            pltpu.VMEM((total, heads * 256), BF),
            pltpu.VMEM((total, heads * 256), BF),
            pltpu.VMEM((total, 256), F32),
            pltpu.VMEM((total, 256), F32),
        ],
        compiler_params=params(1),
        cost_estimate=cost(heads * total * total * 2 * 256 * 5, 8 * total * 256 * 2),
        name="attend_back",
    )(length, table, near, projected, projected, projected, grad_out, lse)


def split_heads(projected, groups, heads):
    parts = projected.reshape(projected.shape[0], groups, 3, heads, 64)
    return [parts[:, :, i].reshape(projected.shape[0], groups * heads, 64) for i in range(3)]


def plain_scores(queries, keys, length, table):
    slots = jnp.arange(keys.shape[0], dtype=jnp.int32)
    picked = (bucket_index(slots[None, :] - slots[:, None])[:, :, None] == jnp.arange(32)).astype(F32)
    bias = jnp.einsum("qkb,hb->hqk", picked, table, precision=lax.Precision.HIGHEST)
    scores = jnp.einsum("qhs,khs->hqk", queries, keys, preferred_element_type=F32) + bias
    return jnp.where(slots < length[0], scores, masked_score), picked


def attend_plain(projected, length, table, groups, heads):
    queries, keys, values = split_heads(projected, groups, heads)
    scores, _ = plain_scores(queries, keys, length, table)
    lse = jax.nn.logsumexp(scores, axis=2)
    probs = jnp.exp(scores - lse[:, :, None]).astype(BF)
    out = jnp.einsum("hqk,khs->qhs", probs, values, preferred_element_type=F32)
    return out.astype(BF).reshape(projected.shape[0], -1), lse


def attend_back_plain(projected, length, table, grad_out, lse, groups, heads):
    total = projected.shape[0]
    queries, keys, values = split_heads(projected, groups, heads)
    grads = grad_out.reshape(queries.shape)
    scores, picked = plain_scores(queries, keys, length, table)
    probs = jnp.exp(scores - lse[:, :, None])
    weighed = probs * jnp.einsum("qhs,khs->hqk", grads, values, preferred_element_type=F32)
    wide = weighed - probs * jnp.sum(weighed, axis=2, keepdims=True)
    rounded = wide.astype(BF)
    parts = [
        jnp.einsum("hqk,khs->qhs", rounded, keys, preferred_element_type=F32),
        jnp.einsum("hqk,qhs->khs", rounded, queries, preferred_element_type=F32),
        jnp.einsum("hqk,qhs->khs", probs.astype(BF), grads, preferred_element_type=F32),
    ]
    parts = [part.astype(BF).reshape(total, groups, 1, heads * 64) for part in parts]
    table_grad = jnp.einsum("hqk,qkb->hb", wide, picked, precision=lax.Precision.HIGHEST)
    return (
        jnp.concatenate(parts, axis=2).reshape(total, -1),
        table_grad.reshape(groups * heads, 32, 1),
    )


def hop(value, axis):
    return lax.ppermute(value, axis, swap)


def pick(value, index, axis):
    return lax.dynamic_index_in_dim(value, index, axis, keepdims=False)


def paired(mine, other, axis, place=0):
    return jnp.where(
        lax.axis_index(axis) == 0,
        jnp.stack([mine, other], axis=place),
        jnp.stack([other, mine], axis=place),
    )


def after(value, *others):
    return lax.optimization_barrier((value, *others))[0]


def gather_plain(part, *beside):
    return lax.all_gather(part, ("x", "y"), axis=1, tiled=True), (), ()


def gather_tokens(part, *beside):
    half = part.shape[0] // 2
    low, high = part[:half], part[half:]
    low_x, high_y = hop(low, "x"), hop(high, "y")
    if beside:
        low_x, high_y = after(low_x, *beside), after(high_y, *beside)
    low_y, high_x = hop(low, "y"), hop(high, "x")
    low_xy, high_xy = hop(low_x, "y"), hop(high_y, "x")
    pieces = [low, low_y, low_x, low_xy, high, high_y, high_x, high_xy]
    return pieces, (low_x, high_y), (low_y, low_xy, high_x, high_xy)


def scatter_plain(parts, beside=(), beside_last=()):
    whole = parts[0].astype(F32)
    return lax.psum_scatter(whole, ("x", "y"), scatter_dimension=1, tiled=True), (), ()


def scatter_tokens(parts, beside=(), beside_last=()):
    low_out, low_keep, high_out, high_keep = parts
    low_in, high_in = hop(low_out, "x"), hop(high_out, "y")
    if beside:
        low_in, high_in = after(low_in, *beside), after(high_in, *beside)

    def add(keep, arrived, index):
        return keep[index].astype(F32) + arrived[index].astype(F32)

    low_last = hop(add(low_keep, low_in, 1).astype(BF), "y")
    high_last = hop(add(high_keep, high_in, 1).astype(BF), "x")
    if beside_last:
        low_last, high_last = after(low_last, *beside_last), after(high_last, *beside_last)
    low = add(low_keep, low_in, 0) + low_last.astype(F32)
    high = add(high_keep, high_in, 0) + high_last.astype(F32)
    return jnp.concatenate([low, high], axis=0), (low_in, high_in), (low_last, high_last)


def place_kernel(write, here_ref, *refs):
    pieces, outs = refs[:4], refs[4:]
    step = pl.program_id(0)
    for near in range(4):
        y = here_ref[0] if near < 2 else 1 - here_ref[0]
        c = here_ref[1] if near % 2 == 0 else 1 - here_ref[1]

        @pl.when(step == 2 * y + c)
        def _():
            write(pieces[near], outs)


def place(pieces, here, shapes, write):
    return pl.pallas_call(
        functools.partial(place_kernel, write),
        grid=(4,),
        in_specs=[pl.BlockSpec(memory_space=pltpu.SMEM)]
        + [pl.BlockSpec(piece.shape, lambda q: (0, 0)) for piece in pieces],
        out_specs=[
            pl.BlockSpec(shape, lambda q, rank=len(shape): (q,) + (0,) * (rank - 1)) for shape in shapes
        ],
        out_shape=[jax.ShapeDtypeStruct((4 * shape[0], *shape[1:]), F32) for shape in shapes],
        compiler_params=params(1),
        cost_estimate=cost(0, pieces[0].size),
        name="place",
    )(here, *pieces)


def share(part, *beside):
    over_y = hop(part, "y")
    if beside:
        over_y = after(over_y, *beside)
    return [part, hop(part, "c"), over_y, hop(over_y, "c")], over_y


def share_plain(part):
    return lax.all_gather(part, ("y", "c"), axis=0), part


def to_groups(halves, other, extra):
    count, _, t, width = halves.shape
    both = paired(pick(halves, lax.axis_index("y"), 1), other, "y").reshape(2 * count, t, width)
    if extra is not None:
        wide = jnp.broadcast_to(extra[None], (2 * count, *extra.shape))
        both = jnp.concatenate([both, wide], axis=1)
    return lax.all_to_all(both, "z", 0, 0, tiled=True)


def from_groups(mine):
    nz, t, width = mine.shape
    back = lax.all_to_all(mine, "z", 0, 0, tiled=True).reshape(2, nz // 2, t, width)
    leaving = pick(back, 1 - lax.axis_index("y"), 0)
    return (back, hop(leaving, "y")), leaving


def settle_kernel(y_ref, back_ref, other_ref, out_ref):
    j, y = pl.program_id(0), pl.program_id(1)

    @pl.when(y == y_ref[0])
    def _():
        out_ref[0, 0] = back_ref[y, j].astype(out_ref.dtype)

    @pl.when(y != y_ref[0])
    def _():
        out_ref[0, 0] = other_ref[j].astype(out_ref.dtype)


def settle(arrived, dtype):
    back, other = arrived
    _, count, t, width = back.shape
    y = lax.axis_index("y").astype(jnp.int32).reshape(1)
    out = pl.pallas_call(
        settle_kernel,
        grid=(count, 2),
        in_specs=[
            pl.BlockSpec(memory_space=pltpu.SMEM),
            pl.BlockSpec(back.shape, lambda j, y: (0, 0, 0, 0)),
            pl.BlockSpec(other.shape, lambda j, y: (0, 0, 0)),
        ],
        out_specs=pl.BlockSpec((1, 1, t, width), lambda j, y: (j, y, 0, 0)),
        out_shape=jax.ShapeDtypeStruct((count, 2, t, width), dtype),
        compiler_params=params(2),
        cost_estimate=cost(0, count * t * width),
        name="settle",
    )(y, back, other)
    return out.reshape(count, 2 * t, width)


def settle_plain(arrived, dtype):
    back, other = arrived
    _, count, t, width = back.shape
    both = paired(pick(back, lax.axis_index("y"), 0), other, "y")
    return both.transpose(1, 0, 2, 3).reshape(count, 2 * t, width).astype(dtype)


def sum_plane(value, nx, *earlier):
    value = value + after(hop(value, "c"), *earlier)
    value = value + hop(value, "x") if nx == 2 else lax.psum(value, "x")
    return value + hop(value, "y")


def sum_line(value, nz):
    step = 1
    while step < nz:
        value = value + lax.ppermute(value, "z", [(i, i ^ step) for i in range(nz)])
        step *= 2
    return value


def body(
    nx, nz, nc, inputs, lengths, attn_gain, ffn_gain, query_key, value_proj, out_proj, gate_up, down_proj, bias_table, cotangent
):
    x, y = lax.axis_index("x"), lax.axis_index("y")
    c, z = lax.axis_index("c"), lax.axis_index("z")
    width = inputs.shape[2]
    features = nz * width
    quarter = y * nc + c
    parts = 2 * nc
    buckets, mine = bias_table.shape
    count = inputs.shape[1] // 2

    stored_in = inputs.reshape(inputs.shape[0], 2, count, width)
    stored_cot = cotangent.reshape(stored_in.shape)
    small = jnp.concatenate(
        [attn_gain[None], ffn_gain[None], jnp.pad(bias_table.reshape(1, -1), ((0, 0), (0, width - buckets * mine)))]
    )
    small = jnp.pad(small, ((0, 5), (0, 0)))
    leaving = pick(stored_in, 1 - y, 1)

    query_key_rows = jnp.transpose(query_key, (1, 2, 3, 0))
    value_rows = jnp.transpose(value_proj, (1, 2, 0))
    gate_up_rows = jnp.transpose(gate_up, (1, 2, 3, 0))
    heads = value_rows.shape[0] // parts
    units = gate_up_rows.shape[0] // parts
    unit = gate_up_rows.shape[2]
    local_heads = nc * heads

    def own(rows, size):
        return lax.dynamic_slice_in_dim(rows, quarter * size, size, 0)

    def flat(rows):
        return rows.reshape(-1, width)

    def spread(rows):
        gathered = lax.all_gather(rows, ("z", "c"), axis=0, tiled=True)
        return gathered.reshape(nz, nc, rows.shape[0], width)

    own_pair = own(query_key_rows, heads)
    own_attn = [own_pair[:, 0], own_pair[:, 1], own(value_rows, heads), own(out_proj, heads)]
    own_attn = jnp.concatenate([flat(rows) for rows in own_attn])
    w_attn = spread(own_attn)
    other = after(hop(leaving, "y"), own_attn)
    own_pair = own(after(gate_up_rows, other), units)
    own_gate_up = jnp.concatenate([flat(own_pair[:, 0]), flat(own_pair[:, 1])])
    w_gate_up = spread(own_gate_up)
    own_down = flat(own(after(down_proj, other), units))
    w_down = spread(own_down)
    qkv_count, out_count = 3 * heads * 64, heads * 64

    both_lengths = jnp.stack([lengths, lax.ppermute(lengths, "y", swap)])
    both_lengths = jnp.where(y == 0, both_lengths, both_lengths[::-1]).reshape(-1)
    length = lax.dynamic_slice_in_dim(both_lengths, z, 1, 0)
    slots = (x * 2 + y) * count + jnp.arange(count, dtype=jnp.int32)
    near_x, near_y = jnp.array([0, 0, 1, 1]) ^ x, jnp.array([0, 1, 0, 1]) ^ y
    starts = ((near_x * 2 + near_y) * count).astype(jnp.int32)
    arrived = after(to_groups(stored_in, other, small), own_gate_up, own_down, length, starts)
    tokens = arrived[:, :count].astype(F32)
    small = arrived[:, count:]
    gain_one = small[:, :1].astype(F32)
    gain_two = small[:, 1:2].astype(F32)
    table = small[:, 2, : buckets * mine].reshape(nz, buckets, mine).transpose(0, 2, 1)
    table = table.reshape(-1, buckets).astype(F32)
    table = lax.dynamic_slice_in_dim(table, y * local_heads, local_heads, 0)

    live = (slots < length).astype(F32)[None, :, None]

    def scale_of(values):
        squares = jnp.sum(values * values, axis=(0, 2), keepdims=True)
        return lax.rsqrt(squares / features + norm_eps)

    def norm_back(values, scale, gain, grad):
        inner = jnp.sum(values * gain * grad, axis=(0, 2), keepdims=True)
        out = scale * gain * grad - values * (scale * scale * scale) * inner / features
        return out, jnp.sum(values * scale * grad, axis=1)

    def reduce(partial):
        rows = partial.reshape(nz * partial.shape[1], width)
        return lax.psum_scatter(rows, ("z", "c"), scatter_dimension=0, tiled=True)

    fits = nx == 2 and heads == 4 and count == 256 and units * unit % 640 == 0 and nz % 2 == 0
    if fits:
        forward, backward, gather, scatter = attend, attend_back, gather_tokens, scatter_tokens
        nt, nn, tn, ffn_one, ffn_two = mm_nt, mm_nn, mm_tn, ffn_in, ffn_back
        shared, stored_from = share, settle
    else:
        forward, backward, gather, scatter = attend_plain, attend_back_plain, gather_plain, scatter_plain
        nt, nn, tn, ffn_one, ffn_two = mm_nt_plain, mm_nn_plain, mm_tn_plain, ffn_in_plain, ffn_back_plain
        shared, stored_from = share_plain, settle_plain
    scale_one = scale_of(tokens)
    near = near_bias(table, 4 * count) if fits else table
    normed, _, _ = gather((tokens * scale_one * gain_one).astype(BF), near, live)
    cot_other = hop(pick(stored_cot, 1 - y, 1), "y")
    upstream = live * to_groups(stored_cot, after(cot_other, arrived), None).astype(F32)
    upstream_rounded = after(upstream.astype(BF), w_attn)
    projected = nt(normed, w_attn, 0, qkv_count, starts)
    if fits:
        first = forward(0, projected, length, table, near)
        grad_ffn, cot_first, cot_last = gather(upstream_rounded, first[0])
        second = forward(1, after(projected, first[0], *cot_first), length, table, near)
        attended, lse = (first[0], second[0]), (first[1], second[1])
    else:
        grad_ffn, _, cot_last = gather(upstream_rounded)
        attended, lse = forward(projected, length, table, nc, heads)
        attended = (attended,)
    heads_out = [after(attended[0], *cot_last), *attended[1:]]
    hidden = tokens + scatter(nn(heads_out, w_attn, qkv_count, out_count, starts))[0]
    scale_two = scale_of(hidden)
    normed_two, _, _ = gather((hidden * scale_two * gain_two).astype(BF))
    gate, up, activated = ffn_one(normed_two, w_gate_up, starts)

    down_partial = tn([activated], grad_ffn, starts)
    down_part = reduce(down_partial)
    grad_gate_up = ffn_two(grad_ffn, w_down, after(gate, down_partial), up, starts)
    two_parts = nn([grad_gate_up], w_gate_up, 0, 2 * units * unit, starts)
    grad_two, two_first, _ = scatter(two_parts)
    gate_up_partial = tn([after(grad_gate_up, two_parts[0])], normed_two, starts)
    gate_up_part = reduce(after(gate_up_partial, down_part, *two_first))
    branch_parts = nn([after(activated, gate_up_partial)], w_down, 0, units * unit, starts)
    through, ffn_gain_part = norm_back(hidden, scale_two, gain_two, grad_two)
    grad_hidden = upstream + through
    grad_branch, _, branch_here = gather(after(grad_hidden.astype(BF), branch_parts[0]))
    grad_attended = nt(grad_branch, w_attn, qkv_count, out_count, starts)
    out_partial = tn(attended, grad_branch, starts)
    grad_attended = after(grad_attended, out_partial)
    branch_parts = [after(part, *branch_here) for part in branch_parts]
    down_pieces, down_last = shared(after(down_part, *branch_here))
    if fits:
        first = backward(0, projected, length, table, near, grad_attended, lse[0])
        branch, branch_first, branch_last = scatter(branch_parts, (first[0], down_last))
    else:
        branch, branch_first, branch_last = scatter(branch_parts)
    if fits:
        second = backward(
            1, after(projected, first[0], *branch_last), length, table, near, grad_attended, lse[1]
        )
        grad_projected, table_part = (first[0], second[0]), (first[1], second[1])
    else:
        grads, table_part = backward(projected, length, table, grad_attended, lse, nc, heads)
        grad_projected, table_part = (grads,), table_part[:, :, 0]
    out_part = reduce(after(out_partial, gate_up_part, grad_projected[0], *branch_last))
    outputs = (live * (hidden + branch)).astype(BF)
    outputs, _ = from_groups(outputs)
    qkv_partial = tn(grad_projected, normed, starts)
    gate_up_pieces, gate_up_last = shared(after(gate_up_part, grad_projected[0]))
    qkv_part = reduce(after(qkv_partial, out_part, gate_up_last, outputs[0]))
    one_parts = nn(grad_projected, w_attn, 0, qkv_count, starts)
    if fits:
        here = jnp.stack([y, c]).astype(jnp.int32)

        def write_rows(source, outs):
            outs[0][...] = source[...].astype(F32)

        def write_qkv(source, outs):
            for h in range(heads):
                for i in range(3):
                    value = source[(i * heads + h) * 64 : (i * heads + h + 1) * 64, :].astype(F32)
                    if i == 2:
                        outs[1][h] = value
                    else:
                        outs[0][h, i] = value

        def write_gate_up(source, outs):
            for u in range(units):
                for i in range(2):
                    first = (i * units + u) * unit
                    outs[0][u, i] = source[first : first + unit, :].astype(F32)

        down_pieces = [after(down_pieces[0], outputs[1]), *down_pieces[1:]]
        (down_all,) = place(down_pieces, here, [(units * unit, width)], write_rows)
        (gate_up_all,) = place(gate_up_pieces, here, [(units, 2, unit, width)], write_gate_up)
    beside = (down_all, gate_up_all, outputs[0]) if fits else ()
    table_part = table_sums(table_part, 4 * count) if fits else table_part
    grad_one, _, one_last = scatter(one_parts, beside, (table_part,))
    through, attn_gain_part = norm_back(tokens, scale_one, gain_one, grad_one)
    input_grad, input_leaves = from_groups((grad_hidden + through).astype(BF))

    out_pieces, out_last = shared(out_part)

    every = jnp.zeros((nx * 2 * local_heads, table_part.shape[1]), F32)
    every = lax.dynamic_update_slice_in_dim(every, table_part, (x * 2 + y) * local_heads, 0)
    spare = -every.size % width
    every = jnp.pad(every.reshape(-1), (0, spare)).reshape(-1, width)
    sums = sum_plane(jnp.concatenate([attn_gain_part, ffn_gain_part, every]), nx, out_last)
    all_sums = sum_line(after(sums, input_leaves), nz)
    attn_gain_grad, ffn_gain_grad = all_sums[:nz], all_sums[nz : 2 * nz]
    every = all_sums[2 * nz :].reshape(-1)[: nx * 2 * local_heads * buckets].reshape(-1, buckets)

    outputs = stored_from(outputs, BF)
    if fits:
        (out_all,) = place(out_pieces, here, [(heads * 64, width)], write_rows)
        qkv_pieces, _ = shared(after(qkv_part, sums, *one_last), out_all, outputs)
        query_key_all, value_all = place(
            qkv_pieces, here, [(heads, 2, 64, width), (heads, 64, width)], write_qkv
        )
    else:
        down_all, out_all = down_pieces.astype(F32), out_pieces.astype(F32)
        gate_up_all = gate_up_pieces.astype(F32).reshape(parts, 2, units, unit, width)
        gate_up_all = gate_up_all.transpose(0, 2, 1, 3, 4).reshape(-1, 2, unit, width)
        qkv_all = shared(qkv_part)[0].astype(F32).reshape(parts, 3, heads, 64, width)
        qkv_all = qkv_all.transpose(0, 2, 1, 3, 4).reshape(-1, 3, 64, width)
        query_key_all, value_all = qkv_all[:, :2], qkv_all[:, 2]
    input_grad = stored_from(input_grad, F32)
    down_all, out_all = down_all.reshape(down_proj.shape), out_all.reshape(out_proj.shape)

    table_grad = lax.dynamic_slice_in_dim(every, (x * nz + z) * mine, mine, 0).T
    return (
        outputs,
        input_grad,
        pick(attn_gain_grad, z, 0),
        pick(ffn_gain_grad, z, 0),
        query_key_all.transpose(3, 0, 1, 2),
        value_all.transpose(2, 0, 1),
        out_all,
        gate_up_all.transpose(3, 0, 1, 2),
        down_all,
        table_grad,
    )


def solution(mesh):
    dp, nx, nz = (mesh.shape[name] for name in ("dp", "gx", "gy"))
    nc = dp // 2
    split = Mesh(mesh.devices.reshape(2, nc, nx, nz), ("y", "c", "x", "z"))
    seq = ("y", "c")
    return jax.shard_map(
        functools.partial(body, nx, nz, nc),
        mesh=split,
        in_specs=(
            P(seq, "x", "z"),
            P(seq),
            P("z"),
            P("z"),
            P("z", "x", None, None),
            P("z", "x", None),
            P("x", None, "z"),
            P("z", "x", None, None),
            P("x", None, "z"),
            P(None, ("x", "z")),
            P(seq, "x", "z"),
        ),
        out_specs=(
            P(seq, "x", "z"),
            P(seq, "x", "z"),
            P("z"),
            P("z"),
            P("z", "x", None, None),
            P("z", "x", None),
            P("x", None, "z"),
            P("z", "x", None, None),
            P("x", None, "z"),
            P(None, ("x", "z")),
        ),
        check_vma=False,
    )
```

```python
import functools
import math

import jax
import jax.numpy as jnp
from jax import lax
from jax.experimental import pallas as pl
from jax.experimental.pallas import tpu as pltpu
from jax.sharding import Mesh
from jax.sharding import PartitionSpec as P

norm_eps = 1e-06
masked_score = -1e30
bucket_edges = (12, 16, 23, 32, 46, 64, 91)
BF = jnp.bfloat16
F32 = jnp.float32
LB = 128
VMEM = 60 * 1024 * 1024
swap = [(0, 1), (1, 0)]
gelu_a = math.sqrt(2.0 / math.pi)
gelu_b = 0.044715


def bucket_index(offset):
    magnitude = jnp.abs(offset)
    far_bucket = 8 + sum(((magnitude >= boundary).astype(jnp.int32) for boundary in bucket_edges))
    near_bucket = jnp.where(magnitude < 8, magnitude, far_bucket)
    return near_bucket + 16 * (offset > 0).astype(jnp.int32)


def cost(flops, moved):
    return pl.CostEstimate(flops=int(flops) // 16, bytes_accessed=int(moved) // 16, transcendentals=0)


def params(steps):
    return pltpu.CompilerParams(
        dimension_semantics=("arbitrary",) * steps, vmem_limit_bytes=VMEM
    )


def dot_nt(a, b):
    return lax.dot_general(a, b, (((1,), (1,)), ((), ())), preferred_element_type=F32)


def dot_nn(a, b):
    return lax.dot_general(a, b, (((1,), (0,)), ((), ())), preferred_element_type=F32)


def spot_of(starts_ref, d, count):
    return pl.ds(pl.multiple_of(starts_ref[d], 256), count)


def piece_specs(pieces):
    shape = pieces[0].shape
    return [pl.BlockSpec(shape, lambda *_: (0, 0, 0)) for _ in pieces]


def nt_sum(piece_refs, d, w_of):
    half = piece_refs[0].shape[0]
    acc = None
    for z in range(2 * half):
        part = dot_nt(piece_refs[4 * (z // half) + d][z % half], w_of(z))
        acc = part if acc is None else acc + part
    return acc


def nt_kernel(starts_ref, *refs):
    pieces, (w_ref, out_ref) = refs[:8], refs[8:]
    for d in range(4):
        acc = nt_sum(pieces, d, lambda z: w_ref[z, 0])
        out_ref[spot_of(starts_ref, d, acc.shape[0]), :] = acc.astype(BF)


def mm_nt(pieces, w, first, rows, starts):
    nz, nc, _, width = w.shape
    total = 4 * pieces[0].shape[1]
    count, skip = rows // 256, first // 256
    return pl.pallas_call(
        nt_kernel,
        grid=(nc, count),
        in_specs=[pl.BlockSpec(memory_space=pltpu.SMEM)]
        + piece_specs(pieces)
        + [pl.BlockSpec((nz, 1, 256, width), lambda c, i: (0, c, skip + i, 0))],
        out_specs=pl.BlockSpec((total, 256), lambda c, i: (0, c * count + i)),
        out_shape=jax.ShapeDtypeStruct((total, nc * rows), BF),
        compiler_params=params(2),
        cost_estimate=cost(
            2 * nz * total * width * nc * rows, 2 * nz * width * (total + nc * rows) + 2 * total * nc * rows
        ),
        name="product_nt",
    )(starts, *pieces, w)


def nn_kernel(count, starts_ref, *refs):
    grads, (w_ref, low_out, low_keep, high_out, high_keep) = refs[:count], refs[count:]
    nc, rows, width = w_ref.shape[1:]
    t = grads[0].shape[0] // 4
    in_low = pl.program_id(0) < pl.num_programs(0) // 2

    def product(d):
        spot = spot_of(starts_ref, d, t)
        if count == 1:
            return dot_nn(grads[0][spot, :], w_ref[0].reshape(nc * rows, width)).astype(BF)
        return sum(dot_nn(grads[c][spot, :], w_ref[0, c]) for c in range(count)).astype(BF)

    @pl.when(in_low)
    def _():
        for d in range(4):
            (low_out if d // 2 else low_keep)[d % 2, 0] = product(d)

    @pl.when(jnp.logical_not(in_low))
    def _():
        for d in range(4):
            (high_out if d % 2 else high_keep)[d // 2, 0] = product(d)


def mm_nn(grads, w, first, rows, starts):
    total = grads[0].shape[0]
    nz, nc, _, width = w.shape
    skip, half, t = first // rows, nz // 2, total // 4
    low = pl.BlockSpec((2, 1, t, width), lambda z: (0, jnp.minimum(z, half - 1), 0, 0))
    high = pl.BlockSpec((2, 1, t, width), lambda z: (0, jnp.maximum(z - half, 0), 0, 0))
    return pl.pallas_call(
        functools.partial(nn_kernel, len(grads)),
        grid=(nz,),
        in_specs=[pl.BlockSpec(memory_space=pltpu.SMEM)]
        + [pl.BlockSpec(grad.shape, lambda z: (0, 0)) for grad in grads]
        + [pl.BlockSpec((1, nc, rows, width), lambda z: (z, 0, skip, 0))],
        out_specs=[low, low, high, high],
        out_shape=[jax.ShapeDtypeStruct((2, half, t, width), BF)] * 4,
        compiler_params=params(1),
        cost_estimate=cost(
            2 * nz * total * width * nc * rows, 2 * nz * width * (total + nc * rows) + 2 * total * nc * rows
        ),
        name="product_nn",
    )(starts, *grads, w)


def tn_kernel(count, starts_ref, *refs):
    grads, pieces, out_ref = refs[:count], refs[count:-1], refs[-1]
    half, t, _ = pieces[0].shape

    def one(grad_ref):
        turned = [grad_ref[spot_of(starts_ref, d, t), :].T for d in range(4)]
        for z in range(2 * half):
            acc = dot_nn(turned[0], pieces[4 * (z // half)][z % half])
            for d in range(1, 4):
                acc += dot_nn(turned[d], pieces[4 * (z // half) + d][z % half])
            out_ref[z] = acc.astype(BF)

    if count == 1:
        one(grads[0])
    else:
        for c in range(count):

            @pl.when(pl.program_id(0) // (pl.num_programs(0) // count) == c)
            def _():
                one(grads[c])


def mm_tn(grads, pieces, starts):
    total, rows = grads[0].shape
    half, _, width = pieces[0].shape
    nz, count = 2 * half, len(grads)
    block = next(b for b in (640, 384, 256) if rows % b == 0)
    steps = rows // block

    def spec(c):
        return pl.BlockSpec((total, block), lambda i: (0, jnp.clip(i - c * steps, 0, steps - 1)))

    return pl.pallas_call(
        functools.partial(tn_kernel, count),
        grid=(count * steps,),
        in_specs=[pl.BlockSpec(memory_space=pltpu.SMEM)]
        + [spec(c) for c in range(count)]
        + piece_specs(pieces),
        out_specs=pl.BlockSpec((nz, block, width), lambda i: (0, i, 0)),
        out_shape=jax.ShapeDtypeStruct((nz, count * rows, width), BF),
        compiler_params=params(1),
        cost_estimate=cost(
            2 * nz * total * width * count * rows, 2 * nz * width * (total + count * rows) + 2 * total * count * rows
        ),
        name="product_tn",
    )(starts, *grads, *pieces)


def gelu_parts(gate):
    curve = jnp.tanh(gelu_a * (gate + gelu_b * gate * gate * gate))
    value = 0.5 * gate * (1.0 + curve)
    slope = 0.5 * (1.0 + curve) + 0.5 * gate * (1.0 - curve * curve) * gelu_a * (
        1.0 + 3.0 * gelu_b * gate * gate
    )
    return value, slope


def ffn_in_kernel(starts_ref, *refs):
    pieces, (w_ref, gate_ref, up_ref, active_ref) = refs[:8], refs[8:]
    _, _, _, block, width = w_ref.shape
    for d in range(4):
        acc = nt_sum(pieces, d, lambda z: w_ref[z, 0].reshape(2 * block, width))
        spot = spot_of(starts_ref, d, acc.shape[0])
        gate, up = acc[:, :block], acc[:, block:]
        value = 0.5 * gate * (1.0 + jnp.tanh(gelu_a * (gate + gelu_b * gate * gate * gate)))
        gate_ref[spot, :] = gate.astype(BF)
        up_ref[spot, :] = up.astype(BF)
        active_ref[spot, :] = (value * up).astype(BF)


def ffn_in(pieces, w, starts):
    nz, nc, rows, width = w.shape
    half, total = rows // 2, 4 * pieces[0].shape[1]
    count = half // 128
    block = pl.BlockSpec((total, 128), lambda c, i: (0, c * count + i))
    return pl.pallas_call(
        ffn_in_kernel,
        grid=(nc, count),
        in_specs=[pl.BlockSpec(memory_space=pltpu.SMEM)]
        + piece_specs(pieces)
        + [pl.BlockSpec((nz, 1, 2, 128, width), lambda c, i: (0, c, 0, i, 0))],
        out_specs=[block, block, block],
        out_shape=[jax.ShapeDtypeStruct((total, nc * half), BF)] * 3,
        compiler_params=params(2),
        cost_estimate=cost(
            2 * nz * total * width * nc * rows, 2 * nz * width * (total + nc * rows) + 3 * total * nc * rows
        ),
        name="ffn_in",
    )(starts, *pieces, w.reshape(nz, nc, 2, half, width))


def ffn_back_kernel(starts_ref, *refs):
    pieces, (w_ref, gate_ref, up_ref, out_ref) = refs[:8], refs[8:]
    half = w_ref.shape[2]
    for d in range(4):
        acc = nt_sum(pieces, d, lambda z: w_ref[z, 0])
        spot = spot_of(starts_ref, d, acc.shape[0])
        value, slope = gelu_parts(gate_ref[spot, :].astype(F32))
        out_ref[spot, :half] = (acc * up_ref[spot, :].astype(F32) * slope).astype(BF)
        out_ref[spot, half:] = (acc * value).astype(BF)


def ffn_back(pieces, w, gate, up, starts):
    nz, nc, half, width = w.shape
    total = gate.shape[0]
    kept = pl.BlockSpec((total, half), lambda c: (0, c))
    return pl.pallas_call(
        ffn_back_kernel,
        grid=(nc,),
        in_specs=[pl.BlockSpec(memory_space=pltpu.SMEM)]
        + piece_specs(pieces)
        + [pl.BlockSpec((nz, 1, half, width), lambda c: (0, c, 0, 0)), kept, kept],
        out_specs=pl.BlockSpec((total, 2 * half), lambda c: (0, c)),
        out_shape=jax.ShapeDtypeStruct((total, nc * 2 * half), BF),
        compiler_params=params(1),
        cost_estimate=cost(
            2 * nz * total * width * nc * half, 2 * nz * width * (total + nc * half) + 8 * total * nc * half
        ),
        name="ffn_back",
    )(starts, *pieces, w, gate, up)


def mm_nt_plain(act, w, first, rows, starts):
    part = lax.slice_in_dim(w, first, first + rows, axis=2)
    out = jnp.einsum("ztf,zcrf->tcr", act, part, preferred_element_type=F32)
    return out.astype(BF).reshape(act.shape[1], -1)


def mm_nn_plain(grads, w, first, rows, starts):
    grad = grads[0]
    part = lax.slice_in_dim(w, first, first + rows, axis=2)
    split = grad.reshape(grad.shape[0], w.shape[1], rows)
    out = jnp.einsum("tcr,zcrf->ztf", split, part, preferred_element_type=F32)
    return [out.astype(BF)]


def mm_tn_plain(grads, act, starts):
    return jnp.einsum("tr,ztf->zrf", grads[0], act, preferred_element_type=F32).astype(BF)


def ffn_in_plain(act, w, starts):
    _, nc, rows, _ = w.shape
    total = act.shape[1]
    both = jnp.einsum("ztf,zcrf->tcr", act, w, preferred_element_type=F32)
    gate, up = both[:, :, : rows // 2], both[:, :, rows // 2 :]
    value, _ = gelu_parts(gate)
    return [part.astype(BF).reshape(total, -1) for part in (gate, up, value * up)]


def ffn_back_plain(act, w, gate, up, starts):
    total, nc = gate.shape[0], w.shape[1]
    grad = jnp.einsum("ztf,zcrf->tcr", act, w, preferred_element_type=F32)
    value, slope = gelu_parts(gate.astype(F32).reshape(grad.shape))
    both = [grad * up.astype(F32).reshape(grad.shape) * slope, grad * value]
    return jnp.concatenate(both, axis=2).astype(BF).reshape(total, -1)


def near_buckets(tile, total):
    first = (total // LB - 2 + tile) * LB
    rows = lax.broadcasted_iota(jnp.int32, (LB, LB), 0)
    lanes = lax.broadcasted_iota(jnp.int32, (LB, LB), 1)
    return bucket_index(first + rows - (total - LB) - lanes)


def near_kernel(total, table_ref, out_ref):
    heads = out_ref.shape[0]

    def one_tile(tile, _):
        index = near_buckets(tile, total)
        vals = [jnp.full((LB, LB), table_ref[h, 0], F32) for h in range(heads)]
        for b in range(1, 32):
            hit = index == b
            vals = [jnp.where(hit, table_ref[h, b], vals[h]) for h in range(heads)]
        for h in range(heads):
            out_ref[h, pl.ds(pl.multiple_of(tile * LB, LB), LB)] = vals[h]
        return 0

    lax.fori_loop(0, 3, one_tile, 0)


def near_bias(table, total):
    heads = table.shape[0]
    return pl.pallas_call(
        functools.partial(near_kernel, total),
        in_specs=[pl.BlockSpec(memory_space=pltpu.SMEM)],
        out_specs=pl.BlockSpec((heads, 3 * LB, LB), lambda: (0, 0, 0)),
        out_shape=jax.ShapeDtypeStruct((heads, 3 * LB, LB), F32),
        compiler_params=params(0),
        cost_estimate=cost(0, heads * LB * LB),
        name="near_bias",
    )(table)


def build_strips(table_ref, near_ref, strip_ref, total, group):
    heads = strip_ref.shape[0]
    near = (total // LB - 2) * LB
    for h in range(heads):
        head = group * heads + h
        strip_ref[h, :near] = jnp.full((near, LB), table_ref[head, 15], F32)
        strip_ref[h, near : near + 3 * LB] = near_ref[h]
        strip_ref[h, near + 3 * LB :] = jnp.full((near, LB), table_ref[head, 31], F32)


def table_kernel(total, *refs):
    parts, out_ref = refs[:-1], refs[-1]
    index = [near_buckets(tile, total) for tile in range(3)]
    buckets = [range(1, 16), [b for b in range(32) if b != 16], range(17, 32)]
    for g, part_ref in enumerate(parts):
        heads = part_ref.shape[0]

        def one_head(h, _):
            here = g * heads + h
            out_ref[here] = jnp.zeros((32, LB), F32)
            out_ref[here, 15:16] = part_ref[h, 3 * LB : 3 * LB + 1]
            out_ref[here, 31:32] = part_ref[h, 3 * LB + 8 : 3 * LB + 9]
            for tile in range(3):
                grads = part_ref[h, tile * LB : (tile + 1) * LB]
                for b in buckets[tile]:
                    picked = jnp.where(index[tile] == b, grads, 0.0)
                    out_ref[here, b : b + 1] += jnp.sum(picked, axis=0, keepdims=True)
            return 0

        lax.fori_loop(0, heads, one_head, 0)


def table_sums(parts, total):
    heads = len(parts) * parts[0].shape[0]
    out = pl.pallas_call(
        functools.partial(table_kernel, total),
        in_specs=[pl.BlockSpec(part.shape, lambda: (0, 0, 0)) for part in parts],
        out_specs=pl.BlockSpec((heads, 32, LB), lambda: (0, 0, 0)),
        out_shape=jax.ShapeDtypeStruct((heads, 32, LB), F32),
        compiler_params=params(0),
        cost_estimate=cost(0, heads * LB * LB),
        name="table_sums",
    )(*parts)
    return jnp.sum(out, axis=2)


def head_lanes(shape, h):
    lanes = lax.broadcasted_iota(jnp.int32, shape, 1)
    return lanes // 64 == h, lanes == ((h + 1) % 4) * 64


def mask_keys(keys, length, h):
    own, spare = head_lanes(keys.shape, h)
    dead = lax.broadcasted_iota(jnp.int32, keys.shape, 0) >= length
    mask = jnp.where(jnp.logical_and(spare, dead), masked_score, 0.0)
    return jnp.where(own, keys.astype(F32), mask).astype(BF)


def with_one(queries, h):
    _, spare = head_lanes(queries.shape, h)
    return jnp.where(spare, 1.0, queries.astype(F32)).astype(BF)


def own_lanes(values, h):
    own, _ = head_lanes(values.shape, h)
    return jnp.where(own, values.astype(F32), 0.0).astype(BF)


def block_bias(strip_ref, h, block, total):
    first = total - LB - 2 * block * LB
    left = strip_ref[h, pl.ds(pl.multiple_of(first, LB), total)]
    right = strip_ref[h, pl.ds(pl.multiple_of(first - LB, LB), total)]
    return jnp.concatenate([left, right], axis=1)


def attend_kernel(group, length_ref, table_ref, near_ref, q_ref, k_ref, v_ref, out_ref, lse_ref, strip, heads_k, turned_v, turned_out):
    total = q_ref.shape[0]
    heads = strip.shape[0]
    build_strips(table_ref, near_ref, strip, total, group)
    turned_v[...] = v_ref[...].astype(F32).T.astype(BF)
    for h in range(heads):
        heads_k[h] = mask_keys(k_ref[...], length_ref[0], h)

    def one_block(block, _):
        spot = pl.ds(pl.multiple_of(block * 256, 256), 256)
        queries = q_ref[spot]
        for h in range(heads):
            scores = dot_nt(heads_k[h], with_one(queries, h)) + block_bias(strip, h, block, total)
            largest = jnp.max(scores, axis=0, keepdims=True)
            raised = jnp.exp(scores - largest)
            totals = jnp.sum(raised, axis=0, keepdims=True)
            out = dot_nn(turned_v[h * 64 : (h + 1) * 64], raised.astype(BF))
            turned_out[h * 64 : (h + 1) * 64, spot] = out * (1.0 / totals)
            lse_ref[h : h + 1, spot] = largest + jnp.log(totals)
        return 0

    lax.fori_loop(0, total // 256, one_block, 0)
    out_ref[...] = turned_out[...].T.astype(BF)


def attend_back_kernel(
    group, length_ref, table_ref, near_ref, q_ref, k_ref, v_ref, grad_ref, lse_ref, out_ref, table_grad_ref,
    strip, strip_grad, heads_k, turned_k, turned_q, ds_ref, p_ref, dk_ref, dv_ref,
):
    total = q_ref.shape[0]
    heads = strip.shape[0]
    build_strips(table_ref, near_ref, strip, total, group)
    strip_grad[...] = jnp.zeros_like(strip_grad)
    dk_ref[...] = jnp.zeros_like(dk_ref)
    dv_ref[...] = jnp.zeros_like(dv_ref)
    turned_k[...] = k_ref[...].astype(F32).T.astype(BF)
    for h in range(heads):
        heads_k[h] = mask_keys(k_ref[...], length_ref[0], h)

    def one_block(block, _):
        spot = pl.ds(pl.multiple_of(block * 256, 256), 256)
        queries, grads = q_ref[spot], grad_ref[spot]
        own_q, own_g = [], []
        for h in range(heads):
            own_q.append(own_lanes(queries, h))
            own_g.append(own_lanes(grads, h))
            scores = dot_nt(heads_k[h], with_one(queries, h)) + block_bias(strip, h, block, total)
            probs = jnp.exp(scores - lse_ref[h : h + 1, spot])
            weighed = probs * dot_nt(v_ref[...], own_g[h])
            delta = jnp.sum(weighed, axis=0, keepdims=True)
            grad_scores = weighed - probs * delta
            first = total - LB - 2 * block * LB
            left = pl.ds(pl.multiple_of(first, LB), total)
            right = pl.ds(pl.multiple_of(first - LB, LB), total)
            strip_grad[h, left] += grad_scores[:, :LB]
            strip_grad[h, right] += grad_scores[:, LB:]
            rounded = grad_scores.astype(BF)
            ds_ref[:, h * 256 : (h + 1) * 256] = rounded
            p_ref[:, h * 256 : (h + 1) * 256] = probs.astype(BF)
            turned_q[h * 64 : (h + 1) * 64, spot] = dot_nn(turned_k[h * 64 : (h + 1) * 64], rounded)
        dk_ref[...] += dot_nn(ds_ref[...], jnp.concatenate(own_q, axis=0))
        dv_ref[...] += dot_nn(p_ref[...], jnp.concatenate(own_g, axis=0))
        return 0

    lax.fori_loop(0, total // 256, one_block, 0)
    out_ref[:, :256] = turned_q[...].T.astype(BF)
    out_ref[:, 256:512] = dk_ref[...].astype(BF)
    out_ref[:, 512:] = dv_ref[...].astype(BF)

    near = (total // LB - 2) * LB
    for h in range(heads):
        table_grad_ref[h, : 3 * LB] = strip_grad[h, near : near + 3 * LB]
        left = jnp.sum(strip_grad[h, :near], axis=0, keepdims=True)
        right = jnp.sum(strip_grad[h, near + 3 * LB :], axis=0, keepdims=True)
        table_grad_ref[h, 3 * LB : 3 * LB + 8] = jnp.broadcast_to(left, (8, LB))
        table_grad_ref[h, 3 * LB + 8 :] = jnp.broadcast_to(right, (8, LB))


def block_specs(total, group):
    def spec(i):
        return pl.BlockSpec((total, 256), lambda _: (0, 3 * group + i))

    smem = pl.BlockSpec(memory_space=pltpu.SMEM)
    near = pl.BlockSpec((4, 3 * LB, LB), lambda _: (group, 0, 0))
    return [smem, smem, near, spec(0), spec(1), spec(2)]


def attend(group, projected, length, table, near):
    total = projected.shape[0]
    heads = 4
    return pl.pallas_call(
        functools.partial(attend_kernel, group),
        grid=(1,),
        in_specs=block_specs(total, group),
        out_specs=[
            pl.BlockSpec((total, 256), lambda _: (0, 0)),
            pl.BlockSpec((8, total), lambda _: (0, 0)),
        ],
        out_shape=[
            jax.ShapeDtypeStruct((total, 256), BF),
            jax.ShapeDtypeStruct((8, total), F32),
        ],
        scratch_shapes=[
            pltpu.VMEM((heads, 2 * total - LB, LB), F32),
            pltpu.VMEM((heads, total, 256), BF),
            pltpu.VMEM((256, total), BF),
            pltpu.VMEM((256, total), F32),
        ],
        compiler_params=params(1),
        cost_estimate=cost(heads * total * total * 2 * 256 * 2, 4 * total * 256 * 2),
        name="attend",
    )(length, table, near, projected, projected, projected)


def attend_back(group, projected, length, table, near, grad_out, lse):
    total = projected.shape[0]
    heads = 4
    return pl.pallas_call(
        functools.partial(attend_back_kernel, group),
        grid=(1,),
        in_specs=block_specs(total, group)
        + [
            pl.BlockSpec((total, 256), lambda _: (0, group)),
            pl.BlockSpec((8, total), lambda _: (0, 0)),
        ],
        out_specs=[
            pl.BlockSpec((total, 768), lambda _: (0, 0)),
            pl.BlockSpec((heads, 3 * LB + 16, LB), lambda _: (0, 0, 0)),
        ],
        out_shape=[
            jax.ShapeDtypeStruct((total, 768), BF),
            jax.ShapeDtypeStruct((heads, 3 * LB + 16, LB), F32),
        ],
        scratch_shapes=[
            pltpu.VMEM((heads, 2 * total - LB, LB), F32),
            pltpu.VMEM((heads, 2 * total - LB, LB), F32),
            pltpu.VMEM((heads, total, 256), BF),
            pltpu.VMEM((256, total), BF),
            pltpu.VMEM((256, total), F32),
            pltpu.VMEM((total, heads * 256), BF),
            pltpu.VMEM((total, heads * 256), BF),
            pltpu.VMEM((total, 256), F32),
            pltpu.VMEM((total, 256), F32),
        ],
        compiler_params=params(1),
        cost_estimate=cost(heads * total * total * 2 * 256 * 5, 8 * total * 256 * 2),
        name="attend_back",
    )(length, table, near, projected, projected, projected, grad_out, lse)


def split_heads(projected, groups, heads):
    parts = projected.reshape(projected.shape[0], groups, 3, heads, 64)
    return [parts[:, :, i].reshape(projected.shape[0], groups * heads, 64) for i in range(3)]


def plain_scores(queries, keys, length, table):
    slots = jnp.arange(keys.shape[0], dtype=jnp.int32)
    picked = (bucket_index(slots[None, :] - slots[:, None])[:, :, None] == jnp.arange(32)).astype(F32)
    bias = jnp.einsum("qkb,hb->hqk", picked, table, precision=lax.Precision.HIGHEST)
    scores = jnp.einsum("qhs,khs->hqk", queries, keys, preferred_element_type=F32) + bias
    return jnp.where(slots < length[0], scores, masked_score), picked


def attend_plain(projected, length, table, groups, heads):
    queries, keys, values = split_heads(projected, groups, heads)
    scores, _ = plain_scores(queries, keys, length, table)
    lse = jax.nn.logsumexp(scores, axis=2)
    probs = jnp.exp(scores - lse[:, :, None]).astype(BF)
    out = jnp.einsum("hqk,khs->qhs", probs, values, preferred_element_type=F32)
    return out.astype(BF).reshape(projected.shape[0], -1), lse


def attend_back_plain(projected, length, table, grad_out, lse, groups, heads):
    total = projected.shape[0]
    queries, keys, values = split_heads(projected, groups, heads)
    grads = grad_out.reshape(queries.shape)
    scores, picked = plain_scores(queries, keys, length, table)
    probs = jnp.exp(scores - lse[:, :, None])
    weighed = probs * jnp.einsum("qhs,khs->hqk", grads, values, preferred_element_type=F32)
    wide = weighed - probs * jnp.sum(weighed, axis=2, keepdims=True)
    rounded = wide.astype(BF)
    parts = [
        jnp.einsum("hqk,khs->qhs", rounded, keys, preferred_element_type=F32),
        jnp.einsum("hqk,qhs->khs", rounded, queries, preferred_element_type=F32),
        jnp.einsum("hqk,qhs->khs", probs.astype(BF), grads, preferred_element_type=F32),
    ]
    parts = [part.astype(BF).reshape(total, groups, 1, heads * 64) for part in parts]
    table_grad = jnp.einsum("hqk,qkb->hb", wide, picked, precision=lax.Precision.HIGHEST)
    return (
        jnp.concatenate(parts, axis=2).reshape(total, -1),
        table_grad.reshape(groups * heads, 32, 1),
    )


def hop(value, axis):
    return lax.ppermute(value, axis, swap)


def pick(value, index, axis):
    return lax.dynamic_index_in_dim(value, index, axis, keepdims=False)


def paired(mine, other, axis, place=0):
    return jnp.where(
        lax.axis_index(axis) == 0,
        jnp.stack([mine, other], axis=place),
        jnp.stack([other, mine], axis=place),
    )


def after(value, *others):
    return lax.optimization_barrier((value, *others))[0]


def gather_plain(part, *beside):
    return lax.all_gather(part, ("x", "y"), axis=1, tiled=True), (), ()


def gather_tokens(part, *beside):
    half = part.shape[0] // 2
    low, high = part[:half], part[half:]
    low_x, high_y = hop(low, "x"), hop(high, "y")
    if beside:
        low_x, high_y = after(low_x, *beside), after(high_y, *beside)
    low_y, high_x = hop(low, "y"), hop(high, "x")
    low_xy, high_xy = hop(low_x, "y"), hop(high_y, "x")
    pieces = [low, low_y, low_x, low_xy, high, high_y, high_x, high_xy]
    return pieces, (low_x, high_y), (low_y, low_xy, high_x, high_xy)


def scatter_plain(parts, beside=(), beside_last=()):
    whole = parts[0].astype(F32)
    return lax.psum_scatter(whole, ("x", "y"), scatter_dimension=1, tiled=True), (), ()


def scatter_tokens(parts, beside=(), beside_last=()):
    low_out, low_keep, high_out, high_keep = parts
    low_in, high_in = hop(low_out, "x"), hop(high_out, "y")
    if beside:
        low_in, high_in = after(low_in, *beside), after(high_in, *beside)

    def add(keep, arrived, index):
        return keep[index].astype(F32) + arrived[index].astype(F32)

    low_last = hop(add(low_keep, low_in, 1).astype(BF), "y")
    high_last = hop(add(high_keep, high_in, 1).astype(BF), "x")
    if beside_last:
        low_last, high_last = after(low_last, *beside_last), after(high_last, *beside_last)
    low = add(low_keep, low_in, 0) + low_last.astype(F32)
    high = add(high_keep, high_in, 0) + high_last.astype(F32)
    return jnp.concatenate([low, high], axis=0), (low_in, high_in), (low_last, high_last)


def place_kernel(write, here_ref, *refs):
    pieces, outs = refs[:4], refs[4:]
    step = pl.program_id(0)
    for near in range(4):
        y = here_ref[0] if near < 2 else 1 - here_ref[0]
        c = here_ref[1] if near % 2 == 0 else 1 - here_ref[1]

        @pl.when(step == 2 * y + c)
        def _():
            write(pieces[near], outs)


def place(pieces, here, shapes, write):
    return pl.pallas_call(
        functools.partial(place_kernel, write),
        grid=(4,),
        in_specs=[pl.BlockSpec(memory_space=pltpu.SMEM)]
        + [pl.BlockSpec(piece.shape, lambda q: (0, 0)) for piece in pieces],
        out_specs=[
            pl.BlockSpec(shape, lambda q, rank=len(shape): (q,) + (0,) * (rank - 1)) for shape in shapes
        ],
        out_shape=[jax.ShapeDtypeStruct((4 * shape[0], *shape[1:]), F32) for shape in shapes],
        compiler_params=params(1),
        cost_estimate=cost(0, pieces[0].size),
        name="place",
    )(here, *pieces)


def share(part, *beside):
    over_y = hop(part, "y")
    if beside:
        over_y = after(over_y, *beside)
    return [part, hop(part, "c"), over_y, hop(over_y, "c")], over_y


def share_plain(part):
    return lax.all_gather(part, ("y", "c"), axis=0), part


def to_groups(halves, other, extra):
    count, _, t, width = halves.shape
    both = paired(pick(halves, lax.axis_index("y"), 1), other, "y").reshape(2 * count, t, width)
    if extra is not None:
        wide = jnp.broadcast_to(extra[None], (2 * count, *extra.shape))
        both = jnp.concatenate([both, wide], axis=1)
    return lax.all_to_all(both, "z", 0, 0, tiled=True)


def from_groups(mine):
    nz, t, width = mine.shape
    back = lax.all_to_all(mine, "z", 0, 0, tiled=True).reshape(2, nz // 2, t, width)
    leaving = pick(back, 1 - lax.axis_index("y"), 0)
    return (back, hop(leaving, "y")), leaving


def settle_kernel(y_ref, back_ref, other_ref, out_ref):
    j, y = pl.program_id(0), pl.program_id(1)

    @pl.when(y == y_ref[0])
    def _():
        out_ref[0, 0] = back_ref[y, j].astype(out_ref.dtype)

    @pl.when(y != y_ref[0])
    def _():
        out_ref[0, 0] = other_ref[j].astype(out_ref.dtype)


def settle(arrived, dtype):
    back, other = arrived
    _, count, t, width = back.shape
    y = lax.axis_index("y").astype(jnp.int32).reshape(1)
    out = pl.pallas_call(
        settle_kernel,
        grid=(count, 2),
        in_specs=[
            pl.BlockSpec(memory_space=pltpu.SMEM),
            pl.BlockSpec(back.shape, lambda j, y: (0, 0, 0, 0)),
            pl.BlockSpec(other.shape, lambda j, y: (0, 0, 0)),
        ],
        out_specs=pl.BlockSpec((1, 1, t, width), lambda j, y: (j, y, 0, 0)),
        out_shape=jax.ShapeDtypeStruct((count, 2, t, width), dtype),
        compiler_params=params(2),
        cost_estimate=cost(0, count * t * width),
        name="settle",
    )(y, back, other)
    return out.reshape(count, 2 * t, width)


def settle_plain(arrived, dtype):
    back, other = arrived
    _, count, t, width = back.shape
    both = paired(pick(back, lax.axis_index("y"), 0), other, "y")
    return both.transpose(1, 0, 2, 3).reshape(count, 2 * t, width).astype(dtype)


def sum_plane(value, nx, *earlier):
    value = value + after(hop(value, "c"), *earlier)
    value = value + hop(value, "x") if nx == 2 else lax.psum(value, "x")
    return value + hop(value, "y")


def sum_line(value, nz):
    step = 1
    while step < nz:
        value = value + lax.ppermute(value, "z", [(i, i ^ step) for i in range(nz)])
        step *= 2
    return value


def body(
    nx, nz, nc, inputs, lengths, attn_gain, ffn_gain, query_key, value_proj, out_proj, gate_up, down_proj, bias_table, cotangent
):
    x, y = lax.axis_index("x"), lax.axis_index("y")
    c, z = lax.axis_index("c"), lax.axis_index("z")
    width = inputs.shape[2]
    features = nz * width
    quarter = y * nc + c
    parts = 2 * nc
    buckets, mine = bias_table.shape
    count = inputs.shape[1] // 2

    stored_in = inputs.reshape(inputs.shape[0], 2, count, width)
    stored_cot = cotangent.reshape(stored_in.shape)
    small = jnp.concatenate(
        [attn_gain[None], ffn_gain[None], jnp.pad(bias_table.reshape(1, -1), ((0, 0), (0, width - buckets * mine)))]
    )
    small = jnp.pad(small, ((0, 5), (0, 0)))
    leaving = pick(stored_in, 1 - y, 1)

    query_key_rows = jnp.transpose(query_key, (1, 2, 3, 0))
    value_rows = jnp.transpose(value_proj, (1, 2, 0))
    gate_up_rows = jnp.transpose(gate_up, (1, 2, 3, 0))
    heads = value_rows.shape[0] // parts
    units = gate_up_rows.shape[0] // parts
    unit = gate_up_rows.shape[2]
    local_heads = nc * heads

    def own(rows, size):
        return lax.dynamic_slice_in_dim(rows, quarter * size, size, 0)

    def flat(rows):
        return rows.reshape(-1, width)

    def spread(rows):
        gathered = lax.all_gather(rows, ("z", "c"), axis=0, tiled=True)
        return gathered.reshape(nz, nc, rows.shape[0], width)

    own_pair = own(query_key_rows, heads)
    own_attn = [own_pair[:, 0], own_pair[:, 1], own(value_rows, heads), own(out_proj, heads)]
    own_attn = jnp.concatenate([flat(rows) for rows in own_attn])
    w_attn = spread(own_attn)
    other = after(hop(leaving, "y"), own_attn)
    own_pair = own(after(gate_up_rows, other), units)
    own_gate_up = jnp.concatenate([flat(own_pair[:, 0]), flat(own_pair[:, 1])])
    w_gate_up = spread(own_gate_up)
    own_down = flat(own(after(down_proj, other), units))
    w_down = spread(own_down)
    qkv_count, out_count = 3 * heads * 64, heads * 64

    both_lengths = jnp.stack([lengths, lax.ppermute(lengths, "y", swap)])
    both_lengths = jnp.where(y == 0, both_lengths, both_lengths[::-1]).reshape(-1)
    length = lax.dynamic_slice_in_dim(both_lengths, z, 1, 0)
    slots = (x * 2 + y) * count + jnp.arange(count, dtype=jnp.int32)
    near_x, near_y = jnp.array([0, 0, 1, 1]) ^ x, jnp.array([0, 1, 0, 1]) ^ y
    starts = ((near_x * 2 + near_y) * count).astype(jnp.int32)
    arrived = after(to_groups(stored_in, other, small), own_gate_up, own_down, length, starts)
    tokens = arrived[:, :count].astype(F32)
    small = arrived[:, count:]
    gain_one = small[:, :1].astype(F32)
    gain_two = small[:, 1:2].astype(F32)
    table = small[:, 2, : buckets * mine].reshape(nz, buckets, mine).transpose(0, 2, 1)
    table = table.reshape(-1, buckets).astype(F32)
    table = lax.dynamic_slice_in_dim(table, y * local_heads, local_heads, 0)

    live = (slots < length).astype(F32)[None, :, None]

    def scale_of(values):
        squares = jnp.sum(values * values, axis=(0, 2), keepdims=True)
        return lax.rsqrt(squares / features + norm_eps)

    def norm_back(values, scale, gain, grad):
        inner = jnp.sum(values * gain * grad, axis=(0, 2), keepdims=True)
        out = scale * gain * grad - values * (scale * scale * scale) * inner / features
        return out, jnp.sum(values * scale * grad, axis=1)

    def reduce(partial):
        rows = partial.reshape(nz * partial.shape[1], width)
        return lax.psum_scatter(rows, ("z", "c"), scatter_dimension=0, tiled=True)

    fits = nx == 2 and heads == 4 and count == 256 and units * unit % 640 == 0 and nz % 2 == 0
    if fits:
        forward, backward, gather, scatter = attend, attend_back, gather_tokens, scatter_tokens
        nt, nn, tn, ffn_one, ffn_two = mm_nt, mm_nn, mm_tn, ffn_in, ffn_back
        shared, stored_from = share, settle
    else:
        forward, backward, gather, scatter = attend_plain, attend_back_plain, gather_plain, scatter_plain
        nt, nn, tn, ffn_one, ffn_two = mm_nt_plain, mm_nn_plain, mm_tn_plain, ffn_in_plain, ffn_back_plain
        shared, stored_from = share_plain, settle_plain
    scale_one = scale_of(tokens)
    near = near_bias(table, 4 * count) if fits else table
    normed, _, _ = gather((tokens * scale_one * gain_one).astype(BF), near, live)
    cot_other = hop(pick(stored_cot, 1 - y, 1), "y")
    upstream = live * to_groups(stored_cot, after(cot_other, arrived), None).astype(F32)
    upstream_rounded = after(upstream.astype(BF), w_attn)
    projected = nt(normed, w_attn, 0, qkv_count, starts)
    if fits:
        first = forward(0, projected, length, table, near)
        grad_ffn, cot_first, cot_last = gather(upstream_rounded, first[0])
        second = forward(1, after(projected, first[0], *cot_first), length, table, near)
        attended, lse = (first[0], second[0]), (first[1], second[1])
    else:
        grad_ffn, _, cot_last = gather(upstream_rounded)
        attended, lse = forward(projected, length, table, nc, heads)
        attended = (attended,)
    heads_out = [after(attended[0], *cot_last), *attended[1:]]
    hidden = tokens + scatter(nn(heads_out, w_attn, qkv_count, out_count, starts))[0]
    scale_two = scale_of(hidden)
    normed_two, _, _ = gather((hidden * scale_two * gain_two).astype(BF))
    gate, up, activated = ffn_one(normed_two, w_gate_up, starts)

    down_partial = tn([activated], grad_ffn, starts)
    down_part = reduce(down_partial)
    grad_gate_up = ffn_two(grad_ffn, w_down, after(gate, down_partial), up, starts)
    two_parts = nn([grad_gate_up], w_gate_up, 0, 2 * units * unit, starts)
    grad_two, two_first, _ = scatter(two_parts)
    gate_up_partial = tn([after(grad_gate_up, two_parts[0])], normed_two, starts)
    gate_up_part = reduce(after(gate_up_partial, down_part, *two_first))
    branch_parts = nn([after(activated, gate_up_partial)], w_down, 0, units * unit, starts)
    through, ffn_gain_part = norm_back(hidden, scale_two, gain_two, grad_two)
    grad_hidden = upstream + through
    grad_branch, _, branch_here = gather(after(grad_hidden.astype(BF), branch_parts[0]))
    grad_attended = nt(grad_branch, w_attn, qkv_count, out_count, starts)
    out_partial = tn(attended, grad_branch, starts)
    grad_attended = after(grad_attended, out_partial)
    branch_parts = [after(part, *branch_here) for part in branch_parts]
    down_pieces, down_last = shared(after(down_part, *branch_here))
    if fits:
        first = backward(0, projected, length, table, near, grad_attended, lse[0])
        branch, branch_first, branch_last = scatter(branch_parts, (first[0], down_last))
    else:
        branch, branch_first, branch_last = scatter(branch_parts)
    if fits:
        second = backward(
            1, after(projected, first[0], *branch_last), length, table, near, grad_attended, lse[1]
        )
        grad_projected, table_part = (first[0], second[0]), (first[1], second[1])
    else:
        grads, table_part = backward(projected, length, table, grad_attended, lse, nc, heads)
        grad_projected, table_part = (grads,), table_part[:, :, 0]
    out_part = reduce(after(out_partial, gate_up_part, grad_projected[0], *branch_last))
    outputs = (live * (hidden + branch)).astype(BF)
    outputs, _ = from_groups(outputs)
    qkv_partial = tn(grad_projected, normed, starts)
    gate_up_pieces, gate_up_last = shared(after(gate_up_part, grad_projected[0]))
    qkv_part = reduce(after(qkv_partial, gate_up_last, outputs[0]))
    one_parts = nn(grad_projected, w_attn, 0, qkv_count, starts)
    if fits:
        here = jnp.stack([y, c]).astype(jnp.int32)

        def write_rows(source, outs):
            outs[0][...] = source[...].astype(F32)

        def write_qkv(source, outs):
            for h in range(heads):
                for i in range(3):
                    value = source[(i * heads + h) * 64 : (i * heads + h + 1) * 64, :].astype(F32)
                    if i == 2:
                        outs[1][h] = value
                    else:
                        outs[0][h, i] = value

        def write_gate_up(source, outs):
            for u in range(units):
                for i in range(2):
                    first = (i * units + u) * unit
                    outs[0][u, i] = source[first : first + unit, :].astype(F32)

        down_pieces = [after(down_pieces[0], outputs[1]), *down_pieces[1:]]
        (down_all,) = place(down_pieces, here, [(units * unit, width)], write_rows)
        (gate_up_all,) = place(gate_up_pieces, here, [(units, 2, unit, width)], write_gate_up)
    beside = (down_all, gate_up_all, outputs[0]) if fits else ()
    table_part = table_sums(table_part, 4 * count) if fits else table_part
    grad_one, _, one_last = scatter(one_parts, beside, (table_part,))
    through, attn_gain_part = norm_back(tokens, scale_one, gain_one, grad_one)
    input_grad, input_leaves = from_groups((grad_hidden + through).astype(BF))

    out_pieces, out_last = shared(out_part)

    every = jnp.zeros((nx * 2 * local_heads, table_part.shape[1]), F32)
    every = lax.dynamic_update_slice_in_dim(every, table_part, (x * 2 + y) * local_heads, 0)
    spare = -every.size % width
    every = jnp.pad(every.reshape(-1), (0, spare)).reshape(-1, width)
    sums = sum_plane(jnp.concatenate([attn_gain_part, ffn_gain_part, every]), nx, out_last)
    all_sums = sum_line(after(sums, input_leaves), nz)
    attn_gain_grad, ffn_gain_grad = all_sums[:nz], all_sums[nz : 2 * nz]
    every = all_sums[2 * nz :].reshape(-1)[: nx * 2 * local_heads * buckets].reshape(-1, buckets)

    outputs = stored_from(outputs, BF)
    if fits:
        (out_all,) = place(out_pieces, here, [(heads * 64, width)], write_rows)
        qkv_pieces, _ = shared(after(qkv_part, sums, *one_last), out_all, outputs)
        query_key_all, value_all = place(
            qkv_pieces, here, [(heads, 2, 64, width), (heads, 64, width)], write_qkv
        )
    else:
        down_all, out_all = down_pieces.astype(F32), out_pieces.astype(F32)
        gate_up_all = gate_up_pieces.astype(F32).reshape(parts, 2, units, unit, width)
        gate_up_all = gate_up_all.transpose(0, 2, 1, 3, 4).reshape(-1, 2, unit, width)
        qkv_all = shared(qkv_part)[0].astype(F32).reshape(parts, 3, heads, 64, width)
        qkv_all = qkv_all.transpose(0, 2, 1, 3, 4).reshape(-1, 3, 64, width)
        query_key_all, value_all = qkv_all[:, :2], qkv_all[:, 2]
    back, other = input_grad
    input_grad = stored_from((back, after(other, query_key_all)), F32)
    down_all, out_all = down_all.reshape(down_proj.shape), out_all.reshape(out_proj.shape)

    table_grad = lax.dynamic_slice_in_dim(every, (x * nz + z) * mine, mine, 0).T
    return (
        outputs,
        input_grad,
        pick(attn_gain_grad, z, 0),
        pick(ffn_gain_grad, z, 0),
        query_key_all.transpose(3, 0, 1, 2),
        value_all.transpose(2, 0, 1),
        out_all,
        gate_up_all.transpose(3, 0, 1, 2),
        down_all,
        table_grad,
    )


def solution(mesh):
    dp, nx, nz = (mesh.shape[name] for name in ("dp", "gx", "gy"))
    nc = dp // 2
    split = Mesh(mesh.devices.reshape(2, nc, nx, nz), ("y", "c", "x", "z"))
    seq = ("y", "c")
    return jax.shard_map(
        functools.partial(body, nx, nz, nc),
        mesh=split,
        in_specs=(
            P(seq, "x", "z"),
            P(seq),
            P("z"),
            P("z"),
            P("z", "x", None, None),
            P("z", "x", None),
            P("x", None, "z"),
            P("z", "x", None, None),
            P("x", None, "z"),
            P(None, ("x", "z")),
            P(seq, "x", "z"),
        ),
        out_specs=(
            P(seq, "x", "z"),
            P(seq, "x", "z"),
            P("z"),
            P("z"),
            P("z", "x", None, None),
            P("z", "x", None),
            P("x", None, "z"),
            P("z", "x", None, None),
            P("x", None, "z"),
            P(None, ("x", "z")),
        ),
        check_vma=False,
    )
```

```python
import functools
import math

import jax
import jax.numpy as jnp
from jax import lax
from jax.experimental import pallas as pl
from jax.experimental.pallas import tpu as pltpu
from jax.sharding import Mesh
from jax.sharding import PartitionSpec as P

norm_eps = 1e-06
masked_score = -1e30
bucket_edges = (12, 16, 23, 32, 46, 64, 91)
BF = jnp.bfloat16
F32 = jnp.float32
LB = 128
VMEM = 60 * 1024 * 1024
swap = [(0, 1), (1, 0)]
gelu_a = math.sqrt(2.0 / math.pi)
gelu_b = 0.044715


def bucket_index(offset):
    magnitude = jnp.abs(offset)
    far_bucket = 8 + sum(((magnitude >= boundary).astype(jnp.int32) for boundary in bucket_edges))
    near_bucket = jnp.where(magnitude < 8, magnitude, far_bucket)
    return near_bucket + 16 * (offset > 0).astype(jnp.int32)


def cost(flops, moved):
    return pl.CostEstimate(flops=int(flops) // 16, bytes_accessed=int(moved) // 16, transcendentals=0)


def params(steps):
    return pltpu.CompilerParams(
        dimension_semantics=("arbitrary",) * steps, vmem_limit_bytes=VMEM
    )


def dot_nt(a, b):
    return lax.dot_general(a, b, (((1,), (1,)), ((), ())), preferred_element_type=F32)


def dot_nn(a, b):
    return lax.dot_general(a, b, (((1,), (0,)), ((), ())), preferred_element_type=F32)


def spot_of(starts_ref, d, count):
    return pl.ds(pl.multiple_of(starts_ref[d], 256), count)


def piece_specs(pieces):
    shape = pieces[0].shape
    return [pl.BlockSpec(shape, lambda *_: (0, 0, 0)) for _ in pieces]


def nt_sum(piece_refs, d, w_of):
    half = piece_refs[0].shape[0]
    acc = None
    for z in range(2 * half):
        part = dot_nt(piece_refs[4 * (z // half) + d][z % half], w_of(z))
        acc = part if acc is None else acc + part
    return acc


def nt_kernel(starts_ref, *refs):
    pieces, (w_ref, out_ref) = refs[:8], refs[8:]
    for d in range(4):
        acc = nt_sum(pieces, d, lambda z: w_ref[z, 0])
        out_ref[spot_of(starts_ref, d, acc.shape[0]), :] = acc.astype(BF)


def mm_nt(pieces, w, first, rows, starts):
    nz, nc, _, width = w.shape
    total = 4 * pieces[0].shape[1]
    count, skip = rows // 256, first // 256
    return pl.pallas_call(
        nt_kernel,
        grid=(nc, count),
        in_specs=[pl.BlockSpec(memory_space=pltpu.SMEM)]
        + piece_specs(pieces)
        + [pl.BlockSpec((nz, 1, 256, width), lambda c, i: (0, c, skip + i, 0))],
        out_specs=pl.BlockSpec((total, 256), lambda c, i: (0, c * count + i)),
        out_shape=jax.ShapeDtypeStruct((total, nc * rows), BF),
        compiler_params=params(2),
        cost_estimate=cost(
            2 * nz * total * width * nc * rows, 2 * nz * width * (total + nc * rows) + 2 * total * nc * rows
        ),
        name="product_nt",
    )(starts, *pieces, w)


def nn_kernel(count, starts_ref, *refs):
    grads, (w_ref, low_out, low_keep, high_out, high_keep) = refs[:count], refs[count:]
    nc, rows, width = w_ref.shape[1:]
    t = grads[0].shape[0] // 4
    in_low = pl.program_id(0) < pl.num_programs(0) // 2

    def product(d):
        spot = spot_of(starts_ref, d, t)
        if count == 1:
            return dot_nn(grads[0][spot, :], w_ref[0].reshape(nc * rows, width)).astype(BF)
        return sum(dot_nn(grads[c][spot, :], w_ref[0, c]) for c in range(count)).astype(BF)

    @pl.when(in_low)
    def _():
        for d in range(4):
            (low_out if d // 2 else low_keep)[d % 2, 0] = product(d)

    @pl.when(jnp.logical_not(in_low))
    def _():
        for d in range(4):
            (high_out if d % 2 else high_keep)[d // 2, 0] = product(d)


def mm_nn(grads, w, first, rows, starts):
    total = grads[0].shape[0]
    nz, nc, _, width = w.shape
    skip, half, t = first // rows, nz // 2, total // 4
    low = pl.BlockSpec((2, 1, t, width), lambda z: (0, jnp.minimum(z, half - 1), 0, 0))
    high = pl.BlockSpec((2, 1, t, width), lambda z: (0, jnp.maximum(z - half, 0), 0, 0))
    return pl.pallas_call(
        functools.partial(nn_kernel, len(grads)),
        grid=(nz,),
        in_specs=[pl.BlockSpec(memory_space=pltpu.SMEM)]
        + [pl.BlockSpec(grad.shape, lambda z: (0, 0)) for grad in grads]
        + [pl.BlockSpec((1, nc, rows, width), lambda z: (z, 0, skip, 0))],
        out_specs=[low, low, high, high],
        out_shape=[jax.ShapeDtypeStruct((2, half, t, width), BF)] * 4,
        compiler_params=params(1),
        cost_estimate=cost(
            2 * nz * total * width * nc * rows, 2 * nz * width * (total + nc * rows) + 2 * total * nc * rows
        ),
        name="product_nn",
    )(starts, *grads, w)


def tn_kernel(count, starts_ref, *refs):
    grads, pieces, out_ref = refs[:count], refs[count:-1], refs[-1]
    half, t, _ = pieces[0].shape

    def one(grad_ref):
        turned = [grad_ref[spot_of(starts_ref, d, t), :].T for d in range(4)]
        for z in range(2 * half):
            acc = dot_nn(turned[0], pieces[4 * (z // half)][z % half])
            for d in range(1, 4):
                acc += dot_nn(turned[d], pieces[4 * (z // half) + d][z % half])
            out_ref[z] = acc.astype(BF)

    if count == 1:
        one(grads[0])
    else:
        for c in range(count):

            @pl.when(pl.program_id(0) // (pl.num_programs(0) // count) == c)
            def _():
                one(grads[c])


def mm_tn(grads, pieces, starts):
    total, rows = grads[0].shape
    half, _, width = pieces[0].shape
    nz, count = 2 * half, len(grads)
    block = next(b for b in (640, 384, 256) if rows % b == 0)
    steps = rows // block

    def spec(c):
        return pl.BlockSpec((total, block), lambda i: (0, jnp.clip(i - c * steps, 0, steps - 1)))

    return pl.pallas_call(
        functools.partial(tn_kernel, count),
        grid=(count * steps,),
        in_specs=[pl.BlockSpec(memory_space=pltpu.SMEM)]
        + [spec(c) for c in range(count)]
        + piece_specs(pieces),
        out_specs=pl.BlockSpec((nz, block, width), lambda i: (0, i, 0)),
        out_shape=jax.ShapeDtypeStruct((nz, count * rows, width), BF),
        compiler_params=params(1),
        cost_estimate=cost(
            2 * nz * total * width * count * rows, 2 * nz * width * (total + count * rows) + 2 * total * count * rows
        ),
        name="product_tn",
    )(starts, *grads, *pieces)


def gelu_parts(gate):
    curve = jnp.tanh(gelu_a * (gate + gelu_b * gate * gate * gate))
    value = 0.5 * gate * (1.0 + curve)
    slope = 0.5 * (1.0 + curve) + 0.5 * gate * (1.0 - curve * curve) * gelu_a * (
        1.0 + 3.0 * gelu_b * gate * gate
    )
    return value, slope


def ffn_in_kernel(starts_ref, *refs):
    pieces, (w_ref, gate_ref, up_ref, active_ref) = refs[:8], refs[8:]
    _, _, _, block, width = w_ref.shape
    for d in range(4):
        acc = nt_sum(pieces, d, lambda z: w_ref[z, 0].reshape(2 * block, width))
        spot = spot_of(starts_ref, d, acc.shape[0])
        gate, up = acc[:, :block], acc[:, block:]
        value = 0.5 * gate * (1.0 + jnp.tanh(gelu_a * (gate + gelu_b * gate * gate * gate)))
        gate_ref[spot, :] = gate.astype(BF)
        up_ref[spot, :] = up.astype(BF)
        active_ref[spot, :] = (value * up).astype(BF)


def ffn_in(pieces, w, starts):
    nz, nc, rows, width = w.shape
    half, total = rows // 2, 4 * pieces[0].shape[1]
    count = half // 128
    block = pl.BlockSpec((total, 128), lambda c, i: (0, c * count + i))
    return pl.pallas_call(
        ffn_in_kernel,
        grid=(nc, count),
        in_specs=[pl.BlockSpec(memory_space=pltpu.SMEM)]
        + piece_specs(pieces)
        + [pl.BlockSpec((nz, 1, 2, 128, width), lambda c, i: (0, c, 0, i, 0))],
        out_specs=[block, block, block],
        out_shape=[jax.ShapeDtypeStruct((total, nc * half), BF)] * 3,
        compiler_params=params(2),
        cost_estimate=cost(
            2 * nz * total * width * nc * rows, 2 * nz * width * (total + nc * rows) + 3 * total * nc * rows
        ),
        name="ffn_in",
    )(starts, *pieces, w.reshape(nz, nc, 2, half, width))


def ffn_back_kernel(starts_ref, *refs):
    pieces, (w_ref, gate_ref, up_ref, out_ref) = refs[:8], refs[8:]
    half = w_ref.shape[2]
    for d in range(4):
        acc = nt_sum(pieces, d, lambda z: w_ref[z, 0])
        spot = spot_of(starts_ref, d, acc.shape[0])
        value, slope = gelu_parts(gate_ref[spot, :].astype(F32))
        out_ref[spot, :half] = (acc * up_ref[spot, :].astype(F32) * slope).astype(BF)
        out_ref[spot, half:] = (acc * value).astype(BF)


def ffn_back(pieces, w, gate, up, starts):
    nz, nc, half, width = w.shape
    total = gate.shape[0]
    kept = pl.BlockSpec((total, half), lambda c: (0, c))
    return pl.pallas_call(
        ffn_back_kernel,
        grid=(nc,),
        in_specs=[pl.BlockSpec(memory_space=pltpu.SMEM)]
        + piece_specs(pieces)
        + [pl.BlockSpec((nz, 1, half, width), lambda c: (0, c, 0, 0)), kept, kept],
        out_specs=pl.BlockSpec((total, 2 * half), lambda c: (0, c)),
        out_shape=jax.ShapeDtypeStruct((total, nc * 2 * half), BF),
        compiler_params=params(1),
        cost_estimate=cost(
            2 * nz * total * width * nc * half, 2 * nz * width * (total + nc * half) + 8 * total * nc * half
        ),
        name="ffn_back",
    )(starts, *pieces, w, gate, up)


def mm_nt_plain(act, w, first, rows, starts):
    part = lax.slice_in_dim(w, first, first + rows, axis=2)
    out = jnp.einsum("ztf,zcrf->tcr", act, part, preferred_element_type=F32)
    return out.astype(BF).reshape(act.shape[1], -1)


def mm_nn_plain(grads, w, first, rows, starts):
    grad = grads[0]
    part = lax.slice_in_dim(w, first, first + rows, axis=2)
    split = grad.reshape(grad.shape[0], w.shape[1], rows)
    out = jnp.einsum("tcr,zcrf->ztf", split, part, preferred_element_type=F32)
    return [out.astype(BF)]


def mm_tn_plain(grads, act, starts):
    return jnp.einsum("tr,ztf->zrf", grads[0], act, preferred_element_type=F32).astype(BF)


def ffn_in_plain(act, w, starts):
    _, nc, rows, _ = w.shape
    total = act.shape[1]
    both = jnp.einsum("ztf,zcrf->tcr", act, w, preferred_element_type=F32)
    gate, up = both[:, :, : rows // 2], both[:, :, rows // 2 :]
    value, _ = gelu_parts(gate)
    return [part.astype(BF).reshape(total, -1) for part in (gate, up, value * up)]


def ffn_back_plain(act, w, gate, up, starts):
    total, nc = gate.shape[0], w.shape[1]
    grad = jnp.einsum("ztf,zcrf->tcr", act, w, preferred_element_type=F32)
    value, slope = gelu_parts(gate.astype(F32).reshape(grad.shape))
    both = [grad * up.astype(F32).reshape(grad.shape) * slope, grad * value]
    return jnp.concatenate(both, axis=2).astype(BF).reshape(total, -1)


def near_buckets(tile, total):
    first = (total // LB - 2 + tile) * LB
    rows = lax.broadcasted_iota(jnp.int32, (LB, LB), 0)
    lanes = lax.broadcasted_iota(jnp.int32, (LB, LB), 1)
    return bucket_index(first + rows - (total - LB) - lanes)


def near_kernel(total, table_ref, out_ref):
    heads = out_ref.shape[0]

    def one_tile(tile, _):
        index = near_buckets(tile, total)
        vals = [jnp.full((LB, LB), table_ref[h, 0], F32) for h in range(heads)]
        for b in range(1, 32):
            hit = index == b
            vals = [jnp.where(hit, table_ref[h, b], vals[h]) for h in range(heads)]
        for h in range(heads):
            out_ref[h, pl.ds(pl.multiple_of(tile * LB, LB), LB)] = vals[h]
        return 0

    lax.fori_loop(0, 3, one_tile, 0)


def near_bias(table, total):
    heads = table.shape[0]
    return pl.pallas_call(
        functools.partial(near_kernel, total),
        in_specs=[pl.BlockSpec(memory_space=pltpu.SMEM)],
        out_specs=pl.BlockSpec((heads, 3 * LB, LB), lambda: (0, 0, 0)),
        out_shape=jax.ShapeDtypeStruct((heads, 3 * LB, LB), F32),
        compiler_params=params(0),
        cost_estimate=cost(0, heads * LB * LB),
        name="near_bias",
    )(table)


def build_strips(table_ref, near_ref, strip_ref, total, group):
    heads = strip_ref.shape[0]
    near = (total // LB - 2) * LB
    for h in range(heads):
        head = group * heads + h
        strip_ref[h, :near] = jnp.full((near, LB), table_ref[head, 15], F32)
        strip_ref[h, near : near + 3 * LB] = near_ref[h]
        strip_ref[h, near + 3 * LB :] = jnp.full((near, LB), table_ref[head, 31], F32)


def table_kernel(total, *refs):
    parts, out_ref = refs[:-1], refs[-1]
    index = [near_buckets(tile, total) for tile in range(3)]
    buckets = [range(1, 16), [b for b in range(32) if b != 16], range(17, 32)]
    for g, part_ref in enumerate(parts):
        heads = part_ref.shape[0]

        def one_head(h, _):
            here = g * heads + h
            out_ref[here] = jnp.zeros((32, LB), F32)
            out_ref[here, 15:16] = part_ref[h, 3 * LB : 3 * LB + 1]
            out_ref[here, 31:32] = part_ref[h, 3 * LB + 8 : 3 * LB + 9]
            for tile in range(3):
                grads = part_ref[h, tile * LB : (tile + 1) * LB]
                for b in buckets[tile]:
                    picked = jnp.where(index[tile] == b, grads, 0.0)
                    out_ref[here, b : b + 1] += jnp.sum(picked, axis=0, keepdims=True)
            return 0

        lax.fori_loop(0, heads, one_head, 0)


def table_sums(parts, total):
    heads = len(parts) * parts[0].shape[0]
    out = pl.pallas_call(
        functools.partial(table_kernel, total),
        in_specs=[pl.BlockSpec(part.shape, lambda: (0, 0, 0)) for part in parts],
        out_specs=pl.BlockSpec((heads, 32, LB), lambda: (0, 0, 0)),
        out_shape=jax.ShapeDtypeStruct((heads, 32, LB), F32),
        compiler_params=params(0),
        cost_estimate=cost(0, heads * LB * LB),
        name="table_sums",
    )(*parts)
    return jnp.sum(out, axis=2)


def head_lanes(shape, h):
    lanes = lax.broadcasted_iota(jnp.int32, shape, 1)
    return lanes // 64 == h, lanes == ((h + 1) % 4) * 64


def mask_keys(keys, length, h):
    own, spare = head_lanes(keys.shape, h)
    dead = lax.broadcasted_iota(jnp.int32, keys.shape, 0) >= length
    mask = jnp.where(jnp.logical_and(spare, dead), masked_score, 0.0)
    return jnp.where(own, keys.astype(F32), mask).astype(BF)


def with_one(queries, h):
    _, spare = head_lanes(queries.shape, h)
    return jnp.where(spare, 1.0, queries.astype(F32)).astype(BF)


def own_lanes(values, h):
    own, _ = head_lanes(values.shape, h)
    return jnp.where(own, values.astype(F32), 0.0).astype(BF)


def block_bias(strip_ref, h, block, total):
    first = total - LB - 2 * block * LB
    left = strip_ref[h, pl.ds(pl.multiple_of(first, LB), total)]
    right = strip_ref[h, pl.ds(pl.multiple_of(first - LB, LB), total)]
    return jnp.concatenate([left, right], axis=1)


def attend_kernel(group, length_ref, table_ref, near_ref, q_ref, k_ref, v_ref, out_ref, lse_ref, strip, heads_k, turned_v, turned_out):
    total = q_ref.shape[0]
    heads = strip.shape[0]
    build_strips(table_ref, near_ref, strip, total, group)
    turned_v[...] = v_ref[...].astype(F32).T.astype(BF)
    for h in range(heads):
        heads_k[h] = mask_keys(k_ref[...], length_ref[0], h)

    def one_block(block, _):
        spot = pl.ds(pl.multiple_of(block * 256, 256), 256)
        queries = q_ref[spot]
        for h in range(heads):
            scores = dot_nt(heads_k[h], with_one(queries, h)) + block_bias(strip, h, block, total)
            largest = jnp.max(scores, axis=0, keepdims=True)
            raised = jnp.exp(scores - largest)
            totals = jnp.sum(raised, axis=0, keepdims=True)
            out = dot_nn(turned_v[h * 64 : (h + 1) * 64], raised.astype(BF))
            turned_out[h * 64 : (h + 1) * 64, spot] = out * (1.0 / totals)
            lse_ref[h : h + 1, spot] = largest + jnp.log(totals)
        return 0

    lax.fori_loop(0, total // 256, one_block, 0)
    out_ref[...] = turned_out[...].T.astype(BF)


def attend_back_kernel(
    group, length_ref, table_ref, near_ref, q_ref, k_ref, v_ref, grad_ref, lse_ref, out_ref, table_grad_ref,
    strip, strip_grad, heads_k, turned_k, turned_q, ds_ref, p_ref, dk_ref, dv_ref,
):
    total = q_ref.shape[0]
    heads = strip.shape[0]
    build_strips(table_ref, near_ref, strip, total, group)
    strip_grad[...] = jnp.zeros_like(strip_grad)
    dk_ref[...] = jnp.zeros_like(dk_ref)
    dv_ref[...] = jnp.zeros_like(dv_ref)
    turned_k[...] = k_ref[...].astype(F32).T.astype(BF)
    for h in range(heads):
        heads_k[h] = mask_keys(k_ref[...], length_ref[0], h)

    def one_block(block, _):
        spot = pl.ds(pl.multiple_of(block * 256, 256), 256)
        queries, grads = q_ref[spot], grad_ref[spot]
        own_q, own_g = [], []
        for h in range(heads):
            own_q.append(own_lanes(queries, h))
            own_g.append(own_lanes(grads, h))
            scores = dot_nt(heads_k[h], with_one(queries, h)) + block_bias(strip, h, block, total)
            probs = jnp.exp(scores - lse_ref[h : h + 1, spot])
            weighed = probs * dot_nt(v_ref[...], own_g[h])
            delta = jnp.sum(weighed, axis=0, keepdims=True)
            grad_scores = weighed - probs * delta
            first = total - LB - 2 * block * LB
            left = pl.ds(pl.multiple_of(first, LB), total)
            right = pl.ds(pl.multiple_of(first - LB, LB), total)
            strip_grad[h, left] += grad_scores[:, :LB]
            strip_grad[h, right] += grad_scores[:, LB:]
            rounded = grad_scores.astype(BF)
            ds_ref[:, h * 256 : (h + 1) * 256] = rounded
            p_ref[:, h * 256 : (h + 1) * 256] = probs.astype(BF)
            turned_q[h * 64 : (h + 1) * 64, spot] = dot_nn(turned_k[h * 64 : (h + 1) * 64], rounded)
        dk_ref[...] += dot_nn(ds_ref[...], jnp.concatenate(own_q, axis=0))
        dv_ref[...] += dot_nn(p_ref[...], jnp.concatenate(own_g, axis=0))
        return 0

    lax.fori_loop(0, total // 256, one_block, 0)
    out_ref[:, :256] = turned_q[...].T.astype(BF)
    out_ref[:, 256:512] = dk_ref[...].astype(BF)
    out_ref[:, 512:] = dv_ref[...].astype(BF)

    near = (total // LB - 2) * LB
    for h in range(heads):
        table_grad_ref[h, : 3 * LB] = strip_grad[h, near : near + 3 * LB]
        left = jnp.sum(strip_grad[h, :near], axis=0, keepdims=True)
        right = jnp.sum(strip_grad[h, near + 3 * LB :], axis=0, keepdims=True)
        table_grad_ref[h, 3 * LB : 3 * LB + 8] = jnp.broadcast_to(left, (8, LB))
        table_grad_ref[h, 3 * LB + 8 :] = jnp.broadcast_to(right, (8, LB))


def block_specs(total, group):
    def spec(i):
        return pl.BlockSpec((total, 256), lambda _: (0, 3 * group + i))

    smem = pl.BlockSpec(memory_space=pltpu.SMEM)
    near = pl.BlockSpec((4, 3 * LB, LB), lambda _: (group, 0, 0))
    return [smem, smem, near, spec(0), spec(1), spec(2)]


def attend(group, projected, length, table, near):
    total = projected.shape[0]
    heads = 4
    return pl.pallas_call(
        functools.partial(attend_kernel, group),
        grid=(1,),
        in_specs=block_specs(total, group),
        out_specs=[
            pl.BlockSpec((total, 256), lambda _: (0, 0)),
            pl.BlockSpec((8, total), lambda _: (0, 0)),
        ],
        out_shape=[
            jax.ShapeDtypeStruct((total, 256), BF),
            jax.ShapeDtypeStruct((8, total), F32),
        ],
        scratch_shapes=[
            pltpu.VMEM((heads, 2 * total - LB, LB), F32),
            pltpu.VMEM((heads, total, 256), BF),
            pltpu.VMEM((256, total), BF),
            pltpu.VMEM((256, total), F32),
        ],
        compiler_params=params(1),
        cost_estimate=cost(heads * total * total * 2 * 256 * 2, 4 * total * 256 * 2),
        name="attend",
    )(length, table, near, projected, projected, projected)


def attend_back(group, projected, length, table, near, grad_out, lse):
    total = projected.shape[0]
    heads = 4
    return pl.pallas_call(
        functools.partial(attend_back_kernel, group),
        grid=(1,),
        in_specs=block_specs(total, group)
        + [
            pl.BlockSpec((total, 256), lambda _: (0, group)),
            pl.BlockSpec((8, total), lambda _: (0, 0)),
        ],
        out_specs=[
            pl.BlockSpec((total, 768), lambda _: (0, 0)),
            pl.BlockSpec((heads, 3 * LB + 16, LB), lambda _: (0, 0, 0)),
        ],
        out_shape=[
            jax.ShapeDtypeStruct((total, 768), BF),
            jax.ShapeDtypeStruct((heads, 3 * LB + 16, LB), F32),
        ],
        scratch_shapes=[
            pltpu.VMEM((heads, 2 * total - LB, LB), F32),
            pltpu.VMEM((heads, 2 * total - LB, LB), F32),
            pltpu.VMEM((heads, total, 256), BF),
            pltpu.VMEM((256, total), BF),
            pltpu.VMEM((256, total), F32),
            pltpu.VMEM((total, heads * 256), BF),
            pltpu.VMEM((total, heads * 256), BF),
            pltpu.VMEM((total, 256), F32),
            pltpu.VMEM((total, 256), F32),
        ],
        compiler_params=params(1),
        cost_estimate=cost(heads * total * total * 2 * 256 * 5, 8 * total * 256 * 2),
        name="attend_back",
    )(length, table, near, projected, projected, projected, grad_out, lse)


def split_heads(projected, groups, heads):
    parts = projected.reshape(projected.shape[0], groups, 3, heads, 64)
    return [parts[:, :, i].reshape(projected.shape[0], groups * heads, 64) for i in range(3)]


def plain_scores(queries, keys, length, table):
    slots = jnp.arange(keys.shape[0], dtype=jnp.int32)
    picked = (bucket_index(slots[None, :] - slots[:, None])[:, :, None] == jnp.arange(32)).astype(F32)
    bias = jnp.einsum("qkb,hb->hqk", picked, table, precision=lax.Precision.HIGHEST)
    scores = jnp.einsum("qhs,khs->hqk", queries, keys, preferred_element_type=F32) + bias
    return jnp.where(slots < length[0], scores, masked_score), picked


def attend_plain(projected, length, table, groups, heads):
    queries, keys, values = split_heads(projected, groups, heads)
    scores, _ = plain_scores(queries, keys, length, table)
    lse = jax.nn.logsumexp(scores, axis=2)
    probs = jnp.exp(scores - lse[:, :, None]).astype(BF)
    out = jnp.einsum("hqk,khs->qhs", probs, values, preferred_element_type=F32)
    return out.astype(BF).reshape(projected.shape[0], -1), lse


def attend_back_plain(projected, length, table, grad_out, lse, groups, heads):
    total = projected.shape[0]
    queries, keys, values = split_heads(projected, groups, heads)
    grads = grad_out.reshape(queries.shape)
    scores, picked = plain_scores(queries, keys, length, table)
    probs = jnp.exp(scores - lse[:, :, None])
    weighed = probs * jnp.einsum("qhs,khs->hqk", grads, values, preferred_element_type=F32)
    wide = weighed - probs * jnp.sum(weighed, axis=2, keepdims=True)
    rounded = wide.astype(BF)
    parts = [
        jnp.einsum("hqk,khs->qhs", rounded, keys, preferred_element_type=F32),
        jnp.einsum("hqk,qhs->khs", rounded, queries, preferred_element_type=F32),
        jnp.einsum("hqk,qhs->khs", probs.astype(BF), grads, preferred_element_type=F32),
    ]
    parts = [part.astype(BF).reshape(total, groups, 1, heads * 64) for part in parts]
    table_grad = jnp.einsum("hqk,qkb->hb", wide, picked, precision=lax.Precision.HIGHEST)
    return (
        jnp.concatenate(parts, axis=2).reshape(total, -1),
        table_grad.reshape(groups * heads, 32, 1),
    )


def hop(value, axis):
    return lax.ppermute(value, axis, swap)


def pick(value, index, axis):
    return lax.dynamic_index_in_dim(value, index, axis, keepdims=False)


def paired(mine, other, axis, place=0):
    return jnp.where(
        lax.axis_index(axis) == 0,
        jnp.stack([mine, other], axis=place),
        jnp.stack([other, mine], axis=place),
    )


def after(value, *others):
    return lax.optimization_barrier((value, *others))[0]


def gather_plain(part, *beside):
    return lax.all_gather(part, ("x", "y"), axis=1, tiled=True), (), ()


def gather_tokens(part, *beside):
    half = part.shape[0] // 2
    low, high = part[:half], part[half:]
    low_x, high_y = hop(low, "x"), hop(high, "y")
    if beside:
        low_x, high_y = after(low_x, *beside), after(high_y, *beside)
    low_y, high_x = hop(low, "y"), hop(high, "x")
    low_xy, high_xy = hop(low_x, "y"), hop(high_y, "x")
    pieces = [low, low_y, low_x, low_xy, high, high_y, high_x, high_xy]
    return pieces, (low_x, high_y), (low_y, low_xy, high_x, high_xy)


def scatter_plain(parts, beside=(), beside_last=()):
    whole = parts[0].astype(F32)
    return lax.psum_scatter(whole, ("x", "y"), scatter_dimension=1, tiled=True), (), ()


def scatter_tokens(parts, beside=(), beside_last=()):
    low_out, low_keep, high_out, high_keep = parts
    low_in, high_in = hop(low_out, "x"), hop(high_out, "y")
    if beside:
        low_in, high_in = after(low_in, *beside), after(high_in, *beside)

    def add(keep, arrived, index):
        return keep[index].astype(F32) + arrived[index].astype(F32)

    low_last = hop(add(low_keep, low_in, 1).astype(BF), "y")
    high_last = hop(add(high_keep, high_in, 1).astype(BF), "x")
    if beside_last:
        low_last, high_last = after(low_last, *beside_last), after(high_last, *beside_last)
    low = add(low_keep, low_in, 0) + low_last.astype(F32)
    high = add(high_keep, high_in, 0) + high_last.astype(F32)
    return jnp.concatenate([low, high], axis=0), (low_in, high_in), (low_last, high_last)


def place_kernel(write, here_ref, *refs):
    pieces, outs = refs[:4], refs[4:]
    step = pl.program_id(0)
    for near in range(4):
        y = here_ref[0] if near < 2 else 1 - here_ref[0]
        c = here_ref[1] if near % 2 == 0 else 1 - here_ref[1]

        @pl.when(step == 2 * y + c)
        def _():
            write(pieces[near], outs)


def place(pieces, here, shapes, write):
    return pl.pallas_call(
        functools.partial(place_kernel, write),
        grid=(4,),
        in_specs=[pl.BlockSpec(memory_space=pltpu.SMEM)]
        + [pl.BlockSpec(piece.shape, lambda q: (0, 0)) for piece in pieces],
        out_specs=[
            pl.BlockSpec(shape, lambda q, rank=len(shape): (q,) + (0,) * (rank - 1)) for shape in shapes
        ],
        out_shape=[jax.ShapeDtypeStruct((4 * shape[0], *shape[1:]), F32) for shape in shapes],
        compiler_params=params(1),
        cost_estimate=cost(0, pieces[0].size),
        name="place",
    )(here, *pieces)


def share(part, *beside):
    over_y = hop(part, "y")
    if beside:
        over_y = after(over_y, *beside)
    return [part, hop(part, "c"), over_y, hop(over_y, "c")], over_y


def share_plain(part):
    return lax.all_gather(part, ("y", "c"), axis=0), part


def to_groups(halves, other, extra):
    count, _, t, width = halves.shape
    both = paired(pick(halves, lax.axis_index("y"), 1), other, "y").reshape(2 * count, t, width)
    if extra is not None:
        wide = jnp.broadcast_to(extra[None], (2 * count, *extra.shape))
        both = jnp.concatenate([both, wide], axis=1)
    return lax.all_to_all(both, "z", 0, 0, tiled=True)


def from_groups(mine):
    nz, t, width = mine.shape
    back = lax.all_to_all(mine, "z", 0, 0, tiled=True).reshape(2, nz // 2, t, width)
    leaving = pick(back, 1 - lax.axis_index("y"), 0)
    return (back, hop(leaving, "y")), leaving


def settle_kernel(y_ref, back_ref, other_ref, out_ref):
    j, y = pl.program_id(0), pl.program_id(1)

    @pl.when(y == y_ref[0])
    def _():
        out_ref[0, 0] = back_ref[y, j].astype(out_ref.dtype)

    @pl.when(y != y_ref[0])
    def _():
        out_ref[0, 0] = other_ref[j].astype(out_ref.dtype)


def settle(arrived, dtype):
    back, other = arrived
    _, count, t, width = back.shape
    y = lax.axis_index("y").astype(jnp.int32).reshape(1)
    out = pl.pallas_call(
        settle_kernel,
        grid=(count, 2),
        in_specs=[
            pl.BlockSpec(memory_space=pltpu.SMEM),
            pl.BlockSpec(back.shape, lambda j, y: (0, 0, 0, 0)),
            pl.BlockSpec(other.shape, lambda j, y: (0, 0, 0)),
        ],
        out_specs=pl.BlockSpec((1, 1, t, width), lambda j, y: (j, y, 0, 0)),
        out_shape=jax.ShapeDtypeStruct((count, 2, t, width), dtype),
        compiler_params=params(2),
        cost_estimate=cost(0, count * t * width),
        name="settle",
    )(y, back, other)
    return out.reshape(count, 2 * t, width)


def settle_plain(arrived, dtype):
    back, other = arrived
    _, count, t, width = back.shape
    both = paired(pick(back, lax.axis_index("y"), 0), other, "y")
    return both.transpose(1, 0, 2, 3).reshape(count, 2 * t, width).astype(dtype)


def sum_plane(value, nx, *earlier):
    value = value + after(hop(value, "c"), *earlier)
    value = value + hop(value, "x") if nx == 2 else lax.psum(value, "x")
    return value + hop(value, "y")


def sum_line(value, nz):
    step = 1
    while step < nz:
        value = value + lax.ppermute(value, "z", [(i, i ^ step) for i in range(nz)])
        step *= 2
    return value


def body(
    nx, nz, nc, inputs, lengths, attn_gain, ffn_gain, query_key, value_proj, out_proj, gate_up, down_proj, bias_table, cotangent
):
    x, y = lax.axis_index("x"), lax.axis_index("y")
    c, z = lax.axis_index("c"), lax.axis_index("z")
    width = inputs.shape[2]
    features = nz * width
    quarter = y * nc + c
    parts = 2 * nc
    buckets, mine = bias_table.shape
    count = inputs.shape[1] // 2

    stored_in = inputs.reshape(inputs.shape[0], 2, count, width)
    stored_cot = cotangent.reshape(stored_in.shape)
    small = jnp.concatenate(
        [attn_gain[None], ffn_gain[None], jnp.pad(bias_table.reshape(1, -1), ((0, 0), (0, width - buckets * mine)))]
    )
    small = jnp.pad(small, ((0, 5), (0, 0)))
    leaving = pick(stored_in, 1 - y, 1)

    query_key_rows = jnp.transpose(query_key, (1, 2, 3, 0))
    value_rows = jnp.transpose(value_proj, (1, 2, 0))
    gate_up_rows = jnp.transpose(gate_up, (1, 2, 3, 0))
    heads = value_rows.shape[0] // parts
    units = gate_up_rows.shape[0] // parts
    unit = gate_up_rows.shape[2]
    local_heads = nc * heads

    def own(rows, size):
        return lax.dynamic_slice_in_dim(rows, quarter * size, size, 0)

    def flat(rows):
        return rows.reshape(-1, width)

    def spread(rows):
        gathered = lax.all_gather(rows, ("z", "c"), axis=0, tiled=True)
        return gathered.reshape(nz, nc, rows.shape[0], width)

    own_pair = own(query_key_rows, heads)
    own_attn = [own_pair[:, 0], own_pair[:, 1], own(value_rows, heads), own(out_proj, heads)]
    own_attn = jnp.concatenate([flat(rows) for rows in own_attn])
    w_attn = spread(own_attn)
    other = after(hop(leaving, "y"), own_attn)
    own_pair = own(after(gate_up_rows, other), units)
    own_gate_up = jnp.concatenate([flat(own_pair[:, 0]), flat(own_pair[:, 1])])
    w_gate_up = spread(own_gate_up)
    own_down = flat(own(after(down_proj, other), units))
    w_down = spread(own_down)
    qkv_count, out_count = 3 * heads * 64, heads * 64

    both_lengths = jnp.stack([lengths, lax.ppermute(lengths, "y", swap)])
    both_lengths = jnp.where(y == 0, both_lengths, both_lengths[::-1]).reshape(-1)
    length = lax.dynamic_slice_in_dim(both_lengths, z, 1, 0)
    slots = (x * 2 + y) * count + jnp.arange(count, dtype=jnp.int32)
    near_x, near_y = jnp.array([0, 0, 1, 1]) ^ x, jnp.array([0, 1, 0, 1]) ^ y
    starts = ((near_x * 2 + near_y) * count).astype(jnp.int32)
    arrived = after(to_groups(stored_in, other, small), own_gate_up, own_down, length, starts)
    tokens = arrived[:, :count].astype(F32)
    small = arrived[:, count:]
    gain_one = small[:, :1].astype(F32)
    gain_two = small[:, 1:2].astype(F32)
    table = small[:, 2, : buckets * mine].reshape(nz, buckets, mine).transpose(0, 2, 1)
    table = table.reshape(-1, buckets).astype(F32)
    table = lax.dynamic_slice_in_dim(table, y * local_heads, local_heads, 0)

    live = (slots < length).astype(F32)[None, :, None]

    def scale_of(values):
        squares = jnp.sum(values * values, axis=(0, 2), keepdims=True)
        return lax.rsqrt(squares / features + norm_eps)

    def norm_back(values, scale, gain, grad):
        inner = jnp.sum(values * gain * grad, axis=(0, 2), keepdims=True)
        out = scale * gain * grad - values * (scale * scale * scale) * inner / features
        return out, jnp.sum(values * scale * grad, axis=1)

    def reduce(partial):
        rows = partial.reshape(nz * partial.shape[1], width)
        return lax.psum_scatter(rows, ("z", "c"), scatter_dimension=0, tiled=True)

    fits = nx == 2 and heads == 4 and count == 256 and units * unit % 640 == 0 and nz % 2 == 0
    if fits:
        forward, backward, gather, scatter = attend, attend_back, gather_tokens, scatter_tokens
        nt, nn, tn, ffn_one, ffn_two = mm_nt, mm_nn, mm_tn, ffn_in, ffn_back
        shared, stored_from = share, settle
    else:
        forward, backward, gather, scatter = attend_plain, attend_back_plain, gather_plain, scatter_plain
        nt, nn, tn, ffn_one, ffn_two = mm_nt_plain, mm_nn_plain, mm_tn_plain, ffn_in_plain, ffn_back_plain
        shared, stored_from = share_plain, settle_plain
    scale_one = scale_of(tokens)
    near = near_bias(table, 4 * count) if fits else table
    normed, _, _ = gather((tokens * scale_one * gain_one).astype(BF), near, live)
    cot_other = hop(pick(stored_cot, 1 - y, 1), "y")
    upstream = live * to_groups(stored_cot, after(cot_other, arrived), None).astype(F32)
    upstream_rounded = after(upstream.astype(BF), w_attn)
    projected = nt(normed, w_attn, 0, qkv_count, starts)
    if fits:
        first = forward(0, projected, length, table, near)
        grad_ffn, cot_first, cot_last = gather(upstream_rounded, first[0])
        second = forward(1, after(projected, first[0], *cot_first), length, table, near)
        attended, lse = (first[0], second[0]), (first[1], second[1])
    else:
        grad_ffn, _, cot_last = gather(upstream_rounded)
        attended, lse = forward(projected, length, table, nc, heads)
        attended = (attended,)
    heads_out = [after(attended[0], *cot_last), *attended[1:]]
    hidden = tokens + scatter(nn(heads_out, w_attn, qkv_count, out_count, starts))[0]
    scale_two = scale_of(hidden)
    normed_two, _, _ = gather((hidden * scale_two * gain_two).astype(BF))
    gate, up, activated = ffn_one(normed_two, w_gate_up, starts)

    down_partial = tn([activated], grad_ffn, starts)
    down_part = reduce(down_partial)
    grad_gate_up = ffn_two(grad_ffn, w_down, after(gate, down_partial), up, starts)
    two_parts = nn([grad_gate_up], w_gate_up, 0, 2 * units * unit, starts)
    grad_two, two_first, _ = scatter(two_parts)
    gate_up_partial = tn([after(grad_gate_up, two_parts[0])], normed_two, starts)
    gate_up_part = reduce(after(gate_up_partial, down_part, *two_first))
    branch_parts = nn([after(activated, gate_up_partial)], w_down, 0, units * unit, starts)
    through, ffn_gain_part = norm_back(hidden, scale_two, gain_two, grad_two)
    grad_hidden = upstream + through
    grad_branch, _, branch_here = gather(after(grad_hidden.astype(BF), branch_parts[0]))
    grad_attended = nt(grad_branch, w_attn, qkv_count, out_count, starts)
    out_partial = tn(attended, grad_branch, starts)
    grad_attended = after(grad_attended, out_partial)
    branch_parts = [after(part, *branch_here) for part in branch_parts]
    down_pieces, down_last = shared(after(down_part, *branch_here))
    if fits:
        first = backward(0, projected, length, table, near, grad_attended, lse[0])
        branch, branch_first, branch_last = scatter(branch_parts, (first[0], down_last))
    else:
        branch, branch_first, branch_last = scatter(branch_parts)
    if fits:
        second = backward(
            1, after(projected, first[0], *branch_last), length, table, near, grad_attended, lse[1]
        )
        grad_projected, table_part = (first[0], second[0]), (first[1], second[1])
    else:
        grads, table_part = backward(projected, length, table, grad_attended, lse, nc, heads)
        grad_projected, table_part = (grads,), table_part[:, :, 0]
    out_part = reduce(after(out_partial, gate_up_part, grad_projected[0], *branch_last))
    outputs = (live * (hidden + branch)).astype(BF)
    outputs, _ = from_groups(outputs)
    qkv_partial = tn(grad_projected, normed, starts)
    gate_up_pieces, gate_up_last = shared(after(gate_up_part, grad_projected[0]))
    qkv_part = reduce(after(qkv_partial, out_part, gate_up_last, outputs[0]))
    one_parts = nn(grad_projected, w_attn, 0, qkv_count, starts)
    if fits:
        here = jnp.stack([y, c]).astype(jnp.int32)

        def write_rows(source, outs):
            outs[0][...] = source[...].astype(F32)

        def write_qkv(source, outs):
            for h in range(heads):
                for i in range(3):
                    value = source[(i * heads + h) * 64 : (i * heads + h + 1) * 64, :].astype(F32)
                    if i == 2:
                        outs[1][h] = value
                    else:
                        outs[0][h, i] = value

        def write_gate_up(source, outs):
            for u in range(units):
                for i in range(2):
                    first = (i * units + u) * unit
                    outs[0][u, i] = source[first : first + unit, :].astype(F32)

        down_pieces = [after(down_pieces[0], outputs[1]), *down_pieces[1:]]
        (down_all,) = place(down_pieces, here, [(units * unit, width)], write_rows)
        (gate_up_all,) = place(gate_up_pieces, here, [(units, 2, unit, width)], write_gate_up)
    beside = (down_all, gate_up_all, outputs[0]) if fits else ()
    table_part = table_sums(table_part, 4 * count) if fits else table_part
    grad_one, _, one_last = scatter(one_parts, beside, (table_part,))
    through, attn_gain_part = norm_back(tokens, scale_one, gain_one, grad_one)
    input_grad, input_leaves = from_groups((grad_hidden + through).astype(BF))

    out_pieces, out_last = shared(out_part)

    every = jnp.zeros((nx * 2 * local_heads, table_part.shape[1]), F32)
    every = lax.dynamic_update_slice_in_dim(every, table_part, (x * 2 + y) * local_heads, 0)
    spare = -every.size % width
    every = jnp.pad(every.reshape(-1), (0, spare)).reshape(-1, width)
    sums = sum_plane(jnp.concatenate([attn_gain_part, ffn_gain_part, every]), nx, out_last)
    all_sums = sum_line(after(sums, input_leaves), nz)
    attn_gain_grad, ffn_gain_grad = all_sums[:nz], all_sums[nz : 2 * nz]
    every = all_sums[2 * nz :].reshape(-1)[: nx * 2 * local_heads * buckets].reshape(-1, buckets)

    outputs = stored_from(outputs, BF)
    if fits:
        (out_all,) = place(out_pieces, here, [(heads * 64, width)], write_rows)
        qkv_pieces, _ = shared(after(qkv_part, sums, *one_last), out_all, outputs)
        query_key_all, value_all = place(
            qkv_pieces, here, [(heads, 2, 64, width), (heads, 64, width)], write_qkv
        )
    else:
        down_all, out_all = down_pieces.astype(F32), out_pieces.astype(F32)
        gate_up_all = gate_up_pieces.astype(F32).reshape(parts, 2, units, unit, width)
        gate_up_all = gate_up_all.transpose(0, 2, 1, 3, 4).reshape(-1, 2, unit, width)
        qkv_all = shared(qkv_part)[0].astype(F32).reshape(parts, 3, heads, 64, width)
        qkv_all = qkv_all.transpose(0, 2, 1, 3, 4).reshape(-1, 3, 64, width)
        query_key_all, value_all = qkv_all[:, :2], qkv_all[:, 2]
    back, other = input_grad
    input_grad = stored_from((back, after(other, query_key_all)), F32)
    down_all, out_all = down_all.reshape(down_proj.shape), out_all.reshape(out_proj.shape)

    table_grad = lax.dynamic_slice_in_dim(every, (x * nz + z) * mine, mine, 0).T
    return (
        outputs,
        input_grad,
        pick(attn_gain_grad, z, 0),
        pick(ffn_gain_grad, z, 0),
        query_key_all.transpose(3, 0, 1, 2),
        value_all.transpose(2, 0, 1),
        out_all,
        gate_up_all.transpose(3, 0, 1, 2),
        down_all,
        table_grad,
    )


def solution(mesh):
    dp, nx, nz = (mesh.shape[name] for name in ("dp", "gx", "gy"))
    nc = dp // 2
    split = Mesh(mesh.devices.reshape(2, nc, nx, nz), ("y", "c", "x", "z"))
    seq = ("y", "c")
    return jax.shard_map(
        functools.partial(body, nx, nz, nc),
        mesh=split,
        in_specs=(
            P(seq, "x", "z"),
            P(seq),
            P("z"),
            P("z"),
            P("z", "x", None, None),
            P("z", "x", None),
            P("x", None, "z"),
            P("z", "x", None, None),
            P("x", None, "z"),
            P(None, ("x", "z")),
            P(seq, "x", "z"),
        ),
        out_specs=(
            P(seq, "x", "z"),
            P(seq, "x", "z"),
            P("z"),
            P("z"),
            P("z", "x", None, None),
            P("z", "x", None),
            P("x", None, "z"),
            P("z", "x", None, None),
            P("x", None, "z"),
            P(None, ("x", "z")),
        ),
        check_vma=False,
    )
```
